32 devices in a mesh: gx: 4 (over z), gy: 2 (over x), gz: 4 (over y, core).
Axes of the slice: x: 2, y: 2, z: 4, core: 2. Of those that a mesh axis runs over, the one named last changes fastest.
Arguments:
- features: bfloat16 [32, 16, 16, 256], P('gx', 'gy', 'gz'), may hold values from -64 to 64
- occupancy: int32 [4, 2, 16], P(None, 'gy', 'gz'), may hold values from 0 to 1, as said below
- norm_gain: float32 [2, 32], replicated, may hold values from 0.1 to 1.9
- norm_shift: float32 [2, 32], replicated, may hold values from -3 to 3
- conv_weight: bfloat16 [2, 32, 864], replicated, may hold values from -0.21875 to 0.21875
- conv_bias: float32 [2, 32], replicated, may hold values from -3 to 3
- qkv_weight: bfloat16 [3, 1024, 1024], P(None, 'gx'), may hold values from -1 to 1
Outputs:
- fine_out: bfloat16 [32, 16, 16, 256], P('gx', 'gy', 'gz')
- attention: bfloat16 [8, 256, 1024], P(('gy', 'gz'), 'gx')
The draws below stay inside these ranges and needn't reach their ends.
Inputs may be any that keep to these rules, and one draw needn't show every extreme that they name: `occupancy`: each aligned block of 4 bricks along the third dimension holds at least one occupied brick.
All inputs are finite; a program needn't handle non-finite values.
Results may differ from the reference program's by a relative error of at most 0.015.
The reference program's roundings to bfloat16 on the way count: a program that leaves them out, or rounds other values in their place, can miss the bound.
Values may be sent and summed in bfloat16 or wider, within the bound.
No kernel may reach another device: no remote copies, remote signals or barrier semaphores. Data moves between devices by JAX's collectives and lax.ppermute only.
A program may use at most 64 MiB of HBM per device.

```python
import jax
import jax.numpy as jnp
from jax import lax

C = 32
GROUPS_NORM = 8
HEADS = 16
RZ = 32
D = 1024
HD = 64
RZ_BRICKS = 4
SEQ = 256
GROUPS = 8
NX = 32
NY = 16
NZ = 128
NBZ = 16
N_GX = 4
N_GY = 2
N_GZ = 4


def brick_layout(key):
    base_key = jax.random.fold_in(key, 7)
    subkeys = jax.random.split(base_key, 3)
    density = jax.random.randint(subkeys[0], (N_GX, N_GY, N_GZ, 1), 10, 96)
    rolled = jax.random.randint(subkeys[1], (N_GX, N_GY, N_GZ, RZ_BRICKS), 0, 100)
    forced = jax.random.randint(subkeys[2], (N_GX, N_GY, N_GZ, 1), 0, RZ_BRICKS)
    slot_index = lax.broadcasted_iota(jnp.int32, (N_GX, N_GY, N_GZ, RZ_BRICKS), 3)
    occupied = jnp.logical_or(rolled < density, slot_index == forced).astype(jnp.int32)
    return occupied.reshape(N_GX, N_GY, NBZ)


def draw_occupancy(key, part):
    return brick_layout(key)


def draw_features(key, part):
    subkeys = jax.random.split(jax.random.fold_in(key, 11), 3)
    shape = (C, NX, NY, NZ)
    noise_field = jax.random.truncated_normal(subkeys[0], -4.0, 4.0, shape, jnp.float32)
    channel_scale = jnp.exp(jax.random.uniform(subkeys[1], (C,), jnp.float32, jnp.log(0.5), jnp.log(2.0)))
    brick_scale = jnp.exp(jax.random.uniform(subkeys[2], (N_GX, N_GY, NBZ), jnp.float32, jnp.log(0.5), jnp.log(2.0)))
    brick_voxels = jnp.repeat(jnp.repeat(jnp.repeat(brick_scale, 8, axis=0), 8, axis=1), 8, axis=2)
    index_x = lax.broadcasted_iota(jnp.int32, (NX, NY, NZ), 0)
    index_y = lax.broadcasted_iota(jnp.int32, (NX, NY, NZ), 1)
    index_z = lax.broadcasted_iota(jnp.int32, (NX, NY, NZ), 2)
    ramp_factor = 1.0 + 2.0 * (index_x.astype(jnp.float32) / NX + index_y.astype(jnp.float32) / NY + index_z.astype(jnp.float32) / NZ) / 3.0
    values = noise_field * channel_scale[:, None, None, None] * (brick_voxels * ramp_factor)[None]
    return values.reshape(C, NX, NY, NBZ, 8).transpose(1, 2, 3, 0, 4).reshape(NX, NY, NBZ, C * 8).astype(jnp.bfloat16)


def draw_qkv_weight(key, part):
    subkeys = jax.random.split(jax.random.fold_in(key, 23), 1)
    weight = jax.random.truncated_normal(subkeys[0], -6.0, 6.0, (3, D, D), jnp.float32) * D ** (-0.5)
    return weight.astype(jnp.bfloat16)


def normal_values(key, dims, deviation, reach, dtype=jnp.bfloat16):
    return jnp.clip(deviation * jax.random.normal(key, dims, jnp.float32), -reach, reach).astype(dtype)


def setup_inputs(seed: int = 0) -> dict:
    keys = jax.random.split(jax.random.key(seed), 8)
    features = draw_features(jax.random.fold_in(keys[7], 71), 0)
    occupancy = draw_occupancy(jax.random.fold_in(keys[7], 71), 0)
    norm_gain = jnp.clip(1.0 + 0.18 * jax.random.normal(keys[2], (2, C), jnp.float32), 0.1, 1.9)
    norm_shift = normal_values(keys[3], (2, C), 0.5, 3.0, jnp.float32)
    conv_weight = normal_values(keys[4], (2, C, 27 * C), (27 * C) ** -0.5, 0.21875)
    conv_bias = normal_values(keys[5], (2, C), 0.5, 3.0, jnp.float32)
    qkv_weight = draw_qkv_weight(jax.random.fold_in(keys[7], 71), 0)
    return dict(features=features, occupancy=occupancy, norm_gain=norm_gain, norm_shift=norm_shift, conv_weight=conv_weight, conv_bias=conv_bias, qkv_weight=qkv_weight)


EPS = 1e-05

def expand_mask(occupancy):
    brick_grid = jnp.repeat(jnp.repeat(jnp.repeat(occupancy, 8, axis=0), 8, axis=1), 8, axis=2)
    return brick_grid.astype(jnp.float32)

def to_channels(packed):
    return packed.reshape(NX, NY, NBZ, C, 8).transpose(3, 0, 1, 2, 4).reshape(C, NX, NY, NZ)

def from_channels(field):
    return field.reshape(C, NX, NY, NBZ, 8).transpose(1, 2, 3, 0, 4).reshape(NX, NY, NBZ, C * 8)

def activate(values, voxel_mask, gain_row, shift_row):
    group_width = C // GROUPS_NORM
    shaped = values.reshape(GROUPS_NORM, group_width, NX * NY * NZ)
    flat_mask = voxel_mask.reshape(1, 1, NX * NY * NZ)
    counted = jnp.sum(voxel_mask) * group_width
    centre = lax.optimization_barrier(jnp.sum(shaped * flat_mask, axis=(1, 2))) / counted
    centred = (shaped - centre[:, None, None]) * flat_mask
    spread = lax.optimization_barrier(jnp.sum(centred * centred, axis=(1, 2))) / counted
    normed = (shaped - centre[:, None, None]) * lax.rsqrt(spread + EPS)[:, None, None]
    normed = normed.reshape(C, NX * NY * NZ) * gain_row[:, None] + shift_row[:, None]
    return (jax.nn.silu(normed) * flat_mask.reshape(1, -1)).reshape(C, NX, NY, NZ)

def convolve(field, weight):
    padded = jnp.pad(field, ((0, 0), (1, 1), (1, 1), (1, 1)))
    accumulated = jnp.zeros((C, NX * NY * NZ), jnp.float32)
    for shift_x in range(3):
        for shift_y in range(3):
            for shift_z in range(3):
                offset = (shift_x * 3 + shift_y) * 3 + shift_z
                window = padded[:, shift_x:shift_x + NX, shift_y:shift_y + NY, shift_z:shift_z + NZ].reshape(C, NX * NY * NZ)
                accumulated = accumulated + jnp.dot(weight[:, offset * C:(offset + 1) * C], window, preferred_element_type=jnp.float32)
    return accumulated.reshape(C, NX, NY, NZ)

def tokenize(field):
    shaped = field.reshape(C, N_GX, 4, 2, N_GY, 2, 4, N_GZ, RZ // 4, 4)
    moved = shaped.transpose(4, 7, 1, 2, 5, 8, 0, 3, 6, 9)
    return moved.reshape(GROUPS, SEQ, D)

def token_keep(occupancy):
    bricks = occupancy.reshape(N_GX, N_GY, N_GZ, RZ_BRICKS).astype(jnp.float32)
    bricks = jnp.repeat(bricks, 2, axis=3)
    spread_out = jnp.broadcast_to(bricks[:, :, :, None, None, :], (N_GX, N_GY, N_GZ, 4, 2, RZ // 4))
    return spread_out.transpose(1, 2, 0, 3, 4, 5).reshape(GROUPS, SEQ)

def attend(tokens, key_keep, weight):
    flat_weight = weight.reshape(3 * D, D)
    projected = lax.dot_general(tokens, flat_weight, (((1,), (1,)), ((), ())), preferred_element_type=jnp.float32).astype(jnp.bfloat16)
    projected = projected.reshape(SEQ, 3, HEADS, HD)
    queries = projected[:, 0].transpose(1, 0, 2)
    keys_all = projected[:, 1].transpose(1, 0, 2)
    values_all = projected[:, 2].transpose(1, 0, 2)

    def head_out(members):
        head_queries, head_keys, head_values = members
        scores = jnp.dot(head_queries, head_keys.T, preferred_element_type=jnp.float32) * HD ** (-0.5)
        scores = jnp.where(key_keep[None, :] > 0, scores, -jnp.inf)
        row_max = lax.optimization_barrier(jnp.max(scores, axis=1, keepdims=True))
        weights = jnp.exp(scores - row_max)
        totals = lax.optimization_barrier(jnp.sum(weights, axis=1, keepdims=True))
        return jnp.dot(weights.astype(jnp.bfloat16), head_values, preferred_element_type=jnp.float32) / totals
    results = lax.map(head_out, (queries, keys_all, values_all))
    merged = results.transpose(1, 0, 2).reshape(SEQ, D) * key_keep[:, None]
    return merged.astype(jnp.bfloat16)

def reference(features, occupancy, norm_gain, norm_shift, conv_weight, conv_bias, qkv_weight):
    field = to_channels(features)
    voxel_mask = expand_mask(occupancy)
    inputs = field * voxel_mask.astype(jnp.bfloat16)
    first_act = activate(inputs.astype(jnp.float32), voxel_mask, norm_gain[0], norm_shift[0]).astype(jnp.bfloat16)
    middle = (convolve(first_act, conv_weight[0]) + conv_bias[0][:, None, None, None]) * voxel_mask[None]
    second_act = activate(middle, voxel_mask, norm_gain[1], norm_shift[1]).astype(jnp.bfloat16)
    out_field = ((inputs.astype(jnp.float32) + convolve(second_act, conv_weight[1]) + conv_bias[1][:, None, None, None]) * voxel_mask[None]).astype(jnp.bfloat16)
    tokens = tokenize(out_field)
    keeps = token_keep(occupancy)
    attention = lax.map(lambda member: attend(member[0], member[1], qkv_weight), (tokens, keeps))
    return (from_channels(out_field), attention)
```

```python
import functools

import jax
import jax.numpy as jnp
from jax import lax
from jax.experimental import pallas as pl
from jax.experimental.pallas import tpu as pltpu
from jax.sharding import PartitionSpec as P

C = 32
GW = 4
HD = 64
BR = 8
EPS = 1e-05
SENT = 512.0
BIG = 1e30
ALL = ("gx", "gy", "gz")
F32, BF16 = jnp.float32, jnp.bfloat16
HIGHEST = lax.Precision.HIGHEST


def iota(shape, dim):
    return lax.broadcasted_iota(jnp.int32, shape, dim)


def onehot(cond, dtype=BF16):
    return jnp.where(cond, 1.0, 0.0).astype(dtype)


def exact_dot(a, b):
    return jnp.dot(a, b, precision=HIGHEST, preferred_element_type=F32)


def brick_rows(occ_ref, x, lanes):
    row = iota((8, lanes), 0)
    out = jnp.zeros((8, lanes), F32)
    for b in range(occ_ref.shape[2]):
        out = jnp.where(row == b, occ_ref[x, 0, b].astype(F32), out)
    return out


def pack_stats(total, second, count, out_ref):
    groups = C // GW
    lanes = total.shape[1]
    lane, col = iota((lanes, 128), 0), iota((lanes, 128), 1)
    to_mean = onehot(lane // (lanes // groups) == col, F32)
    to_second = onehot(lane // (lanes // groups) + groups == col, F32)
    row = exact_dot(jnp.broadcast_to(total, (8, lanes)), to_mean)
    row += exact_dot(jnp.broadcast_to(second, (8, lanes)), to_second)
    row = jnp.where(iota((8, 128), 1) == 2 * groups, count, row)
    out_ref[...] = jnp.broadcast_to(row[0:1], out_ref.shape)


def group_mean(total, count, lanes):
    same = onehot(iota((lanes, lanes), 0) // 32 == iota((lanes, lanes), 1) // 32, F32)
    return exact_dot(jnp.broadcast_to(total, (8, lanes)), same)[0:1] / count


def local_moments(shifted, total, keep, count, out_ref):
    lanes = total.shape[1]
    mean = group_mean(total, count, lanes)
    squares = jnp.sum(shifted(mean) * keep, axis=0, keepdims=True)
    pack_stats(total, squares, count, out_ref)


def combine(stats, lanes):
    groups = C // GW
    n = stats[:, 2 * groups : 2 * groups + 1]
    total = jnp.sum(n)
    centre = jnp.sum(stats, axis=0, keepdims=True) / total
    drift = stats / n - centre
    between = jnp.sum(drift * drift * n, axis=0, keepdims=True)
    within = jnp.sum(stats, axis=0, keepdims=True)
    col, lane = iota((128, lanes), 0), iota((128, lanes), 1)
    group = lane // (lanes // groups)
    pick, pick2 = onehot(group == col, F32), onehot(group + groups == col, F32)
    spread = exact_dot(jnp.broadcast_to(between, (8, 128)), pick)
    spread += exact_dot(jnp.broadcast_to(within, (8, 128)), pick2)
    centre = exact_dot(jnp.broadcast_to(centre, (8, 128)), pick)
    return centre[0:1], lax.rsqrt(spread[0:1] / total + EPS)


def silu(u):
    return 0.5 * u * (1.0 + jnp.tanh(0.5 * u))


def edges(act):
    z = iota(act.shape, 2) % BR
    before, after = pltpu.roll(act, 1, 1), pltpu.roll(act, 7, 1)
    return jnp.where(z == BR - 1, before, jnp.where(z == 0, after, 0.0))


def pre_kernel(swap, occ_ref, feat_ref, stats_ref, zlo_ref, zhi_ref, *rest):
    enc = rest[-1]
    faces = rest[:-1]
    sx, sy, sb, lanes = feat_ref.shape
    me = lax.axis_index("gx")
    keep = brick_rows(occ_ref, me, lanes)
    count = jnp.sum(keep[:, 0:1]) * float(sx * sy * BR * GW)
    field = feat_ref[...].astype(F32)
    total = jnp.sum(field.reshape(sx * sy, sb, lanes), axis=0) * keep[:sb]
    total = jnp.sum(total, axis=0, keepdims=True)

    def shifted(mean):
        d = field.reshape(sx * sy, sb, lanes) - mean[None]
        return jnp.sum(d * d, axis=0)

    local_moments(shifted, total, keep[:sb], count, stats_ref)
    coded = jnp.where((keep[:sb] > 0)[None, None], field, SENT)
    for h in range(lanes // 128):
        part = coded[:, :, :, h * 128 : (h + 1) * 128]
        blank = jnp.full((sx, sy, 8 - sb, 128), SENT, F32)
        enc[h] = jnp.concatenate([part, blank], axis=2).reshape(sx * sy * 8, 128)

    def pick(start, count, stride):
        halves = [
            enc[h, pl.ds(start, count, stride=stride), :]
            for h in range(lanes // 128)
        ]
        return jnp.concatenate(halves, axis=1)

    zlo_ref[...] = pick(0, sx * sy, 8).astype(BF16)
    zhi_ref[...] = pick(sb - 1, sx * sy, 8).astype(BF16)

    def face(y0):
        both = []
        for h in range(lanes // 128):
            block = enc[h].reshape(sx, sy, 8, 128)
            low, high = block[:, y0], pltpu.roll(block[:, y0 + 1], 4, 1)
            both.append(jnp.where(iota(low.shape, 1) < 4, low, high).reshape(sx * 8, 128))
        corner = [
            jnp.concatenate(
                [pick((y0 + i) * 8 + b, sx, sy * 8) for i in range(2)], axis=0
            )
            for b in (0, sb - 1)
        ]
        return [jnp.concatenate(both, axis=1)] + corner

    lo, hi = face(0), face(sy - 2)
    if swap:
        first = lax.axis_index("gy") == 0
        out = [jnp.where(first, h, l) for l, h in zip(lo, hi)]
    else:
        out = hi + lo
    for ref, value in zip(faces, out):
        ref[...] = value.astype(BF16)


def plane_kernel(swap, peers, occ_ref, feat_ref, zm_ref, zp_ref, *rest):
    faces = rest[:-4]
    ext_ref, xlo_ref, xhi_ref, buf = rest[-4:]
    sx, sy, sb, lanes = feat_ref.shape
    ey = sy + 4
    me = lax.axis_index("gx")
    keep = brick_rows(occ_ref, me, lanes)[:sb]
    own = jnp.where((keep > 0)[None, None], feat_ref[...].astype(F32), SENT)
    halves = range(lanes // 128)
    for h in halves:
        part = own[:, :, :, h * 128 : (h + 1) * 128]
        blank = jnp.full((sx, sy, 8 - sb, 128), SENT, F32)
        part = jnp.concatenate([part, blank], axis=2)
        for x in range(sx):
            buf[h, (x * ey + 2) * 8 : (x * ey + 2 + sy) * 8, :] = part[x].reshape(sy * 8, 128)

    def put(start, count, stride, value):
        for h in halves:
            buf[h, pl.ds(start, count, stride=stride), :] = value[:, h * 128 : (h + 1) * 128]

    gy, gz = lax.axis_index("gy"), lax.axis_index("gz")
    has_zm, has_zp = gz > 0, gz < peers[1] - 1
    zm = jnp.where(has_zm, zm_ref[...].astype(F32), SENT)
    zp = jnp.where(has_zp, zp_ref[...].astype(F32), SENT)
    for x in range(sx):
        part = slice(x * sy, (x + 1) * sy)
        put((x * ey + 2) * 8 + 7, sy, 8, zm[part])
        put((x * ey + 2) * 8 + sb, sy, 8, zp[part])

    def side(y0, there, face_ref, zm_corner, zp_corner):
        face = jnp.where(there, face_ref[...].astype(F32), SENT).reshape(sx, 8, lanes)
        for h in halves:
            part = face[:, :, h * 128 : (h + 1) * 128]
            inside = iota(part.shape, 1) < sb
            low = jnp.where(inside, part, SENT)
            high = jnp.where(inside, pltpu.roll(part, 4, 1), SENT)
            for x in range(sx):
                buf[h, (x * ey + y0) * 8 : (x * ey + y0 + 2) * 8, :] = jnp.concatenate(
                    [low[x], high[x]], axis=0
                )
        low = jnp.where(there & has_zm, zm_corner[...].astype(F32), SENT)
        high = jnp.where(there & has_zp, zp_corner[...].astype(F32), SENT)
        for i in range(2):
            put((y0 + i) * 8 + 7, sx, ey * 8, low[i * sx : (i + 1) * sx])
            put((y0 + i) * 8 + sb, sx, ey * 8, high[i * sx : (i + 1) * sx])

    if swap:
        side(0, gy == 1, faces[0], faces[1], faces[2])
        side(sy + 2, gy == 0, faces[0], faces[1], faces[2])
    else:
        side(0, gy > 0, faces[0], faces[1], faces[2])
        side(sy + 2, gy < peers[0] - 1, faces[3], faces[4], faces[5])
    slab = 2 * ey * 8
    rows = sx * ey * 8
    whole = jnp.concatenate([buf[h] for h in halves], axis=1).astype(BF16)
    ext_ref[...] = whole
    xlo_ref[...] = whole[0:slab]
    xhi_ref[...] = whole[rows - slab : rows]


def band_kernel(layer, weight_ref, pars_ref, out_ref, rows_ref=None):
    lanes = C * BR
    spread = onehot(iota((C, lanes), 0) == iota((C, lanes), 1) // BR)
    column = onehot(iota((lanes, C), 0) // BR == iota((lanes, C), 1))
    turned = jnp.transpose(weight_ref[layer].astype(F32)).astype(BF16)
    wide = jnp.dot(turned, spread, preferred_element_type=F32).astype(BF16)
    zi, zo = iota((lanes, lanes), 0) % BR, iota((lanes, lanes), 1) % BR
    for ex in range(3):
        for ey in range(3):
            terms = []
            for ez in range(3):
                q = (ex * 3 + ey) * 3 + ez
                terms.append(
                    jnp.dot(column, wide[q * C : (q + 1) * C], preferred_element_type=F32)
                )
            inner = jnp.where(zi == zo - 1, terms[0], 0.0)
            inner = jnp.where(zi == zo, terms[1], inner)
            inner = jnp.where(zi == zo + 1, terms[2], inner)
            outer = jnp.where((zi == BR - 1) & (zo == 0), terms[0], 0.0)
            outer = jnp.where((zi == 0) & (zo == BR - 1), terms[2], outer)
            out_ref[ex, ey * lanes : (ey + 1) * lanes, :] = inner.astype(BF16)
            out_ref[ex, (3 + ey) * lanes : (4 + ey) * lanes, :] = outer.astype(BF16)
    if rows_ref is not None:
        rows_ref[...] = exact_dot(
            pars_ref[...], onehot(iota((C, lanes), 0) == iota((C, lanes), 1) // BR, F32)
        )


def turn_kernel(weight_ref, out_ref):
    kinds, cols, feats = weight_ref.shape
    r = iota((feats, 1), 0)
    source = (r % 128) // 4 * 32 + r // 128 * 4 + r % 4
    pick = onehot(source == iota((feats, feats), 1))
    for k in range(kinds):
        out_ref[:, k * cols : (k + 1) * cols] = lax.dot_general(
            pick, weight_ref[k], (((1,), (1,)), ((), ())), preferred_element_type=F32
        ).astype(BF16)


def first_kernel(peers, stats_ref, ext_ref, xm_ref, xp_ref, weight_ref, rows_ref, occ_ref,
                 mid_ref, out_ref, lhs, msk):
    slab, lanes = xm_ref.shape
    ey = slab // 16
    oy = ey - 2
    sx = ext_ref.shape[0] // (ey * 8)
    centre, scale = combine(stats_ref[...], lanes)
    gain, shift, bias = rows_ref[0:1], rows_ref[1:2], rows_ref[2:3]
    scale = scale * gain
    me = lax.axis_index("gx")
    step = ey * 8
    for x in range(sx + 4):
        if x < 2:
            v = jnp.where(me > 0, xm_ref[x * step : (x + 1) * step].astype(F32), SENT)
        elif x < sx + 2:
            v = ext_ref[(x - 2) * step : (x - 1) * step].astype(F32)
        else:
            i = x - sx - 2
            v = jnp.where(me < peers - 1, xp_ref[i * step : (i + 1) * step].astype(F32), SENT)
        there = v != SENT
        msk[x * step : (x + 1) * step] = onehot(there[:, 0:128], F32)
        act = jnp.where(there, silu((v - centre) * scale + shift), 0.0).reshape(ey, 8, lanes)
        side = edges(act)
        for e in range(3):
            rows = slice(x * oy * 8, (x + 1) * oy * 8)
            lhs[rows, e * lanes : (e + 1) * lanes] = (
                act[e : e + oy].reshape(oy * 8, lanes).astype(BF16)
            )
            lhs[rows, (3 + e) * lanes : (4 + e) * lanes] = (
                side[e : e + oy].reshape(oy * 8, lanes).astype(BF16)
            )
    ox = sx + 2
    size = ox * oy * 8
    acc = bias
    for e in range(3):
        acc = acc + jnp.dot(
            lhs[e * oy * 8 : e * oy * 8 + size, :], weight_ref[e], preferred_element_type=F32
        )
    mid_ref[...] = acc
    keep = brick_rows(occ_ref, me, lanes)
    count = jnp.sum(keep[:, 0:1]) * float(sx * (oy - 2) * BR * GW)
    whole = jnp.zeros((8, lanes), F32)
    for x in range(ox):
        rows = slice(x * oy * 8, (x + 1) * oy * 8)
        own = mid_ref[rows].reshape(oy, 8, lanes)
        if 1 <= x <= sx:
            whole = whole + jnp.sum(own[1 : oy - 1], axis=0)
    total = jnp.sum(whole * keep, axis=0, keepdims=True)

    def shifted(mean):
        squares = jnp.zeros((8, lanes), F32)
        for x in range(1, sx + 1):
            d = mid_ref[(x * oy + 1) * 8 : (x * oy + oy - 1) * 8].reshape(oy - 2, 8, lanes)
            d = d - mean[None]
            squares = squares + jnp.sum(d * d, axis=0)
        return squares

    local_moments(shifted, total, keep, count, out_ref)
    for x in range(ox):
        rows = slice(x * oy * 8, (x + 1) * oy * 8)
        there = msk[(x + 1) * step + 8 : (x + 2) * step - 8] > 0
        there = jnp.concatenate([there.astype(F32)] * (lanes // 128), axis=1) > 0
        mid_ref[rows] = jnp.where(there, mid_ref[rows], BIG)


def second_kernel(stats_ref, mid_ref, weight_ref, rows_ref, occ_ref, feat_ref,
                  fine_ref, tok_ref, lhs, tmp):
    sx, sy, sb, lanes = feat_ref.shape
    ey = sy + 2
    step = ey * 8
    centre, scale = combine(stats_ref[...], lanes)
    gain, shift, bias = rows_ref[3:4], rows_ref[4:5], rows_ref[5:6]
    scale = scale * gain
    for x in range(sx + 2):
        v = mid_ref[x * step : (x + 1) * step]
        act = jnp.where(v < BIG, silu((v - centre) * scale + shift), 0.0).reshape(ey, 8, lanes)
        side = edges(act)
        rows = slice(x * sy * 8, (x + 1) * sy * 8)
        for e in range(3):
            lhs[rows, e * lanes : (e + 1) * lanes] = (
                act[e : e + sy].reshape(sy * 8, lanes).astype(BF16)
            )
            lhs[rows, (3 + e) * lanes : (4 + e) * lanes] = (
                side[e : e + sy].reshape(sy * 8, lanes).astype(BF16)
            )
    size = sx * sy * 8
    acc = bias
    for e in range(3):
        acc = acc + jnp.dot(
            lhs[e * sy * 8 : e * sy * 8 + size, :], weight_ref[e], preferred_element_type=F32
        )
    keep = brick_rows(occ_ref, lax.axis_index("gx"), lanes)[:sb]
    acc = acc.reshape(sx, sy, 8, lanes)
    out = (feat_ref[...].astype(F32) * keep + acc[:, :, :sb]) * keep
    out = out.astype(BF16)
    fine_ref[...] = out
    tmp[:, :, 0:sb, :] = out.astype(F32)
    tmp[:, :, sb:8, :] = jnp.zeros((sx, sy, 8 - sb, lanes), F32)
    i, j = iota((lanes, lanes), 0), iota((lanes, lanes), 1)
    pick = onehot(i == (j % 128) // 4 * 8 + j // 128 * 4 + j % 4)
    moved = jnp.dot(
        tmp[...].reshape(size, lanes).astype(BF16), pick, preferred_element_type=F32
    ).reshape(sx // 2, 2, sy // 4, 4, 8, lanes)
    count = sx // 2 * (sy // 4)
    parts = []
    for x in range(2):
        for y in range(4):
            piece = moved[:, x, :, y].reshape(count, 8, lanes)
            low, high = piece[:, :, :128], pltpu.roll(piece[:, :, 128:], 4, 1)
            both = jnp.where(iota(low.shape, 1) < 4, low, high).reshape(count * 8, 128)
            parts.append(both.astype(BF16))
    tokens = jnp.concatenate(parts, axis=1)
    n = count * 8
    i, j = iota((n, n), 0), iota((n, n), 1)
    order = onehot(j == i // 8 * 8 + i % 2 * 4 + i % 8 // 2)
    tok_ref[...] = jnp.dot(order, tokens, preferred_element_type=F32).astype(BF16)


def attend_kernel(members, occ_ref, weight_ref, *refs):
    tok_refs, out_refs, (toks, proj) = refs[:members], refs[members : 2 * members], refs[-2:]
    own = tok_refs[0].shape[0]
    seq = own * members
    cols = weight_ref.shape[1] // 3
    me = lax.axis_index("gx")
    for k in range(members):
        toks[k * own : (k + 1) * own, :] = tok_refs[k][...]
    proj[...] = jnp.dot(toks[...], weight_ref[...], preferred_element_type=F32).astype(BF16)
    lane, row = iota((1, seq), 1), iota((seq, 1), 0)
    key_keep, row_keep = jnp.zeros((1, seq), F32), jnp.zeros((seq, 1), F32)
    for k in range(members):
        for b in range(occ_ref.shape[2]):
            there = occ_ref[me ^ k, 0, b].astype(F32)
            key_keep = jnp.where((lane // own == k) & (lane % 8 // 2 == b), there, key_keep)
            row_keep = jnp.where((row // own == k) & (row % 8 // 2 == b), there, row_keep)
    width = min(128, cols)
    for t in range(cols // width):
        q = proj[:, t * width : (t + 1) * width]
        keys = proj[:, cols + t * width : cols + (t + 1) * width]
        values = proj[:, 2 * cols + t * width : 2 * cols + (t + 1) * width]
        head = iota((seq, width), 1) // HD
        merged = jnp.zeros((seq, width), F32)
        for h in range(width // HD):
            mine = jnp.where(head == h, q.astype(F32), 0.0).astype(BF16)
            scores = lax.dot_general(
                mine, keys, (((1,), (1,)), ((), ())), preferred_element_type=F32
            ) * float(HD) ** (-0.5)
            scores = jnp.where(key_keep > 0, scores, -BIG)
            probs = jnp.exp(scores - jnp.max(scores, axis=1, keepdims=True))
            total = jnp.sum(probs, axis=1, keepdims=True)
            mixed = jnp.dot(probs.astype(BF16), values, preferred_element_type=F32)
            merged = jnp.where(head == h, mixed * (row_keep / total), merged)
        merged = merged.astype(BF16)
        for k in range(members):
            out_refs[k][:, t * width : (t + 1) * width] = merged[k * own : (k + 1) * own]


def gather_kernel(members, *refs):
    out_ref = refs[-1]
    cols = refs[0].shape[1]
    me = lax.axis_index("gx")
    for k in range(members):
        out_ref[0, :, pl.ds(pl.multiple_of((me ^ k) * cols, cols), cols)] = refs[k][...]


VM = pl.BlockSpec(memory_space=pltpu.VMEM)
SM = pl.BlockSpec(memory_space=pltpu.SMEM)


def call(kernel, name, specs, out, args, scratch=(), flops=0, nbytes=0, mib=32):
    return pl.pallas_call(
        kernel,
        out_shape=out,
        in_specs=list(specs),
        out_specs=jax.tree.map(lambda _: VM, out),
        scratch_shapes=list(scratch),
        name=name,
        cost_estimate=pl.CostEstimate(flops=flops, bytes_accessed=nbytes, transcendentals=0),
        compiler_params=pltpu.CompilerParams(vmem_limit_bytes=mib * 2**20),
    )(*args)


def shape(*dims, dtype=BF16):
    return jax.ShapeDtypeStruct(dims, dtype)


def body(features, occupancy, norm_gain, norm_shift, conv_weight, conv_bias, qkv_weight):
    sx, sy, sb, lanes = features.shape
    nx, ny, nz = (lax.axis_size(a) for a in ALL)
    devices = nx * ny * nz
    swap = ny == 2
    plane = ("gy", "gz")

    def shift(x, dy, dz):
        pairs = []
        for y in range(ny):
            for z in range(nz):
                ty, tz = (y ^ 1 if swap and dy else y + dy), z + dz
                if 0 <= ty < ny and 0 <= tz < nz:
                    pairs.append((y * nz + z, ty * nz + tz))
        return lax.ppermute(x, plane, pairs)

    face = [shape(sx * 8, lanes)] + [shape(2 * sx, lanes)] * 2
    pre = call(
        functools.partial(pre_kernel, swap), "pre", (SM, VM),
        [shape(devices, 128, dtype=F32), shape(sx * sy, lanes), shape(sx * sy, lanes)]
        + face * (1 if swap else 2),
        (occupancy, features),
        [pltpu.VMEM((lanes // 128, sx * sy * 8, 128), F32)], nbytes=10**6,
    )
    stats, zlo, zhi = pre[:3]
    stats = lax.all_to_all(stats, ALL, 0, 0, tiled=True)
    received = [shift(zhi, 0, 1), shift(zlo, 0, -1)]
    for i, dy in enumerate((1,) if swap else (1, -1)):
        y_face, y_low, y_high = pre[3 + 3 * i : 6 + 3 * i]
        received += [shift(y_face, dy, 0), shift(y_high, dy, 1), shift(y_low, dy, -1)]
    ey = sy + 4
    slab = 2 * ey * 8
    ext, xlo, xhi = call(
        functools.partial(plane_kernel, swap, (ny, nz)), "plane", (SM,) + (VM,) * (1 + len(received)),
        [shape(sx * ey * 8, lanes), shape(slab, lanes), shape(slab, lanes)],
        (occupancy, features, *received),
        [pltpu.VMEM((lanes // 128, sx * ey * 8, 128), F32)], nbytes=10**6,
    )
    up = [(i, i + 1) for i in range(nx - 1)]
    down = [(j, i) for i, j in up]
    xm, xp = lax.ppermute(xhi, "gx", up), lax.ppermute(xlo, "gx", down)

    rows = jnp.stack([norm_gain[0], norm_shift[0], conv_bias[0], norm_gain[1], norm_shift[1],
                      conv_bias[1], conv_bias[0], conv_bias[1]])
    band = shape(3, 6 * lanes, lanes)
    band0, rows = call(
        functools.partial(band_kernel, 0), "band0", (VM, VM), [band, shape(8, lanes, dtype=F32)],
        (conv_weight, rows), nbytes=8 * 10**6,
    )
    band1 = call(
        functools.partial(band_kernel, 1), "band1", (VM, VM), band, (conv_weight, rows),
        nbytes=8 * 10**6,
    )
    cols, feats = qkv_weight.shape[1:]
    turned = call(
        turn_kernel, "turn", (VM,), shape(feats, 3 * cols), (qkv_weight,),
        flops=2 * 3 * cols * feats * feats, nbytes=6 * 10**6,
    )

    oy = sy + 2
    size = (sx + 2) * oy * 8
    mid, stats = call(
        functools.partial(first_kernel, nx), "first", (VM,) * 6 + (SM,),
        [shape(size, lanes, dtype=F32), shape(devices, 128, dtype=F32)],
        (stats, ext, xm, xp, band0, rows, occupancy),
        [pltpu.VMEM(((sx + 4) * oy * 8, 6 * lanes), BF16),
         pltpu.VMEM(((sx + 4) * ey * 8, 128), F32)],
        flops=3 * 10**9, nbytes=4 * 10**6,
    )
    stats = lax.all_to_all(stats, ALL, 0, 0, tiled=True)
    own = sx // 2 * (sy // 4) * sb * 2
    fine_out, tokens = call(
        second_kernel, "second", (VM,) * 4 + (SM, VM),
        [shape(*features.shape), shape(own, feats)],
        (stats, mid, band1, rows, occupancy, features),
        [pltpu.VMEM(((sx + 2) * sy * 8, 6 * lanes), BF16), pltpu.VMEM((sx, sy, 8, lanes), F32)],
        flops=2 * 10**9, nbytes=4 * 10**6,
    )
    swaps = [[(i, i ^ k) for i in range(nx)] for k in range(nx)]
    blocks = [tokens] + [lax.ppermute(tokens, "gx", swaps[k]) for k in range(1, nx)]
    outs = call(
        functools.partial(attend_kernel, nx), "attend", (SM,) + (VM,) * (1 + nx),
        [shape(own, cols)] * nx, (occupancy, turned, *blocks),
        [pltpu.VMEM((own * nx, feats), BF16), pltpu.VMEM((own * nx, 3 * cols), BF16)],
        flops=10**9, nbytes=3 * 10**6,
    )
    outs = [outs[0]] + [lax.ppermute(outs[k], "gx", swaps[k]) for k in range(1, nx)]
    if cols % 128 == 0:
        attention = call(
            functools.partial(gather_kernel, nx), "place", (VM,) * nx,
            shape(1, own, nx * cols), outs, nbytes=3 * 10**5, mib=16,
        )
    else:
        stacked, me = jnp.stack(outs), lax.axis_index("gx")
        attention = jnp.concatenate(
            [lax.dynamic_index_in_dim(stacked, me ^ j, 0, keepdims=False) for j in range(nx)],
            axis=1,
        )[None]
    return (fine_out, attention)


def solution(mesh):
    placed = (
        P("gx", "gy", "gz", None),
        P(None, "gy", "gz"),
        P(),
        P(),
        P(),
        P(),
        P(None, "gx", None),
    )
    return jax.shard_map(
        body,
        mesh=mesh,
        in_specs=placed,
        out_specs=(P("gx", "gy", "gz", None), P(("gy", "gz"), "gx", None)),
        check_vma=False,
    )
```

```python
import functools

import jax
import jax.numpy as jnp
from jax import lax
from jax.experimental import pallas as pl
from jax.experimental.pallas import tpu as pltpu
from jax.sharding import PartitionSpec as P

C = 32
GW = 4
HD = 64
BR = 8
EPS = 1e-05
SENT = 512.0
BIG = 1e30
ALL = ("gx", "gy", "gz")
F32, BF16 = jnp.float32, jnp.bfloat16
HIGHEST = lax.Precision.HIGHEST
GROUPS = C // GW
TAIL = 16


def iota(shape, dim):
    return lax.broadcasted_iota(jnp.int32, shape, dim)


def onehot(cond, dtype=BF16):
    return jnp.where(cond, 1.0, 0.0).astype(dtype)


def exact_dot(a, b):
    return jnp.dot(a, b, precision=HIGHEST, preferred_element_type=F32)


def group_of(lanes, dim, shape):
    return iota(shape, dim) // (lanes // GROUPS)


def moments(total, squares_about, count):
    lanes = total.shape[1]
    col = iota((lanes, 128), 1)
    group = group_of(lanes, 0, (lanes, 128))
    sums = exact_dot(jnp.broadcast_to(total, (8, lanes)), onehot(group == col, F32))
    back = onehot(iota((128, lanes), 0) == group_of(lanes, 1, (128, lanes)), F32)
    squares = squares_about(exact_dot(sums / count, back)[0:1])
    second = exact_dot(
        jnp.broadcast_to(squares, (8, lanes)), onehot(group + GROUPS == col, F32)
    )
    return jnp.where(iota((8, 128), 1) == 2 * GROUPS, count, sums + second)


def merge(rows):
    n = rows[:, 2 * GROUPS : 2 * GROUPS + 1]
    whole = jnp.sum(rows, axis=0, keepdims=True)
    drift = rows / jnp.maximum(n, 1.0) - whole / jnp.sum(n)
    between = jnp.sum(drift * drift * n, axis=0, keepdims=True)
    between = jnp.where(iota((8, 128), 1) < GROUPS, between, 0.0)
    return whole + pltpu.roll(between, GROUPS, 1)


def stack_rows(rows):
    index = iota((8, 128), 0)
    out = jnp.zeros((8, 128), F32)
    for i, row in enumerate(rows):
        out = jnp.where(index == i, row, out)
    return out


def centre_scale(merged, lanes):
    row = iota((128, lanes), 0)
    group = group_of(lanes, 1, (128, lanes))
    scaled = merged / merged[0:1, 2 * GROUPS : 2 * GROUPS + 1]
    centre = exact_dot(scaled, onehot(group == row, F32))
    spread = exact_dot(scaled, onehot(group + GROUPS == row, F32))
    return centre[0:1], lax.rsqrt(spread[0:1] + EPS)


def to_tail(row):
    high = row.astype(BF16).astype(F32)
    mid = (row - high).astype(BF16).astype(F32)
    low = row - high - mid
    index = iota((8, 128), 0)
    part = jnp.where(index == 0, high, jnp.where(index == 1, mid, jnp.where(index == 2, low, 0.0)))
    zero = jnp.zeros((8, 128), F32)
    top = jnp.concatenate([part, zero], axis=1)
    return jnp.concatenate([top, jnp.zeros((TAIL - 8, 256), F32)], axis=0).astype(BF16)


def from_tail(message_ref):
    rows = message_ref.shape[0]
    part = message_ref[rows - TAIL : rows, :].astype(F32)[:, 0:128]
    return jnp.broadcast_to(jnp.sum(part, axis=0, keepdims=True), (8, 128))


def silu(u):
    return 0.5 * u * (1.0 + jnp.tanh(0.5 * u))


def pack_pairs(v):
    n, m, _, lanes = v.shape
    v = v.reshape(n, m // 2, 2, 8, lanes)
    low, high = v[:, :, 0].reshape(-1, 8, lanes), v[:, :, 1].reshape(-1, 8, lanes)
    both = jnp.where(iota(low.shape, 1) < 4, low, pltpu.roll(high, 4, 1))
    return both.reshape(n, m // 2, 8, lanes)


def split_pairs(v, blank):
    inside = iota(v.shape, 1) < 4
    return [jnp.where(inside, v, blank), jnp.where(inside, pltpu.roll(v, 4, 1), blank)]


def edges(act):
    z = iota(act.shape, 2) % BR
    before, after = pltpu.roll(act, 1, 1), pltpu.roll(act, 7, 1)
    return jnp.where(z == BR - 1, before, jnp.where(z == 0, after, 0.0))


def columns(act, size):
    side = edges(act)
    z = iota((size,) + act.shape[1:], 2) % BR
    second = pltpu.roll(side, 2, 2)
    third = pltpu.roll(side, 4, 2)
    mixed = jnp.where(
        (z == 1) | (z == 2), second[1 : 1 + size],
        jnp.where((z == 3) | (z == 4), third[2 : 2 + size], side[0:size]),
    )
    return [act[e : e + size] for e in range(3)] + [mixed]


def halves(lanes):
    return range(lanes // 128)


def read(ref, start, count, stride):
    return jnp.concatenate(
        [ref[h, pl.ds(start, count, stride=stride), :] for h in range(ref.shape[0])], axis=1
    )


def write(ref, start, count, stride, value):
    for h in range(ref.shape[0]):
        ref[h, pl.ds(start, count, stride=stride), :] = value[:, h * 128 : (h + 1) * 128]


def write_block(ref, start, value):
    for h in range(ref.shape[0]):
        ref[h, start : start + value.shape[0], :] = value[:, h * 128 : (h + 1) * 128]


def even(axis):
    return lax.axis_index(axis) % 2 == 0


def sides(axis, first, second):
    i, n = lax.axis_index(axis), lax.axis_size(axis)
    blank = jnp.full(first.shape, SENT, F32)
    second = blank if second is None else second
    low, high = jnp.where(even(axis), second, first), jnp.where(even(axis), first, second)
    return jnp.where(i > 0, low, SENT), jnp.where(i < n - 1, high, SENT)


def coded(feat_ref, keep):
    sx, sy, sb, lanes = feat_ref.shape
    field = jnp.where((keep[:sb] > 0)[None, None], feat_ref[...].astype(F32), SENT)
    return jnp.concatenate([field, jnp.full((sx, sy, 8 - sb, lanes), SENT, F32)], axis=2)


def pre_kernel(members, occ_ref, feat_ref, keep_ref, keys_ref, first_ref, second_ref, tail_ref,
               rows_ref=None):
    sx, sy, sb, lanes = feat_ref.shape
    me = lax.axis_index("gx")
    row = iota((8, lanes), 0)
    keep = jnp.zeros((8, lanes), F32)
    count = 0.0
    for b in range(sb):
        there = occ_ref[me, 0, b].astype(F32)
        keep = jnp.where(row == b, there, keep)
        count = count + there
    count = count * float(sx * sy * BR * GW)
    keep_ref[...] = keep
    seq = keys_ref.shape[1]
    lane = iota(keys_ref.shape, 1)
    keys = jnp.zeros(keys_ref.shape, F32)
    for k in range(members):
        for b in range(sb):
            there = occ_ref[me ^ k, 0, b].astype(F32)
            keys = jnp.where(
                (lane // (seq // members) == k) & (lane % (2 * sb) // 2 == b), there, keys
            )
    keys_ref[...] = keys
    field = feat_ref[...].astype(F32).reshape(sx * sy, sb, lanes)
    total = jnp.sum(jnp.sum(field, axis=0) * keep[:sb], axis=0, keepdims=True)

    def squares_about(mean):
        d = field - mean[None]
        return jnp.sum(jnp.sum(d * d, axis=0) * keep[:sb], axis=0, keepdims=True)

    packed = pack_pairs(coded(feat_ref, keep))
    low = packed[0:2].reshape(-1, lanes)
    high = packed[sx - 2 : sx].reshape(-1, lanes)
    size = low.shape[0]
    first_ref[0:size, :] = jnp.where(even("gx"), high, low).astype(BF16)
    second_ref[0:size, :] = jnp.where(even("gx"), low, high).astype(BF16)
    mine = moments(total, squares_about, count)
    tail = to_tail(mine)
    first_ref[size : size + TAIL, :] = tail
    second_ref[size : size + TAIL, :] = tail
    tail_ref[...] = tail
    if rows_ref is not None:
        rows_ref[...] = jnp.broadcast_to(mine[0:1], rows_ref.shape)


def line_kernel(narrow, keep_ref, feat_ref, first_ref, second_ref, *rest):
    tails, (ext_ref, out_ref, buf) = rest[:-3], rest[-3:]
    sx, sy, sb, lanes = feat_ref.shape
    size = 2 * (sy // 2) * 8
    low, high = sides(
        "gx", first_ref[0:size].astype(F32), second_ref[0:size].astype(F32)
    )
    whole = coded(feat_ref, keep_ref[...]).reshape(sx * sy * 8, lanes)
    write_block(buf, 2 * sy * 8, whole)
    for x0, side in ((0, low), (sx + 2, high)):
        for i in range(2):
            part = side[i * (size // 2) : (i + 1) * (size // 2)].reshape(sy // 2, 8, lanes)
            pair = split_pairs(part, SENT)
            for y in range(sy):
                write_block(buf, ((x0 + i) * sy + y) * 8, pair[y % 2][y // 2])
    rows = (sx + 4) * sy * 8
    ext_ref[...] = jnp.concatenate([buf[h] for h in halves(lanes)], axis=1).astype(BF16)
    count = (sx + 4) * sy
    face = jnp.where(even("gz"), read(buf, sb - 1, count, 8), read(buf, 0, count, 8))
    out_ref[0:count, :] = face.astype(BF16)
    mine = [from_tail(ref) for ref in tails]
    if narrow:
        mine = mine + [from_tail(first_ref), from_tail(second_ref)]
    out_ref[count : count + TAIL, :] = to_tail(merge(stack_rows(mine)))


def corner_rows(count):
    return (count + 15) // 16 * 16


def chip_kernel(sb, sy, ext_ref, own_ref, other_ref, *rest):
    out, (buf, stage) = rest[:-2], rest[-2:]
    lanes = ext_ref.shape[1]
    ex = ext_ref.shape[0] // (sy * 8)
    block = ext_ref[...].astype(F32)
    write_block(buf, 0, block)
    write_block(stage, 0, other_ref[0 : ex * sy].astype(F32))
    gap = corner_rows(ex)
    pad = jnp.zeros((gap - ex, lanes), F32)
    tail = to_tail(merge(stack_rows([from_tail(own_ref), from_tail(other_ref)])))
    packed = pack_pairs(block.reshape(ex, sy, 8, lanes))

    def side(y0):
        face = packed[:, y0 // 2].reshape(ex * 8, lanes)
        inner, outer = [], []
        for i in range(2):
            inner += [read(stage, y0 + i, ex, sy), pad]
            start = (y0 + i) * 8
            outer += [
                jnp.where(
                    even("gz"),
                    read(buf, start, ex, sy * 8),
                    read(buf, start + sb - 1, ex, sy * 8),
                ),
                pad,
            ]
        return [face] + inner, outer

    (near_low, far_low), (near_high, far_high) = side(0), side(sy - 2)
    count = ex * sy
    z_face = jnp.where(even("gz"), read(buf, 0, count, 8), read(buf, sb - 1, count, 8))
    out[0][0:count, :] = z_face.astype(BF16)
    out[0][count : count + TAIL, :] = tail
    for k in range((len(out) - 1) // 2):
        up = even("gy") if k == 0 else jnp.logical_not(even("gy"))
        for ref, low, high in (
            (out[1 + 2 * k], near_low, near_high),
            (out[2 + 2 * k], far_low, far_high),
        ):
            value = jnp.where(
                up, jnp.concatenate(high, axis=0), jnp.concatenate(low, axis=0)
            ).astype(BF16)
            ref[0 : value.shape[0], :] = value
            ref[value.shape[0] : value.shape[0] + TAIL, :] = tail


def band_kernel(layer, weight_ref, *rest):
    pars, out_ref, rows_ref = (rest[:3], rest[3], rest[4]) if len(rest) > 1 else ((), rest[0], None)
    lanes = C * BR
    spread = onehot(iota((C, lanes), 0) == iota((C, lanes), 1) // BR)
    column = onehot(iota((lanes, C), 0) // BR == iota((lanes, C), 1))
    turned = jnp.transpose(weight_ref[layer].astype(F32)).astype(BF16)
    wide = jnp.dot(turned, spread, preferred_element_type=F32).astype(BF16)
    row = iota((lanes, lanes), 0)
    zi, zo = row % BR, iota((lanes, lanes), 1) % BR
    for ex in range(3):
        mixed = jnp.zeros((lanes, lanes), F32)
        for ey in range(3):
            terms = []
            for ez in range(3):
                q = (ex * 3 + ey) * 3 + ez
                terms.append(
                    jnp.dot(column, wide[q * C : (q + 1) * C], preferred_element_type=F32)
                )
            inner = jnp.where(zi == zo - 1, terms[0], 0.0)
            inner = jnp.where(zi == zo, terms[1], inner)
            inner = jnp.where(zi == zo + 1, terms[2], inner)
            outer = jnp.where((zi == BR - 1) & (zo == 0), terms[0], 0.0)
            outer = jnp.where((zi == 0) & (zo == BR - 1), terms[2], outer)
            mixed = mixed + (pltpu.roll(outer, 2 * ey, 0) if ey else outer)
            out_ref[ex, ey * lanes : (ey + 1) * lanes, :] = inner.astype(BF16)
        out_ref[ex, 3 * lanes : 4 * lanes, :] = mixed.astype(BF16)
    if rows_ref is not None:
        pick = onehot(iota((C, lanes), 0) == iota((C, lanes), 1) // BR, F32)
        for k, ref in enumerate(pars):
            rows_ref[2 * k : 2 * k + 2, :] = exact_dot(ref[...], pick)
        rows_ref[6:8, :] = jnp.zeros((2, lanes), F32)


def turn_kernel(weight_ref, out_ref):
    kinds, cols, feats = weight_ref.shape
    r = iota((feats, 1), 0)
    source = (r % 128) // 4 * 32 + r // 128 * 4 + r % 4
    pick = onehot(source == iota((feats, feats), 1))
    for k in range(kinds):
        out_ref[:, k * cols : (k + 1) * cols] = lax.dot_general(
            pick, weight_ref[k], (((1,), (1,)), ((), ())), preferred_element_type=F32
        ).astype(BF16)


def first_kernel(narrow, faces, sy, sb, ext_ref, own_ref, core_ref, zface_ref, *rest):
    near, far = rest[0 : 2 * faces : 2], rest[1 : 2 * faces : 2]
    rest = rest[2 * faces :]
    stats_ref = None
    if not narrow:
        stats_ref, rest = rest[0], rest[1:]
    keep_ref, weight_ref, rows_ref, mid_ref, out_ref, buf, lhs, msk = rest
    lanes = ext_ref.shape[1]
    ex = ext_ref.shape[0] // (sy * 8)
    ey = sy + 4
    count = ex * sy
    z_low, z_high = sides(
        "gz", core_ref[0:count].astype(F32), zface_ref[0:count].astype(F32)
    )
    for x in range(ex):
        write_block(
            buf, (x * ey + 2) * 8, ext_ref[x * sy * 8 : (x + 1) * sy * 8].astype(F32)
        )
        part = slice(x * sy, (x + 1) * sy)
        write(buf, (x * ey + 2) * 8 + 7, sy, 8, z_low[part])
        write(buf, (x * ey + 2) * 8 + sb, sy, 8, z_high[part])
    gap = corner_rows(ex)
    size = ex * 8
    face = sides("gy", *[
        near[k][0:size].astype(F32) if k < faces else None for k in range(2)
    ])
    inner = sides("gy", *[
        near[k][size : size + 2 * gap].astype(F32) if k < faces else None for k in range(2)
    ])
    outer = sides("gy", *[
        far[k][0 : 2 * gap].astype(F32) if k < faces else None for k in range(2)
    ])
    for s, y0 in enumerate((0, sy + 2)):
        pair = split_pairs(face[s].reshape(ex, 8, lanes), SENT)
        c_low, c_high = sides("gz", inner[s], outer[s])
        for i in range(2):
            for x in range(ex):
                write_block(buf, (x * ey + y0 + i) * 8, pair[i][x])
            write(buf, (y0 + i) * 8 + 7, ex, ey * 8, c_low[i * gap : i * gap + ex])
            write(buf, (y0 + i) * 8 + sb, ex, ey * 8, c_high[i * gap : i * gap + ex])
    if narrow:
        merged = merge(stack_rows(
            [from_tail(r) for r in (own_ref, zface_ref) + tuple(near) + tuple(far)]
        ))
    else:
        merged = merge(stats_ref[...])
    centre, scale = centre_scale(merged, lanes)
    gain, shift, bias = rows_ref[0:1], rows_ref[2:3], rows_ref[4:5]
    scale = scale * gain
    oy, sx = sy + 2, ex - 4
    step = ey * 8
    for x in range(ex):
        v = jnp.concatenate(
            [buf[h, x * step : (x + 1) * step, :] for h in halves(lanes)], axis=1
        )
        there = v != SENT
        msk[x * step : (x + 1) * step] = onehot(there[:, 0:128], F32)
        act = jnp.where(there, silu((v - centre) * scale + shift), 0.0).reshape(ey, 8, lanes)
        for e, part in enumerate(columns(act, oy)):
            lhs[x * oy * 8 : (x + 1) * oy * 8, e * lanes : (e + 1) * lanes] = (
                part.reshape(oy * 8, lanes).astype(BF16)
            )
    ox = sx + 2
    size = ox * oy * 8
    acc = bias
    for e in range(3):
        acc = acc + jnp.dot(
            lhs[e * oy * 8 : e * oy * 8 + size, :], weight_ref[e], preferred_element_type=F32
        )
    mid_ref[...] = acc
    keep = keep_ref[...]
    entries = jnp.sum(keep[:, 0:1]) * float(sx * sy * BR * GW)

    def over_cells(f):
        out = jnp.zeros((8, lanes), F32)
        for x in range(1, sx + 1):
            own = mid_ref[(x * oy + 1) * 8 : (x * oy + oy - 1) * 8].reshape(sy, 8, lanes)
            out = out + jnp.sum(f(own), axis=0)
        return jnp.sum(out * keep, axis=0, keepdims=True)

    def squares_about(mean):
        return over_cells(lambda v: (v - mean[None]) * (v - mean[None]))

    mine = moments(over_cells(lambda v: v), squares_about, entries)
    out_ref[...] = jnp.broadcast_to(mine[0:1], out_ref.shape)
    for x in range(ox):
        rows = slice(x * oy * 8, (x + 1) * oy * 8)
        there = msk[(x + 1) * step + 8 : (x + 2) * step - 8]
        there = jnp.concatenate([there] * (lanes // 128), axis=1) > 0
        mid_ref[rows] = jnp.where(there, mid_ref[rows], BIG)


def second_kernel(stats_ref, mid_ref, weight_ref, rows_ref, keep_ref, feat_ref,
                  fine_ref, tok_ref, lhs):
    sx, sy, sb, lanes = feat_ref.shape
    step = (sy + 2) * 8
    centre, scale = centre_scale(merge(stats_ref[...]), lanes)
    gain, shift, bias = rows_ref[1:2], rows_ref[3:4], rows_ref[5:6]
    scale = scale * gain
    half = sy // 2 * 8
    for x in range(sx + 2):
        v = mid_ref[x * step : (x + 1) * step]
        act = jnp.where(v < BIG, silu((v - centre) * scale + shift), 0.0)
        for e, part in enumerate(columns(act.reshape(sy + 2, 8, lanes), sy)):
            lhs[x * half : (x + 1) * half, e * lanes : (e + 1) * lanes] = (
                pack_pairs(part[None]).reshape(half, lanes).astype(BF16)
            )
    size = sx * half
    acc = bias
    for e in range(3):
        acc = acc + jnp.dot(
            lhs[e * half : e * half + size, :], weight_ref[e], preferred_element_type=F32
        )
    keep = keep_ref[...]
    keep = jnp.where(iota(keep.shape, 0) < sb, keep, pltpu.roll(keep, sb, 0))
    blank = jnp.zeros((sx, sy, 8 - sb, lanes), F32)
    field = pack_pairs(jnp.concatenate([feat_ref[...].astype(F32), blank], axis=2))
    out = (field.reshape(-1, 8, lanes) * keep + acc.reshape(-1, 8, lanes)) * keep
    out = out.astype(BF16)
    wide = out.astype(F32)
    other = pltpu.roll(wide, 4, 1)
    fine = jnp.stack([wide[:, :sb], other[:, :sb]], axis=1)
    fine_ref[...] = fine.reshape(sx, sy, sb, lanes).astype(BF16)
    i, j = iota((lanes, lanes), 0), iota((lanes, lanes), 1)
    pick = onehot(i == (j % 128) // 4 * 8 + j // 128 * 4 + j % 4)
    moved = jnp.dot(out.reshape(size, lanes), pick, preferred_element_type=F32).reshape(
        sx // 2, 2, sy // 4, 2, 8, lanes
    )
    count = sx // 2 * (sy // 4)
    parts = []
    for x in range(2):
        for y in range(2):
            piece = moved[:, x, :, y].reshape(count, 8, lanes)
            low, high = piece[:, :, :128], piece[:, :, 128:]
            inside = iota(low.shape, 1) < 4
            for both in (
                jnp.where(inside, low, pltpu.roll(high, 4, 1)),
                jnp.where(inside, pltpu.roll(low, 4, 1), high),
            ):
                parts.append(both.reshape(count * 8, 128).astype(BF16))
    tokens = jnp.concatenate(parts, axis=1)
    n = count * 8
    i, j = iota((n, n), 0), iota((n, n), 1)
    order = onehot(j == i // 8 * 8 + i % 2 * 4 + i % 8 // 2)
    tok_ref[...] = jnp.dot(order, tokens, preferred_element_type=F32).astype(BF16)


def attend_kernel(members, keys_ref, weight_ref, *refs):
    tok_refs, out_refs, (toks, proj) = refs[:members], refs[members : 2 * members], refs[-2:]
    own = tok_refs[0].shape[0]
    seq = own * members
    cols = weight_ref.shape[1] // 3
    for k in range(members):
        toks[k * own : (k + 1) * own, :] = tok_refs[k][...]
    proj[...] = jnp.dot(toks[...], weight_ref[...], preferred_element_type=F32).astype(BF16)
    there = keys_ref[0:1] > 0
    width = min(128, cols)
    for t in range(cols // width):
        q = proj[:, t * width : (t + 1) * width]
        keys = proj[:, cols + t * width : cols + (t + 1) * width]
        values = proj[:, 2 * cols + t * width : 2 * cols + (t + 1) * width]
        head = iota((seq, width), 1) // HD
        merged = jnp.zeros((seq, width), F32)
        for h in range(width // HD):
            mine = jnp.where(head == h, q.astype(F32), 0.0).astype(BF16)
            scores = lax.dot_general(
                mine, keys, (((1,), (1,)), ((), ())), preferred_element_type=F32
            ) * float(HD) ** (-0.5)
            scores = jnp.where(there, scores, -BIG)
            probs = jnp.exp(scores - jnp.max(scores, axis=1, keepdims=True))
            total = jnp.sum(probs, axis=1, keepdims=True)
            mixed = jnp.dot(probs.astype(BF16), values, preferred_element_type=F32)
            merged = jnp.where(head == h, mixed / total, merged)
        merged = merged.astype(BF16)
        for k in range(members):
            out_refs[k][:, t * width : (t + 1) * width] = merged[k * own : (k + 1) * own]


def place_kernel(members, keep_ref, *refs):
    out_ref = refs[-1]
    own, cols = refs[0].shape
    me = lax.axis_index("gx")
    row = iota((8, cols), 0)
    keep = jnp.zeros((8, cols), F32)
    for b in range(4):
        keep = jnp.where(row // 2 == b, jnp.broadcast_to(keep_ref[b : b + 1, :cols], (8, cols)), keep)
    for k in range(members):
        value = refs[k][...].astype(F32).reshape(own // 8, 8, cols)
        value = jnp.where((keep > 0)[None], value, 0.0).reshape(own, cols).astype(BF16)
        if cols % 128 == 0:
            out_ref[0, :, pl.ds(pl.multiple_of((me ^ k) * cols, cols), cols)] = value
        else:
            out_ref[k] = value


VM = pl.BlockSpec(memory_space=pltpu.VMEM)
SM = pl.BlockSpec(memory_space=pltpu.SMEM)


def call(kernel, name, specs, out, args, scratch=(), flops=0, nbytes=0, mib=16):
    return pl.pallas_call(
        kernel,
        out_shape=out,
        in_specs=list(specs),
        out_specs=jax.tree.map(lambda _: VM, out),
        scratch_shapes=list(scratch),
        name=name,
        cost_estimate=pl.CostEstimate(flops=flops, bytes_accessed=nbytes, transcendentals=0),
        compiler_params=pltpu.CompilerParams(vmem_limit_bytes=mib * 2**20),
    )(*args)


def shape(*dims, dtype=BF16):
    return jax.ShapeDtypeStruct(dims, dtype)


def pairing(n, odd, closed):
    partner = {i: (i ^ 1 if not odd else (i + 1 if i % 2 else i - 1)) for i in range(n)}
    if closed:
        partner = {i: j % n for i, j in partner.items()}
    return {i: j for i, j in partner.items() if 0 <= j < n and i != j}


def body(features, occupancy, norm_gain, norm_shift, conv_weight, conv_bias, qkv_weight):
    sx, sy, sb, lanes = features.shape
    nx, ny, nz = (lax.axis_size(a) for a in ALL)
    devices = nx * ny * nz
    narrow = nx == 4 and ny == 2 and nz == 4
    own = sx // 2 * (sy // 4) * sb * 2
    ex = sx + 4
    row_shape = [] if narrow else [shape(devices, 128, dtype=F32)]

    slab = sy * 8 + TAIL
    keep, keys, first, second, tail, *stats = call(
        functools.partial(pre_kernel, nx), "pre", (SM, VM),
        [shape(8, lanes, dtype=F32), shape(8, own * nx, dtype=F32), shape(slab, lanes),
         shape(slab, lanes), shape(TAIL, lanes)] + row_shape,
        (occupancy, features), nbytes=10**6,
    )
    stats = [lax.all_to_all(s, ALL, 0, 0, tiled=True) for s in stats]
    got = [
        lax.ppermute(first, "gx", list(pairing(nx, False, False).items())),
        lax.ppermute(second, "gx", list(pairing(nx, True, narrow).items())),
    ]
    tails = [tail]
    if narrow:
        tails.append(lax.ppermute(tail, "gx", [(i, i ^ 2) for i in range(nx)]))
    count = ex * sy
    ext, mine = call(
        functools.partial(line_kernel, narrow), "line", (VM,) * (4 + len(tails)),
        [shape(count * 8, lanes), shape(count + TAIL, lanes)],
        (keep, features, *got, *tails),
        [pltpu.VMEM((lanes // 128, count * 8, 128), F32)], nbytes=10**6,
    )
    core = lax.ppermute(mine, "gz", list(pairing(nz, False, False).items()))

    faces = 1 if ny == 2 else 2
    gap = corner_rows(ex)
    near, far = ex * 8 + 2 * gap + TAIL, 2 * gap + TAIL
    zface, *yfaces = call(
        functools.partial(chip_kernel, sb, sy), "chip", (VM,) * 3,
        [shape(count + TAIL, lanes)] + [shape(near, lanes), shape(far, lanes)] * faces,
        (ext, mine, core),
        [pltpu.VMEM((lanes // 128, count * 8, 128), F32),
         pltpu.VMEM((lanes // 128, count, 128), F32)], nbytes=10**6,
    )
    odd_z = pairing(nz, True, narrow)
    own_tail = zface
    zgot = lax.ppermute(zface, "gz", list(odd_z.items()))
    ygot = []
    for k in range(faces):
        along = pairing(ny, k == 1, False)
        ygot.append(lax.ppermute(yfaces[2 * k], "gy", list(along.items())))
        both = [
            (y * nz + z, along[y] * nz + odd_z[z]) for y in along for z in odd_z
        ]
        ygot.append(lax.ppermute(yfaces[2 * k + 1], ("gy", "gz"), both))

    band = shape(3, 4 * lanes, lanes)
    band0, rows = call(
        functools.partial(band_kernel, 0), "band0", (VM,) * 4, [band, shape(8, lanes, dtype=F32)],
        (conv_weight, norm_gain, norm_shift, conv_bias), nbytes=8 * 10**6,
    )
    band1 = call(
        functools.partial(band_kernel, 1), "band1", (VM,), band, (conv_weight,), nbytes=8 * 10**6,
    )
    cols, feats = qkv_weight.shape[1:]
    turned = call(
        turn_kernel, "turn", (VM,), shape(feats, 3 * cols), (qkv_weight,),
        flops=2 * 3 * cols * feats * feats, nbytes=6 * 10**6,
    )

    ey, oy = sy + 4, sy + 2
    size = (sx + 2) * oy * 8
    mid, mine = call(
        functools.partial(first_kernel, narrow, faces, sy, sb), "first",
        (VM,) * (7 + 2 * faces + len(stats)),
        [shape(size, lanes, dtype=F32), shape(devices, 128, dtype=F32)],
        (ext, own_tail, core, zgot, *ygot, *stats, keep, band0, rows),
        [pltpu.VMEM((lanes // 128, ex * ey * 8, 128), F32),
         pltpu.VMEM((ex * oy * 8, 4 * lanes), BF16),
         pltpu.VMEM((ex * ey * 8, 128), F32)],
        flops=2 * 10**9, nbytes=4 * 10**6, mib=20,
    )
    stats = lax.all_to_all(mine, ALL, 0, 0, tiled=True)
    fine_out, tokens = call(
        second_kernel, "second", (VM,) * 6,
        [shape(*features.shape), shape(own, feats)],
        (stats, mid, band1, rows, keep, features),
        [pltpu.VMEM(((sx + 2) * sy * 4, 4 * lanes), BF16)],
        flops=10**9, nbytes=4 * 10**6,
    )
    swaps = [[(i, i ^ k) for i in range(nx)] for k in range(nx)]
    blocks = [tokens] + [lax.ppermute(tokens, "gx", swaps[k]) for k in range(1, nx)]
    outs = call(
        functools.partial(attend_kernel, nx), "attend", (VM,) * (2 + nx),
        [shape(own, cols)] * nx, (keys, turned, *blocks),
        [pltpu.VMEM((own * nx, feats), BF16), pltpu.VMEM((own * nx, 3 * cols), BF16)],
        flops=10**9, nbytes=3 * 10**6, mib=16 if narrow else 40,
    )
    outs = [outs[0]] + [lax.ppermute(outs[k], "gx", swaps[k]) for k in range(1, nx)]
    lined = cols % 128 == 0
    attention = call(
        functools.partial(place_kernel, nx), "place", (VM,) * (1 + nx),
        shape(1, own, nx * cols) if lined else shape(nx, own, cols), (keep, *outs),
        nbytes=3 * 10**5, mib=8,
    )
    if not lined:
        me = lax.axis_index("gx")
        attention = jnp.concatenate(
            [lax.dynamic_index_in_dim(attention, me ^ j, 0, keepdims=False) for j in range(nx)],
            axis=1,
        )[None]
    return (fine_out, attention)


def solution(mesh):
    placed = (
        P("gx", "gy", "gz", None),
        P(None, "gy", "gz"),
        P(),
        P(),
        P(),
        P(),
        P(None, "gx", None),
    )
    return jax.shard_map(
        body,
        mesh=mesh,
        in_specs=placed,
        out_specs=(P("gx", "gy", "gz", None), P(("gy", "gz"), "gx", None)),
        check_vma=False,
    )
```

```python
import functools

import jax
import jax.numpy as jnp
from jax import lax
from jax.experimental import pallas as pl
from jax.experimental.pallas import tpu as pltpu
from jax.sharding import PartitionSpec as P

C = 32
GW = 4
HD = 64
BR = 8
EPS = 1e-05
SENT = 512.0
BIG = 1e30
ALL = ("gx", "gy", "gz")
F32, BF16 = jnp.float32, jnp.bfloat16
HIGHEST = lax.Precision.HIGHEST
TAIL = 16


def iota(shape, dim):
    return lax.broadcasted_iota(jnp.int32, shape, dim)


def onehot(cond, dtype=BF16):
    return jnp.where(cond, 1.0, 0.0).astype(dtype)


def exact_dot(a, b):
    return jnp.dot(a, b, precision=HIGHEST, preferred_element_type=F32)


def spread_sum(v):
    lane = iota(v.shape, 1)
    s = 1
    while s < GW * BR:
        v = v + jnp.where(lane & s == 0, pltpu.roll(v, 128 - s, 1), pltpu.roll(v, s, 1))
        s *= 2
    return v


def group_sum(total):
    k = total.shape[1] // 128
    rows = [jnp.broadcast_to(total[:, h * 128 : (h + 1) * 128], (8, 128)) for h in range(k)]
    out = spread_sum(jnp.concatenate(rows, axis=0))
    return jnp.concatenate([out[h * 8 : (h + 1) * 8] for h in range(k)], axis=1)


def moments(total, squares_about, count):
    sums = group_sum(total)
    squares = group_sum(squares_about((sums / count)[0:1]))
    return sums, squares, jnp.zeros(sums.shape, F32) + count


def merge(parts):
    n = sum(p[2] for p in parts)
    sums = sum(p[0] for p in parts)
    centre = sums / n
    squares = sum(p[1] + p[2] * (p[0] / p[2] - centre) ** 2 for p in parts)
    return sums, squares, n


def centre_scale(part):
    return part[0] / part[2], lax.rsqrt(part[1] / part[2] + EPS)


def to_row(part):
    j = iota((8, 128), 1) % (GW * BR)
    row = jnp.zeros((8, 128), F32)
    for h in range(2):
        for k in range(3):
            row = jnp.where(j == 4 * h + k, part[k][:, h * 128 : (h + 1) * 128], row)
    return row


def from_rows(rows):
    n = jnp.maximum(pltpu.roll(rows, 126, 1), 1.0)
    total = jnp.sum(n, axis=0, keepdims=True)
    centre = jnp.sum(rows, axis=0, keepdims=True) / total
    drift = rows / n - centre
    squares = pltpu.roll(rows, 127, 1) + n * drift * drift
    spread = jnp.sum(squares, axis=0, keepdims=True) / total
    j = iota((8, 128), 1) % (GW * BR)
    blocks = [
        jnp.where(j == 4 * h, jnp.broadcast_to(v, (8, 128)), 0.0)
        for v in (centre, spread) for h in range(2)
    ]
    out = spread_sum(jnp.concatenate(blocks, axis=0))
    out = [out[8 * i : 8 * i + 1] for i in range(4)]
    return (
        jnp.concatenate(out[:2], axis=1),
        lax.rsqrt(jnp.concatenate(out[2:], axis=1) + EPS),
    )


def to_tail(part):
    index = iota((8, 256), 0)
    blocks = [jnp.zeros((8, 256), F32), jnp.zeros((8, 256), F32)]
    for k, value in enumerate(part):
        value = jnp.broadcast_to(value[0:1], (8, 256))
        high = value.astype(BF16).astype(F32)
        mid = (value - high).astype(BF16).astype(F32)
        for i, piece in enumerate((high, mid, value - high - mid)):
            blocks[k // 2] = jnp.where(index == 3 * (k % 2) + i, piece, blocks[k // 2])
    return jnp.concatenate(blocks, axis=0).astype(BF16)


def from_tail(message_ref):
    rows = message_ref.shape[0]
    part = message_ref[rows - TAIL : rows, :].astype(F32)
    return [
        jnp.sum(part[r : r + 3], axis=0, keepdims=True) for r in (0, 3, 8)
    ]


def silu(u):
    return 0.5 * u * (1.0 + jnp.tanh(0.5 * u))


def pack_pairs(v):
    n, m, _, lanes = v.shape
    v = v.reshape(n, m // 2, 2, 8, lanes)
    low, high = v[:, :, 0].reshape(-1, 8, lanes), v[:, :, 1].reshape(-1, 8, lanes)
    both = jnp.where(iota(low.shape, 1) < 4, low, pltpu.roll(high, 4, 1))
    return both.reshape(n, m // 2, 8, lanes)


def split_pairs(v, blank):
    inside = iota(v.shape, 1) < 4
    return [jnp.where(inside, v, blank), jnp.where(inside, pltpu.roll(v, 4, 1), blank)]


def edges(act):
    z = iota(act.shape, 2) % BR
    before, after = pltpu.roll(act, 1, 1), pltpu.roll(act, 7, 1)
    return jnp.where(z == BR - 1, before, jnp.where(z == 0, after, 0.0))


def columns(act, size):
    side = edges(act)
    z = iota((size,) + act.shape[1:], 2) % BR
    second = pltpu.roll(side, 2, 2)
    third = pltpu.roll(side, 4, 2)
    mixed = jnp.where(
        (z == 1) | (z == 2), second[1 : 1 + size],
        jnp.where((z == 3) | (z == 4), third[2 : 2 + size], side[0:size]),
    )
    return [act[e : e + size] for e in range(3)] + [mixed]


def halves(lanes):
    return range(lanes // 128)


def read(ref, start, count, stride):
    return jnp.concatenate(
        [ref[h, pl.ds(start, count, stride=stride), :] for h in range(ref.shape[0])], axis=1
    )


def write(ref, start, count, stride, value):
    for h in range(ref.shape[0]):
        ref[h, pl.ds(start, count, stride=stride), :] = value[:, h * 128 : (h + 1) * 128]


def write_block(ref, start, value):
    for h in range(ref.shape[0]):
        ref[h, start : start + value.shape[0], :] = value[:, h * 128 : (h + 1) * 128]


def even(axis):
    return lax.axis_index(axis) % 2 == 0


def sides(axis, first, second):
    i, n = lax.axis_index(axis), lax.axis_size(axis)
    blank = jnp.full(first.shape, SENT, F32)
    second = blank if second is None else second
    low, high = jnp.where(even(axis), second, first), jnp.where(even(axis), first, second)
    return jnp.where(i > 0, low, SENT), jnp.where(i < n - 1, high, SENT)


def pre_kernel(members, occ_ref, feat_ref, keep_ref, keys_ref, coded_ref, first_ref, second_ref,
               tail_ref, rows_ref=None):
    sx, sy, sb, lanes = feat_ref.shape
    me = lax.axis_index("gx")
    row = iota((8, lanes), 0)
    keep = jnp.zeros((8, lanes), F32)
    count = 0.0
    for b in range(sb):
        there = occ_ref[me, 0, b].astype(F32)
        keep = jnp.where(row == b, there, keep)
        count = count + there
    count = count * float(sx * sy * BR * GW)
    keep_ref[...] = keep
    seq = keys_ref.shape[1]
    lane = iota(keys_ref.shape, 1)
    keys = jnp.zeros(keys_ref.shape, F32)
    for k in range(members):
        for b in range(sb):
            there = occ_ref[me ^ k, 0, b].astype(F32)
            keys = jnp.where(
                (lane // (seq // members) == k) & (lane % (2 * sb) // 2 == b), there, keys
            )
    keys_ref[...] = keys
    field = feat_ref[...].astype(F32)
    wide = jnp.concatenate([field, jnp.zeros((sx, sy, 8 - sb, lanes), F32)], axis=2)
    wide = wide.reshape(sx * sy, 8, lanes)
    total = jnp.sum(jnp.sum(wide, axis=0) * keep, axis=0, keepdims=True)

    def squares_about(mean):
        d = wide - mean[None]
        return jnp.sum(jnp.sum(d * d, axis=0) * keep, axis=0, keepdims=True)

    code = jnp.where((keep > 0)[None], wide, SENT)
    coded_ref[...] = code.reshape(sx * sy * 8, lanes).astype(BF16)
    packed = pack_pairs(code.reshape(sx, sy, 8, lanes))
    low = packed[0:2].reshape(-1, lanes)
    high = packed[sx - 2 : sx].reshape(-1, lanes)
    size = low.shape[0]
    first_ref[0:size, :] = jnp.where(even("gx"), high, low).astype(BF16)
    second_ref[0:size, :] = jnp.where(even("gx"), low, high).astype(BF16)
    mine = moments(total, squares_about, count)
    tail = to_tail(mine)
    first_ref[size : size + TAIL, :] = tail
    second_ref[size : size + TAIL, :] = tail
    tail_ref[...] = tail
    if rows_ref is not None:
        rows_ref[...] = jnp.broadcast_to(to_row(mine)[0:1], rows_ref.shape)


def line_kernel(narrow, sy, sb, rows_ref, coded_ref, first_ref, second_ref, *rest):
    tails, (ext_ref, out_ref, buf) = rest[:-3], rest[-3:]
    lanes = coded_ref.shape[1]
    sx = coded_ref.shape[0] // (sy * 8)
    size = 2 * (sy // 2) * 8
    low, high = sides(
        "gx", first_ref[0:size].astype(F32), second_ref[0:size].astype(F32)
    )
    write_block(buf, 2 * sy * 8, coded_ref[...].astype(F32))
    for x0, side in ((0, low), (sx + 2, high)):
        for i in range(2):
            part = side[i * (size // 2) : (i + 1) * (size // 2)].reshape(sy // 2, 8, lanes)
            pair = split_pairs(part, SENT)
            for y in range(sy):
                write_block(buf, ((x0 + i) * sy + y) * 8, pair[y % 2][y // 2])
    rows = (sx + 4) * sy * 8
    ext_ref[...] = jnp.concatenate([buf[h] for h in halves(lanes)], axis=1).astype(BF16)
    count = (sx + 4) * sy
    face = jnp.where(even("gz"), read(buf, sb - 1, count, 8), read(buf, 0, count, 8))
    out_ref[0:count, :] = face.astype(BF16)
    mine = [from_tail(ref) for ref in tails]
    if narrow:
        mine = mine + [from_tail(first_ref), from_tail(second_ref)]
    out_ref[count : count + TAIL, :] = to_tail(merge(mine))


def corner_rows(count):
    return (count + 15) // 16 * 16


def chip_kernel(sb, sy, ext_ref, own_ref, other_ref, *rest):
    out, (buf, stage) = rest[:-2], rest[-2:]
    lanes = ext_ref.shape[1]
    ex = ext_ref.shape[0] // (sy * 8)
    block = ext_ref[...].astype(F32)
    write_block(buf, 0, block)
    write_block(stage, 0, other_ref[0 : ex * sy].astype(F32))
    gap = corner_rows(ex)
    pad = jnp.zeros((gap - ex, lanes), F32)
    tail = to_tail(merge([from_tail(own_ref), from_tail(other_ref)]))
    packed = pack_pairs(block.reshape(ex, sy, 8, lanes))

    def side(y0):
        face = packed[:, y0 // 2].reshape(ex * 8, lanes)
        inner, outer = [], []
        for i in range(2):
            inner += [read(stage, y0 + i, ex, sy), pad]
            start = (y0 + i) * 8
            outer += [
                jnp.where(
                    even("gz"),
                    read(buf, start, ex, sy * 8),
                    read(buf, start + sb - 1, ex, sy * 8),
                ),
                pad,
            ]
        return [face] + inner, outer

    (near_low, far_low), (near_high, far_high) = side(0), side(sy - 2)
    count = ex * sy
    z_face = jnp.where(even("gz"), read(buf, 0, count, 8), read(buf, sb - 1, count, 8))
    out[0][0:count, :] = z_face.astype(BF16)
    out[0][count : count + TAIL, :] = tail
    for k in range((len(out) - 1) // 2):
        up = even("gy") if k == 0 else jnp.logical_not(even("gy"))
        for ref, low, high in (
            (out[1 + 2 * k], near_low, near_high),
            (out[2 + 2 * k], far_low, far_high),
        ):
            value = jnp.where(
                up, jnp.concatenate(high, axis=0), jnp.concatenate(low, axis=0)
            ).astype(BF16)
            ref[0 : value.shape[0], :] = value
            ref[value.shape[0] : value.shape[0] + TAIL, :] = tail


def band_kernel(weight_ref, *rest):
    out_ref, rows_ref = rest[-2:] if len(rest) == 2 else rest[1:3]
    lanes = C * BR
    spread = onehot(iota((C, lanes), 0) == iota((C, lanes), 1) // BR)
    column = onehot(iota((lanes, C), 0) // BR == iota((lanes, C), 1))
    turned = jnp.transpose(weight_ref[0].astype(F32)).astype(BF16)
    wide = jnp.dot(turned, spread, preferred_element_type=F32).astype(BF16)
    row = iota((lanes, lanes), 0)
    zi, zo = row % BR, iota((lanes, lanes), 1) % BR
    for ex in range(3):
        mixed = jnp.zeros((lanes, lanes), F32)
        for ey in range(3):
            terms = []
            for ez in range(3):
                q = (ex * 3 + ey) * 3 + ez
                terms.append(
                    jnp.dot(column, wide[q * C : (q + 1) * C], preferred_element_type=F32)
                )
            inner = jnp.where(zi == zo - 1, terms[0], 0.0)
            inner = jnp.where(zi == zo, terms[1], inner)
            inner = jnp.where(zi == zo + 1, terms[2], inner)
            outer = jnp.where((zi == BR - 1) & (zo == 0), terms[0], 0.0)
            outer = jnp.where((zi == 0) & (zo == BR - 1), terms[2], outer)
            mixed = mixed + (pltpu.roll(outer, 2 * ey, 0) if ey else outer)
            out_ref[ex, ey * lanes : (ey + 1) * lanes, :] = inner.astype(BF16)
        out_ref[ex, 3 * lanes : 4 * lanes, :] = mixed.astype(BF16)
    if len(rest) > 2:
        pick = onehot(iota((C, lanes), 0) == iota((C, lanes), 1) // BR, F32)
        rows_ref[...] = jnp.zeros(rows_ref.shape, F32)
        rows_ref[0 : rest[0].shape[0], :] = exact_dot(rest[0][...], pick)
        rest[3][...] = weight_ref[1:2]
    else:
        rows_ref[...] = jnp.zeros(rows_ref.shape, F32)


def turn_kernel(weight_ref, out_ref):
    kinds, cols, feats = weight_ref.shape
    r = iota((feats, 1), 0)
    source = (r % 128) // 4 * 32 + r // 128 * 4 + r % 4
    pick = onehot(source == iota((feats, feats), 1))
    for k in range(kinds):
        out_ref[:, k * cols : (k + 1) * cols] = lax.dot_general(
            pick, weight_ref[k], (((1,), (1,)), ((), ())), preferred_element_type=F32
        ).astype(BF16)


def first_kernel(narrow, faces, sy, sb, ext_ref, own_ref, core_ref, zface_ref, *rest):
    near, far = rest[0 : 2 * faces : 2], rest[1 : 2 * faces : 2]
    rest = rest[2 * faces :]
    stats_ref = None
    if not narrow:
        stats_ref, rest = rest[0], rest[1:]
    keep_ref, weight_ref, rows_ref, _, mid_ref, out_ref, buf, lhs, msk = rest
    lanes = ext_ref.shape[1]
    ex = ext_ref.shape[0] // (sy * 8)
    ey = sy + 4
    count = ex * sy
    z_low, z_high = sides(
        "gz", core_ref[0:count].astype(F32), zface_ref[0:count].astype(F32)
    )
    for x in range(ex):
        write_block(
            buf, (x * ey + 2) * 8, ext_ref[x * sy * 8 : (x + 1) * sy * 8].astype(F32)
        )
        part = slice(x * sy, (x + 1) * sy)
        write(buf, (x * ey + 2) * 8 + 7, sy, 8, z_low[part])
        write(buf, (x * ey + 2) * 8 + sb, sy, 8, z_high[part])
    gap = corner_rows(ex)
    size = ex * 8
    face = sides("gy", *[
        near[k][0:size].astype(F32) if k < faces else None for k in range(2)
    ])
    inner = sides("gy", *[
        near[k][size : size + 2 * gap].astype(F32) if k < faces else None for k in range(2)
    ])
    outer = sides("gy", *[
        far[k][0 : 2 * gap].astype(F32) if k < faces else None for k in range(2)
    ])
    for s, y0 in enumerate((0, sy + 2)):
        pair = split_pairs(face[s].reshape(ex, 8, lanes), SENT)
        c_low, c_high = sides("gz", inner[s], outer[s])
        for i in range(2):
            for x in range(ex):
                write_block(buf, (x * ey + y0 + i) * 8, pair[i][x])
            write(buf, (y0 + i) * 8 + 7, ex, ey * 8, c_low[i * gap : i * gap + ex])
            write(buf, (y0 + i) * 8 + sb, ex, ey * 8, c_high[i * gap : i * gap + ex])
    if narrow:
        centre, scale = centre_scale(merge(
            [from_tail(r) for r in (own_ref, zface_ref) + tuple(near) + tuple(far)]
        ))
    else:
        centre, scale = from_rows(stats_ref[...])
    gain, shift, bias = rows_ref[0:1], rows_ref[2:3], rows_ref[4:5]
    scale = scale * gain
    oy, sx = sy + 2, ex - 4
    step = ey * 8
    for x in range(ex):
        v = jnp.concatenate(
            [buf[h, x * step : (x + 1) * step, :] for h in halves(lanes)], axis=1
        )
        there = v != SENT
        msk[x * step : (x + 1) * step] = onehot(there[:, 0:128], F32)
        act = jnp.where(there, silu((v - centre) * scale + shift), 0.0).reshape(ey, 8, lanes)
        for e, part in enumerate(columns(act, oy)):
            lhs[x * oy * 8 : (x + 1) * oy * 8, e * lanes : (e + 1) * lanes] = (
                part.reshape(oy * 8, lanes).astype(BF16)
            )
    ox = sx + 2
    size = ox * oy * 8
    acc = bias
    for e in range(3):
        acc = acc + jnp.dot(
            lhs[e * oy * 8 : e * oy * 8 + size, :], weight_ref[e], preferred_element_type=F32
        )
    mid_ref[...] = acc
    keep = keep_ref[...]
    entries = jnp.sum(keep[:, 0:1]) * float(sx * sy * BR * GW)

    def over_cells(f):
        out = jnp.zeros((8, lanes), F32)
        for x in range(1, sx + 1):
            own = mid_ref[(x * oy + 1) * 8 : (x * oy + oy - 1) * 8].reshape(sy, 8, lanes)
            out = out + jnp.sum(f(own), axis=0)
        return jnp.sum(out * keep, axis=0, keepdims=True)

    def squares_about(mean):
        return over_cells(lambda v: (v - mean[None]) * (v - mean[None]))

    mine = moments(over_cells(lambda v: v), squares_about, entries)
    out_ref[...] = jnp.broadcast_to(to_row(mine)[0:1], out_ref.shape)
    for x in range(ox):
        rows = slice(x * oy * 8, (x + 1) * oy * 8)
        there = msk[(x + 1) * step + 8 : (x + 2) * step - 8]
        there = jnp.concatenate([there] * (lanes // 128), axis=1) > 0
        mid_ref[rows] = jnp.where(there, mid_ref[rows], BIG)


def second_kernel(stats_ref, mid_ref, weight_ref, rows_ref, coded_ref, fine_ref, tok_ref, lhs):
    sx, sy, sb, lanes = fine_ref.shape
    step = (sy + 2) * 8
    centre, scale = from_rows(stats_ref[...])
    gain, shift, bias = rows_ref[1:2], rows_ref[3:4], rows_ref[5:6]
    scale = scale * gain
    half = sy // 2 * 8
    for x in range(sx + 2):
        v = mid_ref[x * step : (x + 1) * step]
        act = jnp.where(v < BIG, silu((v - centre) * scale + shift), 0.0)
        for e, part in enumerate(columns(act.reshape(sy + 2, 8, lanes), sy)):
            lhs[x * half : (x + 1) * half, e * lanes : (e + 1) * lanes] = (
                pack_pairs(part[None]).reshape(half, lanes).astype(BF16)
            )
    size = sx * half
    acc = bias
    for e in range(3):
        acc = acc + jnp.dot(
            lhs[e * half : e * half + size, :], weight_ref[e], preferred_element_type=F32
        )
    field = pack_pairs(coded_ref[...].astype(F32).reshape(sx, sy, 8, lanes))
    field = field.reshape(size, lanes)
    out = jnp.where(field != SENT, field + acc, 0.0).reshape(-1, 8, lanes)
    out = out.astype(BF16)
    wide = out.astype(F32)
    other = pltpu.roll(wide, 4, 1)
    fine = jnp.stack([wide[:, :sb], other[:, :sb]], axis=1)
    fine_ref[...] = fine.reshape(sx, sy, sb, lanes).astype(BF16)
    i, j = iota((lanes, lanes), 0), iota((lanes, lanes), 1)
    pick = onehot(i == (j % 128) // 4 * 8 + j // 128 * 4 + j % 4)
    moved = jnp.dot(out.reshape(size, lanes), pick, preferred_element_type=F32).reshape(
        sx // 2, 2, sy // 4, 2, 8, lanes
    )
    count = sx // 2 * (sy // 4)
    parts = []
    for x in range(2):
        for y in range(2):
            piece = moved[:, x, :, y].reshape(count, 8, lanes)
            low, high = piece[:, :, :128], piece[:, :, 128:]
            inside = iota(low.shape, 1) < 4
            for both in (
                jnp.where(inside, low, pltpu.roll(high, 4, 1)),
                jnp.where(inside, pltpu.roll(low, 4, 1), high),
            ):
                parts.append(both.reshape(count * 8, 128).astype(BF16))
    tokens = jnp.concatenate(parts, axis=1)
    n = count * 8
    i, j = iota((n, n), 0), iota((n, n), 1)
    order = onehot(j == i // 8 * 8 + i % 2 * 4 + i % 8 // 2)
    tok_ref[...] = jnp.dot(order, tokens, preferred_element_type=F32).astype(BF16)


def attend_kernel(members, keys_ref, weight_ref, *refs):
    tok_refs, out_refs, (toks, proj) = refs[:members], refs[members : 2 * members], refs[-2:]
    own = tok_refs[0].shape[0]
    seq = own * members
    cols = weight_ref.shape[1] // 3
    for k in range(members):
        toks[k * own : (k + 1) * own, :] = tok_refs[k][...]
    proj[...] = jnp.dot(toks[...], weight_ref[...], preferred_element_type=F32).astype(BF16)
    there = keys_ref[0:1] > 0
    width = min(128, cols)
    for t in range(cols // width):
        q = proj[:, t * width : (t + 1) * width]
        keys = proj[:, cols + t * width : cols + (t + 1) * width]
        values = proj[:, 2 * cols + t * width : 2 * cols + (t + 1) * width]
        head = iota((seq, width), 1) // HD
        merged = jnp.zeros((seq, width), F32)
        for h in range(width // HD):
            mine = jnp.where(head == h, q.astype(F32), 0.0).astype(BF16)
            scores = lax.dot_general(
                mine, keys, (((1,), (1,)), ((), ())), preferred_element_type=F32
            ) * float(HD) ** (-0.5)
            scores = jnp.where(there, scores, -BIG)
            probs = jnp.exp(scores - jnp.max(scores, axis=1, keepdims=True))
            total = jnp.sum(probs, axis=1, keepdims=True)
            mixed = jnp.dot(probs.astype(BF16), values, preferred_element_type=F32)
            merged = jnp.where(head == h, mixed / total, merged)
        merged = merged.astype(BF16)
        for k in range(members):
            out_refs[k][:, t * width : (t + 1) * width] = merged[k * own : (k + 1) * own]


def place_kernel(members, keep_ref, *refs):
    out_ref = refs[-1]
    own, cols = refs[0].shape
    me = lax.axis_index("gx")
    row = iota((8, cols), 0)
    keep = jnp.zeros((8, cols), F32)
    for b in range(4):
        keep = jnp.where(row // 2 == b, jnp.broadcast_to(keep_ref[b : b + 1, :cols], (8, cols)), keep)
    for k in range(members):
        value = refs[k][...].astype(F32).reshape(own // 8, 8, cols)
        value = jnp.where((keep > 0)[None], value, 0.0).reshape(own, cols).astype(BF16)
        if cols % 128 == 0:
            out_ref[0, :, pl.ds(pl.multiple_of((me ^ k) * cols, cols), cols)] = value
        else:
            out_ref[k] = value


VM = pl.BlockSpec(memory_space=pltpu.VMEM)
SM = pl.BlockSpec(memory_space=pltpu.SMEM)


def call(kernel, name, specs, out, args, scratch=(), flops=0, nbytes=0, mib=16):
    return pl.pallas_call(
        kernel,
        out_shape=out,
        in_specs=list(specs),
        out_specs=jax.tree.map(lambda _: VM, out),
        scratch_shapes=list(scratch),
        name=name,
        cost_estimate=pl.CostEstimate(flops=flops, bytes_accessed=nbytes, transcendentals=0),
        compiler_params=pltpu.CompilerParams(vmem_limit_bytes=mib * 2**20),
    )(*args)


def shape(*dims, dtype=BF16):
    return jax.ShapeDtypeStruct(dims, dtype)


def pairing(n, odd, closed):
    partner = {i: (i ^ 1 if not odd else (i + 1 if i % 2 else i - 1)) for i in range(n)}
    if closed:
        partner = {i: j % n for i, j in partner.items()}
    return {i: j for i, j in partner.items() if 0 <= j < n and i != j}


def body(features, occupancy, norm_gain, norm_shift, conv_weight, conv_bias, qkv_weight):
    sx, sy, sb, lanes = features.shape
    nx, ny, nz = (lax.axis_size(a) for a in ALL)
    devices = nx * ny * nz
    narrow = nx == 4 and ny == 2 and nz == 4
    own = sx // 2 * (sy // 4) * sb * 2
    ex = sx + 4
    row_shape = [] if narrow else [shape(devices, 128, dtype=F32)]

    slab = sy * 8 + TAIL
    keep, keys, coded, first, second, tail, *stats = call(
        functools.partial(pre_kernel, nx), "pre", (SM, VM),
        [shape(8, lanes, dtype=F32), shape(8, own * nx, dtype=F32),
         shape(sx * sy * 8, lanes), shape(slab, lanes), shape(slab, lanes), shape(TAIL, lanes)]
        + row_shape,
        (occupancy, features), nbytes=10**6,
    )
    stats = [lax.all_to_all(s, ALL, 0, 0, tiled=True) for s in stats]
    got = [
        lax.ppermute(first, "gx", list(pairing(nx, False, False).items())),
        lax.ppermute(second, "gx", list(pairing(nx, True, narrow).items())),
    ]
    tails = [tail]
    if narrow:
        tails.append(lax.ppermute(tail, "gx", [(i, i ^ 2) for i in range(nx)]))
    band = shape(3, 4 * lanes, lanes)
    pars = jnp.concatenate([norm_gain, norm_shift, conv_bias], axis=0)
    later = shape(1, *conv_weight.shape[1:])
    band0, rows, later = call(
        band_kernel, "band0", (VM,) * 2, [band, shape(8, lanes, dtype=F32), later],
        (conv_weight, pars), nbytes=8 * 10**6,
    )
    band1, mark = call(
        band_kernel, "band1", (VM,), [band, shape(8, 128, dtype=F32)], (later,), nbytes=8 * 10**6,
    )
    count = ex * sy
    ext, mine = call(
        functools.partial(line_kernel, narrow, sy, sb), "line", (VM,) * (4 + len(tails)),
        [shape(count * 8, lanes), shape(count + TAIL, lanes)],
        (rows, coded, *got, *tails),
        [pltpu.VMEM((lanes // 128, count * 8, 128), F32)], nbytes=10**6,
    )
    core = lax.ppermute(mine, "gz", list(pairing(nz, False, False).items()))

    faces = 1 if ny == 2 else 2
    gap = corner_rows(ex)
    near, far = ex * 8 + 2 * gap + TAIL, 2 * gap + TAIL
    zface, *yfaces = call(
        functools.partial(chip_kernel, sb, sy), "chip", (VM,) * 3,
        [shape(count + TAIL, lanes)] + [shape(near, lanes), shape(far, lanes)] * faces,
        (ext, mine, core),
        [pltpu.VMEM((lanes // 128, count * 8, 128), F32),
         pltpu.VMEM((lanes // 128, count, 128), F32)], nbytes=10**6,
    )
    odd_z = pairing(nz, True, narrow)
    own_tail = zface
    zgot = lax.ppermute(zface, "gz", list(odd_z.items()))
    ygot = []
    for k in range(faces):
        along = pairing(ny, k == 1, False)
        ygot.append(lax.ppermute(yfaces[2 * k], "gy", list(along.items())))
        both = [
            (y * nz + z, along[y] * nz + odd_z[z]) for y in along for z in odd_z
        ]
        ygot.append(lax.ppermute(yfaces[2 * k + 1], ("gy", "gz"), both))

    cols, feats = qkv_weight.shape[1:]
    turned = call(
        turn_kernel, "turn", (VM,), shape(feats, 3 * cols), (qkv_weight,),
        flops=2 * 3 * cols * feats * feats, nbytes=6 * 10**6,
    )

    ey, oy = sy + 4, sy + 2
    size = (sx + 2) * oy * 8
    mid, mine = call(
        functools.partial(first_kernel, narrow, faces, sy, sb), "first",
        (VM,) * (8 + 2 * faces + len(stats)),
        [shape(size, lanes, dtype=F32), shape(devices, 128, dtype=F32)],
        (ext, own_tail, core, zgot, *ygot, *stats, keep, band0, rows, mark),
        [pltpu.VMEM((lanes // 128, ex * ey * 8, 128), F32),
         pltpu.VMEM((ex * oy * 8, 4 * lanes), BF16),
         pltpu.VMEM((ex * ey * 8, 128), F32)],
        flops=2 * 10**9, nbytes=4 * 10**6, mib=20,
    )
    stats = lax.all_to_all(mine, ALL, 0, 0, tiled=True)
    fine_out, tokens = call(
        second_kernel, "second", (VM,) * 5,
        [shape(*features.shape), shape(own, feats)],
        (stats, mid, band1, rows, coded),
        [pltpu.VMEM(((sx + 2) * sy * 4, 4 * lanes), BF16)],
        flops=10**9, nbytes=4 * 10**6,
    )
    swaps = [[(i, i ^ k) for i in range(nx)] for k in range(nx)]
    blocks = {k: lax.ppermute(tokens, "gx", swaps[k]) for k in range(nx - 1, 0, -1)}
    blocks = [tokens] + [blocks[k] for k in range(1, nx)]
    outs = call(
        functools.partial(attend_kernel, nx), "attend", (VM,) * (2 + nx),
        [shape(own, cols)] * nx, (keys, turned, *blocks),
        [pltpu.VMEM((own * nx, feats), BF16), pltpu.VMEM((own * nx, 3 * cols), BF16)],
        flops=10**9, nbytes=3 * 10**6, mib=16 if narrow else 40,
    )
    outs = [outs[0]] + [lax.ppermute(outs[k], "gx", swaps[k]) for k in range(1, nx)]
    lined = cols % 128 == 0
    attention = call(
        functools.partial(place_kernel, nx), "place", (VM,) * (1 + nx),
        shape(1, own, nx * cols) if lined else shape(nx, own, cols), (keep, *outs),
        nbytes=3 * 10**5, mib=8,
    )
    if not lined:
        me = lax.axis_index("gx")
        attention = jnp.concatenate(
            [lax.dynamic_index_in_dim(attention, me ^ j, 0, keepdims=False) for j in range(nx)],
            axis=1,
        )[None]
    return (fine_out, attention)


def solution(mesh):
    placed = (
        P("gx", "gy", "gz", None),
        P(None, "gy", "gz"),
        P(),
        P(),
        P(),
        P(),
        P(None, "gx", None),
    )
    return jax.shard_map(
        body,
        mesh=mesh,
        in_specs=placed,
        out_specs=(P("gx", "gy", "gz", None), P(("gy", "gz"), "gx", None)),
        check_vma=False,
    )
```

```python
import functools

import jax
import jax.numpy as jnp
from jax import lax
from jax.experimental import pallas as pl
from jax.experimental.pallas import tpu as pltpu
from jax.sharding import PartitionSpec as P

C = 32
GW = 4
HD = 64
BR = 8
EPS = 1e-05
SENT = 512.0
BIG = 1e30
ALL = ("gx", "gy", "gz")
F32, BF16 = jnp.float32, jnp.bfloat16
HIGHEST = lax.Precision.HIGHEST
TAIL = 16


def iota(shape, dim):
    return lax.broadcasted_iota(jnp.int32, shape, dim)


def onehot(cond, dtype=BF16):
    return jnp.where(cond, 1.0, 0.0).astype(dtype)


def exact_dot(a, b):
    return jnp.dot(a, b, precision=HIGHEST, preferred_element_type=F32)


def spread_sum(v):
    lane = iota(v.shape, 1)
    s = 1
    while s < GW * BR:
        v = v + jnp.where(lane & s == 0, pltpu.roll(v, 128 - s, 1), pltpu.roll(v, s, 1))
        s *= 2
    return v


def group_sum(total):
    k = total.shape[1] // 128
    rows = [jnp.broadcast_to(total[:, h * 128 : (h + 1) * 128], (8, 128)) for h in range(k)]
    out = spread_sum(jnp.concatenate(rows, axis=0))
    return jnp.concatenate([out[h * 8 : (h + 1) * 8] for h in range(k)], axis=1)


def moments(total, squares_about, count):
    sums = group_sum(total)
    squares = group_sum(squares_about((sums / count)[0:1]))
    return sums, squares, jnp.zeros(sums.shape, F32) + count


def merge(parts):
    n = sum(p[2] for p in parts)
    sums = sum(p[0] for p in parts)
    centre = sums / n
    squares = sum(p[1] + p[2] * (p[0] / p[2] - centre) ** 2 for p in parts)
    return sums, squares, n


def centre_scale(part):
    return part[0] / part[2], lax.rsqrt(part[1] / part[2] + EPS)


def to_row(part):
    j = iota((8, 128), 1) % (GW * BR)
    row = jnp.zeros((8, 128), F32)
    for h in range(2):
        for k in range(3):
            row = jnp.where(j == 4 * h + k, part[k][:, h * 128 : (h + 1) * 128], row)
    return row


def from_rows(rows):
    n = jnp.maximum(pltpu.roll(rows, 126, 1), 1.0)
    total = jnp.sum(n, axis=0, keepdims=True)
    centre = jnp.sum(rows, axis=0, keepdims=True) / total
    drift = rows / n - centre
    squares = pltpu.roll(rows, 127, 1) + n * drift * drift
    spread = jnp.sum(squares, axis=0, keepdims=True) / total
    j = iota((8, 128), 1) % (GW * BR)
    blocks = [
        jnp.where(j == 4 * h, jnp.broadcast_to(v, (8, 128)), 0.0)
        for v in (centre, spread) for h in range(2)
    ]
    out = spread_sum(jnp.concatenate(blocks, axis=0))
    out = [out[8 * i : 8 * i + 1] for i in range(4)]
    return (
        jnp.concatenate(out[:2], axis=1),
        lax.rsqrt(jnp.concatenate(out[2:], axis=1) + EPS),
    )


def to_tail(part):
    index = iota((8, 256), 0)
    blocks = [jnp.zeros((8, 256), F32), jnp.zeros((8, 256), F32)]
    for k, value in enumerate(part):
        value = jnp.broadcast_to(value[0:1], (8, 256))
        high = value.astype(BF16).astype(F32)
        mid = (value - high).astype(BF16).astype(F32)
        for i, piece in enumerate((high, mid, value - high - mid)):
            blocks[k // 2] = jnp.where(index == 3 * (k % 2) + i, piece, blocks[k // 2])
    return jnp.concatenate(blocks, axis=0).astype(BF16)


def from_tail(message_ref):
    rows = message_ref.shape[0]
    part = message_ref[rows - TAIL : rows, :].astype(F32)
    return [
        jnp.sum(part[r : r + 3], axis=0, keepdims=True) for r in (0, 3, 8)
    ]


def silu(u):
    return 0.5 * u * (1.0 + jnp.tanh(0.5 * u))


def pack_pairs(v):
    n, m, _, lanes = v.shape
    v = v.reshape(n, m // 2, 2, 8, lanes)
    low, high = v[:, :, 0].reshape(-1, 8, lanes), v[:, :, 1].reshape(-1, 8, lanes)
    both = jnp.where(iota(low.shape, 1) < 4, low, pltpu.roll(high, 4, 1))
    return both.reshape(n, m // 2, 8, lanes)


def split_pairs(v, blank):
    inside = iota(v.shape, 1) < 4
    return [jnp.where(inside, v, blank), jnp.where(inside, pltpu.roll(v, 4, 1), blank)]


def edges(act):
    z = iota(act.shape, 2) % BR
    before, after = pltpu.roll(act, 1, 1), pltpu.roll(act, 7, 1)
    return jnp.where(z == BR - 1, before, jnp.where(z == 0, after, 0.0))


def columns(act, size):
    side = edges(act)
    z = iota((size,) + act.shape[1:], 2) % BR
    second = pltpu.roll(side, 2, 2)
    third = pltpu.roll(side, 4, 2)
    mixed = jnp.where(
        (z == 1) | (z == 2), second[1 : 1 + size],
        jnp.where((z == 3) | (z == 4), third[2 : 2 + size], side[0:size]),
    )
    return [act[e : e + size] for e in range(3)] + [mixed]


def halves(lanes):
    return range(lanes // 128)


def read(ref, start, count, stride):
    return jnp.concatenate(
        [ref[h, pl.ds(start, count, stride=stride), :] for h in range(ref.shape[0])], axis=1
    )


def write(ref, start, count, stride, value):
    for h in range(ref.shape[0]):
        ref[h, pl.ds(start, count, stride=stride), :] = value[:, h * 128 : (h + 1) * 128]


def write_block(ref, start, value):
    for h in range(ref.shape[0]):
        ref[h, start : start + value.shape[0], :] = value[:, h * 128 : (h + 1) * 128]


def even(axis):
    return lax.axis_index(axis) % 2 == 0


def sides(axis, first, second):
    i, n = lax.axis_index(axis), lax.axis_size(axis)
    blank = jnp.full(first.shape, SENT, F32)
    second = blank if second is None else second
    low, high = jnp.where(even(axis), second, first), jnp.where(even(axis), first, second)
    return jnp.where(i > 0, low, SENT), jnp.where(i < n - 1, high, SENT)


def pre_kernel(members, occ_ref, feat_ref, keep_ref, keys_ref, coded_ref, first_ref, second_ref,
               tail_ref, rows_ref=None):
    sx, sy, sb, lanes = feat_ref.shape
    me = lax.axis_index("gx")
    bricks = [occ_ref[x].astype(F32) for x in range(members)]

    def row_of(x):
        return sum(jnp.where(x == i, v, 0.0) for i, v in enumerate(bricks))

    mine = jnp.broadcast_to(row_of(me), (8, sb))
    keep = jnp.where(iota((8, sb), 0) == iota((8, sb), 1), mine, 0.0)
    keep = jnp.broadcast_to(jnp.sum(keep, axis=1, keepdims=True), (8, lanes))
    count = jnp.sum(keep, axis=0, keepdims=True) * float(sx * sy * BR * GW)
    keep_ref[...] = keep
    seq = keys_ref.shape[1]
    lane = iota((1, seq), 1)
    keys = jnp.zeros((1, seq), F32)
    for k in range(members):
        there = row_of(me ^ k)
        for b in range(sb):
            keys = jnp.where(
                (lane // (seq // members) == k) & (lane % (2 * sb) // 2 == b),
                there[:, b : b + 1], keys,
            )
    keys_ref[...] = jnp.broadcast_to(keys, keys_ref.shape)
    field = feat_ref[...].astype(F32)
    wide = jnp.concatenate([field, jnp.zeros((sx, sy, 8 - sb, lanes), F32)], axis=2)
    wide = wide.reshape(sx * sy, 8, lanes)
    total = jnp.sum(jnp.sum(wide, axis=0) * keep, axis=0, keepdims=True)

    def squares_about(mean):
        d = wide - mean[None]
        return jnp.sum(jnp.sum(d * d, axis=0) * keep, axis=0, keepdims=True)

    code = jnp.where((keep > 0)[None], wide, SENT)
    coded_ref[...] = code.reshape(sx * sy * 8, lanes).astype(BF16)
    packed = pack_pairs(code.reshape(sx, sy, 8, lanes))
    low = packed[0:2].reshape(-1, lanes)
    high = packed[sx - 2 : sx].reshape(-1, lanes)
    size = low.shape[0]
    first_ref[0:size, :] = jnp.where(even("gx"), high, low).astype(BF16)
    second_ref[0:size, :] = jnp.where(even("gx"), low, high).astype(BF16)
    mine = moments(total, squares_about, count)
    tail = to_tail(mine)
    first_ref[size : size + TAIL, :] = tail
    second_ref[size : size + TAIL, :] = tail
    tail_ref[...] = tail
    if rows_ref is not None:
        rows_ref[...] = jnp.broadcast_to(to_row(mine)[0:1], rows_ref.shape)


def line_kernel(narrow, sy, sb, _, coded_ref, first_ref, second_ref, *rest):
    tails, (ext_ref, out_ref, buf) = rest[:-3], rest[-3:]
    lanes = coded_ref.shape[1]
    sx = coded_ref.shape[0] // (sy * 8)
    size = 2 * (sy // 2) * 8
    low, high = sides(
        "gx", first_ref[0:size].astype(F32), second_ref[0:size].astype(F32)
    )
    write_block(buf, 2 * sy * 8, coded_ref[...].astype(F32))
    for x0, side in ((0, low), (sx + 2, high)):
        for i in range(2):
            part = side[i * (size // 2) : (i + 1) * (size // 2)].reshape(sy // 2, 8, lanes)
            pair = split_pairs(part, SENT)
            for y in range(sy):
                write_block(buf, ((x0 + i) * sy + y) * 8, pair[y % 2][y // 2])
    rows = (sx + 4) * sy * 8
    ext_ref[...] = jnp.concatenate([buf[h] for h in halves(lanes)], axis=1).astype(BF16)
    count = (sx + 4) * sy
    face = jnp.where(even("gz"), read(buf, sb - 1, count, 8), read(buf, 0, count, 8))
    out_ref[0:count, :] = face.astype(BF16)
    mine = [from_tail(ref) for ref in tails]
    if narrow:
        mine = mine + [from_tail(first_ref), from_tail(second_ref)]
    out_ref[count : count + TAIL, :] = to_tail(merge(mine))


def corner_rows(count):
    return (count + 15) // 16 * 16


def chip_kernel(sb, sy, ext_ref, own_ref, other_ref, *rest):
    out, (buf, stage) = rest[:-2], rest[-2:]
    lanes = ext_ref.shape[1]
    ex = ext_ref.shape[0] // (sy * 8)
    block = ext_ref[...].astype(F32)
    write_block(buf, 0, block)
    write_block(stage, 0, other_ref[0 : ex * sy].astype(F32))
    gap = corner_rows(ex)
    pad = jnp.zeros((gap - ex, lanes), F32)
    tail = to_tail(merge([from_tail(own_ref), from_tail(other_ref)]))
    packed = pack_pairs(block.reshape(ex, sy, 8, lanes))

    def side(y0):
        face = packed[:, y0 // 2].reshape(ex * 8, lanes)
        inner, outer = [], []
        for i in range(2):
            inner += [read(stage, y0 + i, ex, sy), pad]
            start = (y0 + i) * 8
            outer += [
                jnp.where(
                    even("gz"),
                    read(buf, start, ex, sy * 8),
                    read(buf, start + sb - 1, ex, sy * 8),
                ),
                pad,
            ]
        return [face] + inner, outer

    (near_low, far_low), (near_high, far_high) = side(0), side(sy - 2)
    count = ex * sy
    z_face = jnp.where(even("gz"), read(buf, 0, count, 8), read(buf, sb - 1, count, 8))
    out[0][0:count, :] = z_face.astype(BF16)
    out[0][count : count + TAIL, :] = tail
    for k in range((len(out) - 1) // 2):
        up = even("gy") if k == 0 else jnp.logical_not(even("gy"))
        for ref, low, high in (
            (out[1 + 2 * k], near_low, near_high),
            (out[2 + 2 * k], far_low, far_high),
        ):
            value = jnp.where(
                up, jnp.concatenate(high, axis=0), jnp.concatenate(low, axis=0)
            ).astype(BF16)
            ref[0 : value.shape[0], :] = value
            ref[value.shape[0] : value.shape[0] + TAIL, :] = tail


def band_kernel(weight_ref, *rest):
    pars, (out_ref, more_ref) = rest[:-2], rest[-2:]
    lanes = C * BR
    spread = onehot(iota((C, lanes), 0) == iota((C, lanes), 1) // BR)
    turned = jnp.transpose(weight_ref[0].astype(F32)).astype(BF16)
    wide = jnp.dot(turned, spread, preferred_element_type=F32)
    full = (C, BR, lanes)
    zi, zo = iota((1, BR, lanes), 1), iota((1, BR, lanes), 2) % BR

    def rows(value):
        return jnp.broadcast_to(value[:, None, :], full)

    for ex in range(3):
        mixed = jnp.zeros(full, F32)
        for ey in range(3):
            q = (ex * 3 + ey) * 3
            terms = [wide[(q + e) * C : (q + e + 1) * C] for e in range(3)]
            inner = jnp.where(zi == zo - 1, rows(terms[0]), 0.0)
            inner = jnp.where(zi == zo, rows(terms[1]), inner)
            inner = jnp.where(zi == zo + 1, rows(terms[2]), inner)
            before = pltpu.roll(terms[0], 1, 0) if ey else terms[0]
            low = 2 * ey - 1 if ey else BR - 1
            mixed = jnp.where((zi == low) & (zo == 0), rows(before), mixed)
            mixed = jnp.where((zi == 2 * ey) & (zo == BR - 1), rows(terms[2]), mixed)
            out_ref[ex, ey * lanes : (ey + 1) * lanes, :] = (
                inner.reshape(C * BR, lanes).astype(BF16)
            )
        out_ref[ex, 3 * lanes : 4 * lanes, :] = mixed.reshape(C * BR, lanes).astype(BF16)
    if pars:
        pick = onehot(iota((C, lanes), 0) == iota((C, lanes), 1) // BR, F32)
        more_ref[...] = jnp.zeros(more_ref.shape, F32)
        more_ref[0 : pars[0].shape[0], :] = exact_dot(pars[0][...], pick)
    else:
        more_ref[...] = weight_ref[1:2]


def turn_kernel(weight_ref, out_ref):
    kinds, cols, feats = weight_ref.shape
    r = iota((feats, 1), 0)
    source = (r % 128) // 4 * 32 + r // 128 * 4 + r % 4
    pick = onehot(source == iota((feats, feats), 1))
    for k in range(kinds):
        out_ref[:, k * cols : (k + 1) * cols] = lax.dot_general(
            pick, weight_ref[k], (((1,), (1,)), ((), ())), preferred_element_type=F32
        ).astype(BF16)


def first_kernel(narrow, faces, sy, sb, ext_ref, own_ref, core_ref, zface_ref, *rest):
    near, far = rest[0 : 2 * faces : 2], rest[1 : 2 * faces : 2]
    rest = rest[2 * faces :]
    stats_ref = None
    if not narrow:
        stats_ref, rest = rest[0], rest[1:]
    keep_ref, weight_ref, rows_ref, mid_ref, out_ref, buf, lhs, msk = rest
    lanes = ext_ref.shape[1]
    ex = ext_ref.shape[0] // (sy * 8)
    ey = sy + 4
    count = ex * sy
    z_low, z_high = sides(
        "gz", core_ref[0:count].astype(F32), zface_ref[0:count].astype(F32)
    )
    for x in range(ex):
        write_block(
            buf, (x * ey + 2) * 8, ext_ref[x * sy * 8 : (x + 1) * sy * 8].astype(F32)
        )
        part = slice(x * sy, (x + 1) * sy)
        write(buf, (x * ey + 2) * 8 + 7, sy, 8, z_low[part])
        write(buf, (x * ey + 2) * 8 + sb, sy, 8, z_high[part])
    gap = corner_rows(ex)
    size = ex * 8
    face = sides("gy", *[
        near[k][0:size].astype(F32) if k < faces else None for k in range(2)
    ])
    inner = sides("gy", *[
        near[k][size : size + 2 * gap].astype(F32) if k < faces else None for k in range(2)
    ])
    outer = sides("gy", *[
        far[k][0 : 2 * gap].astype(F32) if k < faces else None for k in range(2)
    ])
    for s, y0 in enumerate((0, sy + 2)):
        pair = split_pairs(face[s].reshape(ex, 8, lanes), SENT)
        c_low, c_high = sides("gz", inner[s], outer[s])
        for i in range(2):
            for x in range(ex):
                write_block(buf, (x * ey + y0 + i) * 8, pair[i][x])
            write(buf, (y0 + i) * 8 + 7, ex, ey * 8, c_low[i * gap : i * gap + ex])
            write(buf, (y0 + i) * 8 + sb, ex, ey * 8, c_high[i * gap : i * gap + ex])
    if narrow:
        centre, scale = centre_scale(merge(
            [from_tail(r) for r in (own_ref, zface_ref) + tuple(near) + tuple(far)]
        ))
    else:
        centre, scale = from_rows(stats_ref[...])
    gain, shift, bias = rows_ref[0:1], rows_ref[2:3], rows_ref[4:5]
    scale = scale * gain
    oy, sx = sy + 2, ex - 4
    step = ey * 8
    for x in range(ex):
        v = jnp.concatenate(
            [buf[h, x * step : (x + 1) * step, :] for h in halves(lanes)], axis=1
        )
        there = v != SENT
        msk[x * step : (x + 1) * step] = onehot(there[:, 0:128], F32)
        act = jnp.where(there, silu((v - centre) * scale + shift), 0.0).reshape(ey, 8, lanes)
        for e, part in enumerate(columns(act, oy)):
            lhs[x * oy * 8 : (x + 1) * oy * 8, e * lanes : (e + 1) * lanes] = (
                part.reshape(oy * 8, lanes).astype(BF16)
            )
    ox = sx + 2
    size = ox * oy * 8
    acc = bias
    for e in range(3):
        acc = acc + jnp.dot(
            lhs[e * oy * 8 : e * oy * 8 + size, :], weight_ref[e], preferred_element_type=F32
        )
    mid_ref[...] = acc
    keep = keep_ref[...]
    entries = jnp.sum(keep[:, 0:1]) * float(sx * sy * BR * GW)

    def over_cells(f):
        out = jnp.zeros((8, lanes), F32)
        for x in range(1, sx + 1):
            own = mid_ref[(x * oy + 1) * 8 : (x * oy + oy - 1) * 8].reshape(sy, 8, lanes)
            out = out + jnp.sum(f(own), axis=0)
        return jnp.sum(out * keep, axis=0, keepdims=True)

    def squares_about(mean):
        return over_cells(lambda v: (v - mean[None]) * (v - mean[None]))

    mine = moments(over_cells(lambda v: v), squares_about, entries)
    out_ref[...] = jnp.broadcast_to(to_row(mine)[0:1], out_ref.shape)
    for x in range(ox):
        rows = slice(x * oy * 8, (x + 1) * oy * 8)
        there = msk[(x + 1) * step + 8 : (x + 2) * step - 8]
        there = jnp.concatenate([there] * (lanes // 128), axis=1) > 0
        mid_ref[rows] = jnp.where(there, mid_ref[rows], BIG)


def second_kernel(stats_ref, mid_ref, weight_ref, rows_ref, coded_ref, fine_ref, tok_ref, lhs):
    sx, sy, sb, lanes = fine_ref.shape
    step = (sy + 2) * 8
    centre, scale = from_rows(stats_ref[...])
    gain, shift, bias = rows_ref[1:2], rows_ref[3:4], rows_ref[5:6]
    scale = scale * gain
    half = sy // 2 * 8
    for x in range(sx + 2):
        v = mid_ref[x * step : (x + 1) * step]
        act = jnp.where(v < BIG, silu((v - centre) * scale + shift), 0.0)
        for e, part in enumerate(columns(act.reshape(sy + 2, 8, lanes), sy)):
            lhs[x * half : (x + 1) * half, e * lanes : (e + 1) * lanes] = (
                pack_pairs(part[None]).reshape(half, lanes).astype(BF16)
            )
    size = sx * half
    acc = bias
    for e in range(3):
        acc = acc + jnp.dot(
            lhs[e * half : e * half + size, :], weight_ref[e], preferred_element_type=F32
        )
    field = pack_pairs(coded_ref[...].astype(F32).reshape(sx, sy, 8, lanes))
    field = field.reshape(size, lanes)
    out = jnp.where(field != SENT, field + acc, 0.0).reshape(-1, 8, lanes)
    out = out.astype(BF16)
    wide = out.astype(F32)
    other = pltpu.roll(wide, 4, 1)
    fine = jnp.stack([wide[:, :sb], other[:, :sb]], axis=1)
    fine_ref[...] = fine.reshape(sx, sy, sb, lanes).astype(BF16)
    i, j = iota((lanes, lanes), 0), iota((lanes, lanes), 1)
    pick = onehot(i == (j % 128) // 4 * 8 + j // 128 * 4 + j % 4)
    moved = jnp.dot(out.reshape(size, lanes), pick, preferred_element_type=F32).reshape(
        sx // 2, 2, sy // 4, 2, 8, lanes
    )
    count = sx // 2 * (sy // 4)
    parts = []
    for x in range(2):
        for y in range(2):
            piece = moved[:, x, :, y].reshape(count, 8, lanes)
            low, high = piece[:, :, :128], piece[:, :, 128:]
            inside = iota(low.shape, 1) < 4
            for both in (
                jnp.where(inside, low, pltpu.roll(high, 4, 1)),
                jnp.where(inside, pltpu.roll(low, 4, 1), high),
            ):
                parts.append(both.reshape(count * 8, 128).astype(BF16))
    tokens = jnp.concatenate(parts, axis=1)
    n = count * 8
    i, j = iota((n, n), 0), iota((n, n), 1)
    order = onehot(j == i // 8 * 8 + i % 2 * 4 + i % 8 // 2)
    tok_ref[...] = jnp.dot(order, tokens, preferred_element_type=F32).astype(BF16)


def attend_kernel(members, keys_ref, weight_ref, *refs):
    tok_refs, out_refs, (toks, proj) = refs[:members], refs[members : 2 * members], refs[-2:]
    own = tok_refs[0].shape[0]
    seq = own * members
    cols = weight_ref.shape[1] // 3
    for k in range(members):
        toks[k * own : (k + 1) * own, :] = tok_refs[k][...]
    proj[...] = jnp.dot(toks[...], weight_ref[...], preferred_element_type=F32).astype(BF16)
    there = keys_ref[0:1] > 0
    width = min(128, cols)
    for t in range(cols // width):
        q = proj[:, t * width : (t + 1) * width]
        keys = proj[:, cols + t * width : cols + (t + 1) * width]
        values = proj[:, 2 * cols + t * width : 2 * cols + (t + 1) * width]
        head = iota((seq, width), 1) // HD
        merged = jnp.zeros((seq, width), F32)
        for h in range(width // HD):
            mine = jnp.where(head == h, q.astype(F32), 0.0).astype(BF16)
            scores = lax.dot_general(
                mine, keys, (((1,), (1,)), ((), ())), preferred_element_type=F32
            ) * float(HD) ** (-0.5)
            scores = jnp.where(there, scores, -BIG)
            probs = jnp.exp(scores - jnp.max(scores, axis=1, keepdims=True))
            total = jnp.sum(probs, axis=1, keepdims=True)
            mixed = jnp.dot(probs.astype(BF16), values, preferred_element_type=F32)
            merged = jnp.where(head == h, mixed / total, merged)
        merged = merged.astype(BF16)
        for k in range(members):
            out_refs[k][:, t * width : (t + 1) * width] = merged[k * own : (k + 1) * own]


def place_kernel(members, keep_ref, *refs):
    out_ref = refs[-1]
    own, cols = refs[0].shape
    me = lax.axis_index("gx")
    row = iota((8, cols), 0)
    keep = jnp.zeros((8, cols), F32)
    for b in range(4):
        keep = jnp.where(row // 2 == b, jnp.broadcast_to(keep_ref[b : b + 1, :cols], (8, cols)), keep)
    for k in range(members):
        value = refs[k][...].astype(F32).reshape(own // 8, 8, cols)
        value = jnp.where((keep > 0)[None], value, 0.0).reshape(own, cols).astype(BF16)
        if cols % 128 == 0:
            out_ref[0, :, pl.ds(pl.multiple_of((me ^ k) * cols, cols), cols)] = value
        else:
            out_ref[k] = value


VM = pl.BlockSpec(memory_space=pltpu.VMEM)


def call(kernel, name, specs, out, args, scratch=(), flops=0, nbytes=0, mib=16):
    return pl.pallas_call(
        kernel,
        out_shape=out,
        in_specs=list(specs),
        out_specs=jax.tree.map(lambda _: VM, out),
        scratch_shapes=list(scratch),
        name=name,
        cost_estimate=pl.CostEstimate(flops=flops, bytes_accessed=nbytes, transcendentals=0),
        compiler_params=pltpu.CompilerParams(vmem_limit_bytes=mib * 2**20),
    )(*args)


def shape(*dims, dtype=BF16):
    return jax.ShapeDtypeStruct(dims, dtype)


def pairing(n, odd, closed):
    partner = {i: (i ^ 1 if not odd else (i + 1 if i % 2 else i - 1)) for i in range(n)}
    if closed:
        partner = {i: j % n for i, j in partner.items()}
    return {i: j for i, j in partner.items() if 0 <= j < n and i != j}


def body(features, occupancy, norm_gain, norm_shift, conv_weight, conv_bias, qkv_weight):
    sx, sy, sb, lanes = features.shape
    nx, ny, nz = (lax.axis_size(a) for a in ALL)
    devices = nx * ny * nz
    narrow = nx == 4 and ny == 2 and nz == 4
    own = sx // 2 * (sy // 4) * sb * 2
    ex = sx + 4
    row_shape = [] if narrow else [shape(devices, 128, dtype=F32)]

    slab = sy * 8 + TAIL
    keep, keys, coded, first, second, tail, *stats = call(
        functools.partial(pre_kernel, nx), "pre", (VM, VM),
        [shape(8, lanes, dtype=F32), shape(8, own * nx, dtype=F32),
         shape(sx * sy * 8, lanes), shape(slab, lanes), shape(slab, lanes), shape(TAIL, lanes)]
        + row_shape,
        (occupancy, features), nbytes=10**6,
    )
    stats = [lax.all_to_all(s, ALL, 0, 0, tiled=True) for s in stats]
    got = [
        lax.ppermute(first, "gx", list(pairing(nx, False, False).items())),
        lax.ppermute(second, "gx", list(pairing(nx, True, narrow).items())),
    ]
    tails = [tail]
    if narrow:
        tails.append(lax.ppermute(tail, "gx", [(i, i ^ 2) for i in range(nx)]))
    band = shape(3, 4 * lanes, lanes)
    pars = jnp.concatenate([norm_gain, norm_shift, conv_bias], axis=0)
    later = shape(1, *conv_weight.shape[1:])
    band0, later = call(
        band_kernel, "band0", (VM,), [band, later], (conv_weight,), nbytes=8 * 10**6,
    )
    band1, rows = call(
        band_kernel, "band1", (VM,) * 2, [band, shape(8, lanes, dtype=F32)], (later, pars),
        nbytes=8 * 10**6,
    )
    count = ex * sy
    ext, mine = call(
        functools.partial(line_kernel, narrow, sy, sb), "line", (VM,) * (4 + len(tails)),
        [shape(count * 8, lanes), shape(count + TAIL, lanes)],
        (later, coded, *got, *tails),
        [pltpu.VMEM((lanes // 128, count * 8, 128), F32)], nbytes=10**6,
    )
    core = lax.ppermute(mine, "gz", list(pairing(nz, False, False).items()))

    faces = 1 if ny == 2 else 2
    gap = corner_rows(ex)
    near, far = ex * 8 + 2 * gap + TAIL, 2 * gap + TAIL
    zface, *yfaces = call(
        functools.partial(chip_kernel, sb, sy), "chip", (VM,) * 3,
        [shape(count + TAIL, lanes)] + [shape(near, lanes), shape(far, lanes)] * faces,
        (ext, mine, core),
        [pltpu.VMEM((lanes // 128, count * 8, 128), F32),
         pltpu.VMEM((lanes // 128, count, 128), F32)], nbytes=10**6,
    )
    odd_z = pairing(nz, True, narrow)
    own_tail = zface
    zgot = lax.ppermute(zface, "gz", list(odd_z.items()))
    ygot = []
    for k in range(faces):
        along = pairing(ny, k == 1, False)
        ygot.append(lax.ppermute(yfaces[2 * k], "gy", list(along.items())))
        both = [
            (y * nz + z, along[y] * nz + odd_z[z]) for y in along for z in odd_z
        ]
        ygot.append(lax.ppermute(yfaces[2 * k + 1], ("gy", "gz"), both))

    cols, feats = qkv_weight.shape[1:]
    turned = call(
        turn_kernel, "turn", (VM,), shape(feats, 3 * cols), (qkv_weight,),
        flops=2 * 3 * cols * feats * feats, nbytes=6 * 10**6,
    )

    ey, oy = sy + 4, sy + 2
    size = (sx + 2) * oy * 8
    mid, mine = call(
        functools.partial(first_kernel, narrow, faces, sy, sb), "first",
        (VM,) * (7 + 2 * faces + len(stats)),
        [shape(size, lanes, dtype=F32), shape(devices, 128, dtype=F32)],
        (ext, own_tail, core, zgot, *ygot, *stats, keep, band0, rows),
        [pltpu.VMEM((lanes // 128, ex * ey * 8, 128), F32),
         pltpu.VMEM((ex * oy * 8, 4 * lanes), BF16),
         pltpu.VMEM((ex * ey * 8, 128), F32)],
        flops=2 * 10**9, nbytes=4 * 10**6, mib=20,
    )
    stats = lax.all_to_all(mine, ALL, 0, 0, tiled=True)
    fine_out, tokens = call(
        second_kernel, "second", (VM,) * 5,
        [shape(*features.shape), shape(own, feats)],
        (stats, mid, band1, rows, coded),
        [pltpu.VMEM(((sx + 2) * sy * 4, 4 * lanes), BF16)],
        flops=10**9, nbytes=4 * 10**6,
    )
    swaps = [[(i, i ^ k) for i in range(nx)] for k in range(nx)]
    blocks = {0: tokens}
    for k in sorted(range(1, nx), key=lambda k: (bin(k).count("1"), -k)):
        low = k & -k
        blocks[k] = lax.ppermute(blocks[k ^ low], "gx", swaps[low])
    blocks = [blocks[k] for k in range(nx)]
    outs = call(
        functools.partial(attend_kernel, nx), "attend", (VM,) * (2 + nx),
        [shape(own, cols)] * nx, (keys, turned, *blocks),
        [pltpu.VMEM((own * nx, feats), BF16), pltpu.VMEM((own * nx, 3 * cols), BF16)],
        flops=10**9, nbytes=3 * 10**6, mib=16 if narrow else 40,
    )
    outs = [outs[0]] + [lax.ppermute(outs[k], "gx", swaps[k]) for k in range(1, nx)]
    lined = cols % 128 == 0
    attention = call(
        functools.partial(place_kernel, nx), "place", (VM,) * (1 + nx),
        shape(1, own, nx * cols) if lined else shape(nx, own, cols), (keep, *outs),
        nbytes=3 * 10**5, mib=8,
    )
    if not lined:
        me = lax.axis_index("gx")
        attention = jnp.concatenate(
            [lax.dynamic_index_in_dim(attention, me ^ j, 0, keepdims=False) for j in range(nx)],
            axis=1,
        )[None]
    return (fine_out, attention)


def solution(mesh):
    placed = (
        P("gx", "gy", "gz", None),
        P(None, "gy", "gz"),
        P(),
        P(),
        P(),
        P(),
        P(None, "gx", None),
    )
    return jax.shard_map(
        body,
        mesh=mesh,
        in_specs=placed,
        out_specs=(P("gx", "gy", "gz", None), P(("gy", "gz"), "gx", None)),
        check_vma=False,
    )
```

```python
import functools

import jax
import jax.numpy as jnp
from jax import lax
from jax.experimental import pallas as pl
from jax.experimental.pallas import tpu as pltpu
from jax.sharding import PartitionSpec as P

C = 32
GW = 4
HD = 64
BR = 8
EPS = 1e-05
SENT = 512.0
BIG = 1e30
ALL = ("gx", "gy", "gz")
F32, BF16 = jnp.float32, jnp.bfloat16
HIGHEST = lax.Precision.HIGHEST
TAIL = 16


def iota(shape, dim):
    return lax.broadcasted_iota(jnp.int32, shape, dim)


def onehot(cond, dtype=BF16):
    return jnp.where(cond, 1.0, 0.0).astype(dtype)


def exact_dot(a, b):
    return jnp.dot(a, b, precision=HIGHEST, preferred_element_type=F32)


def spread_sum(v):
    lane = iota(v.shape, 1)
    s = 1
    while s < GW * BR:
        v = v + jnp.where(lane & s == 0, pltpu.roll(v, 128 - s, 1), pltpu.roll(v, s, 1))
        s *= 2
    return v


def group_sum(total):
    k = total.shape[1] // 128
    rows = [jnp.broadcast_to(total[:, h * 128 : (h + 1) * 128], (8, 128)) for h in range(k)]
    out = spread_sum(jnp.concatenate(rows, axis=0))
    return jnp.concatenate([out[h * 8 : (h + 1) * 8] for h in range(k)], axis=1)


def moments(total, squares_about, count):
    sums = group_sum(total)
    squares = group_sum(squares_about((sums / count)[0:1]))
    return sums, squares, jnp.zeros(sums.shape, F32) + count


def merge(parts):
    n = sum(p[2] for p in parts)
    sums = sum(p[0] for p in parts)
    centre = sums / n
    squares = sum(p[1] + p[2] * (p[0] / p[2] - centre) ** 2 for p in parts)
    return sums, squares, n


def centre_scale(part):
    return part[0] / part[2], lax.rsqrt(part[1] / part[2] + EPS)


def to_row(part):
    j = iota((8, 128), 1) % (GW * BR)
    row = jnp.zeros((8, 128), F32)
    for h in range(2):
        for k in range(3):
            row = jnp.where(j == 4 * h + k, part[k][:, h * 128 : (h + 1) * 128], row)
    return row


def from_rows(rows):
    n = jnp.maximum(pltpu.roll(rows, 126, 1), 1.0)
    total = jnp.sum(n, axis=0, keepdims=True)
    centre = jnp.sum(rows, axis=0, keepdims=True) / total
    drift = rows / n - centre
    squares = pltpu.roll(rows, 127, 1) + n * drift * drift
    spread = jnp.sum(squares, axis=0, keepdims=True) / total
    j = iota((8, 128), 1) % (GW * BR)
    blocks = [
        jnp.where(j == 4 * h, jnp.broadcast_to(v, (8, 128)), 0.0)
        for v in (centre, spread) for h in range(2)
    ]
    out = spread_sum(jnp.concatenate(blocks, axis=0))
    out = [out[8 * i : 8 * i + 1] for i in range(4)]
    return (
        jnp.concatenate(out[:2], axis=1),
        lax.rsqrt(jnp.concatenate(out[2:], axis=1) + EPS),
    )


def to_tail(part):
    index = iota((8, 256), 0)
    blocks = [jnp.zeros((8, 256), F32), jnp.zeros((8, 256), F32)]
    for k, value in enumerate(part):
        value = jnp.broadcast_to(value[0:1], (8, 256))
        high = value.astype(BF16).astype(F32)
        mid = (value - high).astype(BF16).astype(F32)
        for i, piece in enumerate((high, mid, value - high - mid)):
            blocks[k // 2] = jnp.where(index == 3 * (k % 2) + i, piece, blocks[k // 2])
    return jnp.concatenate(blocks, axis=0).astype(BF16)


def from_tail(message_ref):
    rows = message_ref.shape[0]
    part = message_ref[rows - TAIL : rows, :].astype(F32)
    return [
        jnp.sum(part[r : r + 3], axis=0, keepdims=True) for r in (0, 3, 8)
    ]


def silu(u):
    return 0.5 * u * (1.0 + jnp.tanh(0.5 * u))


def pack_pairs(v):
    n, m, _, lanes = v.shape
    v = v.reshape(n, m // 2, 2, 8, lanes)
    low, high = v[:, :, 0].reshape(-1, 8, lanes), v[:, :, 1].reshape(-1, 8, lanes)
    both = jnp.where(iota(low.shape, 1) < 4, low, pltpu.roll(high, 4, 1))
    return both.reshape(n, m // 2, 8, lanes)


def split_pairs(v, blank):
    inside = iota(v.shape, 1) < 4
    return [jnp.where(inside, v, blank), jnp.where(inside, pltpu.roll(v, 4, 1), blank)]


def edges(act):
    z = iota(act.shape, 2) % BR
    before, after = pltpu.roll(act, 1, 1), pltpu.roll(act, 7, 1)
    return jnp.where(z == BR - 1, before, jnp.where(z == 0, after, 0.0))


def columns(act, size):
    side = edges(act)
    z = iota((size,) + act.shape[1:], 2) % BR
    second = pltpu.roll(side, 2, 2)
    third = pltpu.roll(side, 4, 2)
    mixed = jnp.where(
        (z == 1) | (z == 2), second[1 : 1 + size],
        jnp.where((z == 3) | (z == 4), third[2 : 2 + size], side[0:size]),
    )
    return [act[e : e + size] for e in range(3)] + [mixed]


def halves(lanes):
    return range(lanes // 128)


def read(ref, start, count, stride):
    return jnp.concatenate(
        [ref[h, pl.ds(start, count, stride=stride), :] for h in range(ref.shape[0])], axis=1
    )


def write(ref, start, count, stride, value):
    for h in range(ref.shape[0]):
        ref[h, pl.ds(start, count, stride=stride), :] = value[:, h * 128 : (h + 1) * 128]


def write_block(ref, start, value):
    for h in range(ref.shape[0]):
        ref[h, start : start + value.shape[0], :] = value[:, h * 128 : (h + 1) * 128]


def even(axis):
    return lax.axis_index(axis) % 2 == 0


def sides(axis, first, second):
    i, n = lax.axis_index(axis), lax.axis_size(axis)
    blank = jnp.full(first.shape, SENT, F32)
    second = blank if second is None else second
    low, high = jnp.where(even(axis), second, first), jnp.where(even(axis), first, second)
    return jnp.where(i > 0, low, SENT), jnp.where(i < n - 1, high, SENT)


def pre_kernel(members, occ_ref, feat_ref, keep_ref, keys_ref, coded_ref, first_ref, second_ref,
               tail_ref, rows_ref=None):
    sx, sy, sb, lanes = feat_ref.shape
    me = lax.axis_index("gx")
    bricks = [occ_ref[x] for x in range(members)]

    def row_of(x):
        return sum(jnp.where(x == i, v, 0.0) for i, v in enumerate(bricks))

    mine = jnp.broadcast_to(row_of(me), (8, sb))
    keep = jnp.where(iota((8, sb), 0) == iota((8, sb), 1), mine, 0.0)
    keep = jnp.broadcast_to(jnp.sum(keep, axis=1, keepdims=True), (8, lanes))
    count = jnp.sum(keep, axis=0, keepdims=True) * float(sx * sy * BR * GW)
    keep_ref[...] = keep
    seq = keys_ref.shape[1]
    lane = iota((1, seq), 1)
    keys = jnp.zeros((1, seq), F32)
    for k in range(members):
        there = row_of(me ^ k)
        for b in range(sb):
            keys = jnp.where(
                (lane // (seq // members) == k) & (lane % (2 * sb) // 2 == b),
                there[:, b : b + 1], keys,
            )
    keys_ref[...] = jnp.broadcast_to(keys, keys_ref.shape)
    field = feat_ref[...].astype(F32)
    wide = jnp.concatenate([field, jnp.zeros((sx, sy, 8 - sb, lanes), F32)], axis=2)
    wide = wide.reshape(sx * sy, 8, lanes)
    total = jnp.sum(jnp.sum(wide, axis=0) * keep, axis=0, keepdims=True)

    def squares_about(mean):
        d = wide - mean[None]
        return jnp.sum(jnp.sum(d * d, axis=0) * keep, axis=0, keepdims=True)

    code = jnp.where((keep > 0)[None], wide, SENT)
    coded_ref[...] = code.reshape(sx * sy * 8, lanes).astype(BF16)
    packed = pack_pairs(code.reshape(sx, sy, 8, lanes))
    low = packed[0:2].reshape(-1, lanes)
    high = packed[sx - 2 : sx].reshape(-1, lanes)
    size = low.shape[0]
    first_ref[0:size, :] = jnp.where(even("gx"), high, low).astype(BF16)
    second_ref[0:size, :] = jnp.where(even("gx"), low, high).astype(BF16)
    mine = moments(total, squares_about, count)
    tail = to_tail(mine)
    first_ref[size : size + TAIL, :] = tail
    second_ref[size : size + TAIL, :] = tail
    tail_ref[...] = tail
    if rows_ref is not None:
        rows_ref[...] = jnp.broadcast_to(to_row(mine)[0:1], rows_ref.shape)


def line_kernel(narrow, sy, sb, _, coded_ref, first_ref, second_ref, *rest):
    tails, (ext_ref, out_ref, buf) = rest[:-3], rest[-3:]
    lanes = coded_ref.shape[1]
    sx = coded_ref.shape[0] // (sy * 8)
    size = 2 * (sy // 2) * 8
    low, high = sides(
        "gx", first_ref[0:size].astype(F32), second_ref[0:size].astype(F32)
    )
    write_block(buf, 2 * sy * 8, coded_ref[...].astype(F32))
    for x0, side in ((0, low), (sx + 2, high)):
        for i in range(2):
            part = side[i * (size // 2) : (i + 1) * (size // 2)].reshape(sy // 2, 8, lanes)
            pair = split_pairs(part, SENT)
            for y in range(sy):
                write_block(buf, ((x0 + i) * sy + y) * 8, pair[y % 2][y // 2])
    rows = (sx + 4) * sy * 8
    ext_ref[...] = jnp.concatenate([buf[h] for h in halves(lanes)], axis=1).astype(BF16)
    count = (sx + 4) * sy
    face = jnp.where(even("gz"), read(buf, sb - 1, count, 8), read(buf, 0, count, 8))
    out_ref[0:count, :] = face.astype(BF16)
    mine = [from_tail(ref) for ref in tails]
    if narrow:
        mine = mine + [from_tail(first_ref), from_tail(second_ref)]
    out_ref[count : count + TAIL, :] = to_tail(merge(mine))


def corner_rows(count):
    return (count + 15) // 16 * 16


def chip_kernel(sb, sy, pars_ref, ext_ref, own_ref, other_ref, rows_ref, *rest):
    out, (buf, stage) = rest[:-2], rest[-2:]
    lanes = ext_ref.shape[1]
    pick = onehot(iota((C, lanes), 0) == iota((C, lanes), 1) // BR, F32)
    rows_ref[...] = jnp.zeros(rows_ref.shape, F32)
    rows_ref[0 : pars_ref.shape[0], :] = exact_dot(pars_ref[...], pick)
    ex = ext_ref.shape[0] // (sy * 8)
    block = ext_ref[...].astype(F32)
    write_block(buf, 0, block)
    write_block(stage, 0, other_ref[0 : ex * sy].astype(F32))
    gap = corner_rows(ex)
    pad = jnp.zeros((gap - ex, lanes), F32)
    tail = to_tail(merge([from_tail(own_ref), from_tail(other_ref)]))
    packed = pack_pairs(block.reshape(ex, sy, 8, lanes))

    def side(y0):
        face = packed[:, y0 // 2].reshape(ex * 8, lanes)
        inner, outer = [], []
        for i in range(2):
            inner += [read(stage, y0 + i, ex, sy), pad]
            start = (y0 + i) * 8
            outer += [
                jnp.where(
                    even("gz"),
                    read(buf, start, ex, sy * 8),
                    read(buf, start + sb - 1, ex, sy * 8),
                ),
                pad,
            ]
        return [face] + inner, outer

    (near_low, far_low), (near_high, far_high) = side(0), side(sy - 2)
    count = ex * sy
    z_face = jnp.where(even("gz"), read(buf, 0, count, 8), read(buf, sb - 1, count, 8))
    out[0][0:count, :] = z_face.astype(BF16)
    out[0][count : count + TAIL, :] = tail
    for k in range((len(out) - 1) // 2):
        up = even("gy") if k == 0 else jnp.logical_not(even("gy"))
        for ref, low, high in (
            (out[1 + 2 * k], near_low, near_high),
            (out[2 + 2 * k], far_low, far_high),
        ):
            value = jnp.where(
                up, jnp.concatenate(high, axis=0), jnp.concatenate(low, axis=0)
            ).astype(BF16)
            ref[0 : value.shape[0], :] = value
            ref[value.shape[0] : value.shape[0] + TAIL, :] = tail


def band_kernel(weight_ref, out_ref, *later):
    lanes = C * BR
    spread = onehot(iota((C, lanes), 0) == iota((C, lanes), 1) // BR)
    turned = jnp.transpose(weight_ref[0].astype(F32)).astype(BF16)
    wide = jnp.dot(turned, spread, preferred_element_type=F32)
    full = (C, BR, lanes)
    zi, zo = iota((1, BR, lanes), 1), iota((1, BR, lanes), 2) % BR

    def rows(value):
        return jnp.broadcast_to(value[:, None, :], full)

    for ex in range(3):
        mixed = jnp.zeros(full, F32)
        for ey in range(3):
            q = (ex * 3 + ey) * 3
            terms = [wide[(q + e) * C : (q + e + 1) * C] for e in range(3)]
            inner = jnp.where(zi == zo - 1, rows(terms[0]), 0.0)
            inner = jnp.where(zi == zo, rows(terms[1]), inner)
            inner = jnp.where(zi == zo + 1, rows(terms[2]), inner)
            before = pltpu.roll(terms[0], 1, 0) if ey else terms[0]
            low = 2 * ey - 1 if ey else BR - 1
            mixed = jnp.where((zi == low) & (zo == 0), rows(before), mixed)
            mixed = jnp.where((zi == 2 * ey) & (zo == BR - 1), rows(terms[2]), mixed)
            out_ref[ex, ey * lanes : (ey + 1) * lanes, :] = (
                inner.reshape(C * BR, lanes).astype(BF16)
            )
        out_ref[ex, 3 * lanes : 4 * lanes, :] = mixed.reshape(C * BR, lanes).astype(BF16)
    if later:
        later[0][...] = weight_ref[1:2]


def turn_kernel(weight_ref, out_ref):
    kinds, cols, feats = weight_ref.shape
    r = iota((feats, 1), 0)
    source = (r % 128) // 4 * 32 + r // 128 * 4 + r % 4
    pick = onehot(source == iota((feats, feats), 1))
    for k in range(kinds):
        out_ref[:, k * cols : (k + 1) * cols] = lax.dot_general(
            pick, weight_ref[k], (((1,), (1,)), ((), ())), preferred_element_type=F32
        ).astype(BF16)


def first_kernel(narrow, faces, sy, sb, ext_ref, own_ref, core_ref, zface_ref, *rest):
    near, far = rest[0 : 2 * faces : 2], rest[1 : 2 * faces : 2]
    rest = rest[2 * faces :]
    stats_ref = None
    if not narrow:
        stats_ref, rest = rest[0], rest[1:]
    keep_ref, weight_ref, rows_ref, mid_ref, out_ref, buf, lhs, msk = rest
    lanes = ext_ref.shape[1]
    ex = ext_ref.shape[0] // (sy * 8)
    ey = sy + 4
    count = ex * sy
    z_low, z_high = sides(
        "gz", core_ref[0:count].astype(F32), zface_ref[0:count].astype(F32)
    )
    for x in range(ex):
        write_block(
            buf, (x * ey + 2) * 8, ext_ref[x * sy * 8 : (x + 1) * sy * 8].astype(F32)
        )
        part = slice(x * sy, (x + 1) * sy)
        write(buf, (x * ey + 2) * 8 + 7, sy, 8, z_low[part])
        write(buf, (x * ey + 2) * 8 + sb, sy, 8, z_high[part])
    gap = corner_rows(ex)
    size = ex * 8
    face = sides("gy", *[
        near[k][0:size].astype(F32) if k < faces else None for k in range(2)
    ])
    inner = sides("gy", *[
        near[k][size : size + 2 * gap].astype(F32) if k < faces else None for k in range(2)
    ])
    outer = sides("gy", *[
        far[k][0 : 2 * gap].astype(F32) if k < faces else None for k in range(2)
    ])
    for s, y0 in enumerate((0, sy + 2)):
        pair = split_pairs(face[s].reshape(ex, 8, lanes), SENT)
        c_low, c_high = sides("gz", inner[s], outer[s])
        for i in range(2):
            for x in range(ex):
                write_block(buf, (x * ey + y0 + i) * 8, pair[i][x])
            write(buf, (y0 + i) * 8 + 7, ex, ey * 8, c_low[i * gap : i * gap + ex])
            write(buf, (y0 + i) * 8 + sb, ex, ey * 8, c_high[i * gap : i * gap + ex])
    if narrow:
        centre, scale = centre_scale(merge(
            [from_tail(r) for r in (own_ref, zface_ref) + tuple(near) + tuple(far)]
        ))
    else:
        centre, scale = from_rows(stats_ref[...])
    gain, shift, bias = rows_ref[0:1], rows_ref[2:3], rows_ref[4:5]
    scale = scale * gain
    oy, sx = sy + 2, ex - 4
    step = ey * 8
    for x in range(ex):
        v = jnp.concatenate(
            [buf[h, x * step : (x + 1) * step, :] for h in halves(lanes)], axis=1
        )
        there = v != SENT
        msk[x * step : (x + 1) * step] = onehot(there[:, 0:128], F32)
        act = jnp.where(there, silu((v - centre) * scale + shift), 0.0).reshape(ey, 8, lanes)
        for e, part in enumerate(columns(act, oy)):
            lhs[x * oy * 8 : (x + 1) * oy * 8, e * lanes : (e + 1) * lanes] = (
                part.reshape(oy * 8, lanes).astype(BF16)
            )
    ox = sx + 2
    size = ox * oy * 8
    acc = bias
    for e in range(3):
        acc = acc + jnp.dot(
            lhs[e * oy * 8 : e * oy * 8 + size, :], weight_ref[e], preferred_element_type=F32
        )
    mid_ref[...] = acc
    keep = keep_ref[...]
    entries = jnp.sum(keep[:, 0:1]) * float(sx * sy * BR * GW)

    def over_cells(f):
        out = jnp.zeros((8, lanes), F32)
        for x in range(1, sx + 1):
            own = mid_ref[(x * oy + 1) * 8 : (x * oy + oy - 1) * 8].reshape(sy, 8, lanes)
            out = out + jnp.sum(f(own), axis=0)
        return jnp.sum(out * keep, axis=0, keepdims=True)

    def squares_about(mean):
        return over_cells(lambda v: (v - mean[None]) * (v - mean[None]))

    mine = moments(over_cells(lambda v: v), squares_about, entries)
    out_ref[...] = jnp.broadcast_to(to_row(mine)[0:1], out_ref.shape)
    for x in range(ox):
        rows = slice(x * oy * 8, (x + 1) * oy * 8)
        there = msk[(x + 1) * step + 8 : (x + 2) * step - 8]
        there = jnp.concatenate([there] * (lanes // 128), axis=1) > 0
        mid_ref[rows] = jnp.where(there, mid_ref[rows], BIG)


def second_kernel(stats_ref, mid_ref, weight_ref, rows_ref, coded_ref, fine_ref, tok_ref, lhs):
    sx, sy, sb, lanes = fine_ref.shape
    step = (sy + 2) * 8
    centre, scale = from_rows(stats_ref[...])
    gain, shift, bias = rows_ref[1:2], rows_ref[3:4], rows_ref[5:6]
    scale = scale * gain
    half = sy // 2 * 8
    for x in range(sx + 2):
        v = mid_ref[x * step : (x + 1) * step]
        act = jnp.where(v < BIG, silu((v - centre) * scale + shift), 0.0)
        for e, part in enumerate(columns(act.reshape(sy + 2, 8, lanes), sy)):
            lhs[x * half : (x + 1) * half, e * lanes : (e + 1) * lanes] = (
                pack_pairs(part[None]).reshape(half, lanes).astype(BF16)
            )
    size = sx * half
    acc = bias
    for e in range(3):
        acc = acc + jnp.dot(
            lhs[e * half : e * half + size, :], weight_ref[e], preferred_element_type=F32
        )
    field = pack_pairs(coded_ref[...].astype(F32).reshape(sx, sy, 8, lanes))
    field = field.reshape(size, lanes)
    out = jnp.where(field != SENT, field + acc, 0.0).reshape(-1, 8, lanes)
    out = out.astype(BF16)
    wide = out.astype(F32)
    other = pltpu.roll(wide, 4, 1)
    fine = jnp.stack([wide[:, :sb], other[:, :sb]], axis=1)
    fine_ref[...] = fine.reshape(sx, sy, sb, lanes).astype(BF16)
    i, j = iota((lanes, lanes), 0), iota((lanes, lanes), 1)
    pick = onehot(i == (j % 128) // 4 * 8 + j // 128 * 4 + j % 4)
    moved = jnp.dot(out.reshape(size, lanes), pick, preferred_element_type=F32).reshape(
        sx // 2, 2, sy // 4, 2, 8, lanes
    )
    count = sx // 2 * (sy // 4)
    parts = []
    for x in range(2):
        for y in range(2):
            piece = moved[:, x, :, y].reshape(count, 8, lanes)
            low, high = piece[:, :, :128], piece[:, :, 128:]
            inside = iota(low.shape, 1) < 4
            for both in (
                jnp.where(inside, low, pltpu.roll(high, 4, 1)),
                jnp.where(inside, pltpu.roll(low, 4, 1), high),
            ):
                parts.append(both.reshape(count * 8, 128).astype(BF16))
    tokens = jnp.concatenate(parts, axis=1)
    n = count * 8
    i, j = iota((n, n), 0), iota((n, n), 1)
    order = onehot(j == i // 8 * 8 + i % 2 * 4 + i % 8 // 2)
    tok_ref[...] = jnp.dot(order, tokens, preferred_element_type=F32).astype(BF16)


def attend_kernel(members, keys_ref, weight_ref, *refs):
    tok_refs, out_refs, (toks, proj) = refs[:members], refs[members : 2 * members], refs[-2:]
    own = tok_refs[0].shape[0]
    seq = own * members
    cols = weight_ref.shape[1] // 3
    for k in range(members):
        toks[k * own : (k + 1) * own, :] = tok_refs[k][...]
    proj[...] = jnp.dot(toks[...], weight_ref[...], preferred_element_type=F32).astype(BF16)
    there = keys_ref[0:1] > 0
    width = min(128, cols)
    for t in range(cols // width):
        q = proj[:, t * width : (t + 1) * width]
        keys = proj[:, cols + t * width : cols + (t + 1) * width]
        values = proj[:, 2 * cols + t * width : 2 * cols + (t + 1) * width]
        head = iota((seq, width), 1) // HD
        merged = jnp.zeros((seq, width), F32)
        for h in range(width // HD):
            mine = jnp.where(head == h, q.astype(F32), 0.0).astype(BF16)
            scores = lax.dot_general(
                mine, keys, (((1,), (1,)), ((), ())), preferred_element_type=F32
            ) * float(HD) ** (-0.5)
            scores = jnp.where(there, scores, -BIG)
            probs = jnp.exp(scores - jnp.max(scores, axis=1, keepdims=True))
            total = jnp.sum(probs, axis=1, keepdims=True)
            mixed = jnp.dot(probs.astype(BF16), values, preferred_element_type=F32)
            merged = jnp.where(head == h, mixed / total, merged)
        merged = merged.astype(BF16)
        for k in range(members):
            out_refs[k][:, t * width : (t + 1) * width] = merged[k * own : (k + 1) * own]


def place_kernel(members, keep_ref, *refs):
    out_ref = refs[-1]
    own, cols = refs[0].shape
    me = lax.axis_index("gx")
    row = iota((8, cols), 0)
    keep = jnp.zeros((8, cols), F32)
    for b in range(4):
        keep = jnp.where(row // 2 == b, jnp.broadcast_to(keep_ref[b : b + 1, :cols], (8, cols)), keep)
    for k in range(members):
        value = refs[k][...].astype(F32).reshape(own // 8, 8, cols)
        value = jnp.where((keep > 0)[None], value, 0.0).reshape(own, cols).astype(BF16)
        if cols % 128 == 0:
            out_ref[0, :, pl.ds(pl.multiple_of((me ^ k) * cols, cols), cols)] = value
        else:
            out_ref[k] = value


VM = pl.BlockSpec(memory_space=pltpu.VMEM)


def call(kernel, name, specs, out, args, scratch=(), flops=0, nbytes=0, mib=16):
    return pl.pallas_call(
        kernel,
        out_shape=out,
        in_specs=list(specs),
        out_specs=jax.tree.map(lambda _: VM, out),
        scratch_shapes=list(scratch),
        name=name,
        cost_estimate=pl.CostEstimate(flops=flops, bytes_accessed=nbytes, transcendentals=0),
        compiler_params=pltpu.CompilerParams(vmem_limit_bytes=mib * 2**20),
    )(*args)


def shape(*dims, dtype=BF16):
    return jax.ShapeDtypeStruct(dims, dtype)


def pairing(n, odd, closed):
    partner = {i: (i ^ 1 if not odd else (i + 1 if i % 2 else i - 1)) for i in range(n)}
    if closed:
        partner = {i: j % n for i, j in partner.items()}
    return {i: j for i, j in partner.items() if 0 <= j < n and i != j}


def body(features, occupancy, norm_gain, norm_shift, conv_weight, conv_bias, qkv_weight):
    sx, sy, sb, lanes = features.shape
    nx, ny, nz = (lax.axis_size(a) for a in ALL)
    devices = nx * ny * nz
    narrow = nx == 4 and ny == 2 and nz == 4
    own = sx // 2 * (sy // 4) * sb * 2
    ex = sx + 4
    row_shape = [] if narrow else [shape(devices, 128, dtype=F32)]

    slab = sy * 8 + TAIL
    keep, keys, coded, first, second, tail, *stats = call(
        functools.partial(pre_kernel, nx), "pre", (VM, VM),
        [shape(8, lanes, dtype=F32), shape(8, own * nx, dtype=F32),
         shape(sx * sy * 8, lanes), shape(slab, lanes), shape(slab, lanes), shape(TAIL, lanes)]
        + row_shape,
        (occupancy.astype(F32), features), nbytes=10**6,
    )
    stats = [lax.all_to_all(s, ALL, 0, 0, tiled=True) for s in stats]
    got = [
        lax.ppermute(first, "gx", list(pairing(nx, False, False).items())),
        lax.ppermute(second, "gx", list(pairing(nx, True, narrow).items())),
    ]
    tails = [tail]
    if narrow:
        tails.append(lax.ppermute(tail, "gx", [(i, i ^ 2) for i in range(nx)]))
    band = shape(3, 4 * lanes, lanes)
    pars = jnp.concatenate([norm_gain, norm_shift, conv_bias], axis=0)
    later = shape(1, *conv_weight.shape[1:])
    band0, later = call(
        band_kernel, "band0", (VM,), [band, later], (conv_weight,), nbytes=8 * 10**6,
    )
    band1 = call(band_kernel, "band1", (VM,), band, (later,), nbytes=8 * 10**6)
    count = ex * sy
    ext, mine = call(
        functools.partial(line_kernel, narrow, sy, sb), "line", (VM,) * (4 + len(tails)),
        [shape(count * 8, lanes), shape(count + TAIL, lanes)],
        (later, coded, *got, *tails),
        [pltpu.VMEM((lanes // 128, count * 8, 128), F32)], nbytes=10**6,
    )
    core = lax.ppermute(mine, "gz", list(pairing(nz, False, False).items()))

    faces = 1 if ny == 2 else 2
    gap = corner_rows(ex)
    near, far = ex * 8 + 2 * gap + TAIL, 2 * gap + TAIL
    rows, zface, *yfaces = call(
        functools.partial(chip_kernel, sb, sy), "chip", (VM,) * 4,
        [shape(8, lanes, dtype=F32), shape(count + TAIL, lanes)] + [shape(near, lanes), shape(far, lanes)] * faces,
        (pars, ext, mine, core),
        [pltpu.VMEM((lanes // 128, count * 8, 128), F32),
         pltpu.VMEM((lanes // 128, count, 128), F32)], nbytes=10**6,
    )
    odd_z = pairing(nz, True, narrow)
    own_tail = zface
    zgot = lax.ppermute(zface, "gz", list(odd_z.items()))
    ygot = []
    for k in range(faces):
        along = pairing(ny, k == 1, False)
        ygot.append(lax.ppermute(yfaces[2 * k], "gy", list(along.items())))
        both = [
            (y * nz + z, along[y] * nz + odd_z[z]) for y in along for z in odd_z
        ]
        ygot.append(lax.ppermute(yfaces[2 * k + 1], ("gy", "gz"), both))

    cols, feats = qkv_weight.shape[1:]
    turned = call(
        turn_kernel, "turn", (VM,), shape(feats, 3 * cols), (qkv_weight,),
        flops=2 * 3 * cols * feats * feats, nbytes=6 * 10**6,
    )

    ey, oy = sy + 4, sy + 2
    size = (sx + 2) * oy * 8
    mid, mine = call(
        functools.partial(first_kernel, narrow, faces, sy, sb), "first",
        (VM,) * (7 + 2 * faces + len(stats)),
        [shape(size, lanes, dtype=F32), shape(devices, 128, dtype=F32)],
        (ext, own_tail, core, zgot, *ygot, *stats, keep, band0, rows),
        [pltpu.VMEM((lanes // 128, ex * ey * 8, 128), F32),
         pltpu.VMEM((ex * oy * 8, 4 * lanes), BF16),
         pltpu.VMEM((ex * ey * 8, 128), F32)],
        flops=2 * 10**9, nbytes=4 * 10**6, mib=20,
    )
    stats = lax.all_to_all(mine, ALL, 0, 0, tiled=True)
    fine_out, tokens = call(
        second_kernel, "second", (VM,) * 5,
        [shape(*features.shape), shape(own, feats)],
        (stats, mid, band1, rows, coded),
        [pltpu.VMEM(((sx + 2) * sy * 4, 4 * lanes), BF16)],
        flops=10**9, nbytes=4 * 10**6,
    )
    swaps = [[(i, i ^ k) for i in range(nx)] for k in range(nx)]
    blocks = {0: tokens}
    for k in sorted(range(1, nx), key=lambda k: (bin(k).count("1"), -k)):
        low = k & -k
        blocks[k] = lax.ppermute(blocks[k ^ low], "gx", swaps[low])
    blocks = [blocks[k] for k in range(nx)]
    outs = call(
        functools.partial(attend_kernel, nx), "attend", (VM,) * (2 + nx),
        [shape(own, cols)] * nx, (keys, turned, *blocks),
        [pltpu.VMEM((own * nx, feats), BF16), pltpu.VMEM((own * nx, 3 * cols), BF16)],
        flops=10**9, nbytes=3 * 10**6, mib=16 if narrow else 40,
    )
    moved = {k: lax.ppermute(outs[k], "gx", swaps[k]) for k in range(nx - 1, 0, -1)}
    outs = [outs[0]] + [moved[k] for k in range(1, nx)]
    lined = cols % 128 == 0
    attention = call(
        functools.partial(place_kernel, nx), "place", (VM,) * (1 + nx),
        shape(1, own, nx * cols) if lined else shape(nx, own, cols), (keep, *outs),
        nbytes=3 * 10**5, mib=8,
    )
    if not lined:
        me = lax.axis_index("gx")
        attention = jnp.concatenate(
            [lax.dynamic_index_in_dim(attention, me ^ j, 0, keepdims=False) for j in range(nx)],
            axis=1,
        )[None]
    return (fine_out, attention)


def solution(mesh):
    placed = (
        P("gx", "gy", "gz", None),
        P(None, "gy", "gz"),
        P(),
        P(),
        P(),
        P(),
        P(None, "gx", None),
    )
    return jax.shard_map(
        body,
        mesh=mesh,
        in_specs=placed,
        out_specs=(P("gx", "gy", "gz", None), P(("gy", "gz"), "gx", None)),
        check_vma=False,
    )
```

```python
import functools

import jax
import jax.numpy as jnp
from jax import lax
from jax.experimental import pallas as pl
from jax.experimental.pallas import tpu as pltpu
from jax.sharding import PartitionSpec as P

C = 32
GW = 4
HD = 64
BR = 8
EPS = 1e-05
SENT = 512.0
BIG = 1e30
ALL = ("gx", "gy", "gz")
F32, BF16 = jnp.float32, jnp.bfloat16
HIGHEST = lax.Precision.HIGHEST
TAIL = 16


def iota(shape, dim):
    return lax.broadcasted_iota(jnp.int32, shape, dim)


def onehot(cond, dtype=BF16):
    return jnp.where(cond, 1.0, 0.0).astype(dtype)


def exact_dot(a, b):
    return jnp.dot(a, b, precision=HIGHEST, preferred_element_type=F32)


def spread_sum(v):
    lane = iota(v.shape, 1)
    s = 1
    while s < GW * BR:
        v = v + jnp.where(lane & s == 0, pltpu.roll(v, 128 - s, 1), pltpu.roll(v, s, 1))
        s *= 2
    return v


def group_sum(total):
    k = total.shape[1] // 128
    rows = [jnp.broadcast_to(total[:, h * 128 : (h + 1) * 128], (8, 128)) for h in range(k)]
    out = spread_sum(jnp.concatenate(rows, axis=0))
    return jnp.concatenate([out[h * 8 : (h + 1) * 8] for h in range(k)], axis=1)


def moments(total, squares_about, count):
    sums = group_sum(total)
    squares = group_sum(squares_about((sums / count)[0:1]))
    return sums, squares, jnp.zeros(sums.shape, F32) + count


def merge(parts):
    n = sum(p[2] for p in parts)
    sums = sum(p[0] for p in parts)
    centre = sums / n
    squares = sum(p[1] + p[2] * (p[0] / p[2] - centre) ** 2 for p in parts)
    return sums, squares, n


def centre_scale(part):
    return part[0] / part[2], lax.rsqrt(part[1] / part[2] + EPS)


def to_row(part):
    j = iota((8, 128), 1) % (GW * BR)
    row = jnp.zeros((8, 128), F32)
    for h in range(2):
        for k in range(3):
            row = jnp.where(j == 4 * h + k, part[k][:, h * 128 : (h + 1) * 128], row)
    return row


def from_rows(rows):
    n = jnp.maximum(pltpu.roll(rows, 126, 1), 1.0)
    total = jnp.sum(n, axis=0, keepdims=True)
    centre = jnp.sum(rows, axis=0, keepdims=True) / total
    drift = rows / n - centre
    squares = pltpu.roll(rows, 127, 1) + n * drift * drift
    spread = jnp.sum(squares, axis=0, keepdims=True) / total
    j = iota((8, 128), 1) % (GW * BR)
    blocks = [
        jnp.where(j == 4 * h, jnp.broadcast_to(v, (8, 128)), 0.0)
        for v in (centre, spread) for h in range(2)
    ]
    out = spread_sum(jnp.concatenate(blocks, axis=0))
    out = [out[8 * i : 8 * i + 1] for i in range(4)]
    return (
        jnp.concatenate(out[:2], axis=1),
        lax.rsqrt(jnp.concatenate(out[2:], axis=1) + EPS),
    )


def to_tail(part):
    index = iota((8, 256), 0)
    blocks = [jnp.zeros((8, 256), F32), jnp.zeros((8, 256), F32)]
    for k, value in enumerate(part):
        value = jnp.broadcast_to(value[0:1], (8, 256))
        high = value.astype(BF16).astype(F32)
        mid = (value - high).astype(BF16).astype(F32)
        for i, piece in enumerate((high, mid, value - high - mid)):
            blocks[k // 2] = jnp.where(index == 3 * (k % 2) + i, piece, blocks[k // 2])
    return jnp.concatenate(blocks, axis=0).astype(BF16)


def from_tail(message_ref):
    rows = message_ref.shape[0]
    part = message_ref[rows - TAIL : rows, :].astype(F32)
    return [
        jnp.sum(part[r : r + 3], axis=0, keepdims=True) for r in (0, 3, 8)
    ]


def silu(u):
    return 0.5 * u * (1.0 + jnp.tanh(0.5 * u))


def pack_pairs(v):
    n, m, _, lanes = v.shape
    v = v.reshape(n, m // 2, 2, 8, lanes)
    low, high = v[:, :, 0].reshape(-1, 8, lanes), v[:, :, 1].reshape(-1, 8, lanes)
    both = jnp.where(iota(low.shape, 1) < 4, low, pltpu.roll(high, 4, 1))
    return both.reshape(n, m // 2, 8, lanes)


def split_pairs(v, blank):
    inside = iota(v.shape, 1) < 4
    return [jnp.where(inside, v, blank), jnp.where(inside, pltpu.roll(v, 4, 1), blank)]


def edges(act):
    z = iota(act.shape, 2) % BR
    before, after = pltpu.roll(act, 1, 1), pltpu.roll(act, 7, 1)
    return jnp.where(z == BR - 1, before, jnp.where(z == 0, after, 0.0))


def columns(act, size):
    side = edges(act)
    z = iota((size,) + act.shape[1:], 2) % BR
    second = pltpu.roll(side, 2, 2)
    third = pltpu.roll(side, 4, 2)
    mixed = jnp.where(
        (z == 1) | (z == 2), second[1 : 1 + size],
        jnp.where((z == 3) | (z == 4), third[2 : 2 + size], side[0:size]),
    )
    return [act[e : e + size] for e in range(3)] + [mixed]


def halves(lanes):
    return range(lanes // 128)


def read(ref, start, count, stride):
    return jnp.concatenate(
        [ref[h, pl.ds(start, count, stride=stride), :] for h in range(ref.shape[0])], axis=1
    )


def write(ref, start, count, stride, value):
    for h in range(ref.shape[0]):
        ref[h, pl.ds(start, count, stride=stride), :] = value[:, h * 128 : (h + 1) * 128]


def write_block(ref, start, value):
    for h in range(ref.shape[0]):
        ref[h, start : start + value.shape[0], :] = value[:, h * 128 : (h + 1) * 128]


def even(axis):
    return lax.axis_index(axis) % 2 == 0


def sides(axis, first, second):
    i, n = lax.axis_index(axis), lax.axis_size(axis)
    blank = jnp.full(first.shape, SENT, F32)
    second = blank if second is None else second
    low, high = jnp.where(even(axis), second, first), jnp.where(even(axis), first, second)
    return jnp.where(i > 0, low, SENT), jnp.where(i < n - 1, high, SENT)


def pre_kernel(members, occ_ref, feat_ref, keep_ref, keys_ref, coded_ref, first_ref, second_ref,
               tail_ref, rows_ref=None):
    sx, sy, sb, lanes = feat_ref.shape
    me = lax.axis_index("gx")
    bricks = [occ_ref[x].astype(F32) for x in range(members)]

    def row_of(x):
        return sum(jnp.where(x == i, v, 0.0) for i, v in enumerate(bricks))

    mine = jnp.broadcast_to(row_of(me), (8, sb))
    keep = jnp.where(iota((8, sb), 0) == iota((8, sb), 1), mine, 0.0)
    keep = jnp.broadcast_to(jnp.sum(keep, axis=1, keepdims=True), (8, lanes))
    count = jnp.sum(keep, axis=0, keepdims=True) * float(sx * sy * BR * GW)
    keep_ref[...] = keep
    seq = keys_ref.shape[1]
    lane = iota((1, seq), 1)
    keys = jnp.zeros((1, seq), F32)
    for k in range(members):
        there = row_of(me ^ k)
        for b in range(sb):
            keys = jnp.where(
                (lane // (seq // members) == k) & (lane % (2 * sb) // 2 == b),
                there[:, b : b + 1], keys,
            )
    keys_ref[...] = jnp.broadcast_to(keys, keys_ref.shape)
    field = feat_ref[...].astype(F32)
    wide = jnp.concatenate([field, jnp.zeros((sx, sy, 8 - sb, lanes), F32)], axis=2)
    wide = wide.reshape(sx * sy, 8, lanes)
    total = jnp.sum(jnp.sum(wide, axis=0) * keep, axis=0, keepdims=True)

    def squares_about(mean):
        d = wide - mean[None]
        return jnp.sum(jnp.sum(d * d, axis=0) * keep, axis=0, keepdims=True)

    code = jnp.where((keep > 0)[None], wide, SENT)
    coded_ref[...] = code.reshape(sx * sy * 8, lanes).astype(BF16)
    packed = pack_pairs(code.reshape(sx, sy, 8, lanes))
    low = packed[0:2].reshape(-1, lanes)
    high = packed[sx - 2 : sx].reshape(-1, lanes)
    size = low.shape[0]
    first_ref[0:size, :] = jnp.where(even("gx"), high, low).astype(BF16)
    second_ref[0:size, :] = jnp.where(even("gx"), low, high).astype(BF16)
    mine = moments(total, squares_about, count)
    tail = to_tail(mine)
    first_ref[size : size + TAIL, :] = tail
    second_ref[size : size + TAIL, :] = tail
    tail_ref[...] = tail
    if rows_ref is not None:
        rows_ref[...] = jnp.broadcast_to(to_row(mine)[0:1], rows_ref.shape)


def line_kernel(narrow, sy, sb, _, coded_ref, first_ref, second_ref, *rest):
    tails, (ext_ref, out_ref, buf) = rest[:-3], rest[-3:]
    lanes = coded_ref.shape[1]
    sx = coded_ref.shape[0] // (sy * 8)
    size = 2 * (sy // 2) * 8
    low, high = sides(
        "gx", first_ref[0:size].astype(F32), second_ref[0:size].astype(F32)
    )
    write_block(buf, 2 * sy * 8, coded_ref[...].astype(F32))
    for x0, side in ((0, low), (sx + 2, high)):
        for i in range(2):
            part = side[i * (size // 2) : (i + 1) * (size // 2)].reshape(sy // 2, 8, lanes)
            pair = split_pairs(part, SENT)
            for y in range(sy):
                write_block(buf, ((x0 + i) * sy + y) * 8, pair[y % 2][y // 2])
    rows = (sx + 4) * sy * 8
    ext_ref[...] = jnp.concatenate([buf[h] for h in halves(lanes)], axis=1).astype(BF16)
    count = (sx + 4) * sy
    face = jnp.where(even("gz"), read(buf, sb - 1, count, 8), read(buf, 0, count, 8))
    out_ref[0:count, :] = face.astype(BF16)
    mine = [from_tail(ref) for ref in tails]
    if narrow:
        mine = mine + [from_tail(first_ref), from_tail(second_ref)]
    out_ref[count : count + TAIL, :] = to_tail(merge(mine))


def corner_rows(count):
    return (count + 15) // 16 * 16


def chip_kernel(sb, sy, ext_ref, own_ref, other_ref, *rest):
    out, (buf, stage) = rest[:-2], rest[-2:]
    lanes = ext_ref.shape[1]
    ex = ext_ref.shape[0] // (sy * 8)
    block = ext_ref[...].astype(F32)
    write_block(buf, 0, block)
    write_block(stage, 0, other_ref[0 : ex * sy].astype(F32))
    gap = corner_rows(ex)
    pad = jnp.zeros((gap - ex, lanes), F32)
    tail = to_tail(merge([from_tail(own_ref), from_tail(other_ref)]))
    packed = pack_pairs(block.reshape(ex, sy, 8, lanes))

    def side(y0):
        face = packed[:, y0 // 2].reshape(ex * 8, lanes)
        inner, outer = [], []
        for i in range(2):
            inner += [read(stage, y0 + i, ex, sy), pad]
            start = (y0 + i) * 8
            outer += [
                jnp.where(
                    even("gz"),
                    read(buf, start, ex, sy * 8),
                    read(buf, start + sb - 1, ex, sy * 8),
                ),
                pad,
            ]
        return [face] + inner, outer

    (near_low, far_low), (near_high, far_high) = side(0), side(sy - 2)
    count = ex * sy
    z_face = jnp.where(even("gz"), read(buf, 0, count, 8), read(buf, sb - 1, count, 8))
    out[0][0:count, :] = z_face.astype(BF16)
    out[0][count : count + TAIL, :] = tail
    for k in range((len(out) - 1) // 2):
        up = even("gy") if k == 0 else jnp.logical_not(even("gy"))
        for ref, low, high in (
            (out[1 + 2 * k], near_low, near_high),
            (out[2 + 2 * k], far_low, far_high),
        ):
            value = jnp.where(
                up, jnp.concatenate(high, axis=0), jnp.concatenate(low, axis=0)
            ).astype(BF16)
            ref[0 : value.shape[0], :] = value
            ref[value.shape[0] : value.shape[0] + TAIL, :] = tail


def band_kernel(weight_ref, *rest):
    pars, (out_ref, more_ref) = rest[:-2], rest[-2:]
    lanes = C * BR
    spread = onehot(iota((C, lanes), 0) == iota((C, lanes), 1) // BR)
    turned = jnp.transpose(weight_ref[0].astype(F32)).astype(BF16)
    wide = jnp.dot(turned, spread, preferred_element_type=F32)
    full = (C, BR, lanes)
    zi, zo = iota((1, BR, lanes), 1), iota((1, BR, lanes), 2) % BR

    def rows(value):
        return jnp.broadcast_to(value[:, None, :], full)

    for ex in range(3):
        mixed = jnp.zeros(full, F32)
        for ey in range(3):
            q = (ex * 3 + ey) * 3
            terms = [wide[(q + e) * C : (q + e + 1) * C] for e in range(3)]
            inner = jnp.where(zi == zo - 1, rows(terms[0]), 0.0)
            inner = jnp.where(zi == zo, rows(terms[1]), inner)
            inner = jnp.where(zi == zo + 1, rows(terms[2]), inner)
            before = pltpu.roll(terms[0], 1, 0) if ey else terms[0]
            low = 2 * ey - 1 if ey else BR - 1
            mixed = jnp.where((zi == low) & (zo == 0), rows(before), mixed)
            mixed = jnp.where((zi == 2 * ey) & (zo == BR - 1), rows(terms[2]), mixed)
            out_ref[ex, ey * lanes : (ey + 1) * lanes, :] = (
                inner.reshape(C * BR, lanes).astype(BF16)
            )
        out_ref[ex, 3 * lanes : 4 * lanes, :] = mixed.reshape(C * BR, lanes).astype(BF16)
    if pars:
        pick = onehot(iota((C, lanes), 0) == iota((C, lanes), 1) // BR, F32)
        more_ref[...] = jnp.zeros(more_ref.shape, F32)
        more_ref[0 : pars[0].shape[0], :] = exact_dot(pars[0][...], pick)
    else:
        more_ref[...] = weight_ref[1:2]


def turn_kernel(weight_ref, out_ref):
    kinds, cols, feats = weight_ref.shape
    r = iota((feats, 1), 0)
    source = (r % 128) // 4 * 32 + r // 128 * 4 + r % 4
    pick = onehot(source == iota((feats, feats), 1))
    for k in range(kinds):
        out_ref[:, k * cols : (k + 1) * cols] = lax.dot_general(
            pick, weight_ref[k], (((1,), (1,)), ((), ())), preferred_element_type=F32
        ).astype(BF16)


def first_kernel(narrow, faces, sy, sb, ext_ref, own_ref, core_ref, zface_ref, *rest):
    near, far = rest[0 : 2 * faces : 2], rest[1 : 2 * faces : 2]
    rest = rest[2 * faces :]
    stats_ref = None
    if not narrow:
        stats_ref, rest = rest[0], rest[1:]
    keep_ref, weight_ref, rows_ref, mid_ref, out_ref, buf, lhs, msk = rest
    lanes = ext_ref.shape[1]
    ex = ext_ref.shape[0] // (sy * 8)
    ey = sy + 4
    count = ex * sy
    z_low, z_high = sides(
        "gz", core_ref[0:count].astype(F32), zface_ref[0:count].astype(F32)
    )
    for x in range(ex):
        write_block(
            buf, (x * ey + 2) * 8, ext_ref[x * sy * 8 : (x + 1) * sy * 8].astype(F32)
        )
        part = slice(x * sy, (x + 1) * sy)
        write(buf, (x * ey + 2) * 8 + 7, sy, 8, z_low[part])
        write(buf, (x * ey + 2) * 8 + sb, sy, 8, z_high[part])
    gap = corner_rows(ex)
    size = ex * 8
    face = sides("gy", *[
        near[k][0:size].astype(F32) if k < faces else None for k in range(2)
    ])
    inner = sides("gy", *[
        near[k][size : size + 2 * gap].astype(F32) if k < faces else None for k in range(2)
    ])
    outer = sides("gy", *[
        far[k][0 : 2 * gap].astype(F32) if k < faces else None for k in range(2)
    ])
    for s, y0 in enumerate((0, sy + 2)):
        pair = split_pairs(face[s].reshape(ex, 8, lanes), SENT)
        c_low, c_high = sides("gz", inner[s], outer[s])
        for i in range(2):
            for x in range(ex):
                write_block(buf, (x * ey + y0 + i) * 8, pair[i][x])
            write(buf, (y0 + i) * 8 + 7, ex, ey * 8, c_low[i * gap : i * gap + ex])
            write(buf, (y0 + i) * 8 + sb, ex, ey * 8, c_high[i * gap : i * gap + ex])
    if narrow:
        centre, scale = centre_scale(merge(
            [from_tail(r) for r in (own_ref, zface_ref) + tuple(near) + tuple(far)]
        ))
    else:
        centre, scale = from_rows(stats_ref[...])
    gain, shift, bias = rows_ref[0:1], rows_ref[2:3], rows_ref[4:5]
    scale = scale * gain
    oy, sx = sy + 2, ex - 4
    step = ey * 8
    for x in range(ex):
        v = jnp.concatenate(
            [buf[h, x * step : (x + 1) * step, :] for h in halves(lanes)], axis=1
        )
        there = v != SENT
        msk[x * step : (x + 1) * step] = onehot(there[:, 0:128], F32)
        act = jnp.where(there, silu((v - centre) * scale + shift), 0.0).reshape(ey, 8, lanes)
        for e, part in enumerate(columns(act, oy)):
            lhs[x * oy * 8 : (x + 1) * oy * 8, e * lanes : (e + 1) * lanes] = (
                part.reshape(oy * 8, lanes).astype(BF16)
            )
    ox = sx + 2
    size = ox * oy * 8
    acc = bias
    for e in range(3):
        acc = acc + jnp.dot(
            lhs[e * oy * 8 : e * oy * 8 + size, :], weight_ref[e], preferred_element_type=F32
        )
    mid_ref[...] = acc
    keep = keep_ref[...]
    entries = jnp.sum(keep[:, 0:1]) * float(sx * sy * BR * GW)

    def over_cells(f):
        out = jnp.zeros((8, lanes), F32)
        for x in range(1, sx + 1):
            own = mid_ref[(x * oy + 1) * 8 : (x * oy + oy - 1) * 8].reshape(sy, 8, lanes)
            out = out + jnp.sum(f(own), axis=0)
        return jnp.sum(out * keep, axis=0, keepdims=True)

    def squares_about(mean):
        return over_cells(lambda v: (v - mean[None]) * (v - mean[None]))

    mine = moments(over_cells(lambda v: v), squares_about, entries)
    out_ref[...] = jnp.broadcast_to(to_row(mine)[0:1], out_ref.shape)
    for x in range(ox):
        rows = slice(x * oy * 8, (x + 1) * oy * 8)
        there = msk[(x + 1) * step + 8 : (x + 2) * step - 8]
        there = jnp.concatenate([there] * (lanes // 128), axis=1) > 0
        mid_ref[rows] = jnp.where(there, mid_ref[rows], BIG)


def second_kernel(stats_ref, mid_ref, weight_ref, rows_ref, coded_ref, fine_ref, tok_ref, lhs):
    sx, sy, sb, lanes = fine_ref.shape
    step = (sy + 2) * 8
    centre, scale = from_rows(stats_ref[...])
    gain, shift, bias = rows_ref[1:2], rows_ref[3:4], rows_ref[5:6]
    scale = scale * gain
    half = sy // 2 * 8
    for x in range(sx + 2):
        v = mid_ref[x * step : (x + 1) * step]
        act = jnp.where(v < BIG, silu((v - centre) * scale + shift), 0.0)
        for e, part in enumerate(columns(act.reshape(sy + 2, 8, lanes), sy)):
            lhs[x * half : (x + 1) * half, e * lanes : (e + 1) * lanes] = (
                pack_pairs(part[None]).reshape(half, lanes).astype(BF16)
            )
    size = sx * half
    acc = bias
    for e in range(3):
        acc = acc + jnp.dot(
            lhs[e * half : e * half + size, :], weight_ref[e], preferred_element_type=F32
        )
    field = pack_pairs(coded_ref[...].astype(F32).reshape(sx, sy, 8, lanes))
    field = field.reshape(size, lanes)
    out = jnp.where(field != SENT, field + acc, 0.0).reshape(-1, 8, lanes)
    out = out.astype(BF16)
    wide = out.astype(F32)
    other = pltpu.roll(wide, 4, 1)
    fine = jnp.stack([wide[:, :sb], other[:, :sb]], axis=1)
    fine_ref[...] = fine.reshape(sx, sy, sb, lanes).astype(BF16)
    i, j = iota((lanes, lanes), 0), iota((lanes, lanes), 1)
    pick = onehot(i == (j % 128) // 4 * 8 + j // 128 * 4 + j % 4)
    moved = jnp.dot(out.reshape(size, lanes), pick, preferred_element_type=F32).reshape(
        sx // 2, 2, sy // 4, 2, 8, lanes
    )
    count = sx // 2 * (sy // 4)
    parts = []
    for x in range(2):
        for y in range(2):
            piece = moved[:, x, :, y].reshape(count, 8, lanes)
            low, high = piece[:, :, :128], piece[:, :, 128:]
            inside = iota(low.shape, 1) < 4
            for both in (
                jnp.where(inside, low, pltpu.roll(high, 4, 1)),
                jnp.where(inside, pltpu.roll(low, 4, 1), high),
            ):
                parts.append(both.reshape(count * 8, 128).astype(BF16))
    tokens = jnp.concatenate(parts, axis=1)
    n = count * 8
    i, j = iota((n, n), 0), iota((n, n), 1)
    order = onehot(j == i // 8 * 8 + i % 2 * 4 + i % 8 // 2)
    tok_ref[...] = jnp.dot(order, tokens, preferred_element_type=F32).astype(BF16)


def attend_kernel(members, keys_ref, weight_ref, *refs):
    tok_refs, out_refs, (toks, proj) = refs[:members], refs[members : 2 * members], refs[-2:]
    own = tok_refs[0].shape[0]
    seq = own * members
    cols = weight_ref.shape[1] // 3
    for k in range(members):
        toks[k * own : (k + 1) * own, :] = tok_refs[k][...]
    proj[...] = jnp.dot(toks[...], weight_ref[...], preferred_element_type=F32).astype(BF16)
    there = keys_ref[0:1] > 0
    width = min(128, cols)
    for t in range(cols // width):
        q = proj[:, t * width : (t + 1) * width]
        keys = proj[:, cols + t * width : cols + (t + 1) * width]
        values = proj[:, 2 * cols + t * width : 2 * cols + (t + 1) * width]
        head = iota((seq, width), 1) // HD
        merged = jnp.zeros((seq, width), F32)
        for h in range(width // HD):
            mine = jnp.where(head == h, q.astype(F32), 0.0).astype(BF16)
            scores = lax.dot_general(
                mine, keys, (((1,), (1,)), ((), ())), preferred_element_type=F32
            ) * float(HD) ** (-0.5)
            scores = jnp.where(there, scores, -BIG)
            probs = jnp.exp(scores - jnp.max(scores, axis=1, keepdims=True))
            total = jnp.sum(probs, axis=1, keepdims=True)
            mixed = jnp.dot(probs.astype(BF16), values, preferred_element_type=F32)
            merged = jnp.where(head == h, mixed / total, merged)
        merged = merged.astype(BF16)
        for k in range(members):
            out_refs[-1 - k][:, t * width : (t + 1) * width] = merged[k * own : (k + 1) * own]


def place_kernel(members, keep_ref, *refs):
    out_ref = refs[-1]
    own, cols = refs[0].shape
    me = lax.axis_index("gx")
    row = iota((8, cols), 0)
    keep = jnp.zeros((8, cols), F32)
    for b in range(4):
        keep = jnp.where(row // 2 == b, jnp.broadcast_to(keep_ref[b : b + 1, :cols], (8, cols)), keep)
    for k in range(members):
        value = refs[members - 1 - k][...].astype(F32).reshape(own // 8, 8, cols)
        value = jnp.where((keep > 0)[None], value, 0.0).reshape(own, cols).astype(BF16)
        if cols % 128 == 0:
            out_ref[0, :, pl.ds(pl.multiple_of((me ^ k) * cols, cols), cols)] = value
        else:
            out_ref[k] = value


VM = pl.BlockSpec(memory_space=pltpu.VMEM)


def call(kernel, name, specs, out, args, scratch=(), flops=0, nbytes=0, mib=16):
    return pl.pallas_call(
        kernel,
        out_shape=out,
        in_specs=list(specs),
        out_specs=jax.tree.map(lambda _: VM, out),
        scratch_shapes=list(scratch),
        name=name,
        cost_estimate=pl.CostEstimate(flops=flops, bytes_accessed=nbytes, transcendentals=0),
        compiler_params=pltpu.CompilerParams(vmem_limit_bytes=mib * 2**20),
    )(*args)


def shape(*dims, dtype=BF16):
    return jax.ShapeDtypeStruct(dims, dtype)


def pairing(n, odd, closed):
    partner = {i: (i ^ 1 if not odd else (i + 1 if i % 2 else i - 1)) for i in range(n)}
    if closed:
        partner = {i: j % n for i, j in partner.items()}
    return {i: j for i, j in partner.items() if 0 <= j < n and i != j}


def body(features, occupancy, norm_gain, norm_shift, conv_weight, conv_bias, qkv_weight):
    sx, sy, sb, lanes = features.shape
    nx, ny, nz = (lax.axis_size(a) for a in ALL)
    devices = nx * ny * nz
    narrow = nx == 4 and ny == 2 and nz == 4
    own = sx // 2 * (sy // 4) * sb * 2
    ex = sx + 4
    row_shape = [] if narrow else [shape(devices, 128, dtype=F32)]

    slab = sy * 8 + TAIL
    keep, keys, coded, first, second, tail, *stats = call(
        functools.partial(pre_kernel, nx), "pre", (VM, VM),
        [shape(8, lanes, dtype=F32), shape(8, own * nx, dtype=F32),
         shape(sx * sy * 8, lanes), shape(slab, lanes), shape(slab, lanes), shape(TAIL, lanes)]
        + row_shape,
        (occupancy, features), nbytes=10**6,
    )
    stats = [lax.all_to_all(s, ALL, 0, 0, tiled=True) for s in stats]
    got = [
        lax.ppermute(first, "gx", list(pairing(nx, False, False).items())),
        lax.ppermute(second, "gx", list(pairing(nx, True, narrow).items())),
    ]
    tails = [tail]
    if narrow:
        tails.append(lax.ppermute(tail, "gx", [(i, i ^ 2) for i in range(nx)]))
    band = shape(3, 4 * lanes, lanes)
    pars = jnp.concatenate([norm_gain, norm_shift, conv_bias], axis=0)
    later = shape(1, *conv_weight.shape[1:])
    band0, later = call(
        band_kernel, "band0", (VM,), [band, later], (conv_weight,), nbytes=8 * 10**6,
    )
    band1, rows = call(
        band_kernel, "band1", (VM,) * 2, [band, shape(8, lanes, dtype=F32)], (later, pars),
        nbytes=8 * 10**6,
    )
    count = ex * sy
    ext, mine = call(
        functools.partial(line_kernel, narrow, sy, sb), "line", (VM,) * (4 + len(tails)),
        [shape(count * 8, lanes), shape(count + TAIL, lanes)],
        (later, coded, *got, *tails),
        [pltpu.VMEM((lanes // 128, count * 8, 128), F32)], nbytes=10**6,
    )
    core = lax.ppermute(mine, "gz", list(pairing(nz, False, False).items()))

    faces = 1 if ny == 2 else 2
    gap = corner_rows(ex)
    near, far = ex * 8 + 2 * gap + TAIL, 2 * gap + TAIL
    zface, *yfaces = call(
        functools.partial(chip_kernel, sb, sy), "chip", (VM,) * 3,
        [shape(count + TAIL, lanes)] + [shape(near, lanes), shape(far, lanes)] * faces,
        (ext, mine, core),
        [pltpu.VMEM((lanes // 128, count * 8, 128), F32),
         pltpu.VMEM((lanes // 128, count, 128), F32)], nbytes=10**6,
    )
    odd_z = pairing(nz, True, narrow)
    own_tail = zface
    zgot = lax.ppermute(zface, "gz", list(odd_z.items()))
    ygot = []
    for k in range(faces):
        along = pairing(ny, k == 1, False)
        ygot.append(lax.ppermute(yfaces[2 * k], "gy", list(along.items())))
        both = [
            (y * nz + z, along[y] * nz + odd_z[z]) for y in along for z in odd_z
        ]
        ygot.append(lax.ppermute(yfaces[2 * k + 1], ("gy", "gz"), both))

    cols, feats = qkv_weight.shape[1:]
    turned = call(
        turn_kernel, "turn", (VM,), shape(feats, 3 * cols), (qkv_weight,),
        flops=2 * 3 * cols * feats * feats, nbytes=6 * 10**6,
    )

    ey, oy = sy + 4, sy + 2
    size = (sx + 2) * oy * 8
    mid, mine = call(
        functools.partial(first_kernel, narrow, faces, sy, sb), "first",
        (VM,) * (7 + 2 * faces + len(stats)),
        [shape(size, lanes, dtype=F32), shape(devices, 128, dtype=F32)],
        (ext, own_tail, core, zgot, *ygot, *stats, keep, band0, rows),
        [pltpu.VMEM((lanes // 128, ex * ey * 8, 128), F32),
         pltpu.VMEM((ex * oy * 8, 4 * lanes), BF16),
         pltpu.VMEM((ex * ey * 8, 128), F32)],
        flops=2 * 10**9, nbytes=4 * 10**6, mib=20,
    )
    stats = lax.all_to_all(mine, ALL, 0, 0, tiled=True)
    fine_out, tokens = call(
        second_kernel, "second", (VM,) * 5,
        [shape(*features.shape), shape(own, feats)],
        (stats, mid, band1, rows, coded),
        [pltpu.VMEM(((sx + 2) * sy * 4, 4 * lanes), BF16)],
        flops=10**9, nbytes=4 * 10**6,
    )
    swaps = [[(i, i ^ k) for i in range(nx)] for k in range(nx)]
    blocks = {0: tokens}
    for k in sorted(range(1, nx), key=lambda k: (bin(k).count("1"), -k)):
        low = k & -k
        blocks[k] = lax.ppermute(blocks[k ^ low], "gx", swaps[low])
    blocks = [blocks[k] for k in range(nx)]
    outs = call(
        functools.partial(attend_kernel, nx), "attend", (VM,) * (2 + nx),
        [shape(own, cols)] * nx, (keys, turned, *blocks),
        [pltpu.VMEM((own * nx, feats), BF16), pltpu.VMEM((own * nx, 3 * cols), BF16)],
        flops=10**9, nbytes=3 * 10**6, mib=16 if narrow else 40,
    )
    moved = [lax.ppermute(v, "gx", swaps[nx - 1 - i]) for i, v in enumerate(outs[:-1])]
    outs = moved + [outs[-1]]
    lined = cols % 128 == 0
    attention = call(
        functools.partial(place_kernel, nx), "place", (VM,) * (1 + nx),
        shape(1, own, nx * cols) if lined else shape(nx, own, cols), (keep, *outs),
        nbytes=3 * 10**5, mib=8,
    )
    if not lined:
        me = lax.axis_index("gx")
        attention = jnp.concatenate(
            [lax.dynamic_index_in_dim(attention, me ^ j, 0, keepdims=False) for j in range(nx)],
            axis=1,
        )[None]
    return (fine_out, attention)


def solution(mesh):
    placed = (
        P("gx", "gy", "gz", None),
        P(None, "gy", "gz"),
        P(),
        P(),
        P(),
        P(),
        P(None, "gx", None),
    )
    return jax.shard_map(
        body,
        mesh=mesh,
        in_specs=placed,
        out_specs=(P("gx", "gy", "gz", None), P(("gy", "gz"), "gx", None)),
        check_vma=False,
    )
```

```python
import functools

import jax
import jax.numpy as jnp
from jax import lax
from jax.experimental import pallas as pl
from jax.experimental.pallas import tpu as pltpu
from jax.sharding import PartitionSpec as P

C = 32
GW = 4
HD = 64
BR = 8
EPS = 1e-05
SENT = 512.0
BIG = 1e30
ALL = ("gx", "gy", "gz")
F32, BF16 = jnp.float32, jnp.bfloat16
HIGHEST = lax.Precision.HIGHEST
TAIL = 16


def iota(shape, dim):
    return lax.broadcasted_iota(jnp.int32, shape, dim)


def onehot(cond, dtype=BF16):
    return jnp.where(cond, 1.0, 0.0).astype(dtype)


def exact_dot(a, b):
    return jnp.dot(a, b, precision=HIGHEST, preferred_element_type=F32)


def spread_sum(v):
    lane = iota(v.shape, 1)
    s = 1
    while s < GW * BR:
        v = v + jnp.where(lane & s == 0, pltpu.roll(v, 128 - s, 1), pltpu.roll(v, s, 1))
        s *= 2
    return v


def group_sum(total):
    k = total.shape[1] // 128
    rows = [jnp.broadcast_to(total[:, h * 128 : (h + 1) * 128], (8, 128)) for h in range(k)]
    out = spread_sum(jnp.concatenate(rows, axis=0))
    return jnp.concatenate([out[h * 8 : (h + 1) * 8] for h in range(k)], axis=1)


def moments(total, squares_about, count):
    sums = group_sum(total)
    squares = group_sum(squares_about((sums / count)[0:1]))
    return sums, squares, jnp.zeros(sums.shape, F32) + count


def merge(parts):
    n = sum(p[2] for p in parts)
    sums = sum(p[0] for p in parts)
    centre = sums / n
    squares = sum(p[1] + p[2] * (p[0] / p[2] - centre) ** 2 for p in parts)
    return sums, squares, n


def centre_scale(part):
    return part[0] / part[2], lax.rsqrt(part[1] / part[2] + EPS)


def to_row(part):
    j = iota((8, 128), 1) % (GW * BR)
    row = jnp.zeros((8, 128), F32)
    for h in range(2):
        for k in range(3):
            row = jnp.where(j == 4 * h + k, part[k][:, h * 128 : (h + 1) * 128], row)
    return row


def from_rows(rows):
    n = jnp.maximum(pltpu.roll(rows, 126, 1), 1.0)
    total = jnp.sum(n, axis=0, keepdims=True)
    centre = jnp.sum(rows, axis=0, keepdims=True) / total
    drift = rows / n - centre
    squares = pltpu.roll(rows, 127, 1) + n * drift * drift
    spread = jnp.sum(squares, axis=0, keepdims=True) / total
    j = iota((8, 128), 1) % (GW * BR)
    blocks = [
        jnp.where(j == 4 * h, jnp.broadcast_to(v, (8, 128)), 0.0)
        for v in (centre, spread) for h in range(2)
    ]
    out = spread_sum(jnp.concatenate(blocks, axis=0))
    out = [out[8 * i : 8 * i + 1] for i in range(4)]
    return (
        jnp.concatenate(out[:2], axis=1),
        lax.rsqrt(jnp.concatenate(out[2:], axis=1) + EPS),
    )


def to_tail(part):
    index = iota((8, 256), 0)
    blocks = [jnp.zeros((8, 256), F32), jnp.zeros((8, 256), F32)]
    for k, value in enumerate(part):
        value = jnp.broadcast_to(value[0:1], (8, 256))
        high = value.astype(BF16).astype(F32)
        mid = (value - high).astype(BF16).astype(F32)
        for i, piece in enumerate((high, mid, value - high - mid)):
            blocks[k // 2] = jnp.where(index == 3 * (k % 2) + i, piece, blocks[k // 2])
    return jnp.concatenate(blocks, axis=0).astype(BF16)


def from_tail(message_ref):
    rows = message_ref.shape[0]
    part = message_ref[rows - TAIL : rows, :].astype(F32)
    return [
        jnp.sum(part[r : r + 3], axis=0, keepdims=True) for r in (0, 3, 8)
    ]


def silu(u):
    return 0.5 * u * (1.0 + jnp.tanh(0.5 * u))


def pack_pairs(v):
    n, m, _, lanes = v.shape
    v = v.reshape(n, m // 2, 2, 8, lanes)
    low, high = v[:, :, 0].reshape(-1, 8, lanes), v[:, :, 1].reshape(-1, 8, lanes)
    both = jnp.where(iota(low.shape, 1) < 4, low, pltpu.roll(high, 4, 1))
    return both.reshape(n, m // 2, 8, lanes)


def split_pairs(v, blank):
    inside = iota(v.shape, 1) < 4
    return [jnp.where(inside, v, blank), jnp.where(inside, pltpu.roll(v, 4, 1), blank)]


def edges(act):
    z = iota(act.shape, 2) % BR
    before, after = pltpu.roll(act, 1, 1), pltpu.roll(act, 7, 1)
    return jnp.where(z == BR - 1, before, jnp.where(z == 0, after, 0.0))


def columns(act, size):
    side = edges(act)
    z = iota((size,) + act.shape[1:], 2) % BR
    second = pltpu.roll(side, 2, 2)
    third = pltpu.roll(side, 4, 2)
    mixed = jnp.where(
        (z == 1) | (z == 2), second[1 : 1 + size],
        jnp.where((z == 3) | (z == 4), third[2 : 2 + size], side[0:size]),
    )
    return [act[e : e + size] for e in range(3)] + [mixed]


def halves(lanes):
    return range(lanes // 128)


def read(ref, start, count, stride):
    return jnp.concatenate(
        [ref[h, pl.ds(start, count, stride=stride), :] for h in range(ref.shape[0])], axis=1
    )


def write(ref, start, count, stride, value):
    for h in range(ref.shape[0]):
        ref[h, pl.ds(start, count, stride=stride), :] = value[:, h * 128 : (h + 1) * 128]


def write_block(ref, start, value):
    for h in range(ref.shape[0]):
        ref[h, start : start + value.shape[0], :] = value[:, h * 128 : (h + 1) * 128]


def even(axis):
    return lax.axis_index(axis) % 2 == 0


def sides(axis, first, second):
    i, n = lax.axis_index(axis), lax.axis_size(axis)
    blank = jnp.full(first.shape, SENT, F32)
    second = blank if second is None else second
    low, high = jnp.where(even(axis), second, first), jnp.where(even(axis), first, second)
    return jnp.where(i > 0, low, SENT), jnp.where(i < n - 1, high, SENT)


def pre_kernel(members, occ_ref, feat_ref, keep_ref, keys_ref, coded_ref, first_ref, second_ref,
               tail_ref, rows_ref=None):
    sx, sy, sb, lanes = feat_ref.shape
    me = lax.axis_index("gx")
    bricks = [occ_ref[x].astype(F32) for x in range(members)]

    def row_of(x):
        return sum(jnp.where(x == i, v, 0.0) for i, v in enumerate(bricks))

    mine = jnp.broadcast_to(row_of(me), (8, sb))
    keep = jnp.where(iota((8, sb), 0) == iota((8, sb), 1), mine, 0.0)
    keep = jnp.broadcast_to(jnp.sum(keep, axis=1, keepdims=True), (8, lanes))
    count = jnp.sum(keep, axis=0, keepdims=True) * float(sx * sy * BR * GW)
    keep_ref[...] = keep
    seq = keys_ref.shape[1]
    lane = iota((1, seq), 1)
    keys = jnp.zeros((1, seq), F32)
    for k in range(members):
        there = row_of(me ^ k)
        for b in range(sb):
            keys = jnp.where(
                (lane // (seq // members) == k) & (lane % (2 * sb) // 2 == b),
                there[:, b : b + 1], keys,
            )
    keys_ref[...] = jnp.broadcast_to(keys, keys_ref.shape)
    field = feat_ref[...].astype(F32)
    wide = jnp.concatenate([field, jnp.zeros((sx, sy, 8 - sb, lanes), F32)], axis=2)
    wide = wide.reshape(sx * sy, 8, lanes)
    total = jnp.sum(jnp.sum(wide, axis=0) * keep, axis=0, keepdims=True)

    def squares_about(mean):
        d = wide - mean[None]
        return jnp.sum(jnp.sum(d * d, axis=0) * keep, axis=0, keepdims=True)

    code = jnp.where((keep > 0)[None], wide, SENT)
    coded_ref[...] = code.reshape(sx * sy * 8, lanes).astype(BF16)
    packed = pack_pairs(code.reshape(sx, sy, 8, lanes))
    low = packed[0:2].reshape(-1, lanes)
    high = packed[sx - 2 : sx].reshape(-1, lanes)
    size = low.shape[0]
    first_ref[0:size, :] = jnp.where(even("gx"), high, low).astype(BF16)
    second_ref[0:size, :] = jnp.where(even("gx"), low, high).astype(BF16)
    mine = moments(total, squares_about, count)
    tail = to_tail(mine)
    first_ref[size : size + TAIL, :] = tail
    second_ref[size : size + TAIL, :] = tail
    tail_ref[...] = tail
    if rows_ref is not None:
        rows_ref[...] = jnp.broadcast_to(to_row(mine)[0:1], rows_ref.shape)


def line_kernel(narrow, sy, sb, _, coded_ref, first_ref, second_ref, *rest):
    tails, (ext_ref, out_ref, buf) = rest[:-3], rest[-3:]
    lanes = coded_ref.shape[1]
    sx = coded_ref.shape[0] // (sy * 8)
    size = 2 * (sy // 2) * 8
    low, high = sides(
        "gx", first_ref[0:size].astype(F32), second_ref[0:size].astype(F32)
    )
    write_block(buf, 2 * sy * 8, coded_ref[...].astype(F32))
    for x0, side in ((0, low), (sx + 2, high)):
        for i in range(2):
            part = side[i * (size // 2) : (i + 1) * (size // 2)].reshape(sy // 2, 8, lanes)
            pair = split_pairs(part, SENT)
            for y in range(sy):
                write_block(buf, ((x0 + i) * sy + y) * 8, pair[y % 2][y // 2])
    rows = (sx + 4) * sy * 8
    ext_ref[...] = jnp.concatenate([buf[h] for h in halves(lanes)], axis=1).astype(BF16)
    count = (sx + 4) * sy
    face = jnp.where(even("gz"), read(buf, sb - 1, count, 8), read(buf, 0, count, 8))
    out_ref[0:count, :] = face.astype(BF16)
    mine = [from_tail(ref) for ref in tails]
    if narrow:
        mine = mine + [from_tail(first_ref), from_tail(second_ref)]
    out_ref[count : count + TAIL, :] = to_tail(merge(mine))


def corner_rows(count):
    return (count + 15) // 16 * 16


def chip_kernel(sb, sy, ext_ref, own_ref, other_ref, *rest):
    out, (buf, stage) = rest[:-2], rest[-2:]
    lanes = ext_ref.shape[1]
    ex = ext_ref.shape[0] // (sy * 8)
    block = ext_ref[...].astype(F32)
    write_block(buf, 0, block)
    write_block(stage, 0, other_ref[0 : ex * sy].astype(F32))
    gap = corner_rows(ex)
    pad = jnp.zeros((gap - ex, lanes), F32)
    tail = to_tail(merge([from_tail(own_ref), from_tail(other_ref)]))
    packed = pack_pairs(block.reshape(ex, sy, 8, lanes))

    def side(y0):
        face = packed[:, y0 // 2].reshape(ex * 8, lanes)
        inner, outer = [], []
        for i in range(2):
            inner += [read(stage, y0 + i, ex, sy), pad]
            start = (y0 + i) * 8
            outer += [
                jnp.where(
                    even("gz"),
                    read(buf, start, ex, sy * 8),
                    read(buf, start + sb - 1, ex, sy * 8),
                ),
                pad,
            ]
        return [face] + inner, outer

    (near_low, far_low), (near_high, far_high) = side(0), side(sy - 2)
    count = ex * sy
    z_face = jnp.where(even("gz"), read(buf, 0, count, 8), read(buf, sb - 1, count, 8))
    out[0][0:count, :] = z_face.astype(BF16)
    out[0][count : count + TAIL, :] = tail
    for k in range((len(out) - 1) // 2):
        up = even("gy") if k == 0 else jnp.logical_not(even("gy"))
        for ref, low, high in (
            (out[1 + 2 * k], near_low, near_high),
            (out[2 + 2 * k], far_low, far_high),
        ):
            value = jnp.where(
                up, jnp.concatenate(high, axis=0), jnp.concatenate(low, axis=0)
            ).astype(BF16)
            ref[0 : value.shape[0], :] = value
            ref[value.shape[0] : value.shape[0] + TAIL, :] = tail


def band_kernel(weight_ref, *rest):
    pars, (out_ref, more_ref) = rest[:-2], rest[-2:]
    lanes = C * BR
    spread = onehot(iota((C, lanes), 0) == iota((C, lanes), 1) // BR)
    turned = jnp.transpose(weight_ref[0].astype(F32)).astype(BF16)
    wide = jnp.dot(turned, spread, preferred_element_type=F32)
    full = (C, BR, lanes)
    zi, zo = iota((1, BR, lanes), 1), iota((1, BR, lanes), 2) % BR

    def rows(value):
        return jnp.broadcast_to(value[:, None, :], full)

    for ex in range(3):
        mixed = jnp.zeros(full, F32)
        for ey in range(3):
            q = (ex * 3 + ey) * 3
            terms = [wide[(q + e) * C : (q + e + 1) * C] for e in range(3)]
            inner = jnp.where(zi == zo - 1, rows(terms[0]), 0.0)
            inner = jnp.where(zi == zo, rows(terms[1]), inner)
            inner = jnp.where(zi == zo + 1, rows(terms[2]), inner)
            before = pltpu.roll(terms[0], 1, 0) if ey else terms[0]
            low = 2 * ey - 1 if ey else BR - 1
            mixed = jnp.where((zi == low) & (zo == 0), rows(before), mixed)
            mixed = jnp.where((zi == 2 * ey) & (zo == BR - 1), rows(terms[2]), mixed)
            out_ref[ex, ey * lanes : (ey + 1) * lanes, :] = (
                inner.reshape(C * BR, lanes).astype(BF16)
            )
        out_ref[ex, 3 * lanes : 4 * lanes, :] = mixed.reshape(C * BR, lanes).astype(BF16)
    if pars:
        pick = onehot(iota((C, lanes), 0) == iota((C, lanes), 1) // BR, F32)
        more_ref[...] = jnp.zeros(more_ref.shape, F32)
        more_ref[0 : pars[0].shape[0], :] = exact_dot(pars[0][...], pick)
    else:
        more_ref[...] = weight_ref[1:2]


def turn_kernel(weight_ref, out_ref):
    kinds, cols, feats = weight_ref.shape
    r = iota((feats, 1), 0)
    source = (r % 128) // 4 * 32 + r // 128 * 4 + r % 4
    pick = onehot(source == iota((feats, feats), 1))
    for k in range(kinds):
        out_ref[:, k * cols : (k + 1) * cols] = lax.dot_general(
            pick, weight_ref[k], (((1,), (1,)), ((), ())), preferred_element_type=F32
        ).astype(BF16)


def first_kernel(narrow, faces, sy, sb, ext_ref, own_ref, core_ref, zface_ref, *rest):
    near, far = rest[0 : 2 * faces : 2], rest[1 : 2 * faces : 2]
    rest = rest[2 * faces :]
    stats_ref = None
    if not narrow:
        stats_ref, rest = rest[0], rest[1:]
    keep_ref, weight_ref, rows_ref, mid_ref, out_ref, buf, lhs, msk = rest
    lanes = ext_ref.shape[1]
    ex = ext_ref.shape[0] // (sy * 8)
    ey = sy + 4
    count = ex * sy
    z_low, z_high = sides(
        "gz", core_ref[0:count].astype(F32), zface_ref[0:count].astype(F32)
    )
    for x in range(ex):
        write_block(
            buf, (x * ey + 2) * 8, ext_ref[x * sy * 8 : (x + 1) * sy * 8].astype(F32)
        )
        part = slice(x * sy, (x + 1) * sy)
        write(buf, (x * ey + 2) * 8 + 7, sy, 8, z_low[part])
        write(buf, (x * ey + 2) * 8 + sb, sy, 8, z_high[part])
    gap = corner_rows(ex)
    size = ex * 8
    face = sides("gy", *[
        near[k][0:size].astype(F32) if k < faces else None for k in range(2)
    ])
    inner = sides("gy", *[
        near[k][size : size + 2 * gap].astype(F32) if k < faces else None for k in range(2)
    ])
    outer = sides("gy", *[
        far[k][0 : 2 * gap].astype(F32) if k < faces else None for k in range(2)
    ])
    for s, y0 in enumerate((0, sy + 2)):
        pair = split_pairs(face[s].reshape(ex, 8, lanes), SENT)
        c_low, c_high = sides("gz", inner[s], outer[s])
        for i in range(2):
            for x in range(ex):
                write_block(buf, (x * ey + y0 + i) * 8, pair[i][x])
            write(buf, (y0 + i) * 8 + 7, ex, ey * 8, c_low[i * gap : i * gap + ex])
            write(buf, (y0 + i) * 8 + sb, ex, ey * 8, c_high[i * gap : i * gap + ex])
    if narrow:
        centre, scale = centre_scale(merge(
            [from_tail(r) for r in (own_ref, zface_ref) + tuple(near) + tuple(far)]
        ))
    else:
        centre, scale = from_rows(stats_ref[...])
    gain, shift, bias = rows_ref[0:1], rows_ref[2:3], rows_ref[4:5]
    scale = scale * gain
    oy, sx = sy + 2, ex - 4
    step = ey * 8
    for x in range(ex):
        v = jnp.concatenate(
            [buf[h, x * step : (x + 1) * step, :] for h in halves(lanes)], axis=1
        )
        there = v != SENT
        msk[x * step : (x + 1) * step] = onehot(there[:, 0:128], F32)
        act = jnp.where(there, silu((v - centre) * scale + shift), 0.0).reshape(ey, 8, lanes)
        for e, part in enumerate(columns(act, oy)):
            lhs[x * oy * 8 : (x + 1) * oy * 8, e * lanes : (e + 1) * lanes] = (
                part.reshape(oy * 8, lanes).astype(BF16)
            )
    ox = sx + 2
    size = ox * oy * 8
    acc = bias
    for e in range(3):
        acc = acc + jnp.dot(
            lhs[e * oy * 8 : e * oy * 8 + size, :], weight_ref[e], preferred_element_type=F32
        )
    mid_ref[...] = acc
    keep = keep_ref[...]
    entries = jnp.sum(keep[:, 0:1]) * float(sx * sy * BR * GW)

    def over_cells(f):
        out = jnp.zeros((8, lanes), F32)
        for x in range(1, sx + 1):
            own = mid_ref[(x * oy + 1) * 8 : (x * oy + oy - 1) * 8].reshape(sy, 8, lanes)
            out = out + jnp.sum(f(own), axis=0)
        return jnp.sum(out * keep, axis=0, keepdims=True)

    def squares_about(mean):
        return over_cells(lambda v: (v - mean[None]) * (v - mean[None]))

    mine = moments(over_cells(lambda v: v), squares_about, entries)
    out_ref[...] = jnp.broadcast_to(to_row(mine)[0:1], out_ref.shape)
    for x in range(ox):
        rows = slice(x * oy * 8, (x + 1) * oy * 8)
        there = msk[(x + 1) * step + 8 : (x + 2) * step - 8]
        there = jnp.concatenate([there] * (lanes // 128), axis=1) > 0
        mid_ref[rows] = jnp.where(there, mid_ref[rows], BIG)


def second_kernel(stats_ref, mid_ref, weight_ref, rows_ref, coded_ref, fine_ref, tok_ref, lhs):
    sx, sy, sb, lanes = fine_ref.shape
    step = (sy + 2) * 8
    centre, scale = from_rows(stats_ref[...])
    gain, shift, bias = rows_ref[1:2], rows_ref[3:4], rows_ref[5:6]
    scale = scale * gain
    half = sy // 2 * 8
    for x in range(sx + 2):
        v = mid_ref[x * step : (x + 1) * step]
        act = jnp.where(v < BIG, silu((v - centre) * scale + shift), 0.0)
        for e, part in enumerate(columns(act.reshape(sy + 2, 8, lanes), sy)):
            lhs[x * half : (x + 1) * half, e * lanes : (e + 1) * lanes] = (
                pack_pairs(part[None]).reshape(half, lanes).astype(BF16)
            )
    size = sx * half
    acc = bias
    for e in range(3):
        acc = acc + jnp.dot(
            lhs[e * half : e * half + size, :], weight_ref[e], preferred_element_type=F32
        )
    field = pack_pairs(coded_ref[...].astype(F32).reshape(sx, sy, 8, lanes))
    field = field.reshape(size, lanes)
    out = jnp.where(field != SENT, field + acc, 0.0).reshape(-1, 8, lanes)
    out = out.astype(BF16)
    wide = out.astype(F32)
    other = pltpu.roll(wide, 4, 1)
    fine = jnp.stack([wide[:, :sb], other[:, :sb]], axis=1)
    fine_ref[...] = fine.reshape(sx, sy, sb, lanes).astype(BF16)
    i, j = iota((lanes, lanes), 0), iota((lanes, lanes), 1)
    pick = onehot(i == (j % 128) // 4 * 8 + j // 128 * 4 + j % 4)
    moved = jnp.dot(out.reshape(size, lanes), pick, preferred_element_type=F32).reshape(
        sx // 2, 2, sy // 4, 2, 8, lanes
    )
    count = sx // 2 * (sy // 4)
    parts = []
    for x in range(2):
        for y in range(2):
            piece = moved[:, x, :, y].reshape(count, 8, lanes)
            low, high = piece[:, :, :128], piece[:, :, 128:]
            inside = iota(low.shape, 1) < 4
            for both in (
                jnp.where(inside, low, pltpu.roll(high, 4, 1)),
                jnp.where(inside, pltpu.roll(low, 4, 1), high),
            ):
                parts.append(both.reshape(count * 8, 128).astype(BF16))
    tokens = jnp.concatenate(parts, axis=1)
    n = count * 8
    i, j = iota((n, n), 0), iota((n, n), 1)
    order = onehot(j == i // 8 * 8 + i % 2 * 4 + i % 8 // 2)
    tok_ref[...] = jnp.dot(order, tokens, preferred_element_type=F32).astype(BF16)


def attend_kernel(members, keys_ref, weight_ref, *refs):
    tok_refs, (out_ref, toks, proj) = refs[:members], refs[members:]
    own = tok_refs[0].shape[0]
    seq = own * members
    cols = weight_ref.shape[1] // 3
    for k in range(members):
        toks[k * own : (k + 1) * own, :] = tok_refs[k][...]
    proj[...] = jnp.dot(toks[...], weight_ref[...], preferred_element_type=F32).astype(BF16)
    there = keys_ref[0:1] > 0
    me = lax.axis_index("gx")
    width = min(128, cols)
    for t in range(cols // width):
        q = proj[:, t * width : (t + 1) * width]
        keys = proj[:, cols + t * width : cols + (t + 1) * width]
        values = proj[:, 2 * cols + t * width : 2 * cols + (t + 1) * width]
        head = iota((seq, width), 1) // HD
        merged = jnp.zeros((seq, width), F32)
        for h in range(width // HD):
            mine = jnp.where(head == h, q.astype(F32), 0.0).astype(BF16)
            scores = lax.dot_general(
                mine, keys, (((1,), (1,)), ((), ())), preferred_element_type=F32
            ) * float(HD) ** (-0.5)
            scores = jnp.where(there, scores, -BIG)
            probs = jnp.exp(scores - jnp.max(scores, axis=1, keepdims=True))
            total = jnp.sum(probs, axis=1, keepdims=True)
            mixed = jnp.dot(probs.astype(BF16), values, preferred_element_type=F32)
            merged = jnp.where(head == h, mixed / total, merged)
        merged = merged.astype(BF16)
        for k in range(members):
            out_ref[me ^ k, :, t * width : (t + 1) * width] = merged[k * own : (k + 1) * own]


def place_kernel(keep_ref, got_ref, out_ref):
    members, own, cols = got_ref.shape
    row = iota((8, cols), 0)
    keep = jnp.zeros((8, cols), F32)
    for b in range(4):
        keep = jnp.where(row // 2 == b, jnp.broadcast_to(keep_ref[b : b + 1, :cols], (8, cols)), keep)
    for k in range(members):
        value = got_ref[k].astype(F32).reshape(own // 8, 8, cols)
        value = jnp.where((keep > 0)[None], value, 0.0).reshape(own, cols).astype(BF16)
        out_ref[0, :, k * cols : (k + 1) * cols] = value


VM = pl.BlockSpec(memory_space=pltpu.VMEM)


def call(kernel, name, specs, out, args, scratch=(), flops=0, nbytes=0, mib=16):
    return pl.pallas_call(
        kernel,
        out_shape=out,
        in_specs=list(specs),
        out_specs=jax.tree.map(lambda _: VM, out),
        scratch_shapes=list(scratch),
        name=name,
        cost_estimate=pl.CostEstimate(flops=flops, bytes_accessed=nbytes, transcendentals=0),
        compiler_params=pltpu.CompilerParams(vmem_limit_bytes=mib * 2**20),
    )(*args)


def shape(*dims, dtype=BF16):
    return jax.ShapeDtypeStruct(dims, dtype)


def pairing(n, odd, closed):
    partner = {i: (i ^ 1 if not odd else (i + 1 if i % 2 else i - 1)) for i in range(n)}
    if closed:
        partner = {i: j % n for i, j in partner.items()}
    return {i: j for i, j in partner.items() if 0 <= j < n and i != j}


def body(features, occupancy, norm_gain, norm_shift, conv_weight, conv_bias, qkv_weight):
    sx, sy, sb, lanes = features.shape
    nx, ny, nz = (lax.axis_size(a) for a in ALL)
    devices = nx * ny * nz
    narrow = nx == 4 and ny == 2 and nz == 4
    own = sx // 2 * (sy // 4) * sb * 2
    ex = sx + 4
    row_shape = [] if narrow else [shape(devices, 128, dtype=F32)]

    slab = sy * 8 + TAIL
    keep, keys, coded, first, second, tail, *stats = call(
        functools.partial(pre_kernel, nx), "pre", (VM, VM),
        [shape(8, lanes, dtype=F32), shape(8, own * nx, dtype=F32),
         shape(sx * sy * 8, lanes), shape(slab, lanes), shape(slab, lanes), shape(TAIL, lanes)]
        + row_shape,
        (occupancy, features), nbytes=10**6,
    )
    stats = [lax.all_to_all(s, ALL, 0, 0, tiled=True) for s in stats]
    got = [
        lax.ppermute(first, "gx", list(pairing(nx, False, False).items())),
        lax.ppermute(second, "gx", list(pairing(nx, True, narrow).items())),
    ]
    tails = [tail]
    if narrow:
        tails.append(lax.ppermute(tail, "gx", [(i, i ^ 2) for i in range(nx)]))
    band = shape(3, 4 * lanes, lanes)
    pars = jnp.concatenate([norm_gain, norm_shift, conv_bias], axis=0)
    later = shape(1, *conv_weight.shape[1:])
    band0, later = call(
        band_kernel, "band0", (VM,), [band, later], (conv_weight,), nbytes=8 * 10**6,
    )
    band1, rows = call(
        band_kernel, "band1", (VM,) * 2, [band, shape(8, lanes, dtype=F32)], (later, pars),
        nbytes=8 * 10**6,
    )
    count = ex * sy
    ext, mine = call(
        functools.partial(line_kernel, narrow, sy, sb), "line", (VM,) * (4 + len(tails)),
        [shape(count * 8, lanes), shape(count + TAIL, lanes)],
        (later, coded, *got, *tails),
        [pltpu.VMEM((lanes // 128, count * 8, 128), F32)], nbytes=10**6,
    )
    core = lax.ppermute(mine, "gz", list(pairing(nz, False, False).items()))

    faces = 1 if ny == 2 else 2
    gap = corner_rows(ex)
    near, far = ex * 8 + 2 * gap + TAIL, 2 * gap + TAIL
    zface, *yfaces = call(
        functools.partial(chip_kernel, sb, sy), "chip", (VM,) * 3,
        [shape(count + TAIL, lanes)] + [shape(near, lanes), shape(far, lanes)] * faces,
        (ext, mine, core),
        [pltpu.VMEM((lanes // 128, count * 8, 128), F32),
         pltpu.VMEM((lanes // 128, count, 128), F32)], nbytes=10**6,
    )
    odd_z = pairing(nz, True, narrow)
    own_tail = zface
    zgot = lax.ppermute(zface, "gz", list(odd_z.items()))
    ygot = []
    for k in range(faces):
        along = pairing(ny, k == 1, False)
        ygot.append(lax.ppermute(yfaces[2 * k], "gy", list(along.items())))
        both = [
            (y * nz + z, along[y] * nz + odd_z[z]) for y in along for z in odd_z
        ]
        ygot.append(lax.ppermute(yfaces[2 * k + 1], ("gy", "gz"), both))

    cols, feats = qkv_weight.shape[1:]
    turned = call(
        turn_kernel, "turn", (VM,), shape(feats, 3 * cols), (qkv_weight,),
        flops=2 * 3 * cols * feats * feats, nbytes=6 * 10**6,
    )

    ey, oy = sy + 4, sy + 2
    size = (sx + 2) * oy * 8
    mid, mine = call(
        functools.partial(first_kernel, narrow, faces, sy, sb), "first",
        (VM,) * (7 + 2 * faces + len(stats)),
        [shape(size, lanes, dtype=F32), shape(devices, 128, dtype=F32)],
        (ext, own_tail, core, zgot, *ygot, *stats, keep, band0, rows),
        [pltpu.VMEM((lanes // 128, ex * ey * 8, 128), F32),
         pltpu.VMEM((ex * oy * 8, 4 * lanes), BF16),
         pltpu.VMEM((ex * ey * 8, 128), F32)],
        flops=2 * 10**9, nbytes=4 * 10**6, mib=20,
    )
    stats = lax.all_to_all(mine, ALL, 0, 0, tiled=True)
    fine_out, tokens = call(
        second_kernel, "second", (VM,) * 5,
        [shape(*features.shape), shape(own, feats)],
        (stats, mid, band1, rows, coded),
        [pltpu.VMEM(((sx + 2) * sy * 4, 4 * lanes), BF16)],
        flops=10**9, nbytes=4 * 10**6,
    )
    swaps = [[(i, i ^ k) for i in range(nx)] for k in range(nx)]
    blocks = {0: tokens}
    for k in sorted(range(1, nx), key=lambda k: (bin(k).count("1"), -k)):
        low = k & -k
        blocks[k] = lax.ppermute(blocks[k ^ low], "gx", swaps[low])
    blocks = [blocks[k] for k in range(nx)]
    outs = call(
        functools.partial(attend_kernel, nx), "attend", (VM,) * (2 + nx),
        shape(nx, own, cols), (keys, turned, *blocks),
        [pltpu.VMEM((own * nx, feats), BF16), pltpu.VMEM((own * nx, 3 * cols), BF16)],
        flops=10**9, nbytes=3 * 10**6, mib=16 if narrow else 40,
    )
    outs = lax.all_to_all(outs, "gx", 0, 0, tiled=True)
    attention = call(
        place_kernel, "place", (VM,) * 2, shape(1, own, nx * cols), (keep, outs),
        nbytes=3 * 10**5, mib=8,
    )
    return (fine_out, attention)


def solution(mesh):
    placed = (
        P("gx", "gy", "gz", None),
        P(None, "gy", "gz"),
        P(),
        P(),
        P(),
        P(),
        P(None, "gx", None),
    )
    return jax.shard_map(
        body,
        mesh=mesh,
        in_specs=placed,
        out_specs=(P("gx", "gy", "gz", None), P(("gy", "gz"), "gx", None)),
        check_vma=False,
    )
```

```python
import functools

import jax
import jax.numpy as jnp
from jax import lax
from jax.experimental import pallas as pl
from jax.experimental.pallas import tpu as pltpu
from jax.sharding import PartitionSpec as P

C = 32
GW = 4
HD = 64
BR = 8
EPS = 1e-05
SENT = 512.0
BIG = 1e30
ALL = ("gx", "gy", "gz")
F32, BF16 = jnp.float32, jnp.bfloat16
HIGHEST = lax.Precision.HIGHEST
TAIL = 16


def iota(shape, dim):
    return lax.broadcasted_iota(jnp.int32, shape, dim)


def onehot(cond, dtype=BF16):
    return jnp.where(cond, 1.0, 0.0).astype(dtype)


def exact_dot(a, b):
    return jnp.dot(a, b, precision=HIGHEST, preferred_element_type=F32)


def spread_sum(v):
    lane = iota(v.shape, 1)
    s = 1
    while s < GW * BR:
        v = v + jnp.where(lane & s == 0, pltpu.roll(v, 128 - s, 1), pltpu.roll(v, s, 1))
        s *= 2
    return v


def group_sum(total):
    k = total.shape[1] // 128
    rows = [jnp.broadcast_to(total[:, h * 128 : (h + 1) * 128], (8, 128)) for h in range(k)]
    out = spread_sum(jnp.concatenate(rows, axis=0))
    return jnp.concatenate([out[h * 8 : (h + 1) * 8] for h in range(k)], axis=1)


def moments(total, squares_about, count):
    sums = group_sum(total)
    squares = group_sum(squares_about((sums / count)[0:1]))
    return sums, squares, jnp.zeros(sums.shape, F32) + count


def merge(parts):
    n = sum(p[2] for p in parts)
    sums = sum(p[0] for p in parts)
    centre = sums / n
    squares = sum(p[1] + p[2] * (p[0] / p[2] - centre) ** 2 for p in parts)
    return sums, squares, n


def centre_scale(part):
    return part[0] / part[2], lax.rsqrt(part[1] / part[2] + EPS)


def to_row(part):
    j = iota((8, 128), 1) % (GW * BR)
    row = jnp.zeros((8, 128), F32)
    for h in range(2):
        for k in range(3):
            row = jnp.where(j == 4 * h + k, part[k][:, h * 128 : (h + 1) * 128], row)
    return row


def from_rows(rows):
    n = jnp.maximum(pltpu.roll(rows, 126, 1), 1.0)
    total = jnp.sum(n, axis=0, keepdims=True)
    centre = jnp.sum(rows, axis=0, keepdims=True) / total
    drift = rows / n - centre
    squares = pltpu.roll(rows, 127, 1) + n * drift * drift
    spread = jnp.sum(squares, axis=0, keepdims=True) / total
    j = iota((8, 128), 1) % (GW * BR)
    blocks = [
        jnp.where(j == 4 * h, jnp.broadcast_to(v, (8, 128)), 0.0)
        for v in (centre, spread) for h in range(2)
    ]
    out = spread_sum(jnp.concatenate(blocks, axis=0))
    out = [out[8 * i : 8 * i + 1] for i in range(4)]
    return (
        jnp.concatenate(out[:2], axis=1),
        lax.rsqrt(jnp.concatenate(out[2:], axis=1) + EPS),
    )


def to_tail(part):
    index = iota((8, 256), 0)
    blocks = [jnp.zeros((8, 256), F32), jnp.zeros((8, 256), F32)]
    for k, value in enumerate(part):
        value = jnp.broadcast_to(value[0:1], (8, 256))
        high = value.astype(BF16).astype(F32)
        mid = (value - high).astype(BF16).astype(F32)
        for i, piece in enumerate((high, mid, value - high - mid)):
            blocks[k // 2] = jnp.where(index == 3 * (k % 2) + i, piece, blocks[k // 2])
    return jnp.concatenate(blocks, axis=0).astype(BF16)


def from_tail(message_ref):
    rows = message_ref.shape[0]
    part = message_ref[rows - TAIL : rows, :].astype(F32)
    return [
        jnp.sum(part[r : r + 3], axis=0, keepdims=True) for r in (0, 3, 8)
    ]


def silu(u):
    return 0.5 * u * (1.0 + jnp.tanh(0.5 * u))


def pack_pairs(v):
    n, m, _, lanes = v.shape
    v = v.reshape(n, m // 2, 2, 8, lanes)
    low, high = v[:, :, 0].reshape(-1, 8, lanes), v[:, :, 1].reshape(-1, 8, lanes)
    both = jnp.where(iota(low.shape, 1) < 4, low, pltpu.roll(high, 4, 1))
    return both.reshape(n, m // 2, 8, lanes)


def split_pairs(v, blank):
    inside = iota(v.shape, 1) < 4
    return [jnp.where(inside, v, blank), jnp.where(inside, pltpu.roll(v, 4, 1), blank)]


def edges(act):
    z = iota(act.shape, 2) % BR
    before, after = pltpu.roll(act, 1, 1), pltpu.roll(act, 7, 1)
    return jnp.where(z == BR - 1, before, jnp.where(z == 0, after, 0.0))


def columns(act, size):
    side = edges(act)
    z = iota((size,) + act.shape[1:], 2) % BR
    second = pltpu.roll(side, 2, 2)
    third = pltpu.roll(side, 4, 2)
    mixed = jnp.where(
        (z == 1) | (z == 2), second[1 : 1 + size],
        jnp.where((z == 3) | (z == 4), third[2 : 2 + size], side[0:size]),
    )
    return [act[e : e + size] for e in range(3)] + [mixed]


def halves(lanes):
    return range(lanes // 128)


def read(ref, start, count, stride):
    return jnp.concatenate(
        [ref[h, pl.ds(start, count, stride=stride), :] for h in range(ref.shape[0])], axis=1
    )


def write(ref, start, count, stride, value):
    for h in range(ref.shape[0]):
        ref[h, pl.ds(start, count, stride=stride), :] = value[:, h * 128 : (h + 1) * 128]


def write_block(ref, start, value):
    for h in range(ref.shape[0]):
        ref[h, start : start + value.shape[0], :] = value[:, h * 128 : (h + 1) * 128]


def even(axis):
    return lax.axis_index(axis) % 2 == 0


def sides(axis, first, second):
    i, n = lax.axis_index(axis), lax.axis_size(axis)
    blank = jnp.full(first.shape, SENT, F32)
    second = blank if second is None else second
    low, high = jnp.where(even(axis), second, first), jnp.where(even(axis), first, second)
    return jnp.where(i > 0, low, SENT), jnp.where(i < n - 1, high, SENT)


def pre_kernel(members, occ_ref, feat_ref, keep_ref, keys_ref, coded_ref, first_ref, second_ref,
               tail_ref, rows_ref=None):
    sx, sy, sb, lanes = feat_ref.shape
    me = lax.axis_index("gx")
    bricks = [occ_ref[x].astype(F32) for x in range(members)]

    def row_of(x):
        return sum(jnp.where(x == i, v, 0.0) for i, v in enumerate(bricks))

    mine = jnp.broadcast_to(row_of(me), (8, sb))
    keep = jnp.where(iota((8, sb), 0) == iota((8, sb), 1), mine, 0.0)
    keep = jnp.broadcast_to(jnp.sum(keep, axis=1, keepdims=True), (8, lanes))
    count = jnp.sum(keep, axis=0, keepdims=True) * float(sx * sy * BR * GW)
    keep_ref[...] = keep
    seq = keys_ref.shape[1]
    lane = iota((1, seq), 1)
    keys = jnp.zeros((1, seq), F32)
    for k in range(members):
        there = row_of(me ^ k)
        for b in range(sb):
            keys = jnp.where(
                (lane // (seq // members) == k) & (lane % (2 * sb) // 2 == b),
                there[:, b : b + 1], keys,
            )
    keys_ref[...] = jnp.broadcast_to(keys, keys_ref.shape)
    field = feat_ref[...].astype(F32)
    wide = jnp.concatenate([field, jnp.zeros((sx, sy, 8 - sb, lanes), F32)], axis=2)
    wide = wide.reshape(sx * sy, 8, lanes)
    total = jnp.sum(jnp.sum(wide, axis=0) * keep, axis=0, keepdims=True)

    def squares_about(mean):
        d = wide - mean[None]
        return jnp.sum(jnp.sum(d * d, axis=0) * keep, axis=0, keepdims=True)

    code = jnp.where((keep > 0)[None], wide, SENT)
    coded_ref[...] = code.reshape(sx * sy * 8, lanes).astype(BF16)
    packed = pack_pairs(code.reshape(sx, sy, 8, lanes))
    low = packed[0:2].reshape(-1, lanes)
    high = packed[sx - 2 : sx].reshape(-1, lanes)
    size = low.shape[0]
    first_ref[0:size, :] = jnp.where(even("gx"), high, low).astype(BF16)
    second_ref[0:size, :] = jnp.where(even("gx"), low, high).astype(BF16)
    mine = moments(total, squares_about, count)
    tail = to_tail(mine)
    first_ref[size : size + TAIL, :] = tail
    second_ref[size : size + TAIL, :] = tail
    tail_ref[...] = tail
    if rows_ref is not None:
        rows_ref[...] = jnp.broadcast_to(to_row(mine)[0:1], rows_ref.shape)


def line_kernel(narrow, sy, sb, _, coded_ref, first_ref, second_ref, *rest):
    tails, (ext_ref, out_ref, buf) = rest[:-3], rest[-3:]
    lanes = coded_ref.shape[1]
    sx = coded_ref.shape[0] // (sy * 8)
    size = 2 * (sy // 2) * 8
    low, high = sides(
        "gx", first_ref[0:size].astype(F32), second_ref[0:size].astype(F32)
    )
    write_block(buf, 2 * sy * 8, coded_ref[...].astype(F32))
    for x0, side in ((0, low), (sx + 2, high)):
        for i in range(2):
            part = side[i * (size // 2) : (i + 1) * (size // 2)].reshape(sy // 2, 8, lanes)
            pair = split_pairs(part, SENT)
            for y in range(sy):
                write_block(buf, ((x0 + i) * sy + y) * 8, pair[y % 2][y // 2])
    rows = (sx + 4) * sy * 8
    ext_ref[...] = jnp.concatenate([buf[h] for h in halves(lanes)], axis=1).astype(BF16)
    count = (sx + 4) * sy
    face = jnp.where(even("gz"), read(buf, sb - 1, count, 8), read(buf, 0, count, 8))
    out_ref[0:count, :] = face.astype(BF16)
    mine = [from_tail(ref) for ref in tails]
    if narrow:
        mine = mine + [from_tail(first_ref), from_tail(second_ref)]
    out_ref[count : count + TAIL, :] = to_tail(merge(mine))


def corner_rows(count):
    return (count + 15) // 16 * 16


def chip_kernel(sb, sy, ext_ref, own_ref, other_ref, *rest):
    out, (buf, stage) = rest[:-2], rest[-2:]
    lanes = ext_ref.shape[1]
    ex = ext_ref.shape[0] // (sy * 8)
    block = ext_ref[...].astype(F32)
    write_block(buf, 0, block)
    write_block(stage, 0, other_ref[0 : ex * sy].astype(F32))
    gap = corner_rows(ex)
    pad = jnp.zeros((gap - ex, lanes), F32)
    tail = to_tail(merge([from_tail(own_ref), from_tail(other_ref)]))
    packed = pack_pairs(block.reshape(ex, sy, 8, lanes))

    def side(y0):
        face = packed[:, y0 // 2].reshape(ex * 8, lanes)
        inner, outer = [], []
        for i in range(2):
            inner += [read(stage, y0 + i, ex, sy), pad]
            start = (y0 + i) * 8
            outer += [
                jnp.where(
                    even("gz"),
                    read(buf, start, ex, sy * 8),
                    read(buf, start + sb - 1, ex, sy * 8),
                ),
                pad,
            ]
        return [face] + inner, outer

    (near_low, far_low), (near_high, far_high) = side(0), side(sy - 2)
    count = ex * sy
    z_face = jnp.where(even("gz"), read(buf, 0, count, 8), read(buf, sb - 1, count, 8))
    out[0][0:count, :] = z_face.astype(BF16)
    out[0][count : count + TAIL, :] = tail
    for k in range((len(out) - 1) // 2):
        up = even("gy") if k == 0 else jnp.logical_not(even("gy"))
        for ref, low, high in (
            (out[1 + 2 * k], near_low, near_high),
            (out[2 + 2 * k], far_low, far_high),
        ):
            value = jnp.where(
                up, jnp.concatenate(high, axis=0), jnp.concatenate(low, axis=0)
            ).astype(BF16)
            ref[0 : value.shape[0], :] = value
            ref[value.shape[0] : value.shape[0] + TAIL, :] = tail


def band_kernel(weight_ref, *rest):
    pars, (out_ref, more_ref) = rest[:-2], rest[-2:]
    lanes = C * BR
    spread = onehot(iota((C, lanes), 0) == iota((C, lanes), 1) // BR)
    turned = jnp.transpose(weight_ref[0].astype(F32)).astype(BF16)
    wide = jnp.dot(turned, spread, preferred_element_type=F32)
    full = (C, BR, lanes)
    zi, zo = iota((1, BR, lanes), 1), iota((1, BR, lanes), 2) % BR

    def rows(value):
        return jnp.broadcast_to(value[:, None, :], full)

    for ex in range(3):
        mixed = jnp.zeros(full, F32)
        for ey in range(3):
            q = (ex * 3 + ey) * 3
            terms = [wide[(q + e) * C : (q + e + 1) * C] for e in range(3)]
            inner = jnp.where(zi == zo - 1, rows(terms[0]), 0.0)
            inner = jnp.where(zi == zo, rows(terms[1]), inner)
            inner = jnp.where(zi == zo + 1, rows(terms[2]), inner)
            before = pltpu.roll(terms[0], 1, 0) if ey else terms[0]
            low = 2 * ey - 1 if ey else BR - 1
            mixed = jnp.where((zi == low) & (zo == 0), rows(before), mixed)
            mixed = jnp.where((zi == 2 * ey) & (zo == BR - 1), rows(terms[2]), mixed)
            out_ref[ex, ey * lanes : (ey + 1) * lanes, :] = (
                inner.reshape(C * BR, lanes).astype(BF16)
            )
        out_ref[ex, 3 * lanes : 4 * lanes, :] = mixed.reshape(C * BR, lanes).astype(BF16)
    if pars:
        pick = onehot(iota((C, lanes), 0) == iota((C, lanes), 1) // BR, F32)
        more_ref[...] = jnp.zeros(more_ref.shape, F32)
        more_ref[0 : pars[0].shape[0], :] = exact_dot(pars[0][...], pick)
    else:
        more_ref[...] = weight_ref[1:2]


def turn_kernel(weight_ref, out_ref):
    kinds, cols, feats = weight_ref.shape
    r = iota((feats, 1), 0)
    source = (r % 128) // 4 * 32 + r // 128 * 4 + r % 4
    pick = onehot(source == iota((feats, feats), 1))
    for k in range(kinds):
        out_ref[:, k * cols : (k + 1) * cols] = lax.dot_general(
            pick, weight_ref[k], (((1,), (1,)), ((), ())), preferred_element_type=F32
        ).astype(BF16)


def first_kernel(narrow, faces, sy, sb, ext_ref, own_ref, core_ref, zface_ref, *rest):
    near, far = rest[0 : 2 * faces : 2], rest[1 : 2 * faces : 2]
    rest = rest[2 * faces :]
    stats_ref = None
    if not narrow:
        stats_ref, rest = rest[0], rest[1:]
    keep_ref, weight_ref, rows_ref, mid_ref, out_ref, msk, buf, lhs = rest
    lanes = ext_ref.shape[1]
    ex = ext_ref.shape[0] // (sy * 8)
    ey = sy + 4
    count = ex * sy
    z_low, z_high = sides(
        "gz", core_ref[0:count].astype(F32), zface_ref[0:count].astype(F32)
    )
    for x in range(ex):
        write_block(
            buf, (x * ey + 2) * 8, ext_ref[x * sy * 8 : (x + 1) * sy * 8].astype(F32)
        )
        part = slice(x * sy, (x + 1) * sy)
        write(buf, (x * ey + 2) * 8 + 7, sy, 8, z_low[part])
        write(buf, (x * ey + 2) * 8 + sb, sy, 8, z_high[part])
    gap = corner_rows(ex)
    size = ex * 8
    face = sides("gy", *[
        near[k][0:size].astype(F32) if k < faces else None for k in range(2)
    ])
    inner = sides("gy", *[
        near[k][size : size + 2 * gap].astype(F32) if k < faces else None for k in range(2)
    ])
    outer = sides("gy", *[
        far[k][0 : 2 * gap].astype(F32) if k < faces else None for k in range(2)
    ])
    for s, y0 in enumerate((0, sy + 2)):
        pair = split_pairs(face[s].reshape(ex, 8, lanes), SENT)
        c_low, c_high = sides("gz", inner[s], outer[s])
        for i in range(2):
            for x in range(ex):
                write_block(buf, (x * ey + y0 + i) * 8, pair[i][x])
            write(buf, (y0 + i) * 8 + 7, ex, ey * 8, c_low[i * gap : i * gap + ex])
            write(buf, (y0 + i) * 8 + sb, ex, ey * 8, c_high[i * gap : i * gap + ex])
    if narrow:
        centre, scale = centre_scale(merge(
            [from_tail(r) for r in (own_ref, zface_ref) + tuple(near) + tuple(far)]
        ))
    else:
        centre, scale = from_rows(stats_ref[...])
    gain, shift, bias = rows_ref[0:1], rows_ref[2:3], rows_ref[4:5]
    scale = scale * gain
    oy, sx = sy + 2, ex - 4
    step = ey * 8
    for x in range(ex):
        v = jnp.concatenate(
            [buf[h, x * step : (x + 1) * step, :] for h in halves(lanes)], axis=1
        )
        there = v != SENT
        msk[x * step : (x + 1) * step] = onehot(there[:, 0:128], F32)
        act = jnp.where(there, silu((v - centre) * scale + shift), 0.0).reshape(ey, 8, lanes)
        for e, part in enumerate(columns(act, oy)):
            lhs[x * oy * 8 : (x + 1) * oy * 8, e * lanes : (e + 1) * lanes] = (
                part.reshape(oy * 8, lanes).astype(BF16)
            )
    ox = sx + 2
    size = ox * oy * 8
    acc = bias
    for e in range(3):
        acc = acc + jnp.dot(
            lhs[e * oy * 8 : e * oy * 8 + size, :], weight_ref[e], preferred_element_type=F32
        )
    mid_ref[...] = acc
    keep = keep_ref[...]
    entries = jnp.sum(keep[:, 0:1]) * float(sx * sy * BR * GW)

    def over_cells(f):
        out = jnp.zeros((8, lanes), F32)
        for x in range(1, sx + 1):
            own = mid_ref[(x * oy + 1) * 8 : (x * oy + oy - 1) * 8].reshape(sy, 8, lanes)
            out = out + jnp.sum(f(own), axis=0)
        return jnp.sum(out * keep, axis=0, keepdims=True)

    def squares_about(mean):
        return over_cells(lambda v: (v - mean[None]) * (v - mean[None]))

    mine = moments(over_cells(lambda v: v), squares_about, entries)
    out_ref[...] = jnp.broadcast_to(to_row(mine)[0:1], out_ref.shape)


def second_kernel(sx, sy, sb, stats_ref, mid_ref, msk_ref, weight_ref, rows_ref, coded_ref,
                  field_ref, tok_ref, lhs):
    lanes = coded_ref.shape[1]
    step, ext = (sy + 2) * 8, (sy + 4) * 8
    centre, scale = from_rows(stats_ref[...])
    gain, shift, bias = rows_ref[1:2], rows_ref[3:4], rows_ref[5:6]
    scale = scale * gain
    half = sy // 2 * 8
    for x in range(sx + 2):
        v = mid_ref[x * step : (x + 1) * step]
        there = msk_ref[(x + 1) * ext + 8 : (x + 2) * ext - 8]
        there = jnp.concatenate([there] * (lanes // 128), axis=1) > 0
        act = jnp.where(there, silu((v - centre) * scale + shift), 0.0)
        for e, part in enumerate(columns(act.reshape(sy + 2, 8, lanes), sy)):
            lhs[x * half : (x + 1) * half, e * lanes : (e + 1) * lanes] = (
                pack_pairs(part[None]).reshape(half, lanes).astype(BF16)
            )
    size = sx * half
    acc = bias
    for e in range(3):
        acc = acc + jnp.dot(
            lhs[e * half : e * half + size, :], weight_ref[e], preferred_element_type=F32
        )
    field = pack_pairs(coded_ref[...].astype(F32).reshape(sx, sy, 8, lanes))
    field = field.reshape(size, lanes)
    out = jnp.where(field != SENT, field + acc, 0.0).reshape(-1, 8, lanes)
    out = out.astype(BF16)
    field_ref[...] = out.reshape(size, lanes)
    i, j = iota((lanes, lanes), 0), iota((lanes, lanes), 1)
    pick = onehot(i == (j % 128) // 4 * 8 + j // 128 * 4 + j % 4)
    moved = jnp.dot(out.reshape(size, lanes), pick, preferred_element_type=F32).reshape(
        sx // 2, 2, sy // 4, 2, 8, lanes
    )
    count = sx // 2 * (sy // 4)
    parts = []
    for x in range(2):
        for y in range(2):
            piece = moved[:, x, :, y].reshape(count, 8, lanes)
            low, high = piece[:, :, :128], piece[:, :, 128:]
            inside = iota(low.shape, 1) < 4
            for both in (
                jnp.where(inside, low, pltpu.roll(high, 4, 1)),
                jnp.where(inside, pltpu.roll(low, 4, 1), high),
            ):
                parts.append(both.reshape(count * 8, 128).astype(BF16))
    tokens = jnp.concatenate(parts, axis=1)
    n = count * 8
    i, j = iota((n, n), 0), iota((n, n), 1)
    order = onehot(j == i // 8 * 8 + i % 2 * 4 + i % 8 // 2)
    tok_ref[...] = jnp.dot(order, tokens, preferred_element_type=F32).astype(BF16)


def fine_kernel(field_ref, fine_ref):
    sx, sy, sb, lanes = fine_ref.shape
    wide = field_ref[...].astype(F32).reshape(-1, 8, lanes)
    other = pltpu.roll(wide, 4, 1)
    fine = jnp.stack([wide[:, :sb], other[:, :sb]], axis=1)
    fine_ref[...] = fine.reshape(sx, sy, sb, lanes).astype(BF16)


def attend_kernel(members, keys_ref, weight_ref, *refs):
    tok_refs, out_refs, (toks, proj) = refs[:members], refs[members : 2 * members], refs[-2:]
    own = tok_refs[0].shape[0]
    seq = own * members
    cols = weight_ref.shape[1] // 3
    for k in range(members):
        toks[k * own : (k + 1) * own, :] = tok_refs[k][...]
    proj[...] = jnp.dot(toks[...], weight_ref[...], preferred_element_type=F32).astype(BF16)
    there = keys_ref[0:1] > 0
    width = min(128, cols)
    for t in range(cols // width):
        q = proj[:, t * width : (t + 1) * width]
        keys = proj[:, cols + t * width : cols + (t + 1) * width]
        values = proj[:, 2 * cols + t * width : 2 * cols + (t + 1) * width]
        head = iota((seq, width), 1) // HD
        merged = jnp.zeros((seq, width), F32)
        for h in range(width // HD):
            mine = jnp.where(head == h, q.astype(F32), 0.0).astype(BF16)
            scores = lax.dot_general(
                mine, keys, (((1,), (1,)), ((), ())), preferred_element_type=F32
            ) * float(HD) ** (-0.5)
            scores = jnp.where(there, scores, -BIG)
            probs = jnp.exp(scores - jnp.max(scores, axis=1, keepdims=True))
            total = jnp.sum(probs, axis=1, keepdims=True)
            mixed = jnp.dot(probs.astype(BF16), values, preferred_element_type=F32)
            merged = jnp.where(head == h, mixed / total, merged)
        merged = merged.astype(BF16)
        for k in range(members):
            out_refs[-1 - k][:, t * width : (t + 1) * width] = merged[k * own : (k + 1) * own]


def place_kernel(members, keep_ref, *refs):
    out_ref = refs[-1]
    own, cols = refs[0].shape
    me = lax.axis_index("gx")
    row = iota((8, cols), 0)
    keep = jnp.zeros((8, cols), F32)
    for b in range(4):
        keep = jnp.where(row // 2 == b, jnp.broadcast_to(keep_ref[b : b + 1, :cols], (8, cols)), keep)
    for k in range(members):
        value = refs[members - 1 - k][...].astype(F32).reshape(own // 8, 8, cols)
        value = jnp.where((keep > 0)[None], value, 0.0).reshape(own, cols).astype(BF16)
        if cols % 128 == 0:
            out_ref[0, :, pl.ds(pl.multiple_of((me ^ k) * cols, cols), cols)] = value
        else:
            out_ref[k] = value


VM = pl.BlockSpec(memory_space=pltpu.VMEM)


def call(kernel, name, specs, out, args, scratch=(), flops=0, nbytes=0, mib=16):
    return pl.pallas_call(
        kernel,
        out_shape=out,
        in_specs=list(specs),
        out_specs=jax.tree.map(lambda _: VM, out),
        scratch_shapes=list(scratch),
        name=name,
        cost_estimate=pl.CostEstimate(flops=flops, bytes_accessed=nbytes, transcendentals=0),
        compiler_params=pltpu.CompilerParams(vmem_limit_bytes=mib * 2**20),
    )(*args)


def shape(*dims, dtype=BF16):
    return jax.ShapeDtypeStruct(dims, dtype)


def pairing(n, odd, closed):
    partner = {i: (i ^ 1 if not odd else (i + 1 if i % 2 else i - 1)) for i in range(n)}
    if closed:
        partner = {i: j % n for i, j in partner.items()}
    return {i: j for i, j in partner.items() if 0 <= j < n and i != j}


def body(features, occupancy, norm_gain, norm_shift, conv_weight, conv_bias, qkv_weight):
    sx, sy, sb, lanes = features.shape
    nx, ny, nz = (lax.axis_size(a) for a in ALL)
    devices = nx * ny * nz
    narrow = nx == 4 and ny == 2 and nz == 4
    own = sx // 2 * (sy // 4) * sb * 2
    ex = sx + 4
    row_shape = [] if narrow else [shape(devices, 128, dtype=F32)]

    slab = sy * 8 + TAIL
    keep, keys, coded, first, second, tail, *stats = call(
        functools.partial(pre_kernel, nx), "pre", (VM, VM),
        [shape(8, lanes, dtype=F32), shape(8, own * nx, dtype=F32),
         shape(sx * sy * 8, lanes), shape(slab, lanes), shape(slab, lanes), shape(TAIL, lanes)]
        + row_shape,
        (occupancy, features), nbytes=10**6,
    )
    stats = [lax.all_to_all(s, ALL, 0, 0, tiled=True) for s in stats]
    got = [
        lax.ppermute(first, "gx", list(pairing(nx, False, False).items())),
        lax.ppermute(second, "gx", list(pairing(nx, True, narrow).items())),
    ]
    tails = [tail]
    if narrow:
        tails.append(lax.ppermute(tail, "gx", [(i, i ^ 2) for i in range(nx)]))
    band = shape(3, 4 * lanes, lanes)
    pars = jnp.concatenate([norm_gain, norm_shift, conv_bias], axis=0)
    later = shape(1, *conv_weight.shape[1:])
    band0, later = call(
        band_kernel, "band0", (VM,), [band, later], (conv_weight,), nbytes=8 * 10**6,
    )
    band1, rows = call(
        band_kernel, "band1", (VM,) * 2, [band, shape(8, lanes, dtype=F32)], (later, pars),
        nbytes=8 * 10**6,
    )
    count = ex * sy
    ext, mine = call(
        functools.partial(line_kernel, narrow, sy, sb), "line", (VM,) * (4 + len(tails)),
        [shape(count * 8, lanes), shape(count + TAIL, lanes)],
        (later, coded, *got, *tails),
        [pltpu.VMEM((lanes // 128, count * 8, 128), F32)], nbytes=10**6,
    )
    core = lax.ppermute(mine, "gz", list(pairing(nz, False, False).items()))

    faces = 1 if ny == 2 else 2
    gap = corner_rows(ex)
    near, far = ex * 8 + 2 * gap + TAIL, 2 * gap + TAIL
    zface, *yfaces = call(
        functools.partial(chip_kernel, sb, sy), "chip", (VM,) * 3,
        [shape(count + TAIL, lanes)] + [shape(near, lanes), shape(far, lanes)] * faces,
        (ext, mine, core),
        [pltpu.VMEM((lanes // 128, count * 8, 128), F32),
         pltpu.VMEM((lanes // 128, count, 128), F32)], nbytes=10**6,
    )
    odd_z = pairing(nz, True, narrow)
    own_tail = zface
    zgot = lax.ppermute(zface, "gz", list(odd_z.items()))
    ygot = []
    for k in range(faces):
        along = pairing(ny, k == 1, False)
        ygot.append(lax.ppermute(yfaces[2 * k], "gy", list(along.items())))
        both = [
            (y * nz + z, along[y] * nz + odd_z[z]) for y in along for z in odd_z
        ]
        ygot.append(lax.ppermute(yfaces[2 * k + 1], ("gy", "gz"), both))

    cols, feats = qkv_weight.shape[1:]
    turned = call(
        turn_kernel, "turn", (VM,), shape(feats, 3 * cols), (qkv_weight,),
        flops=2 * 3 * cols * feats * feats, nbytes=6 * 10**6,
    )

    ey, oy = sy + 4, sy + 2
    size = (sx + 2) * oy * 8
    mid, mine, there = call(
        functools.partial(first_kernel, narrow, faces, sy, sb), "first",
        (VM,) * (7 + 2 * faces + len(stats)),
        [shape(size, lanes, dtype=F32), shape(devices, 128, dtype=F32),
         shape(ex * ey * 8, 128, dtype=F32)],
        (ext, own_tail, core, zgot, *ygot, *stats, keep, band0, rows),
        [pltpu.VMEM((lanes // 128, ex * ey * 8, 128), F32),
         pltpu.VMEM((ex * oy * 8, 4 * lanes), BF16)],
        flops=2 * 10**9, nbytes=4 * 10**6, mib=20,
    )
    stats = lax.all_to_all(mine, ALL, 0, 0, tiled=True)
    field, tokens = call(
        functools.partial(second_kernel, sx, sy, sb), "second", (VM,) * 6,
        [shape(sx * sy * 4, lanes), shape(own, feats)],
        (stats, mid, there, band1, rows, coded),
        [pltpu.VMEM(((sx + 2) * sy * 4, 4 * lanes), BF16)],
        flops=10**9, nbytes=4 * 10**6,
    )
    fine_out = call(
        fine_kernel, "fine", (VM,), shape(*features.shape), (field,), nbytes=4 * 10**6, mib=8,
    )
    swaps = [[(i, i ^ k) for i in range(nx)] for k in range(nx)]
    blocks = {0: tokens}
    for k in sorted(range(1, nx), key=lambda k: (bin(k).count("1"), -k)):
        low = k & -k
        blocks[k] = lax.ppermute(blocks[k ^ low], "gx", swaps[low])
    blocks = [blocks[k] for k in range(nx)]
    outs = call(
        functools.partial(attend_kernel, nx), "attend", (VM,) * (2 + nx),
        [shape(own, cols)] * nx, (keys, turned, *blocks),
        [pltpu.VMEM((own * nx, feats), BF16), pltpu.VMEM((own * nx, 3 * cols), BF16)],
        flops=10**9, nbytes=3 * 10**6, mib=16 if narrow else 40,
    )
    moved = [lax.ppermute(v, "gx", swaps[nx - 1 - i]) for i, v in enumerate(outs[:-1])]
    outs = moved + [outs[-1]]
    lined = cols % 128 == 0
    attention = call(
        functools.partial(place_kernel, nx), "place", (VM,) * (1 + nx),
        shape(1, own, nx * cols) if lined else shape(nx, own, cols), (keep, *outs),
        nbytes=3 * 10**5, mib=8,
    )
    if not lined:
        me = lax.axis_index("gx")
        attention = jnp.concatenate(
            [lax.dynamic_index_in_dim(attention, me ^ j, 0, keepdims=False) for j in range(nx)],
            axis=1,
        )[None]
    return (fine_out, attention)


def solution(mesh):
    placed = (
        P("gx", "gy", "gz", None),
        P(None, "gy", "gz"),
        P(),
        P(),
        P(),
        P(),
        P(None, "gx", None),
    )
    return jax.shard_map(
        body,
        mesh=mesh,
        in_specs=placed,
        out_specs=(P("gx", "gy", "gz", None), P(("gy", "gz"), "gx", None)),
        check_vma=False,
    )
```

```python
import functools

import jax
import jax.numpy as jnp
from jax import lax
from jax.experimental import pallas as pl
from jax.experimental.pallas import tpu as pltpu
from jax.sharding import PartitionSpec as P

C = 32
GW = 4
HD = 64
BR = 8
EPS = 1e-05
SENT = 512.0
BIG = 1e30
ALL = ("gx", "gy", "gz")
F32, BF16 = jnp.float32, jnp.bfloat16
HIGHEST = lax.Precision.HIGHEST
TAIL = 16


def iota(shape, dim):
    return lax.broadcasted_iota(jnp.int32, shape, dim)


def onehot(cond, dtype=BF16):
    return jnp.where(cond, 1.0, 0.0).astype(dtype)


def exact_dot(a, b):
    return jnp.dot(a, b, precision=HIGHEST, preferred_element_type=F32)


def spread_sum(v):
    lane = iota(v.shape, 1)
    s = 1
    while s < GW * BR:
        v = v + jnp.where(lane & s == 0, pltpu.roll(v, 128 - s, 1), pltpu.roll(v, s, 1))
        s *= 2
    return v


def group_sum(total):
    k = total.shape[1] // 128
    rows = [jnp.broadcast_to(total[:, h * 128 : (h + 1) * 128], (8, 128)) for h in range(k)]
    out = spread_sum(jnp.concatenate(rows, axis=0))
    return jnp.concatenate([out[h * 8 : (h + 1) * 8] for h in range(k)], axis=1)


def moments(total, squares_about, count):
    sums = group_sum(total)
    squares = group_sum(squares_about((sums / count)[0:1]))
    return sums, squares, jnp.zeros(sums.shape, F32) + count


def merge(parts):
    n = sum(p[2] for p in parts)
    sums = sum(p[0] for p in parts)
    centre = sums / n
    squares = sum(p[1] + p[2] * (p[0] / p[2] - centre) ** 2 for p in parts)
    return sums, squares, n


def centre_scale(part):
    return part[0] / part[2], lax.rsqrt(part[1] / part[2] + EPS)


def to_row(part):
    j = iota((8, 128), 1) % (GW * BR)
    row = jnp.zeros((8, 128), F32)
    for h in range(2):
        for k in range(3):
            row = jnp.where(j == 4 * h + k, part[k][:, h * 128 : (h + 1) * 128], row)
    return row


def from_rows(rows):
    n = jnp.maximum(pltpu.roll(rows, 126, 1), 1.0)
    total = jnp.sum(n, axis=0, keepdims=True)
    centre = jnp.sum(rows, axis=0, keepdims=True) / total
    drift = rows / n - centre
    squares = pltpu.roll(rows, 127, 1) + n * drift * drift
    spread = jnp.sum(squares, axis=0, keepdims=True) / total
    j = iota((8, 128), 1) % (GW * BR)
    blocks = [
        jnp.where(j == 4 * h, jnp.broadcast_to(v, (8, 128)), 0.0)
        for v in (centre, spread) for h in range(2)
    ]
    out = spread_sum(jnp.concatenate(blocks, axis=0))
    out = [out[8 * i : 8 * i + 1] for i in range(4)]
    return (
        jnp.concatenate(out[:2], axis=1),
        lax.rsqrt(jnp.concatenate(out[2:], axis=1) + EPS),
    )


def to_tail(part):
    index = iota((8, 256), 0)
    blocks = [jnp.zeros((8, 256), F32), jnp.zeros((8, 256), F32)]
    for k, value in enumerate(part):
        value = jnp.broadcast_to(value[0:1], (8, 256))
        high = value.astype(BF16).astype(F32)
        mid = (value - high).astype(BF16).astype(F32)
        for i, piece in enumerate((high, mid, value - high - mid)):
            blocks[k // 2] = jnp.where(index == 3 * (k % 2) + i, piece, blocks[k // 2])
    return jnp.concatenate(blocks, axis=0).astype(BF16)


def from_tail(message_ref):
    rows = message_ref.shape[0]
    part = message_ref[rows - TAIL : rows, :].astype(F32)
    return [
        jnp.sum(part[r : r + 3], axis=0, keepdims=True) for r in (0, 3, 8)
    ]


def silu(u):
    return 0.5 * u * (1.0 + jnp.tanh(0.5 * u))


def pack_pairs(v):
    n, m, _, lanes = v.shape
    v = v.reshape(n, m // 2, 2, 8, lanes)
    low, high = v[:, :, 0].reshape(-1, 8, lanes), v[:, :, 1].reshape(-1, 8, lanes)
    both = jnp.where(iota(low.shape, 1) < 4, low, pltpu.roll(high, 4, 1))
    return both.reshape(n, m // 2, 8, lanes)


def split_pairs(v, blank):
    inside = iota(v.shape, 1) < 4
    return [jnp.where(inside, v, blank), jnp.where(inside, pltpu.roll(v, 4, 1), blank)]


def edges(act):
    z = iota(act.shape, 2) % BR
    before, after = pltpu.roll(act, 1, 1), pltpu.roll(act, 7, 1)
    return jnp.where(z == BR - 1, before, jnp.where(z == 0, after, 0.0))


def columns(act, size):
    side = edges(act)
    z = iota((size,) + act.shape[1:], 2) % BR
    second = pltpu.roll(side, 2, 2)
    third = pltpu.roll(side, 4, 2)
    mixed = jnp.where(
        (z == 1) | (z == 2), second[1 : 1 + size],
        jnp.where((z == 3) | (z == 4), third[2 : 2 + size], side[0:size]),
    )
    return [act[e : e + size] for e in range(3)] + [mixed]


def halves(lanes):
    return range(lanes // 128)


def read(ref, start, count, stride):
    return jnp.concatenate(
        [ref[h, pl.ds(start, count, stride=stride), :] for h in range(ref.shape[0])], axis=1
    )


def write(ref, start, count, stride, value):
    for h in range(ref.shape[0]):
        ref[h, pl.ds(start, count, stride=stride), :] = value[:, h * 128 : (h + 1) * 128]


def write_block(ref, start, value):
    for h in range(ref.shape[0]):
        ref[h, start : start + value.shape[0], :] = value[:, h * 128 : (h + 1) * 128]


def even(axis):
    return lax.axis_index(axis) % 2 == 0


def sides(axis, first, second):
    i, n = lax.axis_index(axis), lax.axis_size(axis)
    blank = jnp.full(first.shape, SENT, F32)
    second = blank if second is None else second
    low, high = jnp.where(even(axis), second, first), jnp.where(even(axis), first, second)
    return jnp.where(i > 0, low, SENT), jnp.where(i < n - 1, high, SENT)


def pre_kernel(members, occ_ref, feat_ref, keep_ref, keys_ref, coded_ref, first_ref, second_ref,
               tail_ref, rows_ref=None):
    sx, sy, sb, lanes = feat_ref.shape
    me = lax.axis_index("gx")
    bricks = [occ_ref[x].astype(F32) for x in range(members)]

    def row_of(x):
        return sum(jnp.where(x == i, v, 0.0) for i, v in enumerate(bricks))

    mine = jnp.broadcast_to(row_of(me), (8, sb))
    keep = jnp.where(iota((8, sb), 0) == iota((8, sb), 1), mine, 0.0)
    keep = jnp.broadcast_to(jnp.sum(keep, axis=1, keepdims=True), (8, lanes))
    count = jnp.sum(keep, axis=0, keepdims=True) * float(sx * sy * BR * GW)
    keep_ref[...] = keep
    seq = keys_ref.shape[1]
    lane = iota((1, seq), 1)
    keys = jnp.zeros((1, seq), F32)
    for k in range(members):
        there = row_of(me ^ k)
        for b in range(sb):
            keys = jnp.where(
                (lane // (seq // members) == k) & (lane % (2 * sb) // 2 == b),
                there[:, b : b + 1], keys,
            )
    keys_ref[...] = jnp.broadcast_to(keys, keys_ref.shape)
    field = feat_ref[...].astype(F32)
    wide = jnp.concatenate([field, jnp.zeros((sx, sy, 8 - sb, lanes), F32)], axis=2)
    wide = wide.reshape(sx * sy, 8, lanes)
    total = jnp.sum(jnp.sum(wide, axis=0) * keep, axis=0, keepdims=True)

    def squares_about(mean):
        d = wide - mean[None]
        return jnp.sum(jnp.sum(d * d, axis=0) * keep, axis=0, keepdims=True)

    code = jnp.where((keep > 0)[None], wide, SENT)
    coded_ref[...] = code.reshape(sx * sy * 8, lanes).astype(BF16)
    packed = pack_pairs(code.reshape(sx, sy, 8, lanes))
    low = packed[0:2].reshape(-1, lanes)
    high = packed[sx - 2 : sx].reshape(-1, lanes)
    size = low.shape[0]
    first_ref[0:size, :] = jnp.where(even("gx"), high, low).astype(BF16)
    second_ref[0:size, :] = jnp.where(even("gx"), low, high).astype(BF16)
    mine = moments(total, squares_about, count)
    tail = to_tail(mine)
    first_ref[size : size + TAIL, :] = tail
    second_ref[size : size + TAIL, :] = tail
    tail_ref[...] = tail
    if rows_ref is not None:
        rows_ref[...] = jnp.broadcast_to(to_row(mine)[0:1], rows_ref.shape)


def line_kernel(narrow, sy, sb, _, coded_ref, first_ref, second_ref, *rest):
    tails, (ext_ref, out_ref, buf) = rest[:-3], rest[-3:]
    lanes = coded_ref.shape[1]
    sx = coded_ref.shape[0] // (sy * 8)
    size = 2 * (sy // 2) * 8
    low, high = sides(
        "gx", first_ref[0:size].astype(F32), second_ref[0:size].astype(F32)
    )
    write_block(buf, 2 * sy * 8, coded_ref[...].astype(F32))
    for x0, side in ((0, low), (sx + 2, high)):
        for i in range(2):
            part = side[i * (size // 2) : (i + 1) * (size // 2)].reshape(sy // 2, 8, lanes)
            pair = split_pairs(part, SENT)
            for y in range(sy):
                write_block(buf, ((x0 + i) * sy + y) * 8, pair[y % 2][y // 2])
    rows = (sx + 4) * sy * 8
    ext_ref[...] = jnp.concatenate([buf[h] for h in halves(lanes)], axis=1).astype(BF16)
    count = (sx + 4) * sy
    face = jnp.where(even("gz"), read(buf, sb - 1, count, 8), read(buf, 0, count, 8))
    out_ref[0:count, :] = face.astype(BF16)
    mine = [from_tail(ref) for ref in tails]
    if narrow:
        mine = mine + [from_tail(first_ref), from_tail(second_ref)]
    out_ref[count : count + TAIL, :] = to_tail(merge(mine))


def corner_rows(count):
    return (count + 15) // 16 * 16


def chip_kernel(sb, sy, ext_ref, own_ref, other_ref, *rest):
    out, (buf, stage) = rest[:-2], rest[-2:]
    lanes = ext_ref.shape[1]
    ex = ext_ref.shape[0] // (sy * 8)
    block = ext_ref[...].astype(F32)
    write_block(buf, 0, block)
    write_block(stage, 0, other_ref[0 : ex * sy].astype(F32))
    gap = corner_rows(ex)
    pad = jnp.zeros((gap - ex, lanes), F32)
    tail = to_tail(merge([from_tail(own_ref), from_tail(other_ref)]))
    packed = pack_pairs(block.reshape(ex, sy, 8, lanes))

    def side(y0):
        face = packed[:, y0 // 2].reshape(ex * 8, lanes)
        inner, outer = [], []
        for i in range(2):
            inner += [read(stage, y0 + i, ex, sy), pad]
            start = (y0 + i) * 8
            outer += [
                jnp.where(
                    even("gz"),
                    read(buf, start, ex, sy * 8),
                    read(buf, start + sb - 1, ex, sy * 8),
                ),
                pad,
            ]
        return [face] + inner, outer

    (near_low, far_low), (near_high, far_high) = side(0), side(sy - 2)
    count = ex * sy
    z_face = jnp.where(even("gz"), read(buf, 0, count, 8), read(buf, sb - 1, count, 8))
    out[0][0:count, :] = z_face.astype(BF16)
    out[0][count : count + TAIL, :] = tail
    for k in range((len(out) - 1) // 2):
        up = even("gy") if k == 0 else jnp.logical_not(even("gy"))
        for ref, low, high in (
            (out[1 + 2 * k], near_low, near_high),
            (out[2 + 2 * k], far_low, far_high),
        ):
            value = jnp.where(
                up, jnp.concatenate(high, axis=0), jnp.concatenate(low, axis=0)
            ).astype(BF16)
            ref[0 : value.shape[0], :] = value
            ref[value.shape[0] : value.shape[0] + TAIL, :] = tail


def band_kernel(weight_ref, *rest):
    pars, (out_ref, more_ref) = rest[:-2], rest[-2:]
    lanes = C * BR
    spread = onehot(iota((C, lanes), 0) == iota((C, lanes), 1) // BR)
    turned = jnp.transpose(weight_ref[0].astype(F32)).astype(BF16)
    wide = jnp.dot(turned, spread, preferred_element_type=F32)
    full = (C, BR, lanes)
    zi, zo = iota((1, BR, lanes), 1), iota((1, BR, lanes), 2) % BR

    def rows(value):
        return jnp.broadcast_to(value[:, None, :], full)

    for ex in range(3):
        mixed = jnp.zeros(full, F32)
        for ey in range(3):
            q = (ex * 3 + ey) * 3
            terms = [wide[(q + e) * C : (q + e + 1) * C] for e in range(3)]
            inner = jnp.where(zi == zo - 1, rows(terms[0]), 0.0)
            inner = jnp.where(zi == zo, rows(terms[1]), inner)
            inner = jnp.where(zi == zo + 1, rows(terms[2]), inner)
            before = pltpu.roll(terms[0], 1, 0) if ey else terms[0]
            low = 2 * ey - 1 if ey else BR - 1
            mixed = jnp.where((zi == low) & (zo == 0), rows(before), mixed)
            mixed = jnp.where((zi == 2 * ey) & (zo == BR - 1), rows(terms[2]), mixed)
            out_ref[ex, ey * lanes : (ey + 1) * lanes, :] = (
                inner.reshape(C * BR, lanes).astype(BF16)
            )
        out_ref[ex, 3 * lanes : 4 * lanes, :] = mixed.reshape(C * BR, lanes).astype(BF16)
    if pars:
        pick = onehot(iota((C, lanes), 0) == iota((C, lanes), 1) // BR, F32)
        more_ref[...] = jnp.zeros(more_ref.shape, F32)
        more_ref[0 : pars[0].shape[0], :] = exact_dot(pars[0][...], pick)
    else:
        more_ref[...] = weight_ref[1:2]


def turn_kernel(weight_ref, out_ref):
    kinds, cols, feats = weight_ref.shape
    r = iota((feats, 1), 0)
    source = (r % 128) // 4 * 32 + r // 128 * 4 + r % 4
    pick = onehot(source == iota((feats, feats), 1))
    for k in range(kinds):
        out_ref[:, k * cols : (k + 1) * cols] = lax.dot_general(
            pick, weight_ref[k], (((1,), (1,)), ((), ())), preferred_element_type=F32
        ).astype(BF16)


def first_kernel(narrow, faces, sy, sb, ext_ref, own_ref, core_ref, zface_ref, *rest):
    near, far = rest[0 : 2 * faces : 2], rest[1 : 2 * faces : 2]
    rest = rest[2 * faces :]
    stats_ref = None
    if not narrow:
        stats_ref, rest = rest[0], rest[1:]
    keep_ref, weight_ref, rows_ref, mid_ref, out_ref, msk, buf, lhs = rest
    lanes = ext_ref.shape[1]
    ex = ext_ref.shape[0] // (sy * 8)
    ey = sy + 4
    count = ex * sy
    z_low, z_high = sides(
        "gz", core_ref[0:count].astype(F32), zface_ref[0:count].astype(F32)
    )
    for x in range(ex):
        write_block(
            buf, (x * ey + 2) * 8, ext_ref[x * sy * 8 : (x + 1) * sy * 8].astype(F32)
        )
        part = slice(x * sy, (x + 1) * sy)
        write(buf, (x * ey + 2) * 8 + 7, sy, 8, z_low[part])
        write(buf, (x * ey + 2) * 8 + sb, sy, 8, z_high[part])
    gap = corner_rows(ex)
    size = ex * 8
    face = sides("gy", *[
        near[k][0:size].astype(F32) if k < faces else None for k in range(2)
    ])
    inner = sides("gy", *[
        near[k][size : size + 2 * gap].astype(F32) if k < faces else None for k in range(2)
    ])
    outer = sides("gy", *[
        far[k][0 : 2 * gap].astype(F32) if k < faces else None for k in range(2)
    ])
    for s, y0 in enumerate((0, sy + 2)):
        pair = split_pairs(face[s].reshape(ex, 8, lanes), SENT)
        c_low, c_high = sides("gz", inner[s], outer[s])
        for i in range(2):
            for x in range(ex):
                write_block(buf, (x * ey + y0 + i) * 8, pair[i][x])
            write(buf, (y0 + i) * 8 + 7, ex, ey * 8, c_low[i * gap : i * gap + ex])
            write(buf, (y0 + i) * 8 + sb, ex, ey * 8, c_high[i * gap : i * gap + ex])
    if narrow:
        centre, scale = centre_scale(merge(
            [from_tail(r) for r in (own_ref, zface_ref) + tuple(near) + tuple(far)]
        ))
    else:
        centre, scale = from_rows(stats_ref[...])
    gain, shift, bias = rows_ref[0:1], rows_ref[2:3], rows_ref[4:5]
    scale = scale * gain
    oy, sx = sy + 2, ex - 4
    step = ey * 8
    for x in range(ex):
        v = jnp.concatenate(
            [buf[h, x * step : (x + 1) * step, :] for h in halves(lanes)], axis=1
        )
        there = v != SENT
        msk[x * step : (x + 1) * step] = onehot(there[:, 0:128], F32)
        act = jnp.where(there, silu((v - centre) * scale + shift), 0.0).reshape(ey, 8, lanes)
        for e, part in enumerate(columns(act, oy)):
            lhs[x * oy * 8 : (x + 1) * oy * 8, e * lanes : (e + 1) * lanes] = (
                part.reshape(oy * 8, lanes).astype(BF16)
            )
    ox = sx + 2
    size = ox * oy * 8
    acc = bias
    for e in range(3):
        acc = acc + jnp.dot(
            lhs[e * oy * 8 : e * oy * 8 + size, :], weight_ref[e], preferred_element_type=F32
        )
    mid_ref[...] = acc
    keep = keep_ref[...]
    entries = jnp.sum(keep[:, 0:1]) * float(sx * sy * BR * GW)

    def over_cells(f):
        out = jnp.zeros((8, lanes), F32)
        for x in range(1, sx + 1):
            own = mid_ref[(x * oy + 1) * 8 : (x * oy + oy - 1) * 8].reshape(sy, 8, lanes)
            out = out + jnp.sum(f(own), axis=0)
        return jnp.sum(out * keep, axis=0, keepdims=True)

    def squares_about(mean):
        return over_cells(lambda v: (v - mean[None]) * (v - mean[None]))

    mine = moments(over_cells(lambda v: v), squares_about, entries)
    out_ref[...] = jnp.broadcast_to(to_row(mine)[0:1], out_ref.shape)


def second_kernel(sx, sy, sb, stats_ref, mid_ref, msk_ref, weight_ref, rows_ref, coded_ref,
                  field_ref, tok_ref, low_ref, high_ref, lhs):
    lanes = coded_ref.shape[1]
    step, ext = (sy + 2) * 8, (sy + 4) * 8
    centre, scale = from_rows(stats_ref[...])
    gain, shift, bias = rows_ref[1:2], rows_ref[3:4], rows_ref[5:6]
    scale = scale * gain
    half = sy // 2 * 8
    for x in range(sx + 2):
        v = mid_ref[x * step : (x + 1) * step]
        there = msk_ref[(x + 1) * ext + 8 : (x + 2) * ext - 8]
        there = jnp.concatenate([there] * (lanes // 128), axis=1) > 0
        act = jnp.where(there, silu((v - centre) * scale + shift), 0.0)
        for e, part in enumerate(columns(act.reshape(sy + 2, 8, lanes), sy)):
            lhs[x * half : (x + 1) * half, e * lanes : (e + 1) * lanes] = (
                pack_pairs(part[None]).reshape(half, lanes).astype(BF16)
            )
    size = sx * half
    acc = bias
    for e in range(3):
        acc = acc + jnp.dot(
            lhs[e * half : e * half + size, :], weight_ref[e], preferred_element_type=F32
        )
    field = pack_pairs(coded_ref[...].astype(F32).reshape(sx, sy, 8, lanes))
    field = field.reshape(size, lanes)
    out = jnp.where(field != SENT, field + acc, 0.0).reshape(-1, 8, lanes)
    out = out.astype(BF16)
    field_ref[...] = out.reshape(size, lanes)
    i, j = iota((lanes, lanes), 0), iota((lanes, lanes), 1)
    pick = onehot(i == (j % 128) // 4 * 8 + j // 128 * 4 + j % 4)
    moved = jnp.dot(out.reshape(size, lanes), pick, preferred_element_type=F32).reshape(
        sx // 2, 2, sy // 4, 2, 8, lanes
    )
    count = sx // 2 * (sy // 4)
    parts = []
    for x in range(2):
        for y in range(2):
            piece = moved[:, x, :, y].reshape(count, 8, lanes)
            low, high = piece[:, :, :128], piece[:, :, 128:]
            inside = iota(low.shape, 1) < 4
            for both in (
                jnp.where(inside, low, pltpu.roll(high, 4, 1)),
                jnp.where(inside, pltpu.roll(low, 4, 1), high),
            ):
                parts.append(both.reshape(count * 8, 128).astype(BF16))
    tokens = jnp.concatenate(parts, axis=1)
    n = count * 8
    i, j = iota((n, n), 0), iota((n, n), 1)
    order = onehot(j == i // 8 * 8 + i % 2 * 4 + i % 8 // 2)
    tokens = jnp.dot(order, tokens, preferred_element_type=F32).astype(BF16)
    tok_ref[...] = tokens
    low_ref[...] = tokens[0 : n // 2]
    high_ref[...] = tokens[n // 2 : n]


def fine_kernel(field_ref, fine_ref):
    sx, sy, sb, lanes = fine_ref.shape
    wide = field_ref[...].astype(F32).reshape(-1, 8, lanes)
    other = pltpu.roll(wide, 4, 1)
    fine = jnp.stack([wide[:, :sb], other[:, :sb]], axis=1)
    fine_ref[...] = fine.reshape(sx, sy, sb, lanes).astype(BF16)


def attend_kernel(members, keys_ref, weight_ref, *refs):
    tok_refs, out_refs, (toks, proj) = refs[: -2 - members], refs[-2 - members : -2], refs[-2:]
    own, cols = tok_refs[0].shape[0], weight_ref.shape[1] // 3
    seq = own * members
    start = 0
    for ref in tok_refs:
        toks[start : start + ref.shape[0], :] = ref[...]
        start += ref.shape[0]
    proj[...] = jnp.dot(toks[...], weight_ref[...], preferred_element_type=F32).astype(BF16)
    there = keys_ref[0:1] > 0
    width = min(128, cols)
    for t in range(cols // width):
        q = proj[:, t * width : (t + 1) * width]
        keys = proj[:, cols + t * width : cols + (t + 1) * width]
        values = proj[:, 2 * cols + t * width : 2 * cols + (t + 1) * width]
        head = iota((seq, width), 1) // HD
        merged = jnp.zeros((seq, width), F32)
        for h in range(width // HD):
            mine = jnp.where(head == h, q.astype(F32), 0.0).astype(BF16)
            scores = lax.dot_general(
                mine, keys, (((1,), (1,)), ((), ())), preferred_element_type=F32
            ) * float(HD) ** (-0.5)
            scores = jnp.where(there, scores, -BIG)
            probs = jnp.exp(scores - jnp.max(scores, axis=1, keepdims=True))
            total = jnp.sum(probs, axis=1, keepdims=True)
            mixed = jnp.dot(probs.astype(BF16), values, preferred_element_type=F32)
            merged = jnp.where(head == h, mixed / total, merged)
        merged = merged.astype(BF16)
        for k in range(members):
            out_refs[-1 - k][:, t * width : (t + 1) * width] = merged[k * own : (k + 1) * own]


def place_kernel(members, keep_ref, *refs):
    out_ref = refs[-1]
    own, cols = refs[0].shape
    me = lax.axis_index("gx")
    row = iota((8, cols), 0)
    keep = jnp.zeros((8, cols), F32)
    for b in range(4):
        keep = jnp.where(row // 2 == b, jnp.broadcast_to(keep_ref[b : b + 1, :cols], (8, cols)), keep)
    for k in range(members):
        value = refs[members - 1 - k][...].astype(F32).reshape(own // 8, 8, cols)
        value = jnp.where((keep > 0)[None], value, 0.0).reshape(own, cols).astype(BF16)
        if cols % 128 == 0:
            out_ref[0, :, pl.ds(pl.multiple_of((me ^ k) * cols, cols), cols)] = value
        else:
            out_ref[k] = value


VM = pl.BlockSpec(memory_space=pltpu.VMEM)


def call(kernel, name, specs, out, args, scratch=(), flops=0, nbytes=0, mib=16):
    return pl.pallas_call(
        kernel,
        out_shape=out,
        in_specs=list(specs),
        out_specs=jax.tree.map(lambda _: VM, out),
        scratch_shapes=list(scratch),
        name=name,
        cost_estimate=pl.CostEstimate(flops=flops, bytes_accessed=nbytes, transcendentals=0),
        compiler_params=pltpu.CompilerParams(vmem_limit_bytes=mib * 2**20),
    )(*args)


def shape(*dims, dtype=BF16):
    return jax.ShapeDtypeStruct(dims, dtype)


def pairing(n, odd, closed):
    partner = {i: (i ^ 1 if not odd else (i + 1 if i % 2 else i - 1)) for i in range(n)}
    if closed:
        partner = {i: j % n for i, j in partner.items()}
    return {i: j for i, j in partner.items() if 0 <= j < n and i != j}


def body(features, occupancy, norm_gain, norm_shift, conv_weight, conv_bias, qkv_weight):
    sx, sy, sb, lanes = features.shape
    nx, ny, nz = (lax.axis_size(a) for a in ALL)
    devices = nx * ny * nz
    narrow = nx == 4 and ny == 2 and nz == 4
    own = sx // 2 * (sy // 4) * sb * 2
    ex = sx + 4
    row_shape = [] if narrow else [shape(devices, 128, dtype=F32)]

    slab = sy * 8 + TAIL
    keep, keys, coded, first, second, tail, *stats = call(
        functools.partial(pre_kernel, nx), "pre", (VM, VM),
        [shape(8, lanes, dtype=F32), shape(8, own * nx, dtype=F32),
         shape(sx * sy * 8, lanes), shape(slab, lanes), shape(slab, lanes), shape(TAIL, lanes)]
        + row_shape,
        (occupancy, features), nbytes=10**6,
    )
    stats = [lax.all_to_all(s, ALL, 0, 0, tiled=True) for s in stats]
    got = [
        lax.ppermute(first, "gx", list(pairing(nx, False, False).items())),
        lax.ppermute(second, "gx", list(pairing(nx, True, narrow).items())),
    ]
    tails = [tail]
    if narrow:
        tails.append(lax.ppermute(tail, "gx", [(i, i ^ 2) for i in range(nx)]))
    band = shape(3, 4 * lanes, lanes)
    pars = jnp.concatenate([norm_gain, norm_shift, conv_bias], axis=0)
    later = shape(1, *conv_weight.shape[1:])
    band0, later = call(
        band_kernel, "band0", (VM,), [band, later], (conv_weight,), nbytes=8 * 10**6,
    )
    band1, rows = call(
        band_kernel, "band1", (VM,) * 2, [band, shape(8, lanes, dtype=F32)], (later, pars),
        nbytes=8 * 10**6,
    )
    count = ex * sy
    ext, mine = call(
        functools.partial(line_kernel, narrow, sy, sb), "line", (VM,) * (4 + len(tails)),
        [shape(count * 8, lanes), shape(count + TAIL, lanes)],
        (later, coded, *got, *tails),
        [pltpu.VMEM((lanes // 128, count * 8, 128), F32)], nbytes=10**6,
    )
    core = lax.ppermute(mine, "gz", list(pairing(nz, False, False).items()))

    faces = 1 if ny == 2 else 2
    gap = corner_rows(ex)
    near, far = ex * 8 + 2 * gap + TAIL, 2 * gap + TAIL
    zface, *yfaces = call(
        functools.partial(chip_kernel, sb, sy), "chip", (VM,) * 3,
        [shape(count + TAIL, lanes)] + [shape(near, lanes), shape(far, lanes)] * faces,
        (ext, mine, core),
        [pltpu.VMEM((lanes // 128, count * 8, 128), F32),
         pltpu.VMEM((lanes // 128, count, 128), F32)], nbytes=10**6,
    )
    odd_z = pairing(nz, True, narrow)
    own_tail = zface
    zgot = lax.ppermute(zface, "gz", list(odd_z.items()))
    ygot = []
    for k in range(faces):
        along = pairing(ny, k == 1, False)
        ygot.append(lax.ppermute(yfaces[2 * k], "gy", list(along.items())))
        both = [
            (y * nz + z, along[y] * nz + odd_z[z]) for y in along for z in odd_z
        ]
        ygot.append(lax.ppermute(yfaces[2 * k + 1], ("gy", "gz"), both))

    cols, feats = qkv_weight.shape[1:]
    turned = call(
        turn_kernel, "turn", (VM,), shape(feats, 3 * cols), (qkv_weight,),
        flops=2 * 3 * cols * feats * feats, nbytes=6 * 10**6,
    )

    ey, oy = sy + 4, sy + 2
    size = (sx + 2) * oy * 8
    mid, mine, there = call(
        functools.partial(first_kernel, narrow, faces, sy, sb), "first",
        (VM,) * (7 + 2 * faces + len(stats)),
        [shape(size, lanes, dtype=F32), shape(devices, 128, dtype=F32),
         shape(ex * ey * 8, 128, dtype=F32)],
        (ext, own_tail, core, zgot, *ygot, *stats, keep, band0, rows),
        [pltpu.VMEM((lanes // 128, ex * ey * 8, 128), F32),
         pltpu.VMEM((ex * oy * 8, 4 * lanes), BF16)],
        flops=2 * 10**9, nbytes=4 * 10**6, mib=20,
    )
    stats = lax.all_to_all(mine, ALL, 0, 0, tiled=True)
    field, tokens, *parts = call(
        functools.partial(second_kernel, sx, sy, sb), "second", (VM,) * 6,
        [shape(sx * sy * 4, lanes), shape(own, feats)] + [shape(own // 2, feats)] * 2,
        (stats, mid, there, band1, rows, coded),
        [pltpu.VMEM(((sx + 2) * sy * 4, 4 * lanes), BF16)],
        flops=10**9, nbytes=4 * 10**6,
    )
    fine_out = call(
        fine_kernel, "fine", (VM,), shape(*features.shape), (field,), nbytes=4 * 10**6, mib=8,
    )
    swaps = [[(i, i ^ k) for i in range(nx)] for k in range(nx)]
    blocks = {0: parts}
    for k in sorted(range(1, nx), key=lambda k: (bin(k).count("1"), -k)):
        low = k & -k
        source = [tokens] if k == 1 else blocks[k ^ low]
        blocks[k] = [lax.ppermute(v, "gx", swaps[low]) for v in source]
    blocks = [tokens] + [v for k in range(1, nx) for v in blocks[k]]
    outs = call(
        functools.partial(attend_kernel, nx), "attend", (VM,) * (2 + len(blocks)),
        [shape(own, cols)] * nx, (keys, turned, *blocks),
        [pltpu.VMEM((own * nx, feats), BF16), pltpu.VMEM((own * nx, 3 * cols), BF16)],
        flops=10**9, nbytes=3 * 10**6, mib=16 if narrow else 40,
    )
    moved = [lax.ppermute(v, "gx", swaps[nx - 1 - i]) for i, v in enumerate(outs[:-1])]
    outs = moved + [outs[-1]]
    lined = cols % 128 == 0
    attention = call(
        functools.partial(place_kernel, nx), "place", (VM,) * (1 + nx),
        shape(1, own, nx * cols) if lined else shape(nx, own, cols), (keep, *outs),
        nbytes=3 * 10**5, mib=8,
    )
    if not lined:
        me = lax.axis_index("gx")
        attention = jnp.concatenate(
            [lax.dynamic_index_in_dim(attention, me ^ j, 0, keepdims=False) for j in range(nx)],
            axis=1,
        )[None]
    return (fine_out, attention)


def solution(mesh):
    placed = (
        P("gx", "gy", "gz", None),
        P(None, "gy", "gz"),
        P(),
        P(),
        P(),
        P(),
        P(None, "gx", None),
    )
    return jax.shard_map(
        body,
        mesh=mesh,
        in_specs=placed,
        out_specs=(P("gx", "gy", "gz", None), P(("gy", "gz"), "gx", None)),
        check_vma=False,
    )
```

```python
import functools

import jax
import jax.numpy as jnp
from jax import lax
from jax.experimental import pallas as pl
from jax.experimental.pallas import tpu as pltpu
from jax.sharding import PartitionSpec as P

C = 32
GW = 4
HD = 64
BR = 8
EPS = 1e-05
SENT = 512.0
BIG = 1e30
ALL = ("gx", "gy", "gz")
F32, BF16 = jnp.float32, jnp.bfloat16
HIGHEST = lax.Precision.HIGHEST
TAIL = 16


def iota(shape, dim):
    return lax.broadcasted_iota(jnp.int32, shape, dim)


def onehot(cond, dtype=BF16):
    return jnp.where(cond, 1.0, 0.0).astype(dtype)


def exact_dot(a, b):
    return jnp.dot(a, b, precision=HIGHEST, preferred_element_type=F32)


def spread_sum(v):
    lane = iota(v.shape, 1)
    s = 1
    while s < GW * BR:
        v = v + jnp.where(lane & s == 0, pltpu.roll(v, 128 - s, 1), pltpu.roll(v, s, 1))
        s *= 2
    return v


def group_sum(total):
    k = total.shape[1] // 128
    rows = [jnp.broadcast_to(total[:, h * 128 : (h + 1) * 128], (8, 128)) for h in range(k)]
    out = spread_sum(jnp.concatenate(rows, axis=0))
    return jnp.concatenate([out[h * 8 : (h + 1) * 8] for h in range(k)], axis=1)


def moments(total, squares_about, count):
    sums = group_sum(total)
    squares = group_sum(squares_about((sums / count)[0:1]))
    return sums, squares, jnp.zeros(sums.shape, F32) + count


def merge(parts):
    n = sum(p[2] for p in parts)
    sums = sum(p[0] for p in parts)
    centre = sums / n
    squares = sum(p[1] + p[2] * (p[0] / p[2] - centre) ** 2 for p in parts)
    return sums, squares, n


def centre_scale(part):
    return part[0] / part[2], lax.rsqrt(part[1] / part[2] + EPS)


def to_row(part):
    j = iota((8, 128), 1) % (GW * BR)
    row = jnp.zeros((8, 128), F32)
    for h in range(2):
        for k in range(3):
            row = jnp.where(j == 4 * h + k, part[k][:, h * 128 : (h + 1) * 128], row)
    return row


def from_rows(rows):
    n = jnp.maximum(pltpu.roll(rows, 126, 1), 1.0)
    total = jnp.sum(n, axis=0, keepdims=True)
    centre = jnp.sum(rows, axis=0, keepdims=True) / total
    drift = rows / n - centre
    squares = pltpu.roll(rows, 127, 1) + n * drift * drift
    spread = jnp.sum(squares, axis=0, keepdims=True) / total
    j = iota((8, 128), 1) % (GW * BR)
    blocks = [
        jnp.where(j == 4 * h, jnp.broadcast_to(v, (8, 128)), 0.0)
        for v in (centre, spread) for h in range(2)
    ]
    out = spread_sum(jnp.concatenate(blocks, axis=0))
    out = [out[8 * i : 8 * i + 1] for i in range(4)]
    return (
        jnp.concatenate(out[:2], axis=1),
        lax.rsqrt(jnp.concatenate(out[2:], axis=1) + EPS),
    )


def to_tail(part):
    index = iota((8, 256), 0)
    blocks = [jnp.zeros((8, 256), F32), jnp.zeros((8, 256), F32)]
    for k, value in enumerate(part):
        value = jnp.broadcast_to(value[0:1], (8, 256))
        high = value.astype(BF16).astype(F32)
        mid = (value - high).astype(BF16).astype(F32)
        for i, piece in enumerate((high, mid, value - high - mid)):
            blocks[k // 2] = jnp.where(index == 3 * (k % 2) + i, piece, blocks[k // 2])
    return jnp.concatenate(blocks, axis=0).astype(BF16)


def from_tail(message_ref):
    rows = message_ref.shape[0]
    part = message_ref[rows - TAIL : rows, :].astype(F32)
    return [
        jnp.sum(part[r : r + 3], axis=0, keepdims=True) for r in (0, 3, 8)
    ]


def silu(u):
    return 0.5 * u * (1.0 + jnp.tanh(0.5 * u))


def pack_pairs(v):
    n, m, _, lanes = v.shape
    v = v.reshape(n, m // 2, 2, 8, lanes)
    low, high = v[:, :, 0].reshape(-1, 8, lanes), v[:, :, 1].reshape(-1, 8, lanes)
    both = jnp.where(iota(low.shape, 1) < 4, low, pltpu.roll(high, 4, 1))
    return both.reshape(n, m // 2, 8, lanes)


def split_pairs(v, blank):
    inside = iota(v.shape, 1) < 4
    return [jnp.where(inside, v, blank), jnp.where(inside, pltpu.roll(v, 4, 1), blank)]


def edges(act):
    z = iota(act.shape, 2) % BR
    before, after = pltpu.roll(act, 1, 1), pltpu.roll(act, 7, 1)
    return jnp.where(z == BR - 1, before, jnp.where(z == 0, after, 0.0))


def columns(act, size):
    side = edges(act)
    z = iota((size,) + act.shape[1:], 2) % BR
    second = pltpu.roll(side, 2, 2)
    third = pltpu.roll(side, 4, 2)
    mixed = jnp.where(
        (z == 1) | (z == 2), second[1 : 1 + size],
        jnp.where((z == 3) | (z == 4), third[2 : 2 + size], side[0:size]),
    )
    return [act[e : e + size] for e in range(3)] + [mixed]


def halves(lanes):
    return range(lanes // 128)


def read(ref, start, count, stride):
    return jnp.concatenate(
        [ref[h, pl.ds(start, count, stride=stride), :] for h in range(ref.shape[0])], axis=1
    )


def write(ref, start, count, stride, value):
    for h in range(ref.shape[0]):
        ref[h, pl.ds(start, count, stride=stride), :] = value[:, h * 128 : (h + 1) * 128]


def write_block(ref, start, value):
    for h in range(ref.shape[0]):
        ref[h, start : start + value.shape[0], :] = value[:, h * 128 : (h + 1) * 128]


def even(axis):
    return lax.axis_index(axis) % 2 == 0


def sides(axis, first, second):
    i, n = lax.axis_index(axis), lax.axis_size(axis)
    blank = jnp.full(first.shape, SENT, F32)
    second = blank if second is None else second
    low, high = jnp.where(even(axis), second, first), jnp.where(even(axis), first, second)
    return jnp.where(i > 0, low, SENT), jnp.where(i < n - 1, high, SENT)


def pre_kernel(members, occ_ref, feat_ref, keep_ref, keys_ref, coded_ref, first_ref, second_ref,
               tail_ref, rows_ref=None):
    sx, sy, sb, lanes = feat_ref.shape
    me = lax.axis_index("gx")
    bricks = [occ_ref[x].astype(F32) for x in range(members)]

    def row_of(x):
        return sum(jnp.where(x == i, v, 0.0) for i, v in enumerate(bricks))

    mine = jnp.broadcast_to(row_of(me), (8, sb))
    keep = jnp.where(iota((8, sb), 0) == iota((8, sb), 1), mine, 0.0)
    keep = jnp.broadcast_to(jnp.sum(keep, axis=1, keepdims=True), (8, lanes))
    count = jnp.sum(keep, axis=0, keepdims=True) * float(sx * sy * BR * GW)
    keep_ref[...] = keep
    seq = keys_ref.shape[1]
    lane = iota((1, seq), 1)
    keys = jnp.zeros((1, seq), F32)
    for k in range(members):
        there = row_of(me ^ k)
        for b in range(sb):
            keys = jnp.where(
                (lane // (seq // members) == k) & (lane % (2 * sb) // 2 == b),
                there[:, b : b + 1], keys,
            )
    keys_ref[...] = jnp.broadcast_to(keys, keys_ref.shape)
    field = feat_ref[...].astype(F32)
    wide = jnp.concatenate([field, jnp.zeros((sx, sy, 8 - sb, lanes), F32)], axis=2)
    wide = wide.reshape(sx * sy, 8, lanes)
    total = jnp.sum(jnp.sum(wide, axis=0) * keep, axis=0, keepdims=True)

    def squares_about(mean):
        d = wide - mean[None]
        return jnp.sum(jnp.sum(d * d, axis=0) * keep, axis=0, keepdims=True)

    code = jnp.where((keep > 0)[None], wide, SENT)
    coded_ref[...] = code.reshape(sx * sy * 8, lanes).astype(BF16)
    packed = pack_pairs(code.reshape(sx, sy, 8, lanes))
    low = packed[0:2].reshape(-1, lanes)
    high = packed[sx - 2 : sx].reshape(-1, lanes)
    size = low.shape[0]
    first_ref[0:size, :] = jnp.where(even("gx"), high, low).astype(BF16)
    second_ref[0:size, :] = jnp.where(even("gx"), low, high).astype(BF16)
    mine = moments(total, squares_about, count)
    tail = to_tail(mine)
    first_ref[size : size + TAIL, :] = tail
    second_ref[size : size + TAIL, :] = tail
    tail_ref[...] = tail
    if rows_ref is not None:
        rows_ref[...] = jnp.broadcast_to(to_row(mine)[0:1], rows_ref.shape)


def line_kernel(narrow, sy, sb, _, coded_ref, first_ref, second_ref, *rest):
    tails, (ext_ref, out_ref, buf) = rest[:-3], rest[-3:]
    lanes = coded_ref.shape[1]
    sx = coded_ref.shape[0] // (sy * 8)
    size = 2 * (sy // 2) * 8
    low, high = sides(
        "gx", first_ref[0:size].astype(F32), second_ref[0:size].astype(F32)
    )
    write_block(buf, 2 * sy * 8, coded_ref[...].astype(F32))
    for x0, side in ((0, low), (sx + 2, high)):
        for i in range(2):
            part = side[i * (size // 2) : (i + 1) * (size // 2)].reshape(sy // 2, 8, lanes)
            pair = split_pairs(part, SENT)
            for y in range(sy):
                write_block(buf, ((x0 + i) * sy + y) * 8, pair[y % 2][y // 2])
    rows = (sx + 4) * sy * 8
    ext_ref[...] = jnp.concatenate([buf[h] for h in halves(lanes)], axis=1).astype(BF16)
    count = (sx + 4) * sy
    face = jnp.where(even("gz"), read(buf, sb - 1, count, 8), read(buf, 0, count, 8))
    out_ref[0:count, :] = face.astype(BF16)
    mine = [from_tail(ref) for ref in tails]
    if narrow:
        mine = mine + [from_tail(first_ref), from_tail(second_ref)]
    out_ref[count : count + TAIL, :] = to_tail(merge(mine))


def corner_rows(count):
    return (count + 15) // 16 * 16


def chip_kernel(sb, sy, ext_ref, own_ref, other_ref, *rest):
    out, (buf, stage) = rest[:-2], rest[-2:]
    lanes = ext_ref.shape[1]
    ex = ext_ref.shape[0] // (sy * 8)
    block = ext_ref[...].astype(F32)
    write_block(buf, 0, block)
    write_block(stage, 0, other_ref[0 : ex * sy].astype(F32))
    gap = corner_rows(ex)
    pad = jnp.zeros((gap - ex, lanes), F32)
    tail = to_tail(merge([from_tail(own_ref), from_tail(other_ref)]))
    packed = pack_pairs(block.reshape(ex, sy, 8, lanes))

    def side(y0):
        face = packed[:, y0 // 2].reshape(ex * 8, lanes)
        inner, outer = [], []
        for i in range(2):
            inner += [read(stage, y0 + i, ex, sy), pad]
            start = (y0 + i) * 8
            outer += [
                jnp.where(
                    even("gz"),
                    read(buf, start, ex, sy * 8),
                    read(buf, start + sb - 1, ex, sy * 8),
                ),
                pad,
            ]
        return [face] + inner, outer

    (near_low, far_low), (near_high, far_high) = side(0), side(sy - 2)
    count = ex * sy
    z_face = jnp.where(even("gz"), read(buf, 0, count, 8), read(buf, sb - 1, count, 8))
    out[0][0:count, :] = z_face.astype(BF16)
    out[0][count : count + TAIL, :] = tail
    for k in range((len(out) - 1) // 2):
        up = even("gy") if k == 0 else jnp.logical_not(even("gy"))
        for ref, low, high in (
            (out[1 + 2 * k], near_low, near_high),
            (out[2 + 2 * k], far_low, far_high),
        ):
            value = jnp.where(
                up, jnp.concatenate(high, axis=0), jnp.concatenate(low, axis=0)
            ).astype(BF16)
            ref[0 : value.shape[0], :] = value
            ref[value.shape[0] : value.shape[0] + TAIL, :] = tail


def band_kernel(weight_ref, *rest):
    pars, (out_ref, more_ref) = rest[:-2], rest[-2:]
    lanes = C * BR
    spread = onehot(iota((C, lanes), 0) == iota((C, lanes), 1) // BR)
    turned = jnp.transpose(weight_ref[0].astype(F32)).astype(BF16)
    wide = jnp.dot(turned, spread, preferred_element_type=F32)
    full = (C, BR, lanes)
    zi, zo = iota((1, BR, lanes), 1), iota((1, BR, lanes), 2) % BR

    def rows(value):
        return jnp.broadcast_to(value[:, None, :], full)

    for ex in range(3):
        mixed = jnp.zeros(full, F32)
        for ey in range(3):
            q = (ex * 3 + ey) * 3
            terms = [wide[(q + e) * C : (q + e + 1) * C] for e in range(3)]
            inner = jnp.where(zi == zo - 1, rows(terms[0]), 0.0)
            inner = jnp.where(zi == zo, rows(terms[1]), inner)
            inner = jnp.where(zi == zo + 1, rows(terms[2]), inner)
            before = pltpu.roll(terms[0], 1, 0) if ey else terms[0]
            low = 2 * ey - 1 if ey else BR - 1
            mixed = jnp.where((zi == low) & (zo == 0), rows(before), mixed)
            mixed = jnp.where((zi == 2 * ey) & (zo == BR - 1), rows(terms[2]), mixed)
            out_ref[ex, ey * lanes : (ey + 1) * lanes, :] = (
                inner.reshape(C * BR, lanes).astype(BF16)
            )
        out_ref[ex, 3 * lanes : 4 * lanes, :] = mixed.reshape(C * BR, lanes).astype(BF16)
    if pars:
        pick = onehot(iota((C, lanes), 0) == iota((C, lanes), 1) // BR, F32)
        more_ref[...] = jnp.zeros(more_ref.shape, F32)
        more_ref[0 : pars[0].shape[0], :] = exact_dot(pars[0][...], pick)
    else:
        more_ref[...] = weight_ref[1:2]


def turn_kernel(weight_ref, out_ref):
    kinds, cols, feats = weight_ref.shape
    r = iota((feats, 1), 0)
    source = (r % 128) // 4 * 32 + r // 128 * 4 + r % 4
    pick = onehot(source == iota((feats, feats), 1))
    for k in range(kinds):
        out_ref[:, k * cols : (k + 1) * cols] = lax.dot_general(
            pick, weight_ref[k], (((1,), (1,)), ((), ())), preferred_element_type=F32
        ).astype(BF16)


def first_kernel(narrow, faces, sy, sb, ext_ref, own_ref, core_ref, zface_ref, *rest):
    near, far = rest[0 : 2 * faces : 2], rest[1 : 2 * faces : 2]
    rest = rest[2 * faces :]
    stats_ref = None
    if not narrow:
        stats_ref, rest = rest[0], rest[1:]
    keep_ref, weight_ref, rows_ref, mid_ref, out_ref, msk, buf, lhs = rest
    lanes = ext_ref.shape[1]
    ex = ext_ref.shape[0] // (sy * 8)
    ey = sy + 4
    count = ex * sy
    z_low, z_high = sides(
        "gz", core_ref[0:count].astype(F32), zface_ref[0:count].astype(F32)
    )
    for x in range(ex):
        write_block(
            buf, (x * ey + 2) * 8, ext_ref[x * sy * 8 : (x + 1) * sy * 8].astype(F32)
        )
        part = slice(x * sy, (x + 1) * sy)
        write(buf, (x * ey + 2) * 8 + 7, sy, 8, z_low[part])
        write(buf, (x * ey + 2) * 8 + sb, sy, 8, z_high[part])
    gap = corner_rows(ex)
    size = ex * 8
    face = sides("gy", *[
        near[k][0:size].astype(F32) if k < faces else None for k in range(2)
    ])
    inner = sides("gy", *[
        near[k][size : size + 2 * gap].astype(F32) if k < faces else None for k in range(2)
    ])
    outer = sides("gy", *[
        far[k][0 : 2 * gap].astype(F32) if k < faces else None for k in range(2)
    ])
    for s, y0 in enumerate((0, sy + 2)):
        pair = split_pairs(face[s].reshape(ex, 8, lanes), SENT)
        c_low, c_high = sides("gz", inner[s], outer[s])
        for i in range(2):
            for x in range(ex):
                write_block(buf, (x * ey + y0 + i) * 8, pair[i][x])
            write(buf, (y0 + i) * 8 + 7, ex, ey * 8, c_low[i * gap : i * gap + ex])
            write(buf, (y0 + i) * 8 + sb, ex, ey * 8, c_high[i * gap : i * gap + ex])
    if narrow:
        centre, scale = centre_scale(merge(
            [from_tail(r) for r in (own_ref, zface_ref) + tuple(near) + tuple(far)]
        ))
    else:
        centre, scale = from_rows(stats_ref[...])
    gain, shift, bias = rows_ref[0:1], rows_ref[2:3], rows_ref[4:5]
    scale = scale * gain
    oy, sx = sy + 2, ex - 4
    step = ey * 8
    for x in range(ex):
        v = jnp.concatenate(
            [buf[h, x * step : (x + 1) * step, :] for h in halves(lanes)], axis=1
        )
        there = v != SENT
        msk[x * step : (x + 1) * step] = onehot(there[:, 0:128], F32)
        act = jnp.where(there, silu((v - centre) * scale + shift), 0.0).reshape(ey, 8, lanes)
        for e, part in enumerate(columns(act, oy)):
            lhs[x * oy * 8 : (x + 1) * oy * 8, e * lanes : (e + 1) * lanes] = (
                part.reshape(oy * 8, lanes).astype(BF16)
            )
    ox = sx + 2
    size = ox * oy * 8
    acc = bias
    for e in range(3):
        acc = acc + jnp.dot(
            lhs[e * oy * 8 : e * oy * 8 + size, :], weight_ref[e], preferred_element_type=F32
        )
    mid_ref[...] = acc
    keep = keep_ref[...]
    entries = jnp.sum(keep[:, 0:1]) * float(sx * sy * BR * GW)

    def over_cells(f):
        out = jnp.zeros((8, lanes), F32)
        for x in range(1, sx + 1):
            own = mid_ref[(x * oy + 1) * 8 : (x * oy + oy - 1) * 8].reshape(sy, 8, lanes)
            out = out + jnp.sum(f(own), axis=0)
        return jnp.sum(out * keep, axis=0, keepdims=True)

    def squares_about(mean):
        return over_cells(lambda v: (v - mean[None]) * (v - mean[None]))

    mine = moments(over_cells(lambda v: v), squares_about, entries)
    out_ref[...] = jnp.broadcast_to(to_row(mine)[0:1], out_ref.shape)


def second_kernel(sx, sy, sb, stats_ref, mid_ref, msk_ref, weight_ref, rows_ref, coded_ref,
                  field_ref, tok_ref, low_ref, high_ref, lhs):
    lanes = coded_ref.shape[1]
    step, ext = (sy + 2) * 8, (sy + 4) * 8
    centre, scale = from_rows(stats_ref[...])
    gain, shift, bias = rows_ref[1:2], rows_ref[3:4], rows_ref[5:6]
    scale = scale * gain
    half = sy // 2 * 8
    for x in range(sx + 2):
        v = mid_ref[x * step : (x + 1) * step]
        there = msk_ref[(x + 1) * ext + 8 : (x + 2) * ext - 8]
        there = jnp.concatenate([there] * (lanes // 128), axis=1) > 0
        act = jnp.where(there, silu((v - centre) * scale + shift), 0.0)
        for e, part in enumerate(columns(act.reshape(sy + 2, 8, lanes), sy)):
            lhs[x * half : (x + 1) * half, e * lanes : (e + 1) * lanes] = (
                pack_pairs(part[None]).reshape(half, lanes).astype(BF16)
            )
    size = sx * half
    acc = bias
    for e in range(3):
        acc = acc + jnp.dot(
            lhs[e * half : e * half + size, :], weight_ref[e], preferred_element_type=F32
        )
    field = pack_pairs(coded_ref[...].astype(F32).reshape(sx, sy, 8, lanes))
    field = field.reshape(size, lanes)
    out = jnp.where(field != SENT, field + acc, 0.0).reshape(-1, 8, lanes)
    out = out.astype(BF16)
    field_ref[...] = out.reshape(size, lanes)
    i, j = iota((lanes, lanes), 0), iota((lanes, lanes), 1)
    pick = onehot(i == (j % 128) // 4 * 8 + j // 128 * 4 + j % 4)
    moved = jnp.dot(out.reshape(size, lanes), pick, preferred_element_type=F32).reshape(
        sx // 2, 2, sy // 4, 2, 8, lanes
    )
    count = sx // 2 * (sy // 4)
    parts = []
    for x in range(2):
        for y in range(2):
            piece = moved[:, x, :, y].reshape(count, 8, lanes)
            low, high = piece[:, :, :128], piece[:, :, 128:]
            inside = iota(low.shape, 1) < 4
            for both in (
                jnp.where(inside, low, pltpu.roll(high, 4, 1)),
                jnp.where(inside, pltpu.roll(low, 4, 1), high),
            ):
                parts.append(both.reshape(count * 8, 128).astype(BF16))
    tokens = jnp.concatenate(parts, axis=1)
    n = count * 8
    i, j = iota((n, n), 0), iota((n, n), 1)
    order = onehot(j == i // 8 * 8 + i % 2 * 4 + i % 8 // 2)
    tokens = jnp.dot(order, tokens, preferred_element_type=F32).astype(BF16)
    tok_ref[...] = tokens
    low_ref[...] = tokens[0 : n // 2]
    high_ref[...] = tokens[n // 2 : n]


def fine_kernel(field_ref, fine_ref):
    sx, sy, sb, lanes = fine_ref.shape
    wide = field_ref[...].astype(F32).reshape(-1, 8, lanes)
    other = pltpu.roll(wide, 4, 1)
    fine = jnp.stack([wide[:, :sb], other[:, :sb]], axis=1)
    fine_ref[...] = fine.reshape(sx, sy, sb, lanes).astype(BF16)


def attend_kernel(members, keys_ref, weight_ref, *refs):
    tok_refs, out_refs, (toks, proj) = refs[: -2 - members], refs[-2 - members : -2], refs[-2:]
    own, cols = tok_refs[0].shape[0], weight_ref.shape[1] // 3
    seq = own * members
    start = 0
    for ref in tok_refs:
        toks[start : start + ref.shape[0], :] = ref[...]
        start += ref.shape[0]
    proj[...] = jnp.dot(toks[...], weight_ref[...], preferred_element_type=F32).astype(BF16)
    there = keys_ref[0:1] > 0
    width = min(128, cols)
    for t in range(cols // width):
        q = proj[:, t * width : (t + 1) * width]
        keys = proj[:, cols + t * width : cols + (t + 1) * width]
        values = proj[:, 2 * cols + t * width : 2 * cols + (t + 1) * width]
        head = iota((seq, width), 1) // HD
        merged = jnp.zeros((seq, width), F32)
        for h in range(width // HD):
            mine = jnp.where(head == h, q.astype(F32), 0.0).astype(BF16)
            scores = lax.dot_general(
                mine, keys, (((1,), (1,)), ((), ())), preferred_element_type=F32
            ) * float(HD) ** (-0.5)
            scores = jnp.where(there, scores, -BIG)
            probs = jnp.exp(scores - jnp.max(scores, axis=1, keepdims=True))
            total = jnp.sum(probs, axis=1, keepdims=True)
            mixed = jnp.dot(probs.astype(BF16), values, preferred_element_type=F32)
            merged = jnp.where(head == h, mixed / total, merged)
        merged = merged.astype(BF16)
        for k in range(members):
            out_refs[-1 - k][:, t * width : (t + 1) * width] = merged[k * own : (k + 1) * own]


def place_kernel(members, keep_ref, *refs):
    out_ref = refs[-1]
    own, cols = refs[0].shape
    me = lax.axis_index("gx")
    row = iota((8, cols), 0)
    keep = jnp.zeros((8, cols), F32)
    for b in range(4):
        keep = jnp.where(row // 2 == b, jnp.broadcast_to(keep_ref[b : b + 1, :cols], (8, cols)), keep)
    for k in range(members):
        value = refs[members - 1 - k][...].astype(F32).reshape(own // 8, 8, cols)
        value = jnp.where((keep > 0)[None], value, 0.0).reshape(own, cols).astype(BF16)
        if cols % 128 == 0:
            out_ref[0, :, pl.ds(pl.multiple_of((me ^ k) * cols, cols), cols)] = value
        else:
            out_ref[k] = value


VM = pl.BlockSpec(memory_space=pltpu.VMEM)


def call(kernel, name, specs, out, args, scratch=(), flops=0, nbytes=0, mib=16):
    return pl.pallas_call(
        kernel,
        out_shape=out,
        in_specs=list(specs),
        out_specs=jax.tree.map(lambda _: VM, out),
        scratch_shapes=list(scratch),
        name=name,
        cost_estimate=pl.CostEstimate(flops=flops, bytes_accessed=nbytes, transcendentals=0),
        compiler_params=pltpu.CompilerParams(vmem_limit_bytes=mib * 2**20),
    )(*args)


def shape(*dims, dtype=BF16):
    return jax.ShapeDtypeStruct(dims, dtype)


def pairing(n, odd, closed):
    partner = {i: (i ^ 1 if not odd else (i + 1 if i % 2 else i - 1)) for i in range(n)}
    if closed:
        partner = {i: j % n for i, j in partner.items()}
    return {i: j for i, j in partner.items() if 0 <= j < n and i != j}


def body(features, occupancy, norm_gain, norm_shift, conv_weight, conv_bias, qkv_weight):
    sx, sy, sb, lanes = features.shape
    nx, ny, nz = (lax.axis_size(a) for a in ALL)
    devices = nx * ny * nz
    narrow = nx == 4 and ny == 2 and nz == 4
    own = sx // 2 * (sy // 4) * sb * 2
    ex = sx + 4
    row_shape = [] if narrow else [shape(devices, 128, dtype=F32)]

    slab = sy * 8 + TAIL
    keep, keys, coded, first, second, tail, *stats = call(
        functools.partial(pre_kernel, nx), "pre", (VM, VM),
        [shape(8, lanes, dtype=F32), shape(8, own * nx, dtype=F32),
         shape(sx * sy * 8, lanes), shape(slab, lanes), shape(slab, lanes), shape(TAIL, lanes)]
        + row_shape,
        (occupancy, features), nbytes=10**6,
    )
    stats = [lax.all_to_all(s, ALL, 0, 0, tiled=True) for s in stats]
    got = [
        lax.ppermute(first, "gx", list(pairing(nx, False, False).items())),
        lax.ppermute(second, "gx", list(pairing(nx, True, narrow).items())),
    ]
    tails = [tail]
    if narrow:
        tails.append(lax.ppermute(tail, "gx", [(i, i ^ 2) for i in range(nx)]))
    band = shape(3, 4 * lanes, lanes)
    pars = jnp.concatenate([norm_gain, norm_shift, conv_bias], axis=0)
    later = shape(1, *conv_weight.shape[1:])
    band0, later = call(
        band_kernel, "band0", (VM,), [band, later], (conv_weight,), nbytes=8 * 10**6,
    )
    band1, rows = call(
        band_kernel, "band1", (VM,) * 2, [band, shape(8, lanes, dtype=F32)], (later, pars),
        nbytes=8 * 10**6,
    )
    count = ex * sy
    ext, mine = call(
        functools.partial(line_kernel, narrow, sy, sb), "line", (VM,) * (4 + len(tails)),
        [shape(count * 8, lanes), shape(count + TAIL, lanes)],
        (later, coded, *got, *tails),
        [pltpu.VMEM((lanes // 128, count * 8, 128), F32)], nbytes=10**6,
    )
    core = lax.ppermute(mine, "gz", list(pairing(nz, False, False).items()))

    faces = 1 if ny == 2 else 2
    gap = corner_rows(ex)
    near, far = ex * 8 + 2 * gap + TAIL, 2 * gap + TAIL
    zface, *yfaces = call(
        functools.partial(chip_kernel, sb, sy), "chip", (VM,) * 3,
        [shape(count + TAIL, lanes)] + [shape(near, lanes), shape(far, lanes)] * faces,
        (ext, mine, core),
        [pltpu.VMEM((lanes // 128, count * 8, 128), F32),
         pltpu.VMEM((lanes // 128, count, 128), F32)], nbytes=10**6,
    )
    odd_z = pairing(nz, True, narrow)
    own_tail = zface
    zgot = lax.ppermute(zface, "gz", list(odd_z.items()))
    ygot = []
    for k in range(faces):
        along = pairing(ny, k == 1, False)
        ygot.append(lax.ppermute(yfaces[2 * k], "gy", list(along.items())))
        both = [
            (y * nz + z, along[y] * nz + odd_z[z]) for y in along for z in odd_z
        ]
        ygot.append(lax.ppermute(yfaces[2 * k + 1], ("gy", "gz"), both))

    cols, feats = qkv_weight.shape[1:]
    turned = call(
        turn_kernel, "turn", (VM,), shape(feats, 3 * cols), (qkv_weight,),
        flops=2 * 3 * cols * feats * feats, nbytes=6 * 10**6,
    )

    ey, oy = sy + 4, sy + 2
    size = (sx + 2) * oy * 8
    mid, mine, there = call(
        functools.partial(first_kernel, narrow, faces, sy, sb), "first",
        (VM,) * (7 + 2 * faces + len(stats)),
        [shape(size, lanes, dtype=F32), shape(devices, 128, dtype=F32),
         shape(ex * ey * 8, 128, dtype=F32)],
        (ext, own_tail, core, zgot, *ygot, *stats, keep, band0, rows),
        [pltpu.VMEM((lanes // 128, ex * ey * 8, 128), F32),
         pltpu.VMEM((ex * oy * 8, 4 * lanes), BF16)],
        flops=2 * 10**9, nbytes=4 * 10**6, mib=20,
    )
    stats = lax.all_to_all(mine, ALL, 0, 0, tiled=True)
    field, tokens, *parts = call(
        functools.partial(second_kernel, sx, sy, sb), "second", (VM,) * 6,
        [shape(sx * sy * 4, lanes), shape(own, feats)] + [shape(own // 2, feats)] * 2,
        (stats, mid, there, band1, rows, coded),
        [pltpu.VMEM(((sx + 2) * sy * 4, 4 * lanes), BF16)],
        flops=10**9, nbytes=4 * 10**6,
    )
    fine_out = call(
        fine_kernel, "fine", (VM,), shape(*features.shape), (field,), nbytes=4 * 10**6, mib=8,
    )
    swaps = [[(i, i ^ k) for i in range(nx)] for k in range(nx)]
    blocks = {0: parts}
    for k in sorted(range(1, nx), key=lambda k: (bin(k).count("1"), -k)):
        low = k & -k
        source = [tokens] if k == 1 else blocks[k ^ low]
        if k & (k - 1):
            first, turned = lax.optimization_barrier((source[0], turned))
            source = [first] + source[1:]
        blocks[k] = [lax.ppermute(v, "gx", swaps[low]) for v in source]
    blocks = [tokens] + [v for k in range(1, nx) for v in blocks[k]]
    outs = call(
        functools.partial(attend_kernel, nx), "attend", (VM,) * (2 + len(blocks)),
        [shape(own, cols)] * nx, (keys, turned, *blocks),
        [pltpu.VMEM((own * nx, feats), BF16), pltpu.VMEM((own * nx, 3 * cols), BF16)],
        flops=10**9, nbytes=3 * 10**6, mib=16 if narrow else 40,
    )
    moved = [lax.ppermute(v, "gx", swaps[nx - 1 - i]) for i, v in enumerate(outs[:-1])]
    outs = moved + [outs[-1]]
    lined = cols % 128 == 0
    attention = call(
        functools.partial(place_kernel, nx), "place", (VM,) * (1 + nx),
        shape(1, own, nx * cols) if lined else shape(nx, own, cols), (keep, *outs),
        nbytes=3 * 10**5, mib=8,
    )
    if not lined:
        me = lax.axis_index("gx")
        attention = jnp.concatenate(
            [lax.dynamic_index_in_dim(attention, me ^ j, 0, keepdims=False) for j in range(nx)],
            axis=1,
        )[None]
    return (fine_out, attention)


def solution(mesh):
    placed = (
        P("gx", "gy", "gz", None),
        P(None, "gy", "gz"),
        P(),
        P(),
        P(),
        P(),
        P(None, "gx", None),
    )
    return jax.shard_map(
        body,
        mesh=mesh,
        in_specs=placed,
        out_specs=(P("gx", "gy", "gz", None), P(("gy", "gz"), "gx", None)),
        check_vma=False,
    )
```

```python
import functools

import jax
import jax.numpy as jnp
from jax import lax
from jax.experimental import pallas as pl
from jax.experimental.pallas import tpu as pltpu
from jax.sharding import PartitionSpec as P

C = 32
GW = 4
HD = 64
BR = 8
EPS = 1e-05
SENT = 512.0
BIG = 1e30
ALL = ("gx", "gy", "gz")
F32, BF16 = jnp.float32, jnp.bfloat16
HIGHEST = lax.Precision.HIGHEST
TAIL = 16


def iota(shape, dim):
    return lax.broadcasted_iota(jnp.int32, shape, dim)


def onehot(cond, dtype=BF16):
    return jnp.where(cond, 1.0, 0.0).astype(dtype)


def exact_dot(a, b):
    return jnp.dot(a, b, precision=HIGHEST, preferred_element_type=F32)


def spread_sum(v):
    lane = iota(v.shape, 1)
    s = 1
    while s < GW * BR:
        v = v + jnp.where(lane & s == 0, pltpu.roll(v, 128 - s, 1), pltpu.roll(v, s, 1))
        s *= 2
    return v


def group_sum(total):
    k = total.shape[1] // 128
    rows = [jnp.broadcast_to(total[:, h * 128 : (h + 1) * 128], (8, 128)) for h in range(k)]
    out = spread_sum(jnp.concatenate(rows, axis=0))
    return jnp.concatenate([out[h * 8 : (h + 1) * 8] for h in range(k)], axis=1)


def moments(total, squares_about, count):
    sums = group_sum(total)
    squares = group_sum(squares_about((sums / count)[0:1]))
    return sums, squares, jnp.zeros(sums.shape, F32) + count


def merge(parts):
    n = sum(p[2] for p in parts)
    sums = sum(p[0] for p in parts)
    centre = sums / n
    squares = sum(p[1] + p[2] * (p[0] / p[2] - centre) ** 2 for p in parts)
    return sums, squares, n


def centre_scale(part):
    return part[0] / part[2], lax.rsqrt(part[1] / part[2] + EPS)


def to_row(part):
    j = iota((8, 128), 1) % (GW * BR)
    row = jnp.zeros((8, 128), F32)
    for h in range(2):
        for k in range(3):
            row = jnp.where(j == 4 * h + k, part[k][:, h * 128 : (h + 1) * 128], row)
    return row


def from_rows(rows):
    n = jnp.maximum(pltpu.roll(rows, 126, 1), 1.0)
    total = jnp.sum(n, axis=0, keepdims=True)
    centre = jnp.sum(rows, axis=0, keepdims=True) / total
    drift = rows / n - centre
    squares = pltpu.roll(rows, 127, 1) + n * drift * drift
    spread = jnp.sum(squares, axis=0, keepdims=True) / total
    j = iota((8, 128), 1) % (GW * BR)
    blocks = [
        jnp.where(j == 4 * h, jnp.broadcast_to(v, (8, 128)), 0.0)
        for v in (centre, spread) for h in range(2)
    ]
    out = spread_sum(jnp.concatenate(blocks, axis=0))
    out = [out[8 * i : 8 * i + 1] for i in range(4)]
    return (
        jnp.concatenate(out[:2], axis=1),
        lax.rsqrt(jnp.concatenate(out[2:], axis=1) + EPS),
    )


def to_tail(part):
    index = iota((8, 256), 0)
    blocks = [jnp.zeros((8, 256), F32), jnp.zeros((8, 256), F32)]
    for k, value in enumerate(part):
        value = jnp.broadcast_to(value[0:1], (8, 256))
        high = value.astype(BF16).astype(F32)
        mid = (value - high).astype(BF16).astype(F32)
        for i, piece in enumerate((high, mid, value - high - mid)):
            blocks[k // 2] = jnp.where(index == 3 * (k % 2) + i, piece, blocks[k // 2])
    return jnp.concatenate(blocks, axis=0).astype(BF16)


def from_tail(message_ref):
    rows = message_ref.shape[0]
    part = message_ref[rows - TAIL : rows, :].astype(F32)
    return [
        jnp.sum(part[r : r + 3], axis=0, keepdims=True) for r in (0, 3, 8)
    ]


def silu(u):
    return 0.5 * u * (1.0 + jnp.tanh(0.5 * u))


def pack_pairs(v):
    n, m, _, lanes = v.shape
    v = v.reshape(n, m // 2, 2, 8, lanes)
    low, high = v[:, :, 0].reshape(-1, 8, lanes), v[:, :, 1].reshape(-1, 8, lanes)
    both = jnp.where(iota(low.shape, 1) < 4, low, pltpu.roll(high, 4, 1))
    return both.reshape(n, m // 2, 8, lanes)


def split_pairs(v, blank):
    inside = iota(v.shape, 1) < 4
    return [jnp.where(inside, v, blank), jnp.where(inside, pltpu.roll(v, 4, 1), blank)]


def edges(act):
    z = iota(act.shape, 2) % BR
    before, after = pltpu.roll(act, 1, 1), pltpu.roll(act, 7, 1)
    return jnp.where(z == BR - 1, before, jnp.where(z == 0, after, 0.0))


def columns(act, size):
    side = edges(act)
    z = iota((size,) + act.shape[1:], 2) % BR
    second = pltpu.roll(side, 2, 2)
    third = pltpu.roll(side, 4, 2)
    mixed = jnp.where(
        (z == 1) | (z == 2), second[1 : 1 + size],
        jnp.where((z == 3) | (z == 4), third[2 : 2 + size], side[0:size]),
    )
    return [act[e : e + size] for e in range(3)] + [mixed]


def halves(lanes):
    return range(lanes // 128)


def read(ref, start, count, stride):
    return jnp.concatenate(
        [ref[h, pl.ds(start, count, stride=stride), :] for h in range(ref.shape[0])], axis=1
    )


def write(ref, start, count, stride, value):
    for h in range(ref.shape[0]):
        ref[h, pl.ds(start, count, stride=stride), :] = value[:, h * 128 : (h + 1) * 128]


def write_block(ref, start, value):
    for h in range(ref.shape[0]):
        ref[h, start : start + value.shape[0], :] = value[:, h * 128 : (h + 1) * 128]


def even(axis):
    return lax.axis_index(axis) % 2 == 0


def sides(axis, first, second):
    i, n = lax.axis_index(axis), lax.axis_size(axis)
    blank = jnp.full(first.shape, SENT, F32)
    second = blank if second is None else second
    low, high = jnp.where(even(axis), second, first), jnp.where(even(axis), first, second)
    return jnp.where(i > 0, low, SENT), jnp.where(i < n - 1, high, SENT)


def pre_kernel(members, occ_ref, feat_ref, keep_ref, keys_ref, coded_ref, first_ref, second_ref,
               tail_ref, rows_ref=None):
    sx, sy, sb, lanes = feat_ref.shape
    me = lax.axis_index("gx")
    bricks = [occ_ref[x].astype(F32) for x in range(members)]

    def row_of(x):
        return sum(jnp.where(x == i, v, 0.0) for i, v in enumerate(bricks))

    mine = jnp.broadcast_to(row_of(me), (8, sb))
    keep = jnp.where(iota((8, sb), 0) == iota((8, sb), 1), mine, 0.0)
    keep = jnp.broadcast_to(jnp.sum(keep, axis=1, keepdims=True), (8, lanes))
    count = jnp.sum(keep, axis=0, keepdims=True) * float(sx * sy * BR * GW)
    keep_ref[...] = keep
    seq = keys_ref.shape[1]
    lane = iota((1, seq), 1)
    keys = jnp.zeros((1, seq), F32)
    for k in range(members):
        there = row_of(me ^ k)
        for b in range(sb):
            keys = jnp.where(
                (lane // (seq // members) == k) & (lane % (2 * sb) // 2 == b),
                there[:, b : b + 1], keys,
            )
    keys_ref[...] = jnp.broadcast_to(keys, keys_ref.shape)
    field = feat_ref[...].astype(F32)
    wide = jnp.concatenate([field, jnp.zeros((sx, sy, 8 - sb, lanes), F32)], axis=2)
    wide = wide.reshape(sx * sy, 8, lanes)
    total = jnp.sum(jnp.sum(wide, axis=0) * keep, axis=0, keepdims=True)

    def squares_about(mean):
        d = wide - mean[None]
        return jnp.sum(jnp.sum(d * d, axis=0) * keep, axis=0, keepdims=True)

    code = jnp.where((keep > 0)[None], wide, SENT)
    coded_ref[...] = code.reshape(sx * sy * 8, lanes).astype(BF16)
    packed = pack_pairs(code.reshape(sx, sy, 8, lanes))
    low = packed[0:2].reshape(-1, lanes)
    high = packed[sx - 2 : sx].reshape(-1, lanes)
    size = low.shape[0]
    first_ref[0:size, :] = jnp.where(even("gx"), high, low).astype(BF16)
    second_ref[0:size, :] = jnp.where(even("gx"), low, high).astype(BF16)
    mine = moments(total, squares_about, count)
    tail = to_tail(mine)
    first_ref[size : size + TAIL, :] = tail
    second_ref[size : size + TAIL, :] = tail
    tail_ref[...] = tail
    if rows_ref is not None:
        rows_ref[...] = jnp.broadcast_to(to_row(mine)[0:1], rows_ref.shape)


def line_kernel(narrow, sy, sb, _, coded_ref, first_ref, second_ref, *rest):
    tails, (ext_ref, out_ref, buf) = rest[:-3], rest[-3:]
    lanes = coded_ref.shape[1]
    sx = coded_ref.shape[0] // (sy * 8)
    size = 2 * (sy // 2) * 8
    low, high = sides(
        "gx", first_ref[0:size].astype(F32), second_ref[0:size].astype(F32)
    )
    write_block(buf, 2 * sy * 8, coded_ref[...].astype(F32))
    for x0, side in ((0, low), (sx + 2, high)):
        for i in range(2):
            part = side[i * (size // 2) : (i + 1) * (size // 2)].reshape(sy // 2, 8, lanes)
            pair = split_pairs(part, SENT)
            for y in range(sy):
                write_block(buf, ((x0 + i) * sy + y) * 8, pair[y % 2][y // 2])
    rows = (sx + 4) * sy * 8
    ext_ref[...] = jnp.concatenate([buf[h] for h in halves(lanes)], axis=1).astype(BF16)
    count = (sx + 4) * sy
    face = jnp.where(even("gz"), read(buf, sb - 1, count, 8), read(buf, 0, count, 8))
    out_ref[0:count, :] = face.astype(BF16)
    mine = [from_tail(ref) for ref in tails]
    if narrow:
        mine = mine + [from_tail(first_ref), from_tail(second_ref)]
    out_ref[count : count + TAIL, :] = to_tail(merge(mine))


def corner_rows(count):
    return (count + 15) // 16 * 16


def chip_kernel(sb, sy, ext_ref, own_ref, other_ref, *rest):
    out, (buf, stage) = rest[:-2], rest[-2:]
    lanes = ext_ref.shape[1]
    ex = ext_ref.shape[0] // (sy * 8)
    block = ext_ref[...].astype(F32)
    write_block(buf, 0, block)
    write_block(stage, 0, other_ref[0 : ex * sy].astype(F32))
    gap = corner_rows(ex)
    pad = jnp.zeros((gap - ex, lanes), F32)
    tail = to_tail(merge([from_tail(own_ref), from_tail(other_ref)]))
    packed = pack_pairs(block.reshape(ex, sy, 8, lanes))

    def side(y0):
        face = packed[:, y0 // 2].reshape(ex * 8, lanes)
        inner, outer = [], []
        for i in range(2):
            inner += [read(stage, y0 + i, ex, sy), pad]
            start = (y0 + i) * 8
            outer += [
                jnp.where(
                    even("gz"),
                    read(buf, start, ex, sy * 8),
                    read(buf, start + sb - 1, ex, sy * 8),
                ),
                pad,
            ]
        return [face] + inner, outer

    (near_low, far_low), (near_high, far_high) = side(0), side(sy - 2)
    count = ex * sy
    z_face = jnp.where(even("gz"), read(buf, 0, count, 8), read(buf, sb - 1, count, 8))
    out[0][0:count, :] = z_face.astype(BF16)
    out[0][count : count + TAIL, :] = tail
    for k in range((len(out) - 1) // 2):
        up = even("gy") if k == 0 else jnp.logical_not(even("gy"))
        for ref, low, high in (
            (out[1 + 2 * k], near_low, near_high),
            (out[2 + 2 * k], far_low, far_high),
        ):
            value = jnp.where(
                up, jnp.concatenate(high, axis=0), jnp.concatenate(low, axis=0)
            ).astype(BF16)
            ref[0 : value.shape[0], :] = value
            ref[value.shape[0] : value.shape[0] + TAIL, :] = tail


def band_kernel(weight_ref, *rest):
    pars, (out_ref, more_ref) = rest[:-2], rest[-2:]
    lanes = C * BR
    spread = onehot(iota((C, lanes), 0) == iota((C, lanes), 1) // BR)
    turned = jnp.transpose(weight_ref[0].astype(F32)).astype(BF16)
    wide = jnp.dot(turned, spread, preferred_element_type=F32)
    full = (C, BR, lanes)
    zi, zo = iota((1, BR, lanes), 1), iota((1, BR, lanes), 2) % BR

    def rows(value):
        return jnp.broadcast_to(value[:, None, :], full)

    for ex in range(3):
        mixed = jnp.zeros(full, F32)
        for ey in range(3):
            q = (ex * 3 + ey) * 3
            terms = [wide[(q + e) * C : (q + e + 1) * C] for e in range(3)]
            inner = jnp.where(zi == zo - 1, rows(terms[0]), 0.0)
            inner = jnp.where(zi == zo, rows(terms[1]), inner)
            inner = jnp.where(zi == zo + 1, rows(terms[2]), inner)
            before = pltpu.roll(terms[0], 1, 0) if ey else terms[0]
            low = 2 * ey - 1 if ey else BR - 1
            mixed = jnp.where((zi == low) & (zo == 0), rows(before), mixed)
            mixed = jnp.where((zi == 2 * ey) & (zo == BR - 1), rows(terms[2]), mixed)
            out_ref[ex, ey * lanes : (ey + 1) * lanes, :] = (
                inner.reshape(C * BR, lanes).astype(BF16)
            )
        out_ref[ex, 3 * lanes : 4 * lanes, :] = mixed.reshape(C * BR, lanes).astype(BF16)
    if pars:
        pick = onehot(iota((C, lanes), 0) == iota((C, lanes), 1) // BR, F32)
        more_ref[...] = jnp.zeros(more_ref.shape, F32)
        more_ref[0 : pars[0].shape[0], :] = exact_dot(pars[0][...], pick)
    else:
        more_ref[...] = weight_ref[1:2]


def turn_kernel(weight_ref, out_ref):
    kinds, cols, feats = weight_ref.shape
    r = iota((feats, 1), 0)
    source = (r % 128) // 4 * 32 + r // 128 * 4 + r % 4
    pick = onehot(source == iota((feats, feats), 1))
    for k in range(kinds):
        out_ref[:, k * cols : (k + 1) * cols] = lax.dot_general(
            pick, weight_ref[k], (((1,), (1,)), ((), ())), preferred_element_type=F32
        ).astype(BF16)


def first_kernel(narrow, faces, sy, sb, ext_ref, own_ref, core_ref, zface_ref, *rest):
    near, far = rest[0 : 2 * faces : 2], rest[1 : 2 * faces : 2]
    rest = rest[2 * faces :]
    stats_ref = None
    if not narrow:
        stats_ref, rest = rest[0], rest[1:]
    keep_ref, weight_ref, rows_ref, mid_ref, out_ref, msk, buf, lhs = rest
    lanes = ext_ref.shape[1]
    ex = ext_ref.shape[0] // (sy * 8)
    ey = sy + 4
    count = ex * sy
    z_low, z_high = sides(
        "gz", core_ref[0:count].astype(F32), zface_ref[0:count].astype(F32)
    )
    for x in range(ex):
        write_block(
            buf, (x * ey + 2) * 8, ext_ref[x * sy * 8 : (x + 1) * sy * 8].astype(F32)
        )
        part = slice(x * sy, (x + 1) * sy)
        write(buf, (x * ey + 2) * 8 + 7, sy, 8, z_low[part])
        write(buf, (x * ey + 2) * 8 + sb, sy, 8, z_high[part])
    gap = corner_rows(ex)
    size = ex * 8
    face = sides("gy", *[
        near[k][0:size].astype(F32) if k < faces else None for k in range(2)
    ])
    inner = sides("gy", *[
        near[k][size : size + 2 * gap].astype(F32) if k < faces else None for k in range(2)
    ])
    outer = sides("gy", *[
        far[k][0 : 2 * gap].astype(F32) if k < faces else None for k in range(2)
    ])
    for s, y0 in enumerate((0, sy + 2)):
        pair = split_pairs(face[s].reshape(ex, 8, lanes), SENT)
        c_low, c_high = sides("gz", inner[s], outer[s])
        for i in range(2):
            for x in range(ex):
                write_block(buf, (x * ey + y0 + i) * 8, pair[i][x])
            write(buf, (y0 + i) * 8 + 7, ex, ey * 8, c_low[i * gap : i * gap + ex])
            write(buf, (y0 + i) * 8 + sb, ex, ey * 8, c_high[i * gap : i * gap + ex])
    if narrow:
        centre, scale = centre_scale(merge(
            [from_tail(r) for r in (own_ref, zface_ref) + tuple(near) + tuple(far)]
        ))
    else:
        centre, scale = from_rows(stats_ref[...])
    gain, shift, bias = rows_ref[0:1], rows_ref[2:3], rows_ref[4:5]
    scale = scale * gain
    oy, sx = sy + 2, ex - 4
    step = ey * 8
    for x in range(ex):
        v = jnp.concatenate(
            [buf[h, x * step : (x + 1) * step, :] for h in halves(lanes)], axis=1
        )
        there = v != SENT
        msk[x * step : (x + 1) * step] = onehot(there[:, 0:128], F32)
        act = jnp.where(there, silu((v - centre) * scale + shift), 0.0).reshape(ey, 8, lanes)
        for e, part in enumerate(columns(act, oy)):
            lhs[x * oy * 8 : (x + 1) * oy * 8, e * lanes : (e + 1) * lanes] = (
                part.reshape(oy * 8, lanes).astype(BF16)
            )
    ox = sx + 2
    size = ox * oy * 8
    acc = bias
    for e in range(3):
        acc = acc + jnp.dot(
            lhs[e * oy * 8 : e * oy * 8 + size, :], weight_ref[e], preferred_element_type=F32
        )
    mid_ref[...] = acc
    keep = keep_ref[...]
    entries = jnp.sum(keep[:, 0:1]) * float(sx * sy * BR * GW)

    def over_cells(f):
        out = jnp.zeros((8, lanes), F32)
        for x in range(1, sx + 1):
            own = mid_ref[(x * oy + 1) * 8 : (x * oy + oy - 1) * 8].reshape(sy, 8, lanes)
            out = out + jnp.sum(f(own), axis=0)
        return jnp.sum(out * keep, axis=0, keepdims=True)

    def squares_about(mean):
        return over_cells(lambda v: (v - mean[None]) * (v - mean[None]))

    mine = moments(over_cells(lambda v: v), squares_about, entries)
    out_ref[...] = jnp.broadcast_to(to_row(mine)[0:1], out_ref.shape)


def second_kernel(sx, sy, sb, stats_ref, mid_ref, msk_ref, weight_ref, rows_ref, coded_ref,
                  field_ref, tok_ref, low_ref, high_ref, lhs):
    lanes = coded_ref.shape[1]
    step, ext = (sy + 2) * 8, (sy + 4) * 8
    centre, scale = from_rows(stats_ref[...])
    gain, shift, bias = rows_ref[1:2], rows_ref[3:4], rows_ref[5:6]
    scale = scale * gain
    half = sy // 2 * 8
    for x in range(sx + 2):
        v = mid_ref[x * step : (x + 1) * step]
        there = msk_ref[(x + 1) * ext + 8 : (x + 2) * ext - 8]
        there = jnp.concatenate([there] * (lanes // 128), axis=1) > 0
        act = jnp.where(there, silu((v - centre) * scale + shift), 0.0)
        for e, part in enumerate(columns(act.reshape(sy + 2, 8, lanes), sy)):
            lhs[x * half : (x + 1) * half, e * lanes : (e + 1) * lanes] = (
                pack_pairs(part[None]).reshape(half, lanes).astype(BF16)
            )
    size = sx * half
    acc = bias
    for e in range(3):
        acc = acc + jnp.dot(
            lhs[e * half : e * half + size, :], weight_ref[e], preferred_element_type=F32
        )
    field = pack_pairs(coded_ref[...].astype(F32).reshape(sx, sy, 8, lanes))
    field = field.reshape(size, lanes)
    out = jnp.where(field != SENT, field + acc, 0.0).reshape(-1, 8, lanes)
    out = out.astype(BF16)
    field_ref[...] = out.reshape(size, lanes)
    i, j = iota((lanes, lanes), 0), iota((lanes, lanes), 1)
    pick = onehot(i == (j % 128) // 4 * 8 + j // 128 * 4 + j % 4)
    moved = jnp.dot(out.reshape(size, lanes), pick, preferred_element_type=F32).reshape(
        sx // 2, 2, sy // 4, 2, 8, lanes
    )
    count = sx // 2 * (sy // 4)
    parts = []
    for x in range(2):
        for y in range(2):
            piece = moved[:, x, :, y].reshape(count, 8, lanes)
            low, high = piece[:, :, :128], piece[:, :, 128:]
            inside = iota(low.shape, 1) < 4
            for both in (
                jnp.where(inside, low, pltpu.roll(high, 4, 1)),
                jnp.where(inside, pltpu.roll(low, 4, 1), high),
            ):
                parts.append(both.reshape(count * 8, 128).astype(BF16))
    tokens = jnp.concatenate(parts, axis=1)
    n = count * 8
    i, j = iota((n, n), 0), iota((n, n), 1)
    order = onehot(j == i // 8 * 8 + i % 2 * 4 + i % 8 // 2)
    tokens = jnp.dot(order, tokens, preferred_element_type=F32).astype(BF16)
    tok_ref[...] = tokens
    low_ref[...] = tokens[0 : n // 2]
    high_ref[...] = tokens[n // 2 : n]


def fine_kernel(field_ref, fine_ref):
    sx, sy, sb, lanes = fine_ref.shape
    wide = field_ref[...].astype(F32).reshape(-1, 8, lanes)
    other = pltpu.roll(wide, 4, 1)
    fine = jnp.stack([wide[:, :sb], other[:, :sb]], axis=1)
    fine_ref[...] = fine.reshape(sx, sy, sb, lanes).astype(BF16)


def attend_kernel(members, keys_ref, weight_ref, *refs):
    tok_refs, out_refs, (toks, proj) = refs[: -2 - members], refs[-2 - members : -2], refs[-2:]
    own, cols = tok_refs[0].shape[0], weight_ref.shape[1] // 3
    seq = own * members
    start = 0
    for ref in tok_refs:
        toks[start : start + ref.shape[0], :] = ref[...]
        start += ref.shape[0]
    proj[...] = jnp.dot(toks[...], weight_ref[...], preferred_element_type=F32).astype(BF16)
    there = keys_ref[0:1] > 0
    width = min(128, cols)
    for t in range(cols // width):
        q = proj[:, t * width : (t + 1) * width]
        keys = proj[:, cols + t * width : cols + (t + 1) * width]
        values = proj[:, 2 * cols + t * width : 2 * cols + (t + 1) * width]
        head = iota((seq, width), 1) // HD
        merged = jnp.zeros((seq, width), F32)
        for h in range(width // HD):
            mine = jnp.where(head == h, q.astype(F32), 0.0).astype(BF16)
            scores = lax.dot_general(
                mine, keys, (((1,), (1,)), ((), ())), preferred_element_type=F32
            ) * float(HD) ** (-0.5)
            scores = jnp.where(there, scores, -BIG)
            probs = jnp.exp(scores - jnp.max(scores, axis=1, keepdims=True))
            total = jnp.sum(probs, axis=1, keepdims=True)
            mixed = jnp.dot(probs.astype(BF16), values, preferred_element_type=F32)
            merged = jnp.where(head == h, mixed / total, merged)
        merged = merged.astype(BF16)
        for k in range(members):
            out_refs[-1 - k][:, t * width : (t + 1) * width] = merged[k * own : (k + 1) * own]


def place_kernel(members, keep_ref, *refs):
    out_ref = refs[-1]
    own, cols = refs[0].shape
    me = lax.axis_index("gx")
    row = iota((8, cols), 0)
    keep = jnp.zeros((8, cols), F32)
    for b in range(4):
        keep = jnp.where(row // 2 == b, jnp.broadcast_to(keep_ref[b : b + 1, :cols], (8, cols)), keep)
    for k in range(members):
        value = refs[members - 1 - k][...].astype(F32).reshape(own // 8, 8, cols)
        value = jnp.where((keep > 0)[None], value, 0.0).reshape(own, cols).astype(BF16)
        if cols % 128 == 0:
            out_ref[0, :, pl.ds(pl.multiple_of((me ^ k) * cols, cols), cols)] = value
        else:
            out_ref[k] = value


VM = pl.BlockSpec(memory_space=pltpu.VMEM)


def call(kernel, name, specs, out, args, scratch=(), flops=0, nbytes=0, mib=16):
    return pl.pallas_call(
        kernel,
        out_shape=out,
        in_specs=list(specs),
        out_specs=jax.tree.map(lambda _: VM, out),
        scratch_shapes=list(scratch),
        name=name,
        cost_estimate=pl.CostEstimate(flops=flops, bytes_accessed=nbytes, transcendentals=0),
        compiler_params=pltpu.CompilerParams(vmem_limit_bytes=mib * 2**20),
    )(*args)


def shape(*dims, dtype=BF16):
    return jax.ShapeDtypeStruct(dims, dtype)


def pairing(n, odd, closed):
    partner = {i: (i ^ 1 if not odd else (i + 1 if i % 2 else i - 1)) for i in range(n)}
    if closed:
        partner = {i: j % n for i, j in partner.items()}
    return {i: j for i, j in partner.items() if 0 <= j < n and i != j}


def body(features, occupancy, norm_gain, norm_shift, conv_weight, conv_bias, qkv_weight):
    sx, sy, sb, lanes = features.shape
    nx, ny, nz = (lax.axis_size(a) for a in ALL)
    devices = nx * ny * nz
    narrow = nx == 4 and ny == 2 and nz == 4
    own = sx // 2 * (sy // 4) * sb * 2
    ex = sx + 4
    row_shape = [] if narrow else [shape(devices, 128, dtype=F32)]

    slab = sy * 8 + TAIL
    keep, keys, coded, first, second, tail, *stats = call(
        functools.partial(pre_kernel, nx), "pre", (VM, VM),
        [shape(8, lanes, dtype=F32), shape(8, own * nx, dtype=F32),
         shape(sx * sy * 8, lanes), shape(slab, lanes), shape(slab, lanes), shape(TAIL, lanes)]
        + row_shape,
        (occupancy, features), nbytes=10**6,
    )
    stats = [lax.all_to_all(s, ALL, 0, 0, tiled=True) for s in stats]
    got = [
        lax.ppermute(first, "gx", list(pairing(nx, False, False).items())),
        lax.ppermute(second, "gx", list(pairing(nx, True, narrow).items())),
    ]
    tails = [tail]
    if narrow:
        tails.append(lax.ppermute(tail, "gx", [(i, i ^ 2) for i in range(nx)]))
    band = shape(3, 4 * lanes, lanes)
    pars = jnp.concatenate([norm_gain, norm_shift, conv_bias], axis=0)
    later = shape(1, *conv_weight.shape[1:])
    band0, later = call(
        band_kernel, "band0", (VM,), [band, later], (conv_weight,), nbytes=8 * 10**6,
    )
    band1, rows = call(
        band_kernel, "band1", (VM,) * 2, [band, shape(8, lanes, dtype=F32)], (later, pars),
        nbytes=8 * 10**6,
    )
    count = ex * sy
    ext, mine = call(
        functools.partial(line_kernel, narrow, sy, sb), "line", (VM,) * (4 + len(tails)),
        [shape(count * 8, lanes), shape(count + TAIL, lanes)],
        (later, coded, *got, *tails),
        [pltpu.VMEM((lanes // 128, count * 8, 128), F32)], nbytes=10**6,
    )
    core = lax.ppermute(mine, "gz", list(pairing(nz, False, False).items()))

    faces = 1 if ny == 2 else 2
    gap = corner_rows(ex)
    near, far = ex * 8 + 2 * gap + TAIL, 2 * gap + TAIL
    zface, *yfaces = call(
        functools.partial(chip_kernel, sb, sy), "chip", (VM,) * 3,
        [shape(count + TAIL, lanes)] + [shape(near, lanes), shape(far, lanes)] * faces,
        (ext, mine, core),
        [pltpu.VMEM((lanes // 128, count * 8, 128), F32),
         pltpu.VMEM((lanes // 128, count, 128), F32)], nbytes=10**6,
    )
    odd_z = pairing(nz, True, narrow)
    own_tail = zface
    zgot = lax.ppermute(zface, "gz", list(odd_z.items()))
    ygot = []
    for k in range(faces):
        along = pairing(ny, k == 1, False)
        ygot.append(lax.ppermute(yfaces[2 * k], "gy", list(along.items())))
        both = [
            (y * nz + z, along[y] * nz + odd_z[z]) for y in along for z in odd_z
        ]
        ygot.append(lax.ppermute(yfaces[2 * k + 1], ("gy", "gz"), both))

    cols, feats = qkv_weight.shape[1:]
    turned = call(
        turn_kernel, "turn", (VM,), shape(feats, 3 * cols), (qkv_weight,),
        flops=2 * 3 * cols * feats * feats, nbytes=6 * 10**6,
    )

    ey, oy = sy + 4, sy + 2
    size = (sx + 2) * oy * 8
    mid, mine, there = call(
        functools.partial(first_kernel, narrow, faces, sy, sb), "first",
        (VM,) * (7 + 2 * faces + len(stats)),
        [shape(size, lanes, dtype=F32), shape(devices, 128, dtype=F32),
         shape(ex * ey * 8, 128, dtype=F32)],
        (ext, own_tail, core, zgot, *ygot, *stats, keep, band0, rows),
        [pltpu.VMEM((lanes // 128, ex * ey * 8, 128), F32),
         pltpu.VMEM((ex * oy * 8, 4 * lanes), BF16)],
        flops=2 * 10**9, nbytes=4 * 10**6, mib=20,
    )
    stats = lax.all_to_all(mine, ALL, 0, 0, tiled=True)
    field, tokens, *parts = call(
        functools.partial(second_kernel, sx, sy, sb), "second", (VM,) * 6,
        [shape(sx * sy * 4, lanes), shape(own, feats)] + [shape(own // 2, feats)] * 2,
        (stats, mid, there, band1, rows, coded),
        [pltpu.VMEM(((sx + 2) * sy * 4, 4 * lanes), BF16)],
        flops=10**9, nbytes=4 * 10**6,
    )
    fine_out = call(
        fine_kernel, "fine", (VM,), shape(*features.shape), (field,), nbytes=4 * 10**6, mib=8,
    )
    swaps = [[(i, i ^ k) for i in range(nx)] for k in range(nx)]
    blocks = {0: parts}
    for k in sorted(range(1, nx), key=lambda k: (bin(k).count("1"), -k)):
        low = k & -k
        source = [tokens] if k == 1 else blocks[k ^ low]
        if k == 1 and nx > 2:
            part, source[0], turned = lax.optimization_barrier((blocks[2][0], tokens, turned))
            blocks[2] = [part] + blocks[2][1:]
        blocks[k] = [lax.ppermute(v, "gx", swaps[low]) for v in source]
    blocks = [tokens] + [v for k in range(1, nx) for v in blocks[k]]
    outs = call(
        functools.partial(attend_kernel, nx), "attend", (VM,) * (2 + len(blocks)),
        [shape(own, cols)] * nx, (keys, turned, *blocks),
        [pltpu.VMEM((own * nx, feats), BF16), pltpu.VMEM((own * nx, 3 * cols), BF16)],
        flops=10**9, nbytes=3 * 10**6, mib=16 if narrow else 40,
    )
    moved = [lax.ppermute(v, "gx", swaps[nx - 1 - i]) for i, v in enumerate(outs[:-1])]
    outs = moved + [outs[-1]]
    lined = cols % 128 == 0
    attention = call(
        functools.partial(place_kernel, nx), "place", (VM,) * (1 + nx),
        shape(1, own, nx * cols) if lined else shape(nx, own, cols), (keep, *outs),
        nbytes=3 * 10**5, mib=8,
    )
    if not lined:
        me = lax.axis_index("gx")
        attention = jnp.concatenate(
            [lax.dynamic_index_in_dim(attention, me ^ j, 0, keepdims=False) for j in range(nx)],
            axis=1,
        )[None]
    return (fine_out, attention)


def solution(mesh):
    placed = (
        P("gx", "gy", "gz", None),
        P(None, "gy", "gz"),
        P(),
        P(),
        P(),
        P(),
        P(None, "gx", None),
    )
    return jax.shard_map(
        body,
        mesh=mesh,
        in_specs=placed,
        out_specs=(P("gx", "gy", "gz", None), P(("gy", "gz"), "gx", None)),
        check_vma=False,
    )
```

```python
import functools

import jax
import jax.numpy as jnp
from jax import lax
from jax.experimental import pallas as pl
from jax.experimental.pallas import tpu as pltpu
from jax.sharding import PartitionSpec as P

C = 32
GW = 4
HD = 64
BR = 8
EPS = 1e-05
SENT = 512.0
BIG = 1e30
ALL = ("gx", "gy", "gz")
F32, BF16 = jnp.float32, jnp.bfloat16
HIGHEST = lax.Precision.HIGHEST
TAIL = 16


def iota(shape, dim):
    return lax.broadcasted_iota(jnp.int32, shape, dim)


def onehot(cond, dtype=BF16):
    return jnp.where(cond, 1.0, 0.0).astype(dtype)


def exact_dot(a, b):
    return jnp.dot(a, b, precision=HIGHEST, preferred_element_type=F32)


def spread_sum(v):
    lane = iota(v.shape, 1)
    s = 1
    while s < GW * BR:
        v = v + jnp.where(lane & s == 0, pltpu.roll(v, 128 - s, 1), pltpu.roll(v, s, 1))
        s *= 2
    return v


def group_sum(total):
    k = total.shape[1] // 128
    rows = [jnp.broadcast_to(total[:, h * 128 : (h + 1) * 128], (8, 128)) for h in range(k)]
    out = spread_sum(jnp.concatenate(rows, axis=0))
    return jnp.concatenate([out[h * 8 : (h + 1) * 8] for h in range(k)], axis=1)


def moments(total, squares_about, count):
    sums = group_sum(total)
    squares = group_sum(squares_about((sums / count)[0:1]))
    return sums, squares, jnp.zeros(sums.shape, F32) + count


def merge(parts):
    n = sum(p[2] for p in parts)
    sums = sum(p[0] for p in parts)
    centre = sums / n
    squares = sum(p[1] + p[2] * (p[0] / p[2] - centre) ** 2 for p in parts)
    return sums, squares, n


def centre_scale(part):
    return part[0] / part[2], lax.rsqrt(part[1] / part[2] + EPS)


def to_row(part):
    j = iota((8, 128), 1) % (GW * BR)
    row = jnp.zeros((8, 128), F32)
    for h in range(2):
        for k in range(3):
            row = jnp.where(j == 4 * h + k, part[k][:, h * 128 : (h + 1) * 128], row)
    return row


def from_rows(rows):
    n = jnp.maximum(pltpu.roll(rows, 126, 1), 1.0)
    total = jnp.sum(n, axis=0, keepdims=True)
    centre = jnp.sum(rows, axis=0, keepdims=True) / total
    drift = rows / n - centre
    squares = pltpu.roll(rows, 127, 1) + n * drift * drift
    spread = jnp.sum(squares, axis=0, keepdims=True) / total
    j = iota((8, 128), 1) % (GW * BR)
    blocks = [
        jnp.where(j == 4 * h, jnp.broadcast_to(v, (8, 128)), 0.0)
        for v in (centre, spread) for h in range(2)
    ]
    out = spread_sum(jnp.concatenate(blocks, axis=0))
    out = [out[8 * i : 8 * i + 1] for i in range(4)]
    return (
        jnp.concatenate(out[:2], axis=1),
        lax.rsqrt(jnp.concatenate(out[2:], axis=1) + EPS),
    )


def to_tail(part):
    index = iota((8, 256), 0)
    blocks = [jnp.zeros((8, 256), F32), jnp.zeros((8, 256), F32)]
    for k, value in enumerate(part):
        value = jnp.broadcast_to(value[0:1], (8, 256))
        high = value.astype(BF16).astype(F32)
        mid = (value - high).astype(BF16).astype(F32)
        for i, piece in enumerate((high, mid, value - high - mid)):
            blocks[k // 2] = jnp.where(index == 3 * (k % 2) + i, piece, blocks[k // 2])
    return jnp.concatenate(blocks, axis=0).astype(BF16)


def from_tail(message_ref):
    rows = message_ref.shape[0]
    part = message_ref[rows - TAIL : rows, :].astype(F32)
    return [
        jnp.sum(part[r : r + 3], axis=0, keepdims=True) for r in (0, 3, 8)
    ]


def silu(u):
    return 0.5 * u * (1.0 + jnp.tanh(0.5 * u))


def pack_pairs(v):
    n, m, _, lanes = v.shape
    v = v.reshape(n, m // 2, 2, 8, lanes)
    low, high = v[:, :, 0].reshape(-1, 8, lanes), v[:, :, 1].reshape(-1, 8, lanes)
    both = jnp.where(iota(low.shape, 1) < 4, low, pltpu.roll(high, 4, 1))
    return both.reshape(n, m // 2, 8, lanes)


def split_pairs(v, blank):
    inside = iota(v.shape, 1) < 4
    return [jnp.where(inside, v, blank), jnp.where(inside, pltpu.roll(v, 4, 1), blank)]


def edges(act):
    z = iota(act.shape, 2) % BR
    before, after = pltpu.roll(act, 1, 1), pltpu.roll(act, 7, 1)
    return jnp.where(z == BR - 1, before, jnp.where(z == 0, after, 0.0))


def columns(act, size):
    side = edges(act)
    z = iota((size,) + act.shape[1:], 2) % BR
    second = pltpu.roll(side, 2, 2)
    third = pltpu.roll(side, 4, 2)
    mixed = jnp.where(
        (z == 1) | (z == 2), second[1 : 1 + size],
        jnp.where((z == 3) | (z == 4), third[2 : 2 + size], side[0:size]),
    )
    return [act[e : e + size] for e in range(3)] + [mixed]


def halves(lanes):
    return range(lanes // 128)


def read(ref, start, count, stride):
    return jnp.concatenate(
        [ref[h, pl.ds(start, count, stride=stride), :] for h in range(ref.shape[0])], axis=1
    )


def write(ref, start, count, stride, value):
    for h in range(ref.shape[0]):
        ref[h, pl.ds(start, count, stride=stride), :] = value[:, h * 128 : (h + 1) * 128]


def write_block(ref, start, value):
    for h in range(ref.shape[0]):
        ref[h, start : start + value.shape[0], :] = value[:, h * 128 : (h + 1) * 128]


def even(axis):
    return lax.axis_index(axis) % 2 == 0


def sides(axis, first, second):
    i, n = lax.axis_index(axis), lax.axis_size(axis)
    blank = jnp.full(first.shape, SENT, F32)
    second = blank if second is None else second
    low, high = jnp.where(even(axis), second, first), jnp.where(even(axis), first, second)
    return jnp.where(i > 0, low, SENT), jnp.where(i < n - 1, high, SENT)


def pre_kernel(members, occ_ref, feat_ref, keep_ref, keys_ref, coded_ref, first_ref, second_ref,
               tail_ref, rows_ref=None):
    sx, sy, sb, lanes = feat_ref.shape
    me = lax.axis_index("gx")
    bricks = [occ_ref[x].astype(F32) for x in range(members)]

    def row_of(x):
        return sum(jnp.where(x == i, v, 0.0) for i, v in enumerate(bricks))

    mine = jnp.broadcast_to(row_of(me), (8, sb))
    keep = jnp.where(iota((8, sb), 0) == iota((8, sb), 1), mine, 0.0)
    keep = jnp.broadcast_to(jnp.sum(keep, axis=1, keepdims=True), (8, lanes))
    count = jnp.sum(keep, axis=0, keepdims=True) * float(sx * sy * BR * GW)
    keep_ref[...] = keep
    seq = keys_ref.shape[1]
    lane = iota((1, seq), 1)
    keys = jnp.zeros((1, seq), F32)
    for k in range(members):
        there = row_of(me ^ k)
        for b in range(sb):
            keys = jnp.where(
                (lane // (seq // members) == k) & (lane % (2 * sb) // 2 == b),
                there[:, b : b + 1], keys,
            )
    keys_ref[...] = jnp.broadcast_to(keys, keys_ref.shape)
    field = feat_ref[...].astype(F32)
    wide = jnp.concatenate([field, jnp.zeros((sx, sy, 8 - sb, lanes), F32)], axis=2)
    wide = wide.reshape(sx * sy, 8, lanes)
    total = jnp.sum(jnp.sum(wide, axis=0) * keep, axis=0, keepdims=True)

    def squares_about(mean):
        d = wide - mean[None]
        return jnp.sum(jnp.sum(d * d, axis=0) * keep, axis=0, keepdims=True)

    code = jnp.where((keep > 0)[None], wide, SENT)
    coded_ref[...] = code.reshape(sx * sy * 8, lanes).astype(BF16)
    packed = pack_pairs(code.reshape(sx, sy, 8, lanes))
    low = packed[0:2].reshape(-1, lanes)
    high = packed[sx - 2 : sx].reshape(-1, lanes)
    size = low.shape[0]
    first_ref[0:size, :] = jnp.where(even("gx"), high, low).astype(BF16)
    second_ref[0:size, :] = jnp.where(even("gx"), low, high).astype(BF16)
    mine = moments(total, squares_about, count)
    tail = to_tail(mine)
    first_ref[size : size + TAIL, :] = tail
    second_ref[size : size + TAIL, :] = tail
    tail_ref[...] = tail
    if rows_ref is not None:
        rows_ref[...] = jnp.broadcast_to(to_row(mine)[0:1], rows_ref.shape)


def line_kernel(narrow, sy, sb, _, coded_ref, first_ref, second_ref, *rest):
    tails, (ext_ref, out_ref, buf) = rest[:-3], rest[-3:]
    lanes = coded_ref.shape[1]
    sx = coded_ref.shape[0] // (sy * 8)
    size = 2 * (sy // 2) * 8
    low, high = sides(
        "gx", first_ref[0:size].astype(F32), second_ref[0:size].astype(F32)
    )
    write_block(buf, 2 * sy * 8, coded_ref[...].astype(F32))
    for x0, side in ((0, low), (sx + 2, high)):
        for i in range(2):
            part = side[i * (size // 2) : (i + 1) * (size // 2)].reshape(sy // 2, 8, lanes)
            pair = split_pairs(part, SENT)
            for y in range(sy):
                write_block(buf, ((x0 + i) * sy + y) * 8, pair[y % 2][y // 2])
    rows = (sx + 4) * sy * 8
    ext_ref[...] = jnp.concatenate([buf[h] for h in halves(lanes)], axis=1).astype(BF16)
    count = (sx + 4) * sy
    face = jnp.where(even("gz"), read(buf, sb - 1, count, 8), read(buf, 0, count, 8))
    out_ref[0:count, :] = face.astype(BF16)
    mine = [from_tail(ref) for ref in tails]
    if narrow:
        mine = mine + [from_tail(first_ref), from_tail(second_ref)]
    out_ref[count : count + TAIL, :] = to_tail(merge(mine))


def corner_rows(count):
    return (count + 15) // 16 * 16


def chip_kernel(sb, sy, ext_ref, own_ref, other_ref, *rest):
    out, (buf, stage) = rest[:-2], rest[-2:]
    lanes = ext_ref.shape[1]
    ex = ext_ref.shape[0] // (sy * 8)
    block = ext_ref[...].astype(F32)
    write_block(buf, 0, block)
    write_block(stage, 0, other_ref[0 : ex * sy].astype(F32))
    gap = corner_rows(ex)
    pad = jnp.zeros((gap - ex, lanes), F32)
    tail = to_tail(merge([from_tail(own_ref), from_tail(other_ref)]))
    packed = pack_pairs(block.reshape(ex, sy, 8, lanes))

    def side(y0):
        face = packed[:, y0 // 2].reshape(ex * 8, lanes)
        inner, outer = [], []
        for i in range(2):
            inner += [read(stage, y0 + i, ex, sy), pad]
            start = (y0 + i) * 8
            outer += [
                jnp.where(
                    even("gz"),
                    read(buf, start, ex, sy * 8),
                    read(buf, start + sb - 1, ex, sy * 8),
                ),
                pad,
            ]
        return [face] + inner, outer

    (near_low, far_low), (near_high, far_high) = side(0), side(sy - 2)
    count = ex * sy
    z_face = jnp.where(even("gz"), read(buf, 0, count, 8), read(buf, sb - 1, count, 8))
    out[0][0:count, :] = z_face.astype(BF16)
    out[0][count : count + TAIL, :] = tail
    for k in range((len(out) - 1) // 2):
        up = even("gy") if k == 0 else jnp.logical_not(even("gy"))
        for ref, low, high in (
            (out[1 + 2 * k], near_low, near_high),
            (out[2 + 2 * k], far_low, far_high),
        ):
            value = jnp.where(
                up, jnp.concatenate(high, axis=0), jnp.concatenate(low, axis=0)
            ).astype(BF16)
            ref[0 : value.shape[0], :] = value
            ref[value.shape[0] : value.shape[0] + TAIL, :] = tail


def band_kernel(weight_ref, *rest):
    pars, (out_ref, more_ref) = rest[:-2], rest[-2:]
    lanes = C * BR
    spread = onehot(iota((C, lanes), 0) == iota((C, lanes), 1) // BR)
    turned = jnp.transpose(weight_ref[0].astype(F32)).astype(BF16)
    wide = jnp.dot(turned, spread, preferred_element_type=F32)
    full = (C, BR, lanes)
    zi, zo = iota((1, BR, lanes), 1), iota((1, BR, lanes), 2) % BR

    def rows(value):
        return jnp.broadcast_to(value[:, None, :], full)

    for ex in range(3):
        mixed = jnp.zeros(full, F32)
        for ey in range(3):
            q = (ex * 3 + ey) * 3
            terms = [wide[(q + e) * C : (q + e + 1) * C] for e in range(3)]
            inner = jnp.where(zi == zo - 1, rows(terms[0]), 0.0)
            inner = jnp.where(zi == zo, rows(terms[1]), inner)
            inner = jnp.where(zi == zo + 1, rows(terms[2]), inner)
            before = pltpu.roll(terms[0], 1, 0) if ey else terms[0]
            low = 2 * ey - 1 if ey else BR - 1
            mixed = jnp.where((zi == low) & (zo == 0), rows(before), mixed)
            mixed = jnp.where((zi == 2 * ey) & (zo == BR - 1), rows(terms[2]), mixed)
            out_ref[ex, ey * lanes : (ey + 1) * lanes, :] = (
                inner.reshape(C * BR, lanes).astype(BF16)
            )
        out_ref[ex, 3 * lanes : 4 * lanes, :] = mixed.reshape(C * BR, lanes).astype(BF16)
    if pars:
        pick = onehot(iota((C, lanes), 0) == iota((C, lanes), 1) // BR, F32)
        more_ref[...] = jnp.zeros(more_ref.shape, F32)
        more_ref[0 : pars[0].shape[0], :] = exact_dot(pars[0][...], pick)
    else:
        more_ref[...] = weight_ref[1:2]


def turn_kernel(weight_ref, out_ref):
    kinds, cols, feats = weight_ref.shape
    r = iota((feats, 1), 0)
    source = (r % 128) // 4 * 32 + r // 128 * 4 + r % 4
    pick = onehot(source == iota((feats, feats), 1))
    for k in range(kinds):
        out_ref[:, k * cols : (k + 1) * cols] = lax.dot_general(
            pick, weight_ref[k], (((1,), (1,)), ((), ())), preferred_element_type=F32
        ).astype(BF16)


def first_kernel(narrow, faces, sy, sb, ext_ref, own_ref, core_ref, zface_ref, *rest):
    near, far = rest[0 : 2 * faces : 2], rest[1 : 2 * faces : 2]
    rest = rest[2 * faces :]
    stats_ref = None
    if not narrow:
        stats_ref, rest = rest[0], rest[1:]
    keep_ref, weight_ref, rows_ref, mid_ref, out_ref, msk, buf, lhs = rest
    lanes = ext_ref.shape[1]
    ex = ext_ref.shape[0] // (sy * 8)
    ey = sy + 4
    count = ex * sy
    z_low, z_high = sides(
        "gz", core_ref[0:count].astype(F32), zface_ref[0:count].astype(F32)
    )
    for x in range(ex):
        write_block(
            buf, (x * ey + 2) * 8, ext_ref[x * sy * 8 : (x + 1) * sy * 8].astype(F32)
        )
        part = slice(x * sy, (x + 1) * sy)
        write(buf, (x * ey + 2) * 8 + 7, sy, 8, z_low[part])
        write(buf, (x * ey + 2) * 8 + sb, sy, 8, z_high[part])
    gap = corner_rows(ex)
    size = ex * 8
    face = sides("gy", *[
        near[k][0:size].astype(F32) if k < faces else None for k in range(2)
    ])
    inner = sides("gy", *[
        near[k][size : size + 2 * gap].astype(F32) if k < faces else None for k in range(2)
    ])
    outer = sides("gy", *[
        far[k][0 : 2 * gap].astype(F32) if k < faces else None for k in range(2)
    ])
    for s, y0 in enumerate((0, sy + 2)):
        pair = split_pairs(face[s].reshape(ex, 8, lanes), SENT)
        c_low, c_high = sides("gz", inner[s], outer[s])
        for i in range(2):
            for x in range(ex):
                write_block(buf, (x * ey + y0 + i) * 8, pair[i][x])
            write(buf, (y0 + i) * 8 + 7, ex, ey * 8, c_low[i * gap : i * gap + ex])
            write(buf, (y0 + i) * 8 + sb, ex, ey * 8, c_high[i * gap : i * gap + ex])
    if narrow:
        centre, scale = centre_scale(merge(
            [from_tail(r) for r in (own_ref, zface_ref) + tuple(near) + tuple(far)]
        ))
    else:
        centre, scale = from_rows(stats_ref[...])
    gain, shift, bias = rows_ref[0:1], rows_ref[2:3], rows_ref[4:5]
    scale = scale * gain
    oy, sx = sy + 2, ex - 4
    step = ey * 8
    for x in range(ex):
        v = jnp.concatenate(
            [buf[h, x * step : (x + 1) * step, :] for h in halves(lanes)], axis=1
        )
        there = v != SENT
        msk[x * step : (x + 1) * step] = onehot(there[:, 0:128], F32)
        act = jnp.where(there, silu((v - centre) * scale + shift), 0.0).reshape(ey, 8, lanes)
        for e, part in enumerate(columns(act, oy)):
            lhs[x * oy * 8 : (x + 1) * oy * 8, e * lanes : (e + 1) * lanes] = (
                part.reshape(oy * 8, lanes).astype(BF16)
            )
    ox = sx + 2
    size = ox * oy * 8
    acc = bias
    for e in range(3):
        acc = acc + jnp.dot(
            lhs[e * oy * 8 : e * oy * 8 + size, :], weight_ref[e], preferred_element_type=F32
        )
    mid_ref[...] = acc
    keep = keep_ref[...]
    entries = jnp.sum(keep[:, 0:1]) * float(sx * sy * BR * GW)

    def over_cells(f):
        out = jnp.zeros((8, lanes), F32)
        for x in range(1, sx + 1):
            own = mid_ref[(x * oy + 1) * 8 : (x * oy + oy - 1) * 8].reshape(sy, 8, lanes)
            out = out + jnp.sum(f(own), axis=0)
        return jnp.sum(out * keep, axis=0, keepdims=True)

    def squares_about(mean):
        return over_cells(lambda v: (v - mean[None]) * (v - mean[None]))

    mine = moments(over_cells(lambda v: v), squares_about, entries)
    out_ref[...] = jnp.broadcast_to(to_row(mine)[0:1], out_ref.shape)


def second_kernel(sx, sy, sb, stats_ref, mid_ref, msk_ref, weight_ref, rows_ref, coded_ref,
                  field_ref, tok_ref, low_ref, high_ref, lhs):
    lanes = coded_ref.shape[1]
    step, ext = (sy + 2) * 8, (sy + 4) * 8
    centre, scale = from_rows(stats_ref[...])
    gain, shift, bias = rows_ref[1:2], rows_ref[3:4], rows_ref[5:6]
    scale = scale * gain
    half = sy // 2 * 8
    for x in range(sx + 2):
        v = mid_ref[x * step : (x + 1) * step]
        there = msk_ref[(x + 1) * ext + 8 : (x + 2) * ext - 8]
        there = jnp.concatenate([there] * (lanes // 128), axis=1) > 0
        act = jnp.where(there, silu((v - centre) * scale + shift), 0.0)
        for e, part in enumerate(columns(act.reshape(sy + 2, 8, lanes), sy)):
            lhs[x * half : (x + 1) * half, e * lanes : (e + 1) * lanes] = (
                pack_pairs(part[None]).reshape(half, lanes).astype(BF16)
            )
    size = sx * half
    acc = bias
    for e in range(3):
        acc = acc + jnp.dot(
            lhs[e * half : e * half + size, :], weight_ref[e], preferred_element_type=F32
        )
    field = pack_pairs(coded_ref[...].astype(F32).reshape(sx, sy, 8, lanes))
    field = field.reshape(size, lanes)
    out = jnp.where(field != SENT, field + acc, 0.0).reshape(-1, 8, lanes)
    out = out.astype(BF16)
    field_ref[...] = out.reshape(size, lanes)
    i, j = iota((lanes, lanes), 0), iota((lanes, lanes), 1)
    pick = onehot(i == (j % 128) // 4 * 8 + j // 128 * 4 + j % 4)
    moved = jnp.dot(out.reshape(size, lanes), pick, preferred_element_type=F32).reshape(
        sx // 2, 2, sy // 4, 2, 8, lanes
    )
    count = sx // 2 * (sy // 4)
    parts = []
    for x in range(2):
        for y in range(2):
            piece = moved[:, x, :, y].reshape(count, 8, lanes)
            low, high = piece[:, :, :128], piece[:, :, 128:]
            inside = iota(low.shape, 1) < 4
            for both in (
                jnp.where(inside, low, pltpu.roll(high, 4, 1)),
                jnp.where(inside, pltpu.roll(low, 4, 1), high),
            ):
                parts.append(both.reshape(count * 8, 128).astype(BF16))
    tokens = jnp.concatenate(parts, axis=1)
    n = count * 8
    i, j = iota((n, n), 0), iota((n, n), 1)
    order = onehot(j == i // 8 * 8 + i % 2 * 4 + i % 8 // 2)
    tokens = jnp.dot(order, tokens, preferred_element_type=F32).astype(BF16)
    tok_ref[...] = tokens
    low_ref[...] = tokens[0 : n // 2]
    high_ref[...] = tokens[n // 2 : n]


def fine_kernel(field_ref, fine_ref):
    sx, sy, sb, lanes = fine_ref.shape
    wide = field_ref[...].astype(F32).reshape(-1, 8, lanes)
    other = pltpu.roll(wide, 4, 1)
    fine = jnp.stack([wide[:, :sb], other[:, :sb]], axis=1)
    fine_ref[...] = fine.reshape(sx, sy, sb, lanes).astype(BF16)


def attend_kernel(members, keys_ref, weight_ref, *refs):
    tok_refs, out_refs, (toks, proj) = refs[: -2 - members], refs[-2 - members : -2], refs[-2:]
    own, cols = tok_refs[0].shape[0], weight_ref.shape[1] // 3
    seq = own * members
    start = 0
    for ref in tok_refs:
        toks[start : start + ref.shape[0], :] = ref[...]
        start += ref.shape[0]
    proj[...] = jnp.dot(toks[...], weight_ref[...], preferred_element_type=F32).astype(BF16)
    there = keys_ref[0:1] > 0
    width = min(128, cols)
    for t in range(cols // width):
        q = proj[:, t * width : (t + 1) * width]
        keys = proj[:, cols + t * width : cols + (t + 1) * width]
        values = proj[:, 2 * cols + t * width : 2 * cols + (t + 1) * width]
        head = iota((seq, width), 1) // HD
        merged = jnp.zeros((seq, width), F32)
        for h in range(width // HD):
            mine = jnp.where(head == h, q.astype(F32), 0.0).astype(BF16)
            scores = lax.dot_general(
                mine, keys, (((1,), (1,)), ((), ())), preferred_element_type=F32
            ) * float(HD) ** (-0.5)
            scores = jnp.where(there, scores, -BIG)
            probs = jnp.exp(scores - jnp.max(scores, axis=1, keepdims=True))
            total = jnp.sum(probs, axis=1, keepdims=True)
            mixed = jnp.dot(probs.astype(BF16), values, preferred_element_type=F32)
            merged = jnp.where(head == h, mixed / total, merged)
        merged = merged.astype(BF16)
        for k in range(members):
            out_refs[-1 - k][:, t * width : (t + 1) * width] = merged[k * own : (k + 1) * own]


def place_kernel(members, keep_ref, *refs):
    out_ref = refs[-1]
    own, cols = refs[0].shape
    me = lax.axis_index("gx")
    row = iota((8, cols), 0)
    keep = jnp.zeros((8, cols), F32)
    for b in range(4):
        keep = jnp.where(row // 2 == b, jnp.broadcast_to(keep_ref[b : b + 1, :cols], (8, cols)), keep)
    for k in range(members):
        value = refs[members - 1 - k][...].astype(F32).reshape(own // 8, 8, cols)
        value = jnp.where((keep > 0)[None], value, 0.0).reshape(own, cols).astype(BF16)
        if cols % 128 == 0:
            out_ref[0, :, pl.ds(pl.multiple_of((me ^ k) * cols, cols), cols)] = value
        else:
            out_ref[k] = value


VM = pl.BlockSpec(memory_space=pltpu.VMEM)


def call(kernel, name, specs, out, args, scratch=(), flops=0, nbytes=0, mib=16):
    return pl.pallas_call(
        kernel,
        out_shape=out,
        in_specs=list(specs),
        out_specs=jax.tree.map(lambda _: VM, out),
        scratch_shapes=list(scratch),
        name=name,
        cost_estimate=pl.CostEstimate(flops=flops, bytes_accessed=nbytes, transcendentals=0),
        compiler_params=pltpu.CompilerParams(vmem_limit_bytes=mib * 2**20),
    )(*args)


def shape(*dims, dtype=BF16):
    return jax.ShapeDtypeStruct(dims, dtype)


def pairing(n, odd, closed):
    partner = {i: (i ^ 1 if not odd else (i + 1 if i % 2 else i - 1)) for i in range(n)}
    if closed:
        partner = {i: j % n for i, j in partner.items()}
    return {i: j for i, j in partner.items() if 0 <= j < n and i != j}


def body(features, occupancy, norm_gain, norm_shift, conv_weight, conv_bias, qkv_weight):
    sx, sy, sb, lanes = features.shape
    nx, ny, nz = (lax.axis_size(a) for a in ALL)
    devices = nx * ny * nz
    narrow = nx == 4 and ny == 2 and nz == 4
    own = sx // 2 * (sy // 4) * sb * 2
    ex = sx + 4
    row_shape = [] if narrow else [shape(devices, 128, dtype=F32)]

    slab = sy * 8 + TAIL
    keep, keys, coded, first, second, tail, *stats = call(
        functools.partial(pre_kernel, nx), "pre", (VM, VM),
        [shape(8, lanes, dtype=F32), shape(8, own * nx, dtype=F32),
         shape(sx * sy * 8, lanes), shape(slab, lanes), shape(slab, lanes), shape(TAIL, lanes)]
        + row_shape,
        (occupancy, features), nbytes=10**6,
    )
    stats = [lax.all_to_all(s, ALL, 0, 0, tiled=True) for s in stats]
    got = [
        lax.ppermute(first, "gx", list(pairing(nx, False, False).items())),
        lax.ppermute(second, "gx", list(pairing(nx, True, narrow).items())),
    ]
    tails = [tail]
    if narrow:
        tails.append(lax.ppermute(tail, "gx", [(i, i ^ 2) for i in range(nx)]))
    band = shape(3, 4 * lanes, lanes)
    pars = jnp.concatenate([norm_gain, norm_shift, conv_bias], axis=0)
    later = shape(1, *conv_weight.shape[1:])
    band0, later = call(
        band_kernel, "band0", (VM,), [band, later], (conv_weight,), nbytes=8 * 10**6,
    )
    band1, rows = call(
        band_kernel, "band1", (VM,) * 2, [band, shape(8, lanes, dtype=F32)], (later, pars),
        nbytes=8 * 10**6,
    )
    count = ex * sy
    ext, mine = call(
        functools.partial(line_kernel, narrow, sy, sb), "line", (VM,) * (4 + len(tails)),
        [shape(count * 8, lanes), shape(count + TAIL, lanes)],
        (later, coded, *got, *tails),
        [pltpu.VMEM((lanes // 128, count * 8, 128), F32)], nbytes=10**6,
    )
    core = lax.ppermute(mine, "gz", list(pairing(nz, False, False).items()))

    faces = 1 if ny == 2 else 2
    gap = corner_rows(ex)
    near, far = ex * 8 + 2 * gap + TAIL, 2 * gap + TAIL
    zface, *yfaces = call(
        functools.partial(chip_kernel, sb, sy), "chip", (VM,) * 3,
        [shape(count + TAIL, lanes)] + [shape(near, lanes), shape(far, lanes)] * faces,
        (ext, mine, core),
        [pltpu.VMEM((lanes // 128, count * 8, 128), F32),
         pltpu.VMEM((lanes // 128, count, 128), F32)], nbytes=10**6,
    )
    odd_z = pairing(nz, True, narrow)
    own_tail = zface
    zgot = lax.ppermute(zface, "gz", list(odd_z.items()))
    ygot = []
    for k in range(faces):
        along = pairing(ny, k == 1, False)
        ygot.append(lax.ppermute(yfaces[2 * k], "gy", list(along.items())))
        both = [
            (y * nz + z, along[y] * nz + odd_z[z]) for y in along for z in odd_z
        ]
        ygot.append(lax.ppermute(yfaces[2 * k + 1], ("gy", "gz"), both))

    cols, feats = qkv_weight.shape[1:]
    turned = call(
        turn_kernel, "turn", (VM,), shape(feats, 3 * cols), (qkv_weight,),
        flops=2 * 3 * cols * feats * feats, nbytes=6 * 10**6,
    )

    ey, oy = sy + 4, sy + 2
    size = (sx + 2) * oy * 8
    mid, mine, there = call(
        functools.partial(first_kernel, narrow, faces, sy, sb), "first",
        (VM,) * (7 + 2 * faces + len(stats)),
        [shape(size, lanes, dtype=F32), shape(devices, 128, dtype=F32),
         shape(ex * ey * 8, 128, dtype=F32)],
        (ext, own_tail, core, zgot, *ygot, *stats, keep, band0, rows),
        [pltpu.VMEM((lanes // 128, ex * ey * 8, 128), F32),
         pltpu.VMEM((ex * oy * 8, 4 * lanes), BF16)],
        flops=2 * 10**9, nbytes=4 * 10**6, mib=20,
    )
    stats = lax.all_to_all(mine, ALL, 0, 0, tiled=True)
    field, tokens, *parts = call(
        functools.partial(second_kernel, sx, sy, sb), "second", (VM,) * 6,
        [shape(sx * sy * 4, lanes), shape(own, feats)] + [shape(own // 2, feats)] * 2,
        (stats, mid, there, band1, rows, coded),
        [pltpu.VMEM(((sx + 2) * sy * 4, 4 * lanes), BF16)],
        flops=10**9, nbytes=4 * 10**6,
    )
    fine_out = call(
        fine_kernel, "fine", (VM,), shape(*features.shape), (field,), nbytes=4 * 10**6, mib=8,
    )
    swaps = [[(i, i ^ k) for i in range(nx)] for k in range(nx)]
    blocks = {0: parts}
    for k in sorted(range(1, nx), key=lambda k: (bin(k).count("1"), -k)):
        low = k & -k
        source = [tokens] if k == 1 else blocks[k ^ low]
        if k == 1 and nx > 2:
            part, source[0] = lax.optimization_barrier((blocks[2][0], tokens))
            blocks[2] = [part] + blocks[2][1:]
        blocks[k] = [lax.ppermute(v, "gx", swaps[low]) for v in source]
    blocks = [tokens] + [v for k in range(1, nx) for v in blocks[k]]
    outs = call(
        functools.partial(attend_kernel, nx), "attend", (VM,) * (2 + len(blocks)),
        [shape(own, cols)] * nx, (keys, turned, *blocks),
        [pltpu.VMEM((own * nx, feats), BF16), pltpu.VMEM((own * nx, 3 * cols), BF16)],
        flops=10**9, nbytes=3 * 10**6, mib=16 if narrow else 40,
    )
    moved = [lax.ppermute(v, "gx", swaps[nx - 1 - i]) for i, v in enumerate(outs[:-1])]
    outs = moved + [outs[-1]]
    lined = cols % 128 == 0
    attention = call(
        functools.partial(place_kernel, nx), "place", (VM,) * (1 + nx),
        shape(1, own, nx * cols) if lined else shape(nx, own, cols), (keep, *outs),
        nbytes=3 * 10**5, mib=8,
    )
    if not lined:
        me = lax.axis_index("gx")
        attention = jnp.concatenate(
            [lax.dynamic_index_in_dim(attention, me ^ j, 0, keepdims=False) for j in range(nx)],
            axis=1,
        )[None]
    return (fine_out, attention)


def solution(mesh):
    placed = (
        P("gx", "gy", "gz", None),
        P(None, "gy", "gz"),
        P(),
        P(),
        P(),
        P(),
        P(None, "gx", None),
    )
    return jax.shard_map(
        body,
        mesh=mesh,
        in_specs=placed,
        out_specs=(P("gx", "gy", "gz", None), P(("gy", "gz"), "gx", None)),
        check_vma=False,
    )
```

```python
import functools

import jax
import jax.numpy as jnp
from jax import lax
from jax.experimental import pallas as pl
from jax.experimental.pallas import tpu as pltpu
from jax.sharding import PartitionSpec as P

C = 32
GW = 4
HD = 64
BR = 8
EPS = 1e-05
SENT = 512.0
BIG = 1e30
ALL = ("gx", "gy", "gz")
F32, BF16 = jnp.float32, jnp.bfloat16
HIGHEST = lax.Precision.HIGHEST
TAIL = 16


def iota(shape, dim):
    return lax.broadcasted_iota(jnp.int32, shape, dim)


def onehot(cond, dtype=BF16):
    return jnp.where(cond, 1.0, 0.0).astype(dtype)


def exact_dot(a, b):
    return jnp.dot(a, b, precision=HIGHEST, preferred_element_type=F32)


def spread_sum(v):
    lane = iota(v.shape, 1)
    s = 1
    while s < GW * BR:
        v = v + jnp.where(lane & s == 0, pltpu.roll(v, 128 - s, 1), pltpu.roll(v, s, 1))
        s *= 2
    return v


def group_sum(total):
    k = total.shape[1] // 128
    rows = [jnp.broadcast_to(total[:, h * 128 : (h + 1) * 128], (8, 128)) for h in range(k)]
    out = spread_sum(jnp.concatenate(rows, axis=0))
    return jnp.concatenate([out[h * 8 : (h + 1) * 8] for h in range(k)], axis=1)


def moments(total, squares_about, count):
    sums = group_sum(total)
    squares = group_sum(squares_about((sums / count)[0:1]))
    return sums, squares, jnp.zeros(sums.shape, F32) + count


def merge(parts):
    n = sum(p[2] for p in parts)
    sums = sum(p[0] for p in parts)
    centre = sums / n
    squares = sum(p[1] + p[2] * (p[0] / p[2] - centre) ** 2 for p in parts)
    return sums, squares, n


def centre_scale(part):
    return part[0] / part[2], lax.rsqrt(part[1] / part[2] + EPS)


def to_row(part):
    j = iota((8, 128), 1) % (GW * BR)
    row = jnp.zeros((8, 128), F32)
    for h in range(2):
        for k in range(3):
            row = jnp.where(j == 4 * h + k, part[k][:, h * 128 : (h + 1) * 128], row)
    return row


def from_rows(rows):
    n = jnp.maximum(pltpu.roll(rows, 126, 1), 1.0)
    total = jnp.sum(n, axis=0, keepdims=True)
    centre = jnp.sum(rows, axis=0, keepdims=True) / total
    drift = rows / n - centre
    squares = pltpu.roll(rows, 127, 1) + n * drift * drift
    spread = jnp.sum(squares, axis=0, keepdims=True) / total
    j = iota((8, 128), 1) % (GW * BR)
    blocks = [
        jnp.where(j == 4 * h, jnp.broadcast_to(v, (8, 128)), 0.0)
        for v in (centre, spread) for h in range(2)
    ]
    out = spread_sum(jnp.concatenate(blocks, axis=0))
    out = [out[8 * i : 8 * i + 1] for i in range(4)]
    return (
        jnp.concatenate(out[:2], axis=1),
        lax.rsqrt(jnp.concatenate(out[2:], axis=1) + EPS),
    )


def to_tail(part):
    index = iota((8, 256), 0)
    blocks = [jnp.zeros((8, 256), F32), jnp.zeros((8, 256), F32)]
    for k, value in enumerate(part):
        value = jnp.broadcast_to(value[0:1], (8, 256))
        high = value.astype(BF16).astype(F32)
        mid = (value - high).astype(BF16).astype(F32)
        for i, piece in enumerate((high, mid, value - high - mid)):
            blocks[k // 2] = jnp.where(index == 3 * (k % 2) + i, piece, blocks[k // 2])
    return jnp.concatenate(blocks, axis=0).astype(BF16)


def from_tail(message_ref):
    rows = message_ref.shape[0]
    part = message_ref[rows - TAIL : rows, :].astype(F32)
    return [
        jnp.sum(part[r : r + 3], axis=0, keepdims=True) for r in (0, 3, 8)
    ]


def silu(u):
    return 0.5 * u * (1.0 + jnp.tanh(0.5 * u))


def pack_pairs(v):
    n, m, _, lanes = v.shape
    v = v.reshape(n, m // 2, 2, 8, lanes)
    low, high = v[:, :, 0].reshape(-1, 8, lanes), v[:, :, 1].reshape(-1, 8, lanes)
    both = jnp.where(iota(low.shape, 1) < 4, low, pltpu.roll(high, 4, 1))
    return both.reshape(n, m // 2, 8, lanes)


def split_pairs(v, blank):
    inside = iota(v.shape, 1) < 4
    return [jnp.where(inside, v, blank), jnp.where(inside, pltpu.roll(v, 4, 1), blank)]


def edges(act):
    z = iota(act.shape, 2) % BR
    before, after = pltpu.roll(act, 1, 1), pltpu.roll(act, 7, 1)
    return jnp.where(z == BR - 1, before, jnp.where(z == 0, after, 0.0))


def columns(act, size):
    side = edges(act)
    z = iota((size,) + act.shape[1:], 2) % BR
    second = pltpu.roll(side, 2, 2)
    third = pltpu.roll(side, 4, 2)
    mixed = jnp.where(
        (z == 1) | (z == 2), second[1 : 1 + size],
        jnp.where((z == 3) | (z == 4), third[2 : 2 + size], side[0:size]),
    )
    return [act[e : e + size] for e in range(3)] + [mixed]


def halves(lanes):
    return range(lanes // 128)


def read(ref, start, count, stride):
    return jnp.concatenate(
        [ref[h, pl.ds(start, count, stride=stride), :] for h in range(ref.shape[0])], axis=1
    )


def write(ref, start, count, stride, value):
    for h in range(ref.shape[0]):
        ref[h, pl.ds(start, count, stride=stride), :] = value[:, h * 128 : (h + 1) * 128]


def write_block(ref, start, value):
    for h in range(ref.shape[0]):
        ref[h, start : start + value.shape[0], :] = value[:, h * 128 : (h + 1) * 128]


def even(axis):
    return lax.axis_index(axis) % 2 == 0


def sides(axis, first, second):
    i, n = lax.axis_index(axis), lax.axis_size(axis)
    blank = jnp.full(first.shape, SENT, F32)
    second = blank if second is None else second
    low, high = jnp.where(even(axis), second, first), jnp.where(even(axis), first, second)
    return jnp.where(i > 0, low, SENT), jnp.where(i < n - 1, high, SENT)


def pre_kernel(members, occ_ref, feat_ref, keep_ref, keys_ref, coded_ref, first_ref, second_ref,
               tail_ref, rows_ref=None):
    sx, sy, sb, lanes = feat_ref.shape
    me = lax.axis_index("gx")
    bricks = [occ_ref[x].astype(F32) for x in range(members)]

    def row_of(x):
        return sum(jnp.where(x == i, v, 0.0) for i, v in enumerate(bricks))

    mine = jnp.broadcast_to(row_of(me), (8, sb))
    keep = jnp.where(iota((8, sb), 0) == iota((8, sb), 1), mine, 0.0)
    keep = jnp.broadcast_to(jnp.sum(keep, axis=1, keepdims=True), (8, lanes))
    count = jnp.sum(keep, axis=0, keepdims=True) * float(sx * sy * BR * GW)
    keep_ref[...] = keep
    seq = keys_ref.shape[1]
    lane = iota((1, seq), 1)
    keys = jnp.zeros((1, seq), F32)
    for k in range(members):
        there = row_of(me ^ k)
        for b in range(sb):
            keys = jnp.where(
                (lane // (seq // members) == k) & (lane % (2 * sb) // 2 == b),
                there[:, b : b + 1], keys,
            )
    keys_ref[...] = jnp.broadcast_to(keys, keys_ref.shape)
    field = feat_ref[...].astype(F32)
    wide = jnp.concatenate([field, jnp.zeros((sx, sy, 8 - sb, lanes), F32)], axis=2)
    wide = wide.reshape(sx * sy, 8, lanes)
    total = jnp.sum(jnp.sum(wide, axis=0) * keep, axis=0, keepdims=True)

    def squares_about(mean):
        d = wide - mean[None]
        return jnp.sum(jnp.sum(d * d, axis=0) * keep, axis=0, keepdims=True)

    code = jnp.where((keep > 0)[None], wide, SENT)
    coded_ref[...] = code.reshape(sx * sy * 8, lanes).astype(BF16)
    packed = pack_pairs(code.reshape(sx, sy, 8, lanes))
    low = packed[0:2].reshape(-1, lanes)
    high = packed[sx - 2 : sx].reshape(-1, lanes)
    size = low.shape[0]
    first_ref[0:size, :] = jnp.where(even("gx"), high, low).astype(BF16)
    second_ref[0:size, :] = jnp.where(even("gx"), low, high).astype(BF16)
    mine = moments(total, squares_about, count)
    tail = to_tail(mine)
    first_ref[size : size + TAIL, :] = tail
    second_ref[size : size + TAIL, :] = tail
    tail_ref[...] = tail
    if rows_ref is not None:
        rows_ref[...] = jnp.broadcast_to(to_row(mine)[0:1], rows_ref.shape)


def line_kernel(narrow, sy, sb, _, coded_ref, first_ref, second_ref, *rest):
    tails, (ext_ref, out_ref, buf) = rest[:-3], rest[-3:]
    lanes = coded_ref.shape[1]
    sx = coded_ref.shape[0] // (sy * 8)
    size = 2 * (sy // 2) * 8
    low, high = sides(
        "gx", first_ref[0:size].astype(F32), second_ref[0:size].astype(F32)
    )
    write_block(buf, 2 * sy * 8, coded_ref[...].astype(F32))
    for x0, side in ((0, low), (sx + 2, high)):
        for i in range(2):
            part = side[i * (size // 2) : (i + 1) * (size // 2)].reshape(sy // 2, 8, lanes)
            pair = split_pairs(part, SENT)
            for y in range(sy):
                write_block(buf, ((x0 + i) * sy + y) * 8, pair[y % 2][y // 2])
    rows = (sx + 4) * sy * 8
    ext_ref[...] = jnp.concatenate([buf[h] for h in halves(lanes)], axis=1).astype(BF16)
    count = (sx + 4) * sy
    face = jnp.where(even("gz"), read(buf, sb - 1, count, 8), read(buf, 0, count, 8))
    out_ref[0:count, :] = face.astype(BF16)
    mine = [from_tail(ref) for ref in tails]
    if narrow:
        mine = mine + [from_tail(first_ref), from_tail(second_ref)]
    out_ref[count : count + TAIL, :] = to_tail(merge(mine))


def corner_rows(count):
    return (count + 15) // 16 * 16


def chip_kernel(sb, sy, ext_ref, own_ref, other_ref, *rest):
    out, (buf, stage) = rest[:-2], rest[-2:]
    lanes = ext_ref.shape[1]
    ex = ext_ref.shape[0] // (sy * 8)
    block = ext_ref[...].astype(F32)
    write_block(buf, 0, block)
    write_block(stage, 0, other_ref[0 : ex * sy].astype(F32))
    gap = corner_rows(ex)
    pad = jnp.zeros((gap - ex, lanes), F32)
    tail = to_tail(merge([from_tail(own_ref), from_tail(other_ref)]))
    packed = pack_pairs(block.reshape(ex, sy, 8, lanes))

    def side(y0):
        face = packed[:, y0 // 2].reshape(ex * 8, lanes)
        inner, outer = [], []
        for i in range(2):
            inner += [read(stage, y0 + i, ex, sy), pad]
            start = (y0 + i) * 8
            outer += [
                jnp.where(
                    even("gz"),
                    read(buf, start, ex, sy * 8),
                    read(buf, start + sb - 1, ex, sy * 8),
                ),
                pad,
            ]
        return [face] + inner, outer

    (near_low, far_low), (near_high, far_high) = side(0), side(sy - 2)
    count = ex * sy
    z_face = jnp.where(even("gz"), read(buf, 0, count, 8), read(buf, sb - 1, count, 8))
    out[0][0:count, :] = z_face.astype(BF16)
    out[0][count : count + TAIL, :] = tail
    for k in range((len(out) - 1) // 2):
        up = even("gy") if k == 0 else jnp.logical_not(even("gy"))
        for ref, low, high in (
            (out[1 + 2 * k], near_low, near_high),
            (out[2 + 2 * k], far_low, far_high),
        ):
            value = jnp.where(
                up, jnp.concatenate(high, axis=0), jnp.concatenate(low, axis=0)
            ).astype(BF16)
            ref[0 : value.shape[0], :] = value
            ref[value.shape[0] : value.shape[0] + TAIL, :] = tail


def band_kernel(weight_ref, *rest):
    pars, (out_ref, more_ref) = rest[:-2], rest[-2:]
    lanes = C * BR
    spread = onehot(iota((C, lanes), 0) == iota((C, lanes), 1) // BR)
    turned = jnp.transpose(weight_ref[0].astype(F32)).astype(BF16)
    wide = jnp.dot(turned, spread, preferred_element_type=F32)
    full = (C, BR, lanes)
    zi, zo = iota((1, BR, lanes), 1), iota((1, BR, lanes), 2) % BR

    def rows(value):
        return jnp.broadcast_to(value[:, None, :], full)

    for ex in range(3):
        mixed = jnp.zeros(full, F32)
        for ey in range(3):
            q = (ex * 3 + ey) * 3
            terms = [wide[(q + e) * C : (q + e + 1) * C] for e in range(3)]
            inner = jnp.where(zi == zo - 1, rows(terms[0]), 0.0)
            inner = jnp.where(zi == zo, rows(terms[1]), inner)
            inner = jnp.where(zi == zo + 1, rows(terms[2]), inner)
            before = pltpu.roll(terms[0], 1, 0) if ey else terms[0]
            low = 2 * ey - 1 if ey else BR - 1
            mixed = jnp.where((zi == low) & (zo == 0), rows(before), mixed)
            mixed = jnp.where((zi == 2 * ey) & (zo == BR - 1), rows(terms[2]), mixed)
            out_ref[ex, ey * lanes : (ey + 1) * lanes, :] = (
                inner.reshape(C * BR, lanes).astype(BF16)
            )
        out_ref[ex, 3 * lanes : 4 * lanes, :] = mixed.reshape(C * BR, lanes).astype(BF16)
    if pars:
        pick = onehot(iota((C, lanes), 0) == iota((C, lanes), 1) // BR, F32)
        more_ref[...] = jnp.zeros(more_ref.shape, F32)
        more_ref[0 : pars[0].shape[0], :] = exact_dot(pars[0][...], pick)
    else:
        more_ref[...] = weight_ref[1:2]


def turn_kernel(weight_ref, out_ref):
    kinds, cols, feats = weight_ref.shape
    r = iota((feats, 1), 0)
    source = (r % 128) // 4 * 32 + r // 128 * 4 + r % 4
    pick = onehot(source == iota((feats, feats), 1))
    for k in range(kinds):
        out_ref[:, k * cols : (k + 1) * cols] = lax.dot_general(
            pick, weight_ref[k], (((1,), (1,)), ((), ())), preferred_element_type=F32
        ).astype(BF16)


def first_kernel(narrow, faces, sy, sb, ext_ref, own_ref, core_ref, zface_ref, *rest):
    near, far = rest[0 : 2 * faces : 2], rest[1 : 2 * faces : 2]
    rest = rest[2 * faces :]
    stats_ref = None
    if not narrow:
        stats_ref, rest = rest[0], rest[1:]
    keep_ref, weight_ref, rows_ref, mid_ref, out_ref, msk, buf, lhs = rest
    lanes = ext_ref.shape[1]
    ex = ext_ref.shape[0] // (sy * 8)
    ey = sy + 4
    count = ex * sy
    z_low, z_high = sides(
        "gz", core_ref[0:count].astype(F32), zface_ref[0:count].astype(F32)
    )
    for x in range(ex):
        write_block(
            buf, (x * ey + 2) * 8, ext_ref[x * sy * 8 : (x + 1) * sy * 8].astype(F32)
        )
        part = slice(x * sy, (x + 1) * sy)
        write(buf, (x * ey + 2) * 8 + 7, sy, 8, z_low[part])
        write(buf, (x * ey + 2) * 8 + sb, sy, 8, z_high[part])
    gap = corner_rows(ex)
    size = ex * 8
    face = sides("gy", *[
        near[k][0:size].astype(F32) if k < faces else None for k in range(2)
    ])
    inner = sides("gy", *[
        near[k][size : size + 2 * gap].astype(F32) if k < faces else None for k in range(2)
    ])
    outer = sides("gy", *[
        far[k][0 : 2 * gap].astype(F32) if k < faces else None for k in range(2)
    ])
    for s, y0 in enumerate((0, sy + 2)):
        pair = split_pairs(face[s].reshape(ex, 8, lanes), SENT)
        c_low, c_high = sides("gz", inner[s], outer[s])
        for i in range(2):
            for x in range(ex):
                write_block(buf, (x * ey + y0 + i) * 8, pair[i][x])
            write(buf, (y0 + i) * 8 + 7, ex, ey * 8, c_low[i * gap : i * gap + ex])
            write(buf, (y0 + i) * 8 + sb, ex, ey * 8, c_high[i * gap : i * gap + ex])
    if narrow:
        centre, scale = centre_scale(merge(
            [from_tail(r) for r in (own_ref, zface_ref) + tuple(near) + tuple(far)]
        ))
    else:
        centre, scale = from_rows(stats_ref[...])
    gain, shift, bias = rows_ref[0:1], rows_ref[2:3], rows_ref[4:5]
    scale = scale * gain
    oy, sx = sy + 2, ex - 4
    step = ey * 8
    for x in range(ex):
        v = jnp.concatenate(
            [buf[h, x * step : (x + 1) * step, :] for h in halves(lanes)], axis=1
        )
        there = v != SENT
        msk[x * step : (x + 1) * step] = onehot(there[:, 0:128], F32)
        act = jnp.where(there, silu((v - centre) * scale + shift), 0.0).reshape(ey, 8, lanes)
        for e, part in enumerate(columns(act, oy)):
            lhs[x * oy * 8 : (x + 1) * oy * 8, e * lanes : (e + 1) * lanes] = (
                part.reshape(oy * 8, lanes).astype(BF16)
            )
    ox = sx + 2
    size = ox * oy * 8
    acc = bias
    for e in range(3):
        acc = acc + jnp.dot(
            lhs[e * oy * 8 : e * oy * 8 + size, :], weight_ref[e], preferred_element_type=F32
        )
    mid_ref[...] = acc
    keep = keep_ref[...]
    entries = jnp.sum(keep[:, 0:1]) * float(sx * sy * BR * GW)

    def over_cells(f):
        out = jnp.zeros((8, lanes), F32)
        for x in range(1, sx + 1):
            own = mid_ref[(x * oy + 1) * 8 : (x * oy + oy - 1) * 8].reshape(sy, 8, lanes)
            out = out + jnp.sum(f(own), axis=0)
        return jnp.sum(out * keep, axis=0, keepdims=True)

    def squares_about(mean):
        return over_cells(lambda v: (v - mean[None]) * (v - mean[None]))

    mine = moments(over_cells(lambda v: v), squares_about, entries)
    out_ref[...] = jnp.broadcast_to(to_row(mine)[0:1], out_ref.shape)


def second_kernel(sx, sy, sb, stats_ref, mid_ref, msk_ref, weight_ref, rows_ref, coded_ref,
                  field_ref, tok_ref, low_ref, high_ref, lhs):
    lanes = coded_ref.shape[1]
    step, ext = (sy + 2) * 8, (sy + 4) * 8
    centre, scale = from_rows(stats_ref[...])
    gain, shift, bias = rows_ref[1:2], rows_ref[3:4], rows_ref[5:6]
    scale = scale * gain
    half = sy // 2 * 8
    for x in range(sx + 2):
        v = mid_ref[x * step : (x + 1) * step]
        there = msk_ref[(x + 1) * ext + 8 : (x + 2) * ext - 8]
        there = jnp.concatenate([there] * (lanes // 128), axis=1) > 0
        act = jnp.where(there, silu((v - centre) * scale + shift), 0.0)
        for e, part in enumerate(columns(act.reshape(sy + 2, 8, lanes), sy)):
            lhs[x * half : (x + 1) * half, e * lanes : (e + 1) * lanes] = (
                pack_pairs(part[None]).reshape(half, lanes).astype(BF16)
            )
    size = sx * half
    acc = bias
    for e in range(3):
        acc = acc + jnp.dot(
            lhs[e * half : e * half + size, :], weight_ref[e], preferred_element_type=F32
        )
    field = pack_pairs(coded_ref[...].astype(F32).reshape(sx, sy, 8, lanes))
    field = field.reshape(size, lanes)
    out = jnp.where(field != SENT, field + acc, 0.0).reshape(-1, 8, lanes)
    out = out.astype(BF16)
    field_ref[...] = out.reshape(size, lanes)
    i, j = iota((lanes, lanes), 0), iota((lanes, lanes), 1)
    pick = onehot(i == (j % 128) // 4 * 8 + j // 128 * 4 + j % 4)
    moved = jnp.dot(out.reshape(size, lanes), pick, preferred_element_type=F32).reshape(
        sx // 2, 2, sy // 4, 2, 8, lanes
    )
    count = sx // 2 * (sy // 4)
    parts = []
    for x in range(2):
        for y in range(2):
            piece = moved[:, x, :, y].reshape(count, 8, lanes)
            low, high = piece[:, :, :128], piece[:, :, 128:]
            inside = iota(low.shape, 1) < 4
            for both in (
                jnp.where(inside, low, pltpu.roll(high, 4, 1)),
                jnp.where(inside, pltpu.roll(low, 4, 1), high),
            ):
                parts.append(both.reshape(count * 8, 128).astype(BF16))
    tokens = jnp.concatenate(parts, axis=1)
    n = count * 8
    i, j = iota((n, n), 0), iota((n, n), 1)
    order = onehot(j == i // 8 * 8 + i % 2 * 4 + i % 8 // 2)
    tokens = jnp.dot(order, tokens, preferred_element_type=F32).astype(BF16)
    tok_ref[...] = tokens
    low_ref[...] = tokens[0 : n // 2]
    high_ref[...] = tokens[n // 2 : n]


def fine_kernel(field_ref, fine_ref):
    sx, sy, sb, lanes = fine_ref.shape
    wide = field_ref[...].astype(F32).reshape(-1, 8, lanes)
    other = pltpu.roll(wide, 4, 1)
    fine = jnp.stack([wide[:, :sb], other[:, :sb]], axis=1)
    fine_ref[...] = fine.reshape(sx, sy, sb, lanes).astype(BF16)


def attend_kernel(members, keys_ref, weight_ref, *refs):
    tok_refs, out_refs, (toks, proj) = refs[: -2 - members], refs[-2 - members : -2], refs[-2:]
    own, cols = tok_refs[0].shape[0], weight_ref.shape[1] // 3
    seq = own * members
    start = 0
    for ref in tok_refs:
        toks[start : start + ref.shape[0], :] = ref[...]
        start += ref.shape[0]
    proj[...] = jnp.dot(toks[...], weight_ref[...], preferred_element_type=F32).astype(BF16)
    there = keys_ref[0:1] > 0
    width = min(128, cols)
    for t in range(cols // width):
        q = proj[:, t * width : (t + 1) * width]
        keys = proj[:, cols + t * width : cols + (t + 1) * width]
        values = proj[:, 2 * cols + t * width : 2 * cols + (t + 1) * width]
        head = iota((seq, width), 1) // HD
        merged = jnp.zeros((seq, width), F32)
        for h in range(width // HD):
            mine = jnp.where(head == h, q.astype(F32), 0.0).astype(BF16)
            scores = lax.dot_general(
                mine, keys, (((1,), (1,)), ((), ())), preferred_element_type=F32
            ) * float(HD) ** (-0.5)
            scores = jnp.where(there, scores, -BIG)
            probs = jnp.exp(scores - jnp.max(scores, axis=1, keepdims=True))
            total = jnp.sum(probs, axis=1, keepdims=True)
            mixed = jnp.dot(probs.astype(BF16), values, preferred_element_type=F32)
            merged = jnp.where(head == h, mixed / total, merged)
        merged = merged.astype(BF16)
        for k in range(members):
            out_refs[-1 - k][:, t * width : (t + 1) * width] = merged[k * own : (k + 1) * own]


def place_kernel(members, keep_ref, *refs):
    out_ref = refs[-1]
    own, cols = refs[0].shape
    me = lax.axis_index("gx")
    row = iota((8, cols), 0)
    keep = jnp.zeros((8, cols), F32)
    for b in range(4):
        keep = jnp.where(row // 2 == b, jnp.broadcast_to(keep_ref[b : b + 1, :cols], (8, cols)), keep)
    for k in range(members):
        value = refs[members - 1 - k][...].astype(F32).reshape(own // 8, 8, cols)
        value = jnp.where((keep > 0)[None], value, 0.0).reshape(own, cols).astype(BF16)
        if cols % 128 == 0:
            out_ref[0, :, pl.ds(pl.multiple_of((me ^ k) * cols, cols), cols)] = value
        else:
            out_ref[k] = value


VM = pl.BlockSpec(memory_space=pltpu.VMEM)


def call(kernel, name, specs, out, args, scratch=(), flops=0, nbytes=0, mib=16):
    return pl.pallas_call(
        kernel,
        out_shape=out,
        in_specs=list(specs),
        out_specs=jax.tree.map(lambda _: VM, out),
        scratch_shapes=list(scratch),
        name=name,
        cost_estimate=pl.CostEstimate(flops=flops, bytes_accessed=nbytes, transcendentals=0),
        compiler_params=pltpu.CompilerParams(vmem_limit_bytes=mib * 2**20),
    )(*args)


def shape(*dims, dtype=BF16):
    return jax.ShapeDtypeStruct(dims, dtype)


def pairing(n, odd, closed):
    partner = {i: (i ^ 1 if not odd else (i + 1 if i % 2 else i - 1)) for i in range(n)}
    if closed:
        partner = {i: j % n for i, j in partner.items()}
    return {i: j for i, j in partner.items() if 0 <= j < n and i != j}


def body(features, occupancy, norm_gain, norm_shift, conv_weight, conv_bias, qkv_weight):
    sx, sy, sb, lanes = features.shape
    nx, ny, nz = (lax.axis_size(a) for a in ALL)
    devices = nx * ny * nz
    narrow = nx == 4 and ny == 2 and nz == 4
    own = sx // 2 * (sy // 4) * sb * 2
    ex = sx + 4
    row_shape = [] if narrow else [shape(devices, 128, dtype=F32)]

    slab = sy * 8 + TAIL
    keep, keys, coded, first, second, tail, *stats = call(
        functools.partial(pre_kernel, nx), "pre", (VM, VM),
        [shape(8, lanes, dtype=F32), shape(8, own * nx, dtype=F32),
         shape(sx * sy * 8, lanes), shape(slab, lanes), shape(slab, lanes), shape(TAIL, lanes)]
        + row_shape,
        (occupancy, features), nbytes=10**6,
    )
    stats = [lax.all_to_all(s, ALL, 0, 0, tiled=True) for s in stats]
    got = [
        lax.ppermute(first, "gx", list(pairing(nx, False, False).items())),
        lax.ppermute(second, "gx", list(pairing(nx, True, narrow).items())),
    ]
    tails = [tail]
    if narrow:
        tails.append(lax.ppermute(tail, "gx", [(i, i ^ 2) for i in range(nx)]))
    band = shape(3, 4 * lanes, lanes)
    pars = jnp.concatenate([norm_gain, norm_shift, conv_bias], axis=0)
    later = shape(1, *conv_weight.shape[1:])
    band0, later = call(
        band_kernel, "band0", (VM,), [band, later], (conv_weight,), nbytes=8 * 10**6,
    )
    band1, rows = call(
        band_kernel, "band1", (VM,) * 2, [band, shape(8, lanes, dtype=F32)], (later, pars),
        nbytes=8 * 10**6,
    )
    count = ex * sy
    ext, mine = call(
        functools.partial(line_kernel, narrow, sy, sb), "line", (VM,) * (4 + len(tails)),
        [shape(count * 8, lanes), shape(count + TAIL, lanes)],
        (later, coded, *got, *tails),
        [pltpu.VMEM((lanes // 128, count * 8, 128), F32)], nbytes=10**6,
    )
    core = lax.ppermute(mine, "gz", list(pairing(nz, False, False).items()))

    faces = 1 if ny == 2 else 2
    gap = corner_rows(ex)
    near, far = ex * 8 + 2 * gap + TAIL, 2 * gap + TAIL
    zface, *yfaces = call(
        functools.partial(chip_kernel, sb, sy), "chip", (VM,) * 3,
        [shape(count + TAIL, lanes)] + [shape(near, lanes), shape(far, lanes)] * faces,
        (ext, mine, core),
        [pltpu.VMEM((lanes // 128, count * 8, 128), F32),
         pltpu.VMEM((lanes // 128, count, 128), F32)], nbytes=10**6,
    )
    odd_z = pairing(nz, True, narrow)
    own_tail = zface
    zgot = lax.ppermute(zface, "gz", list(odd_z.items()))
    ygot = []
    for k in range(faces):
        along = pairing(ny, k == 1, False)
        ygot.append(lax.ppermute(yfaces[2 * k], "gy", list(along.items())))
        both = [
            (y * nz + z, along[y] * nz + odd_z[z]) for y in along for z in odd_z
        ]
        ygot.append(lax.ppermute(yfaces[2 * k + 1], ("gy", "gz"), both))

    cols, feats = qkv_weight.shape[1:]
    turned = call(
        turn_kernel, "turn", (VM,), shape(feats, 3 * cols), (qkv_weight,),
        flops=2 * 3 * cols * feats * feats, nbytes=6 * 10**6,
    )

    ey, oy = sy + 4, sy + 2
    size = (sx + 2) * oy * 8
    mid, mine, there = call(
        functools.partial(first_kernel, narrow, faces, sy, sb), "first",
        (VM,) * (7 + 2 * faces + len(stats)),
        [shape(size, lanes, dtype=F32), shape(devices, 128, dtype=F32),
         shape(ex * ey * 8, 128, dtype=F32)],
        (ext, own_tail, core, zgot, *ygot, *stats, keep, band0, rows),
        [pltpu.VMEM((lanes // 128, ex * ey * 8, 128), F32),
         pltpu.VMEM((ex * oy * 8, 4 * lanes), BF16)],
        flops=2 * 10**9, nbytes=4 * 10**6, mib=20,
    )
    stats = lax.all_to_all(mine, ALL, 0, 0, tiled=True)
    field, tokens, *parts = call(
        functools.partial(second_kernel, sx, sy, sb), "second", (VM,) * 6,
        [shape(sx * sy * 4, lanes), shape(own, feats)] + [shape(own // 2, feats)] * 2,
        (stats, mid, there, band1, rows, coded),
        [pltpu.VMEM(((sx + 2) * sy * 4, 4 * lanes), BF16)],
        flops=10**9, nbytes=4 * 10**6,
    )
    fine_out = call(
        fine_kernel, "fine", (VM,), shape(*features.shape), (field,), nbytes=4 * 10**6, mib=8,
    )
    swaps = [[(i, i ^ k) for i in range(nx)] for k in range(nx)]
    blocks = {0: parts}
    for k in sorted(range(1, nx), key=lambda k: (bin(k).count("1"), -k)):
        low = k & -k
        if k == 1:
            blocks[k] = [lax.ppermute(tokens, "gx", swaps[k])]
        else:
            blocks[k] = [
                lax.ppermute(blocks[k ^ low][0], "gx", swaps[low]),
                lax.ppermute(parts[1], "gx", swaps[k]),
            ]
    blocks = [tokens] + [v for k in range(1, nx) for v in blocks[k]]
    outs = call(
        functools.partial(attend_kernel, nx), "attend", (VM,) * (2 + len(blocks)),
        [shape(own, cols)] * nx, (keys, turned, *blocks),
        [pltpu.VMEM((own * nx, feats), BF16), pltpu.VMEM((own * nx, 3 * cols), BF16)],
        flops=10**9, nbytes=3 * 10**6, mib=16 if narrow else 40,
    )
    moved = [lax.ppermute(v, "gx", swaps[nx - 1 - i]) for i, v in enumerate(outs[:-1])]
    outs = moved + [outs[-1]]
    lined = cols % 128 == 0
    attention = call(
        functools.partial(place_kernel, nx), "place", (VM,) * (1 + nx),
        shape(1, own, nx * cols) if lined else shape(nx, own, cols), (keep, *outs),
        nbytes=3 * 10**5, mib=8,
    )
    if not lined:
        me = lax.axis_index("gx")
        attention = jnp.concatenate(
            [lax.dynamic_index_in_dim(attention, me ^ j, 0, keepdims=False) for j in range(nx)],
            axis=1,
        )[None]
    return (fine_out, attention)


def solution(mesh):
    placed = (
        P("gx", "gy", "gz", None),
        P(None, "gy", "gz"),
        P(),
        P(),
        P(),
        P(),
        P(None, "gx", None),
    )
    return jax.shard_map(
        body,
        mesh=mesh,
        in_specs=placed,
        out_specs=(P("gx", "gy", "gz", None), P(("gy", "gz"), "gx", None)),
        check_vma=False,
    )
```

```python
import functools

import jax
import jax.numpy as jnp
from jax import lax
from jax.experimental import pallas as pl
from jax.experimental.pallas import tpu as pltpu
from jax.sharding import PartitionSpec as P

C = 32
GW = 4
HD = 64
BR = 8
EPS = 1e-05
SENT = 512.0
BIG = 1e30
ALL = ("gx", "gy", "gz")
F32, BF16 = jnp.float32, jnp.bfloat16
HIGHEST = lax.Precision.HIGHEST
TAIL = 16


def iota(shape, dim):
    return lax.broadcasted_iota(jnp.int32, shape, dim)


def onehot(cond, dtype=BF16):
    return jnp.where(cond, 1.0, 0.0).astype(dtype)


def exact_dot(a, b):
    return jnp.dot(a, b, precision=HIGHEST, preferred_element_type=F32)


def spread_sum(v):
    lane = iota(v.shape, 1)
    s = 1
    while s < GW * BR:
        v = v + jnp.where(lane & s == 0, pltpu.roll(v, 128 - s, 1), pltpu.roll(v, s, 1))
        s *= 2
    return v


def group_sum(total):
    k = total.shape[1] // 128
    rows = [jnp.broadcast_to(total[:, h * 128 : (h + 1) * 128], (8, 128)) for h in range(k)]
    out = spread_sum(jnp.concatenate(rows, axis=0))
    return jnp.concatenate([out[h * 8 : (h + 1) * 8] for h in range(k)], axis=1)


def moments(total, squares_about, count):
    sums = group_sum(total)
    squares = group_sum(squares_about((sums / count)[0:1]))
    return sums, squares, jnp.zeros(sums.shape, F32) + count


def merge(parts):
    n = sum(p[2] for p in parts)
    sums = sum(p[0] for p in parts)
    centre = sums / n
    squares = sum(p[1] + p[2] * (p[0] / p[2] - centre) ** 2 for p in parts)
    return sums, squares, n


def centre_scale(part):
    return part[0] / part[2], lax.rsqrt(part[1] / part[2] + EPS)


def to_row(part):
    j = iota((8, 128), 1) % (GW * BR)
    row = jnp.zeros((8, 128), F32)
    for h in range(2):
        for k in range(3):
            row = jnp.where(j == 4 * h + k, part[k][:, h * 128 : (h + 1) * 128], row)
    return row


def from_rows(rows):
    n = jnp.maximum(pltpu.roll(rows, 126, 1), 1.0)
    total = jnp.sum(n, axis=0, keepdims=True)
    centre = jnp.sum(rows, axis=0, keepdims=True) / total
    drift = rows / n - centre
    squares = pltpu.roll(rows, 127, 1) + n * drift * drift
    spread = jnp.sum(squares, axis=0, keepdims=True) / total
    j = iota((8, 128), 1) % (GW * BR)
    blocks = [
        jnp.where(j == 4 * h, jnp.broadcast_to(v, (8, 128)), 0.0)
        for v in (centre, spread) for h in range(2)
    ]
    out = spread_sum(jnp.concatenate(blocks, axis=0))
    out = [out[8 * i : 8 * i + 1] for i in range(4)]
    return (
        jnp.concatenate(out[:2], axis=1),
        lax.rsqrt(jnp.concatenate(out[2:], axis=1) + EPS),
    )


def to_tail(part):
    index = iota((8, 256), 0)
    blocks = [jnp.zeros((8, 256), F32), jnp.zeros((8, 256), F32)]
    for k, value in enumerate(part):
        value = jnp.broadcast_to(value[0:1], (8, 256))
        high = value.astype(BF16).astype(F32)
        mid = (value - high).astype(BF16).astype(F32)
        for i, piece in enumerate((high, mid, value - high - mid)):
            blocks[k // 2] = jnp.where(index == 3 * (k % 2) + i, piece, blocks[k // 2])
    return jnp.concatenate(blocks, axis=0).astype(BF16)


def from_tail(message_ref):
    rows = message_ref.shape[0]
    part = message_ref[rows - TAIL : rows, :].astype(F32)
    return [
        jnp.sum(part[r : r + 3], axis=0, keepdims=True) for r in (0, 3, 8)
    ]


def silu(u):
    return 0.5 * u * (1.0 + jnp.tanh(0.5 * u))


def pack_pairs(v):
    n, m, _, lanes = v.shape
    v = v.reshape(n, m // 2, 2, 8, lanes)
    low, high = v[:, :, 0].reshape(-1, 8, lanes), v[:, :, 1].reshape(-1, 8, lanes)
    both = jnp.where(iota(low.shape, 1) < 4, low, pltpu.roll(high, 4, 1))
    return both.reshape(n, m // 2, 8, lanes)


def split_pairs(v, blank):
    inside = iota(v.shape, 1) < 4
    return [jnp.where(inside, v, blank), jnp.where(inside, pltpu.roll(v, 4, 1), blank)]


def edges(act):
    z = iota(act.shape, 2) % BR
    before, after = pltpu.roll(act, 1, 1), pltpu.roll(act, 7, 1)
    return jnp.where(z == BR - 1, before, jnp.where(z == 0, after, 0.0))


def columns(act, size):
    side = edges(act)
    z = iota((size,) + act.shape[1:], 2) % BR
    second = pltpu.roll(side, 2, 2)
    third = pltpu.roll(side, 4, 2)
    mixed = jnp.where(
        (z == 1) | (z == 2), second[1 : 1 + size],
        jnp.where((z == 3) | (z == 4), third[2 : 2 + size], side[0:size]),
    )
    return [act[e : e + size] for e in range(3)] + [mixed]


def halves(lanes):
    return range(lanes // 128)


def read(ref, start, count, stride):
    return jnp.concatenate(
        [ref[h, pl.ds(start, count, stride=stride), :] for h in range(ref.shape[0])], axis=1
    )


def write(ref, start, count, stride, value):
    for h in range(ref.shape[0]):
        ref[h, pl.ds(start, count, stride=stride), :] = value[:, h * 128 : (h + 1) * 128]


def write_block(ref, start, value):
    for h in range(ref.shape[0]):
        ref[h, start : start + value.shape[0], :] = value[:, h * 128 : (h + 1) * 128]


def even(axis):
    return lax.axis_index(axis) % 2 == 0


def sides(axis, first, second):
    i, n = lax.axis_index(axis), lax.axis_size(axis)
    blank = jnp.full(first.shape, SENT, F32)
    second = blank if second is None else second
    low, high = jnp.where(even(axis), second, first), jnp.where(even(axis), first, second)
    return jnp.where(i > 0, low, SENT), jnp.where(i < n - 1, high, SENT)


def pre_kernel(members, occ_ref, feat_ref, keep_ref, keys_ref, coded_ref, first_ref, second_ref,
               tail_ref, rows_ref=None):
    sx, sy, sb, lanes = feat_ref.shape
    me = lax.axis_index("gx")
    bricks = [occ_ref[x].astype(F32) for x in range(members)]

    def row_of(x):
        return sum(jnp.where(x == i, v, 0.0) for i, v in enumerate(bricks))

    mine = jnp.broadcast_to(row_of(me), (8, sb))
    keep = jnp.where(iota((8, sb), 0) == iota((8, sb), 1), mine, 0.0)
    keep = jnp.broadcast_to(jnp.sum(keep, axis=1, keepdims=True), (8, lanes))
    count = jnp.sum(keep, axis=0, keepdims=True) * float(sx * sy * BR * GW)
    keep_ref[...] = keep
    seq = keys_ref.shape[1]
    lane = iota((1, seq), 1)
    keys = jnp.zeros((1, seq), F32)
    for k in range(members):
        there = row_of(me ^ k)
        for b in range(sb):
            keys = jnp.where(
                (lane // (seq // members) == k) & (lane % (2 * sb) // 2 == b),
                there[:, b : b + 1], keys,
            )
    keys_ref[...] = jnp.broadcast_to(keys, keys_ref.shape)
    field = feat_ref[...].astype(F32)
    wide = jnp.concatenate([field, jnp.zeros((sx, sy, 8 - sb, lanes), F32)], axis=2)
    wide = wide.reshape(sx * sy, 8, lanes)
    total = jnp.sum(jnp.sum(wide, axis=0) * keep, axis=0, keepdims=True)

    def squares_about(mean):
        d = wide - mean[None]
        return jnp.sum(jnp.sum(d * d, axis=0) * keep, axis=0, keepdims=True)

    code = jnp.where((keep > 0)[None], wide, SENT)
    coded_ref[...] = code.reshape(sx * sy * 8, lanes).astype(BF16)
    packed = pack_pairs(code.reshape(sx, sy, 8, lanes))
    low = packed[0:2].reshape(-1, lanes)
    high = packed[sx - 2 : sx].reshape(-1, lanes)
    size = low.shape[0]
    first_ref[0:size, :] = jnp.where(even("gx"), high, low).astype(BF16)
    second_ref[0:size, :] = jnp.where(even("gx"), low, high).astype(BF16)
    mine = moments(total, squares_about, count)
    tail = to_tail(mine)
    first_ref[size : size + TAIL, :] = tail
    second_ref[size : size + TAIL, :] = tail
    tail_ref[...] = tail
    if rows_ref is not None:
        rows_ref[...] = jnp.broadcast_to(to_row(mine)[0:1], rows_ref.shape)


def line_kernel(narrow, sy, sb, _, coded_ref, first_ref, second_ref, *rest):
    tails, (ext_ref, out_ref, buf) = rest[:-3], rest[-3:]
    lanes = coded_ref.shape[1]
    sx = coded_ref.shape[0] // (sy * 8)
    size = 2 * (sy // 2) * 8
    low, high = sides(
        "gx", first_ref[0:size].astype(F32), second_ref[0:size].astype(F32)
    )
    write_block(buf, 2 * sy * 8, coded_ref[...].astype(F32))
    for x0, side in ((0, low), (sx + 2, high)):
        for i in range(2):
            part = side[i * (size // 2) : (i + 1) * (size // 2)].reshape(sy // 2, 8, lanes)
            pair = split_pairs(part, SENT)
            for y in range(sy):
                write_block(buf, ((x0 + i) * sy + y) * 8, pair[y % 2][y // 2])
    rows = (sx + 4) * sy * 8
    ext_ref[...] = jnp.concatenate([buf[h] for h in halves(lanes)], axis=1).astype(BF16)
    count = (sx + 4) * sy
    face = jnp.where(even("gz"), read(buf, sb - 1, count, 8), read(buf, 0, count, 8))
    out_ref[0:count, :] = face.astype(BF16)
    mine = [from_tail(ref) for ref in tails]
    if narrow:
        mine = mine + [from_tail(first_ref), from_tail(second_ref)]
    out_ref[count : count + TAIL, :] = to_tail(merge(mine))


def corner_rows(count):
    return (count + 15) // 16 * 16


def chip_kernel(sb, sy, ext_ref, own_ref, other_ref, *rest):
    out, (buf, stage) = rest[:-2], rest[-2:]
    lanes = ext_ref.shape[1]
    ex = ext_ref.shape[0] // (sy * 8)
    block = ext_ref[...].astype(F32)
    write_block(buf, 0, block)
    write_block(stage, 0, other_ref[0 : ex * sy].astype(F32))
    gap = corner_rows(ex)
    pad = jnp.zeros((gap - ex, lanes), F32)
    tail = to_tail(merge([from_tail(own_ref), from_tail(other_ref)]))
    packed = pack_pairs(block.reshape(ex, sy, 8, lanes))

    def side(y0):
        face = packed[:, y0 // 2].reshape(ex * 8, lanes)
        inner, outer = [], []
        for i in range(2):
            inner += [read(stage, y0 + i, ex, sy), pad]
            start = (y0 + i) * 8
            outer += [
                jnp.where(
                    even("gz"),
                    read(buf, start, ex, sy * 8),
                    read(buf, start + sb - 1, ex, sy * 8),
                ),
                pad,
            ]
        return [face] + inner, outer

    (near_low, far_low), (near_high, far_high) = side(0), side(sy - 2)
    count = ex * sy
    z_face = jnp.where(even("gz"), read(buf, 0, count, 8), read(buf, sb - 1, count, 8))
    out[0][0:count, :] = z_face.astype(BF16)
    out[0][count : count + TAIL, :] = tail
    for k in range((len(out) - 1) // 2):
        up = even("gy") if k == 0 else jnp.logical_not(even("gy"))
        for ref, low, high in (
            (out[1 + 2 * k], near_low, near_high),
            (out[2 + 2 * k], far_low, far_high),
        ):
            value = jnp.where(
                up, jnp.concatenate(high, axis=0), jnp.concatenate(low, axis=0)
            ).astype(BF16)
            ref[0 : value.shape[0], :] = value
            ref[value.shape[0] : value.shape[0] + TAIL, :] = tail


def band_kernel(weight_ref, *rest):
    pars, (out_ref, more_ref) = rest[:-2], rest[-2:]
    lanes = C * BR
    spread = onehot(iota((C, lanes), 0) == iota((C, lanes), 1) // BR)
    turned = jnp.transpose(weight_ref[0].astype(F32)).astype(BF16)
    wide = jnp.dot(turned, spread, preferred_element_type=F32)
    full = (C, BR, lanes)
    zi, zo = iota((1, BR, lanes), 1), iota((1, BR, lanes), 2) % BR

    def rows(value):
        return jnp.broadcast_to(value[:, None, :], full)

    for ex in range(3):
        mixed = jnp.zeros(full, F32)
        for ey in range(3):
            q = (ex * 3 + ey) * 3
            terms = [wide[(q + e) * C : (q + e + 1) * C] for e in range(3)]
            inner = jnp.where(zi == zo - 1, rows(terms[0]), 0.0)
            inner = jnp.where(zi == zo, rows(terms[1]), inner)
            inner = jnp.where(zi == zo + 1, rows(terms[2]), inner)
            before = pltpu.roll(terms[0], 1, 0) if ey else terms[0]
            low = 2 * ey - 1 if ey else BR - 1
            mixed = jnp.where((zi == low) & (zo == 0), rows(before), mixed)
            mixed = jnp.where((zi == 2 * ey) & (zo == BR - 1), rows(terms[2]), mixed)
            out_ref[ex, ey * lanes : (ey + 1) * lanes, :] = (
                inner.reshape(C * BR, lanes).astype(BF16)
            )
        out_ref[ex, 3 * lanes : 4 * lanes, :] = mixed.reshape(C * BR, lanes).astype(BF16)
    if pars:
        pick = onehot(iota((C, lanes), 0) == iota((C, lanes), 1) // BR, F32)
        more_ref[...] = jnp.zeros(more_ref.shape, F32)
        more_ref[0 : pars[0].shape[0], :] = exact_dot(pars[0][...], pick)
    else:
        more_ref[...] = weight_ref[1:2]


def turn_kernel(weight_ref, out_ref):
    kinds, cols, feats = weight_ref.shape
    r = iota((feats, 1), 0)
    source = (r % 128) // 4 * 32 + r // 128 * 4 + r % 4
    pick = onehot(source == iota((feats, feats), 1))
    for k in range(kinds):
        out_ref[:, k * cols : (k + 1) * cols] = lax.dot_general(
            pick, weight_ref[k], (((1,), (1,)), ((), ())), preferred_element_type=F32
        ).astype(BF16)


def first_kernel(narrow, faces, sy, sb, ext_ref, own_ref, core_ref, zface_ref, *rest):
    near, far = rest[0 : 2 * faces : 2], rest[1 : 2 * faces : 2]
    rest = rest[2 * faces :]
    stats_ref = None
    if not narrow:
        stats_ref, rest = rest[0], rest[1:]
    keep_ref, weight_ref, rows_ref, mid_ref, out_ref, msk, buf, lhs = rest
    lanes = ext_ref.shape[1]
    ex = ext_ref.shape[0] // (sy * 8)
    ey = sy + 4
    count = ex * sy
    z_low, z_high = sides(
        "gz", core_ref[0:count].astype(F32), zface_ref[0:count].astype(F32)
    )
    for x in range(ex):
        write_block(
            buf, (x * ey + 2) * 8, ext_ref[x * sy * 8 : (x + 1) * sy * 8].astype(F32)
        )
        part = slice(x * sy, (x + 1) * sy)
        write(buf, (x * ey + 2) * 8 + 7, sy, 8, z_low[part])
        write(buf, (x * ey + 2) * 8 + sb, sy, 8, z_high[part])
    gap = corner_rows(ex)
    size = ex * 8
    face = sides("gy", *[
        near[k][0:size].astype(F32) if k < faces else None for k in range(2)
    ])
    inner = sides("gy", *[
        near[k][size : size + 2 * gap].astype(F32) if k < faces else None for k in range(2)
    ])
    outer = sides("gy", *[
        far[k][0 : 2 * gap].astype(F32) if k < faces else None for k in range(2)
    ])
    for s, y0 in enumerate((0, sy + 2)):
        pair = split_pairs(face[s].reshape(ex, 8, lanes), SENT)
        c_low, c_high = sides("gz", inner[s], outer[s])
        for i in range(2):
            for x in range(ex):
                write_block(buf, (x * ey + y0 + i) * 8, pair[i][x])
            write(buf, (y0 + i) * 8 + 7, ex, ey * 8, c_low[i * gap : i * gap + ex])
            write(buf, (y0 + i) * 8 + sb, ex, ey * 8, c_high[i * gap : i * gap + ex])
    if narrow:
        centre, scale = centre_scale(merge(
            [from_tail(r) for r in (own_ref, zface_ref) + tuple(near) + tuple(far)]
        ))
    else:
        centre, scale = from_rows(stats_ref[...])
    gain, shift, bias = rows_ref[0:1], rows_ref[2:3], rows_ref[4:5]
    scale = scale * gain
    oy, sx = sy + 2, ex - 4
    step = ey * 8
    for x in range(ex):
        v = jnp.concatenate(
            [buf[h, x * step : (x + 1) * step, :] for h in halves(lanes)], axis=1
        )
        there = v != SENT
        msk[x * step : (x + 1) * step] = onehot(there[:, 0:128], F32)
        act = jnp.where(there, silu((v - centre) * scale + shift), 0.0).reshape(ey, 8, lanes)
        for e, part in enumerate(columns(act, oy)):
            lhs[x * oy * 8 : (x + 1) * oy * 8, e * lanes : (e + 1) * lanes] = (
                part.reshape(oy * 8, lanes).astype(BF16)
            )
    ox = sx + 2
    size = ox * oy * 8
    acc = bias
    for e in range(3):
        acc = acc + jnp.dot(
            lhs[e * oy * 8 : e * oy * 8 + size, :], weight_ref[e], preferred_element_type=F32
        )
    mid_ref[...] = acc
    keep = keep_ref[...]
    entries = jnp.sum(keep[:, 0:1]) * float(sx * sy * BR * GW)

    def over_cells(f):
        out = jnp.zeros((8, lanes), F32)
        for x in range(1, sx + 1):
            own = mid_ref[(x * oy + 1) * 8 : (x * oy + oy - 1) * 8].reshape(sy, 8, lanes)
            out = out + jnp.sum(f(own), axis=0)
        return jnp.sum(out * keep, axis=0, keepdims=True)

    def squares_about(mean):
        return over_cells(lambda v: (v - mean[None]) * (v - mean[None]))

    mine = moments(over_cells(lambda v: v), squares_about, entries)
    out_ref[...] = jnp.broadcast_to(to_row(mine)[0:1], out_ref.shape)


def second_kernel(sx, sy, sb, stats_ref, mid_ref, msk_ref, weight_ref, rows_ref, coded_ref,
                  field_ref, tok_ref, low_ref, high_ref, lhs):
    lanes = coded_ref.shape[1]
    step, ext = (sy + 2) * 8, (sy + 4) * 8
    centre, scale = from_rows(stats_ref[...])
    gain, shift, bias = rows_ref[1:2], rows_ref[3:4], rows_ref[5:6]
    scale = scale * gain
    half = sy // 2 * 8
    for x in range(sx + 2):
        v = mid_ref[x * step : (x + 1) * step]
        there = msk_ref[(x + 1) * ext + 8 : (x + 2) * ext - 8]
        there = jnp.concatenate([there] * (lanes // 128), axis=1) > 0
        act = jnp.where(there, silu((v - centre) * scale + shift), 0.0)
        for e, part in enumerate(columns(act.reshape(sy + 2, 8, lanes), sy)):
            lhs[x * half : (x + 1) * half, e * lanes : (e + 1) * lanes] = (
                pack_pairs(part[None]).reshape(half, lanes).astype(BF16)
            )
    size = sx * half
    acc = bias
    for e in range(3):
        acc = acc + jnp.dot(
            lhs[e * half : e * half + size, :], weight_ref[e], preferred_element_type=F32
        )
    field = pack_pairs(coded_ref[...].astype(F32).reshape(sx, sy, 8, lanes))
    field = field.reshape(size, lanes)
    out = jnp.where(field != SENT, field + acc, 0.0).reshape(-1, 8, lanes)
    out = out.astype(BF16)
    field_ref[...] = out.reshape(size, lanes)
    i, j = iota((lanes, lanes), 0), iota((lanes, lanes), 1)
    pick = onehot(i == (j % 128) // 4 * 8 + j // 128 * 4 + j % 4)
    moved = jnp.dot(out.reshape(size, lanes), pick, preferred_element_type=F32).reshape(
        sx // 2, 2, sy // 4, 2, 8, lanes
    )
    count = sx // 2 * (sy // 4)
    parts = []
    for x in range(2):
        for y in range(2):
            piece = moved[:, x, :, y].reshape(count, 8, lanes)
            low, high = piece[:, :, :128], piece[:, :, 128:]
            inside = iota(low.shape, 1) < 4
            for both in (
                jnp.where(inside, low, pltpu.roll(high, 4, 1)),
                jnp.where(inside, pltpu.roll(low, 4, 1), high),
            ):
                parts.append(both.reshape(count * 8, 128).astype(BF16))
    tokens = jnp.concatenate(parts, axis=1)
    n = count * 8
    i, j = iota((n, n), 0), iota((n, n), 1)
    order = onehot(j == i // 8 * 8 + i % 2 * 4 + i % 8 // 2)
    tokens = jnp.dot(order, tokens, preferred_element_type=F32).astype(BF16)
    tok_ref[...] = tokens
    cut = low_ref.shape[0]
    low_ref[...] = tokens[0:cut]
    high_ref[...] = tokens[cut:n]


def fine_kernel(field_ref, fine_ref):
    sx, sy, sb, lanes = fine_ref.shape
    wide = field_ref[...].astype(F32).reshape(-1, 8, lanes)
    other = pltpu.roll(wide, 4, 1)
    fine = jnp.stack([wide[:, :sb], other[:, :sb]], axis=1)
    fine_ref[...] = fine.reshape(sx, sy, sb, lanes).astype(BF16)


def attend_kernel(members, keys_ref, weight_ref, *refs):
    tok_refs, out_refs, (toks, proj) = refs[: -2 - members], refs[-2 - members : -2], refs[-2:]
    own, cols = tok_refs[0].shape[0], weight_ref.shape[1] // 3
    seq = own * members
    start = 0
    for ref in tok_refs:
        toks[start : start + ref.shape[0], :] = ref[...]
        start += ref.shape[0]
    proj[...] = jnp.dot(toks[...], weight_ref[...], preferred_element_type=F32).astype(BF16)
    there = keys_ref[0:1] > 0
    width = min(128, cols)
    for t in range(cols // width):
        q = proj[:, t * width : (t + 1) * width]
        keys = proj[:, cols + t * width : cols + (t + 1) * width]
        values = proj[:, 2 * cols + t * width : 2 * cols + (t + 1) * width]
        head = iota((seq, width), 1) // HD
        merged = jnp.zeros((seq, width), F32)
        for h in range(width // HD):
            mine = jnp.where(head == h, q.astype(F32), 0.0).astype(BF16)
            scores = lax.dot_general(
                mine, keys, (((1,), (1,)), ((), ())), preferred_element_type=F32
            ) * float(HD) ** (-0.5)
            scores = jnp.where(there, scores, -BIG)
            probs = jnp.exp(scores - jnp.max(scores, axis=1, keepdims=True))
            total = jnp.sum(probs, axis=1, keepdims=True)
            mixed = jnp.dot(probs.astype(BF16), values, preferred_element_type=F32)
            merged = jnp.where(head == h, mixed / total, merged)
        merged = merged.astype(BF16)
        for k in range(members):
            out_refs[-1 - k][:, t * width : (t + 1) * width] = merged[k * own : (k + 1) * own]


def place_kernel(members, keep_ref, *refs):
    out_ref = refs[-1]
    own, cols = refs[0].shape
    me = lax.axis_index("gx")
    row = iota((8, cols), 0)
    keep = jnp.zeros((8, cols), F32)
    for b in range(4):
        keep = jnp.where(row // 2 == b, jnp.broadcast_to(keep_ref[b : b + 1, :cols], (8, cols)), keep)
    for k in range(members):
        value = refs[members - 1 - k][...].astype(F32).reshape(own // 8, 8, cols)
        value = jnp.where((keep > 0)[None], value, 0.0).reshape(own, cols).astype(BF16)
        if cols % 128 == 0:
            out_ref[0, :, pl.ds(pl.multiple_of((me ^ k) * cols, cols), cols)] = value
        else:
            out_ref[k] = value


VM = pl.BlockSpec(memory_space=pltpu.VMEM)


def call(kernel, name, specs, out, args, scratch=(), flops=0, nbytes=0, mib=16):
    return pl.pallas_call(
        kernel,
        out_shape=out,
        in_specs=list(specs),
        out_specs=jax.tree.map(lambda _: VM, out),
        scratch_shapes=list(scratch),
        name=name,
        cost_estimate=pl.CostEstimate(flops=flops, bytes_accessed=nbytes, transcendentals=0),
        compiler_params=pltpu.CompilerParams(vmem_limit_bytes=mib * 2**20),
    )(*args)


def shape(*dims, dtype=BF16):
    return jax.ShapeDtypeStruct(dims, dtype)


def pairing(n, odd, closed):
    partner = {i: (i ^ 1 if not odd else (i + 1 if i % 2 else i - 1)) for i in range(n)}
    if closed:
        partner = {i: j % n for i, j in partner.items()}
    return {i: j for i, j in partner.items() if 0 <= j < n and i != j}


def body(features, occupancy, norm_gain, norm_shift, conv_weight, conv_bias, qkv_weight):
    sx, sy, sb, lanes = features.shape
    nx, ny, nz = (lax.axis_size(a) for a in ALL)
    devices = nx * ny * nz
    narrow = nx == 4 and ny == 2 and nz == 4
    own = sx // 2 * (sy // 4) * sb * 2
    ex = sx + 4
    row_shape = [] if narrow else [shape(devices, 128, dtype=F32)]

    slab = sy * 8 + TAIL
    keep, keys, coded, first, second, tail, *stats = call(
        functools.partial(pre_kernel, nx), "pre", (VM, VM),
        [shape(8, lanes, dtype=F32), shape(8, own * nx, dtype=F32),
         shape(sx * sy * 8, lanes), shape(slab, lanes), shape(slab, lanes), shape(TAIL, lanes)]
        + row_shape,
        (occupancy, features), nbytes=10**6,
    )
    stats = [lax.all_to_all(s, ALL, 0, 0, tiled=True) for s in stats]
    got = [
        lax.ppermute(first, "gx", list(pairing(nx, False, False).items())),
        lax.ppermute(second, "gx", list(pairing(nx, True, narrow).items())),
    ]
    tails = [tail]
    if narrow:
        tails.append(lax.ppermute(tail, "gx", [(i, i ^ 2) for i in range(nx)]))
    band = shape(3, 4 * lanes, lanes)
    pars = jnp.concatenate([norm_gain, norm_shift, conv_bias], axis=0)
    later = shape(1, *conv_weight.shape[1:])
    band0, later = call(
        band_kernel, "band0", (VM,), [band, later], (conv_weight,), nbytes=8 * 10**6,
    )
    band1, rows = call(
        band_kernel, "band1", (VM,) * 2, [band, shape(8, lanes, dtype=F32)], (later, pars),
        nbytes=8 * 10**6,
    )
    count = ex * sy
    ext, mine = call(
        functools.partial(line_kernel, narrow, sy, sb), "line", (VM,) * (4 + len(tails)),
        [shape(count * 8, lanes), shape(count + TAIL, lanes)],
        (later, coded, *got, *tails),
        [pltpu.VMEM((lanes // 128, count * 8, 128), F32)], nbytes=10**6,
    )
    core = lax.ppermute(mine, "gz", list(pairing(nz, False, False).items()))

    faces = 1 if ny == 2 else 2
    gap = corner_rows(ex)
    near, far = ex * 8 + 2 * gap + TAIL, 2 * gap + TAIL
    zface, *yfaces = call(
        functools.partial(chip_kernel, sb, sy), "chip", (VM,) * 3,
        [shape(count + TAIL, lanes)] + [shape(near, lanes), shape(far, lanes)] * faces,
        (ext, mine, core),
        [pltpu.VMEM((lanes // 128, count * 8, 128), F32),
         pltpu.VMEM((lanes // 128, count, 128), F32)], nbytes=10**6,
    )
    odd_z = pairing(nz, True, narrow)
    own_tail = zface
    zgot = lax.ppermute(zface, "gz", list(odd_z.items()))
    ygot = []
    for k in range(faces):
        along = pairing(ny, k == 1, False)
        ygot.append(lax.ppermute(yfaces[2 * k], "gy", list(along.items())))
        both = [
            (y * nz + z, along[y] * nz + odd_z[z]) for y in along for z in odd_z
        ]
        ygot.append(lax.ppermute(yfaces[2 * k + 1], ("gy", "gz"), both))

    cols, feats = qkv_weight.shape[1:]
    turned = call(
        turn_kernel, "turn", (VM,), shape(feats, 3 * cols), (qkv_weight,),
        flops=2 * 3 * cols * feats * feats, nbytes=6 * 10**6,
    )

    ey, oy = sy + 4, sy + 2
    size = (sx + 2) * oy * 8
    mid, mine, there = call(
        functools.partial(first_kernel, narrow, faces, sy, sb), "first",
        (VM,) * (7 + 2 * faces + len(stats)),
        [shape(size, lanes, dtype=F32), shape(devices, 128, dtype=F32),
         shape(ex * ey * 8, 128, dtype=F32)],
        (ext, own_tail, core, zgot, *ygot, *stats, keep, band0, rows),
        [pltpu.VMEM((lanes // 128, ex * ey * 8, 128), F32),
         pltpu.VMEM((ex * oy * 8, 4 * lanes), BF16)],
        flops=2 * 10**9, nbytes=4 * 10**6, mib=20,
    )
    stats = lax.all_to_all(mine, ALL, 0, 0, tiled=True)
    field, tokens, *parts = call(
        functools.partial(second_kernel, sx, sy, sb), "second", (VM,) * 6,
        [shape(sx * sy * 4, lanes), shape(own, feats)] + [shape(own // 4 * 3, feats), shape(own // 4, feats)],
        (stats, mid, there, band1, rows, coded),
        [pltpu.VMEM(((sx + 2) * sy * 4, 4 * lanes), BF16)],
        flops=10**9, nbytes=4 * 10**6,
    )
    fine_out = call(
        fine_kernel, "fine", (VM,), shape(*features.shape), (field,), nbytes=4 * 10**6, mib=8,
    )
    swaps = [[(i, i ^ k) for i in range(nx)] for k in range(nx)]
    blocks = {0: parts}
    for k in sorted(range(1, nx), key=lambda k: (bin(k).count("1"), -k)):
        low = k & -k
        source = [tokens] if k == 1 else blocks[k ^ low]
        blocks[k] = [lax.ppermute(v, "gx", swaps[low]) for v in source]
    blocks = [tokens] + [v for k in range(1, nx) for v in blocks[k]]
    outs = call(
        functools.partial(attend_kernel, nx), "attend", (VM,) * (2 + len(blocks)),
        [shape(own, cols)] * nx, (keys, turned, *blocks),
        [pltpu.VMEM((own * nx, feats), BF16), pltpu.VMEM((own * nx, 3 * cols), BF16)],
        flops=10**9, nbytes=3 * 10**6, mib=16 if narrow else 40,
    )
    moved = [lax.ppermute(v, "gx", swaps[nx - 1 - i]) for i, v in enumerate(outs[:-1])]
    outs = moved + [outs[-1]]
    lined = cols % 128 == 0
    attention = call(
        functools.partial(place_kernel, nx), "place", (VM,) * (1 + nx),
        shape(1, own, nx * cols) if lined else shape(nx, own, cols), (keep, *outs),
        nbytes=3 * 10**5, mib=8,
    )
    if not lined:
        me = lax.axis_index("gx")
        attention = jnp.concatenate(
            [lax.dynamic_index_in_dim(attention, me ^ j, 0, keepdims=False) for j in range(nx)],
            axis=1,
        )[None]
    return (fine_out, attention)


def solution(mesh):
    placed = (
        P("gx", "gy", "gz", None),
        P(None, "gy", "gz"),
        P(),
        P(),
        P(),
        P(),
        P(None, "gx", None),
    )
    return jax.shard_map(
        body,
        mesh=mesh,
        in_specs=placed,
        out_specs=(P("gx", "gy", "gz", None), P(("gy", "gz"), "gx", None)),
        check_vma=False,
    )
```

```python
import functools

import jax
import jax.numpy as jnp
from jax import lax
from jax.experimental import pallas as pl
from jax.experimental.pallas import tpu as pltpu
from jax.sharding import PartitionSpec as P

C = 32
GW = 4
HD = 64
BR = 8
EPS = 1e-05
SENT = 512.0
BIG = 1e30
ALL = ("gx", "gy", "gz")
F32, BF16 = jnp.float32, jnp.bfloat16
HIGHEST = lax.Precision.HIGHEST
TAIL = 16


def iota(shape, dim):
    return lax.broadcasted_iota(jnp.int32, shape, dim)


def onehot(cond, dtype=BF16):
    return jnp.where(cond, 1.0, 0.0).astype(dtype)


def exact_dot(a, b):
    return jnp.dot(a, b, precision=HIGHEST, preferred_element_type=F32)


def spread_sum(v):
    lane = iota(v.shape, 1)
    s = 1
    while s < GW * BR:
        v = v + jnp.where(lane & s == 0, pltpu.roll(v, 128 - s, 1), pltpu.roll(v, s, 1))
        s *= 2
    return v


def group_sum(total):
    k = total.shape[1] // 128
    rows = [jnp.broadcast_to(total[:, h * 128 : (h + 1) * 128], (8, 128)) for h in range(k)]
    out = spread_sum(jnp.concatenate(rows, axis=0))
    return jnp.concatenate([out[h * 8 : (h + 1) * 8] for h in range(k)], axis=1)


def moments(total, squares_about, count):
    sums = group_sum(total)
    squares = group_sum(squares_about((sums / count)[0:1]))
    return sums, squares, jnp.zeros(sums.shape, F32) + count


def merge(parts):
    n = sum(p[2] for p in parts)
    sums = sum(p[0] for p in parts)
    centre = sums / n
    squares = sum(p[1] + p[2] * (p[0] / p[2] - centre) ** 2 for p in parts)
    return sums, squares, n


def centre_scale(part):
    return part[0] / part[2], lax.rsqrt(part[1] / part[2] + EPS)


def to_row(part):
    j = iota((8, 128), 1) % (GW * BR)
    row = jnp.zeros((8, 128), F32)
    for h in range(2):
        for k in range(3):
            row = jnp.where(j == 4 * h + k, part[k][:, h * 128 : (h + 1) * 128], row)
    return row


def from_rows(rows):
    n = jnp.maximum(pltpu.roll(rows, 126, 1), 1.0)
    total = jnp.sum(n, axis=0, keepdims=True)
    centre = jnp.sum(rows, axis=0, keepdims=True) / total
    drift = rows / n - centre
    squares = pltpu.roll(rows, 127, 1) + n * drift * drift
    spread = jnp.sum(squares, axis=0, keepdims=True) / total
    j = iota((8, 128), 1) % (GW * BR)
    blocks = [
        jnp.where(j == 4 * h, jnp.broadcast_to(v, (8, 128)), 0.0)
        for v in (centre, spread) for h in range(2)
    ]
    out = spread_sum(jnp.concatenate(blocks, axis=0))
    out = [out[8 * i : 8 * i + 1] for i in range(4)]
    return (
        jnp.concatenate(out[:2], axis=1),
        lax.rsqrt(jnp.concatenate(out[2:], axis=1) + EPS),
    )


def to_tail(part):
    index = iota((8, 256), 0)
    blocks = [jnp.zeros((8, 256), F32), jnp.zeros((8, 256), F32)]
    for k, value in enumerate(part):
        value = jnp.broadcast_to(value[0:1], (8, 256))
        high = value.astype(BF16).astype(F32)
        mid = (value - high).astype(BF16).astype(F32)
        for i, piece in enumerate((high, mid, value - high - mid)):
            blocks[k // 2] = jnp.where(index == 3 * (k % 2) + i, piece, blocks[k // 2])
    return jnp.concatenate(blocks, axis=0).astype(BF16)


def from_tail(message_ref):
    rows = message_ref.shape[0]
    part = message_ref[rows - TAIL : rows, :].astype(F32)
    return [
        jnp.sum(part[r : r + 3], axis=0, keepdims=True) for r in (0, 3, 8)
    ]


def silu(u):
    return 0.5 * u * (1.0 + jnp.tanh(0.5 * u))


def pack_pairs(v):
    n, m, _, lanes = v.shape
    v = v.reshape(n, m // 2, 2, 8, lanes)
    low, high = v[:, :, 0].reshape(-1, 8, lanes), v[:, :, 1].reshape(-1, 8, lanes)
    both = jnp.where(iota(low.shape, 1) < 4, low, pltpu.roll(high, 4, 1))
    return both.reshape(n, m // 2, 8, lanes)


def split_pairs(v, blank):
    inside = iota(v.shape, 1) < 4
    return [jnp.where(inside, v, blank), jnp.where(inside, pltpu.roll(v, 4, 1), blank)]


def edges(act):
    z = iota(act.shape, 2) % BR
    before, after = pltpu.roll(act, 1, 1), pltpu.roll(act, 7, 1)
    return jnp.where(z == BR - 1, before, jnp.where(z == 0, after, 0.0))


def columns(act, size):
    side = edges(act)
    z = iota((size,) + act.shape[1:], 2) % BR
    second = pltpu.roll(side, 2, 2)
    third = pltpu.roll(side, 4, 2)
    mixed = jnp.where(
        (z == 1) | (z == 2), second[1 : 1 + size],
        jnp.where((z == 3) | (z == 4), third[2 : 2 + size], side[0:size]),
    )
    return [act[e : e + size] for e in range(3)] + [mixed]


def halves(lanes):
    return range(lanes // 128)


def read(ref, start, count, stride):
    return jnp.concatenate(
        [ref[h, pl.ds(start, count, stride=stride), :] for h in range(ref.shape[0])], axis=1
    )


def write(ref, start, count, stride, value):
    for h in range(ref.shape[0]):
        ref[h, pl.ds(start, count, stride=stride), :] = value[:, h * 128 : (h + 1) * 128]


def write_block(ref, start, value):
    for h in range(ref.shape[0]):
        ref[h, start : start + value.shape[0], :] = value[:, h * 128 : (h + 1) * 128]


def even(axis):
    return lax.axis_index(axis) % 2 == 0


def sides(axis, first, second):
    i, n = lax.axis_index(axis), lax.axis_size(axis)
    blank = jnp.full(first.shape, SENT, F32)
    second = blank if second is None else second
    low, high = jnp.where(even(axis), second, first), jnp.where(even(axis), first, second)
    return jnp.where(i > 0, low, SENT), jnp.where(i < n - 1, high, SENT)


def pre_kernel(members, occ_ref, feat_ref, keep_ref, keys_ref, coded_ref, first_ref, second_ref,
               tail_ref, rows_ref=None):
    sx, sy, sb, lanes = feat_ref.shape
    me = lax.axis_index("gx")
    bricks = [occ_ref[x].astype(F32) for x in range(members)]

    def row_of(x):
        return sum(jnp.where(x == i, v, 0.0) for i, v in enumerate(bricks))

    mine = jnp.broadcast_to(row_of(me), (8, sb))
    keep = jnp.where(iota((8, sb), 0) == iota((8, sb), 1), mine, 0.0)
    keep = jnp.broadcast_to(jnp.sum(keep, axis=1, keepdims=True), (8, lanes))
    count = jnp.sum(keep, axis=0, keepdims=True) * float(sx * sy * BR * GW)
    keep_ref[...] = keep
    seq = keys_ref.shape[1]
    lane = iota((1, seq), 1)
    keys = jnp.zeros((1, seq), F32)
    for k in range(members):
        there = row_of(me ^ k)
        for b in range(sb):
            keys = jnp.where(
                (lane // (seq // members) == k) & (lane % (2 * sb) // 2 == b),
                there[:, b : b + 1], keys,
            )
    keys_ref[...] = jnp.broadcast_to(keys, keys_ref.shape)
    field = feat_ref[...].astype(F32)
    wide = jnp.concatenate([field, jnp.zeros((sx, sy, 8 - sb, lanes), F32)], axis=2)
    wide = wide.reshape(sx * sy, 8, lanes)
    total = jnp.sum(jnp.sum(wide, axis=0) * keep, axis=0, keepdims=True)

    def squares_about(mean):
        d = wide - mean[None]
        return jnp.sum(jnp.sum(d * d, axis=0) * keep, axis=0, keepdims=True)

    code = jnp.where((keep > 0)[None], wide, SENT)
    coded_ref[...] = code.reshape(sx * sy * 8, lanes).astype(BF16)
    packed = pack_pairs(code.reshape(sx, sy, 8, lanes))
    low = packed[0:2].reshape(-1, lanes)
    high = packed[sx - 2 : sx].reshape(-1, lanes)
    size = low.shape[0]
    first_ref[0:size, :] = jnp.where(even("gx"), high, low).astype(BF16)
    second_ref[0:size, :] = jnp.where(even("gx"), low, high).astype(BF16)
    mine = moments(total, squares_about, count)
    tail = to_tail(mine)
    first_ref[size : size + TAIL, :] = tail
    second_ref[size : size + TAIL, :] = tail
    tail_ref[...] = tail
    if rows_ref is not None:
        rows_ref[...] = jnp.broadcast_to(to_row(mine)[0:1], rows_ref.shape)


def line_kernel(narrow, sy, sb, _, coded_ref, first_ref, second_ref, *rest):
    tails, (ext_ref, out_ref, buf) = rest[:-3], rest[-3:]
    lanes = coded_ref.shape[1]
    sx = coded_ref.shape[0] // (sy * 8)
    size = 2 * (sy // 2) * 8
    low, high = sides(
        "gx", first_ref[0:size].astype(F32), second_ref[0:size].astype(F32)
    )
    write_block(buf, 2 * sy * 8, coded_ref[...].astype(F32))
    for x0, side in ((0, low), (sx + 2, high)):
        for i in range(2):
            part = side[i * (size // 2) : (i + 1) * (size // 2)].reshape(sy // 2, 8, lanes)
            pair = split_pairs(part, SENT)
            for y in range(sy):
                write_block(buf, ((x0 + i) * sy + y) * 8, pair[y % 2][y // 2])
    rows = (sx + 4) * sy * 8
    ext_ref[...] = jnp.concatenate([buf[h] for h in halves(lanes)], axis=1).astype(BF16)
    count = (sx + 4) * sy
    face = jnp.where(even("gz"), read(buf, sb - 1, count, 8), read(buf, 0, count, 8))
    out_ref[0:count, :] = face.astype(BF16)
    mine = [from_tail(ref) for ref in tails]
    if narrow:
        mine = mine + [from_tail(first_ref), from_tail(second_ref)]
    out_ref[count : count + TAIL, :] = to_tail(merge(mine))


def corner_rows(count):
    return (count + 15) // 16 * 16


def chip_kernel(sb, sy, ext_ref, own_ref, other_ref, *rest):
    out, (buf, stage) = rest[:-2], rest[-2:]
    lanes = ext_ref.shape[1]
    ex = ext_ref.shape[0] // (sy * 8)
    block = ext_ref[...].astype(F32)
    write_block(buf, 0, block)
    write_block(stage, 0, other_ref[0 : ex * sy].astype(F32))
    gap = corner_rows(ex)
    pad = jnp.zeros((gap - ex, lanes), F32)
    tail = to_tail(merge([from_tail(own_ref), from_tail(other_ref)]))
    packed = pack_pairs(block.reshape(ex, sy, 8, lanes))

    def side(y0):
        face = packed[:, y0 // 2].reshape(ex * 8, lanes)
        inner, outer = [], []
        for i in range(2):
            inner += [read(stage, y0 + i, ex, sy), pad]
            start = (y0 + i) * 8
            outer += [
                jnp.where(
                    even("gz"),
                    read(buf, start, ex, sy * 8),
                    read(buf, start + sb - 1, ex, sy * 8),
                ),
                pad,
            ]
        return [face] + inner, outer

    (near_low, far_low), (near_high, far_high) = side(0), side(sy - 2)
    count = ex * sy
    z_face = jnp.where(even("gz"), read(buf, 0, count, 8), read(buf, sb - 1, count, 8))
    out[0][0:count, :] = z_face.astype(BF16)
    out[0][count : count + TAIL, :] = tail
    for k in range((len(out) - 1) // 2):
        up = even("gy") if k == 0 else jnp.logical_not(even("gy"))
        for ref, low, high in (
            (out[1 + 2 * k], near_low, near_high),
            (out[2 + 2 * k], far_low, far_high),
        ):
            value = jnp.where(
                up, jnp.concatenate(high, axis=0), jnp.concatenate(low, axis=0)
            ).astype(BF16)
            ref[0 : value.shape[0], :] = value
            ref[value.shape[0] : value.shape[0] + TAIL, :] = tail


def band_kernel(weight_ref, *rest):
    pars, (out_ref, more_ref) = rest[:-2], rest[-2:]
    lanes = C * BR
    spread = onehot(iota((C, lanes), 0) == iota((C, lanes), 1) // BR)
    turned = jnp.transpose(weight_ref[0].astype(F32)).astype(BF16)
    wide = jnp.dot(turned, spread, preferred_element_type=F32)
    full = (C, BR, lanes)
    zi, zo = iota((1, BR, lanes), 1), iota((1, BR, lanes), 2) % BR

    def rows(value):
        return jnp.broadcast_to(value[:, None, :], full)

    for ex in range(3):
        mixed = jnp.zeros(full, F32)
        for ey in range(3):
            q = (ex * 3 + ey) * 3
            terms = [wide[(q + e) * C : (q + e + 1) * C] for e in range(3)]
            inner = jnp.where(zi == zo - 1, rows(terms[0]), 0.0)
            inner = jnp.where(zi == zo, rows(terms[1]), inner)
            inner = jnp.where(zi == zo + 1, rows(terms[2]), inner)
            before = pltpu.roll(terms[0], 1, 0) if ey else terms[0]
            low = 2 * ey - 1 if ey else BR - 1
            mixed = jnp.where((zi == low) & (zo == 0), rows(before), mixed)
            mixed = jnp.where((zi == 2 * ey) & (zo == BR - 1), rows(terms[2]), mixed)
            out_ref[ex, ey * lanes : (ey + 1) * lanes, :] = (
                inner.reshape(C * BR, lanes).astype(BF16)
            )
        out_ref[ex, 3 * lanes : 4 * lanes, :] = mixed.reshape(C * BR, lanes).astype(BF16)
    if pars:
        pick = onehot(iota((C, lanes), 0) == iota((C, lanes), 1) // BR, F32)
        more_ref[...] = jnp.zeros(more_ref.shape, F32)
        more_ref[0 : pars[0].shape[0], :] = exact_dot(pars[0][...], pick)
    else:
        more_ref[...] = weight_ref[1:2]


def turn_kernel(weight_ref, out_ref):
    kinds, cols, feats = weight_ref.shape
    r = iota((feats, 1), 0)
    source = (r % 128) // 4 * 32 + r // 128 * 4 + r % 4
    pick = onehot(source == iota((feats, feats), 1))
    for k in range(kinds):
        out_ref[:, k * cols : (k + 1) * cols] = lax.dot_general(
            pick, weight_ref[k], (((1,), (1,)), ((), ())), preferred_element_type=F32
        ).astype(BF16)


def first_kernel(narrow, faces, sy, sb, ext_ref, own_ref, core_ref, zface_ref, *rest):
    near, far = rest[0 : 2 * faces : 2], rest[1 : 2 * faces : 2]
    rest = rest[2 * faces :]
    stats_ref = None
    if not narrow:
        stats_ref, rest = rest[0], rest[1:]
    keep_ref, weight_ref, rows_ref, mid_ref, out_ref, msk, buf, lhs = rest
    lanes = ext_ref.shape[1]
    ex = ext_ref.shape[0] // (sy * 8)
    ey = sy + 4
    count = ex * sy
    z_low, z_high = sides(
        "gz", core_ref[0:count].astype(F32), zface_ref[0:count].astype(F32)
    )
    for x in range(ex):
        write_block(
            buf, (x * ey + 2) * 8, ext_ref[x * sy * 8 : (x + 1) * sy * 8].astype(F32)
        )
        part = slice(x * sy, (x + 1) * sy)
        write(buf, (x * ey + 2) * 8 + 7, sy, 8, z_low[part])
        write(buf, (x * ey + 2) * 8 + sb, sy, 8, z_high[part])
    gap = corner_rows(ex)
    size = ex * 8
    face = sides("gy", *[
        near[k][0:size].astype(F32) if k < faces else None for k in range(2)
    ])
    inner = sides("gy", *[
        near[k][size : size + 2 * gap].astype(F32) if k < faces else None for k in range(2)
    ])
    outer = sides("gy", *[
        far[k][0 : 2 * gap].astype(F32) if k < faces else None for k in range(2)
    ])
    for s, y0 in enumerate((0, sy + 2)):
        pair = split_pairs(face[s].reshape(ex, 8, lanes), SENT)
        c_low, c_high = sides("gz", inner[s], outer[s])
        for i in range(2):
            for x in range(ex):
                write_block(buf, (x * ey + y0 + i) * 8, pair[i][x])
            write(buf, (y0 + i) * 8 + 7, ex, ey * 8, c_low[i * gap : i * gap + ex])
            write(buf, (y0 + i) * 8 + sb, ex, ey * 8, c_high[i * gap : i * gap + ex])
    if narrow:
        centre, scale = centre_scale(merge(
            [from_tail(r) for r in (own_ref, zface_ref) + tuple(near) + tuple(far)]
        ))
    else:
        centre, scale = from_rows(stats_ref[...])
    gain, shift, bias = rows_ref[0:1], rows_ref[2:3], rows_ref[4:5]
    scale = scale * gain
    oy, sx = sy + 2, ex - 4
    step = ey * 8
    for x in range(ex):
        v = jnp.concatenate(
            [buf[h, x * step : (x + 1) * step, :] for h in halves(lanes)], axis=1
        )
        there = v != SENT
        msk[x * step : (x + 1) * step] = onehot(there[:, 0:128], F32)
        act = jnp.where(there, silu((v - centre) * scale + shift), 0.0).reshape(ey, 8, lanes)
        for e, part in enumerate(columns(act, oy)):
            lhs[x * oy * 8 : (x + 1) * oy * 8, e * lanes : (e + 1) * lanes] = (
                part.reshape(oy * 8, lanes).astype(BF16)
            )
    ox = sx + 2
    size = ox * oy * 8
    acc = bias
    for e in range(3):
        acc = acc + jnp.dot(
            lhs[e * oy * 8 : e * oy * 8 + size, :], weight_ref[e], preferred_element_type=F32
        )
    mid_ref[...] = acc
    keep = keep_ref[...]
    entries = jnp.sum(keep[:, 0:1]) * float(sx * sy * BR * GW)

    def over_cells(f):
        out = jnp.zeros((8, lanes), F32)
        for x in range(1, sx + 1):
            own = mid_ref[(x * oy + 1) * 8 : (x * oy + oy - 1) * 8].reshape(sy, 8, lanes)
            out = out + jnp.sum(f(own), axis=0)
        return jnp.sum(out * keep, axis=0, keepdims=True)

    def squares_about(mean):
        return over_cells(lambda v: (v - mean[None]) * (v - mean[None]))

    mine = moments(over_cells(lambda v: v), squares_about, entries)
    out_ref[...] = jnp.broadcast_to(to_row(mine)[0:1], out_ref.shape)


def second_kernel(sx, sy, sb, stats_ref, mid_ref, msk_ref, weight_ref, rows_ref, coded_ref,
                  field_ref, tok_ref, low_ref, high_ref, lhs):
    lanes = coded_ref.shape[1]
    step, ext = (sy + 2) * 8, (sy + 4) * 8
    centre, scale = from_rows(stats_ref[...])
    gain, shift, bias = rows_ref[1:2], rows_ref[3:4], rows_ref[5:6]
    scale = scale * gain
    half = sy // 2 * 8
    for x in range(sx + 2):
        v = mid_ref[x * step : (x + 1) * step]
        there = msk_ref[(x + 1) * ext + 8 : (x + 2) * ext - 8]
        there = jnp.concatenate([there] * (lanes // 128), axis=1) > 0
        act = jnp.where(there, silu((v - centre) * scale + shift), 0.0)
        for e, part in enumerate(columns(act.reshape(sy + 2, 8, lanes), sy)):
            lhs[x * half : (x + 1) * half, e * lanes : (e + 1) * lanes] = (
                pack_pairs(part[None]).reshape(half, lanes).astype(BF16)
            )
    size = sx * half
    acc = bias
    for e in range(3):
        acc = acc + jnp.dot(
            lhs[e * half : e * half + size, :], weight_ref[e], preferred_element_type=F32
        )
    field = pack_pairs(coded_ref[...].astype(F32).reshape(sx, sy, 8, lanes))
    field = field.reshape(size, lanes)
    out = jnp.where(field != SENT, field + acc, 0.0).reshape(-1, 8, lanes)
    out = out.astype(BF16)
    field_ref[...] = out.reshape(size, lanes)
    i, j = iota((lanes, lanes), 0), iota((lanes, lanes), 1)
    pick = onehot(i == (j % 128) // 4 * 8 + j // 128 * 4 + j % 4)
    moved = jnp.dot(out.reshape(size, lanes), pick, preferred_element_type=F32).reshape(
        sx // 2, 2, sy // 4, 2, 8, lanes
    )
    count = sx // 2 * (sy // 4)
    parts = []
    for x in range(2):
        for y in range(2):
            piece = moved[:, x, :, y].reshape(count, 8, lanes)
            low, high = piece[:, :, :128], piece[:, :, 128:]
            inside = iota(low.shape, 1) < 4
            for both in (
                jnp.where(inside, low, pltpu.roll(high, 4, 1)),
                jnp.where(inside, pltpu.roll(low, 4, 1), high),
            ):
                parts.append(both.reshape(count * 8, 128).astype(BF16))
    tokens = jnp.concatenate(parts, axis=1)
    n = count * 8
    i, j = iota((n, n), 0), iota((n, n), 1)
    order = onehot(j == i // 8 * 8 + i % 2 * 4 + i % 8 // 2)
    tokens = jnp.dot(order, tokens, preferred_element_type=F32).astype(BF16)
    tok_ref[...] = tokens
    low_ref[...] = tokens[0 : n // 2]
    high_ref[...] = tokens[n // 2 : n]


def fine_kernel(field_ref, fine_ref):
    sx, sy, sb, lanes = fine_ref.shape
    wide = field_ref[...].astype(F32).reshape(-1, 8, lanes)
    other = pltpu.roll(wide, 4, 1)
    fine = jnp.stack([wide[:, :sb], other[:, :sb]], axis=1)
    fine_ref[...] = fine.reshape(sx, sy, sb, lanes).astype(BF16)


def attend_kernel(members, keys_ref, weight_ref, *refs):
    tok_refs, out_refs, (toks, proj) = refs[: -2 - members], refs[-2 - members : -2], refs[-2:]
    own, cols = tok_refs[0].shape[0], weight_ref.shape[1] // 3
    seq = own * members
    start = 0
    for ref in tok_refs:
        toks[start : start + ref.shape[0], :] = ref[...]
        start += ref.shape[0]
    proj[...] = jnp.dot(toks[...], weight_ref[...], preferred_element_type=F32).astype(BF16)
    there = keys_ref[0:1] > 0
    width = min(128, cols)
    for t in range(cols // width):
        q = proj[:, t * width : (t + 1) * width]
        keys = proj[:, cols + t * width : cols + (t + 1) * width]
        values = proj[:, 2 * cols + t * width : 2 * cols + (t + 1) * width]
        head = iota((seq, width), 1) // HD
        merged = jnp.zeros((seq, width), F32)
        for h in range(width // HD):
            mine = jnp.where(head == h, q.astype(F32) * float(HD) ** (-0.5), 0.0).astype(BF16)
            scores = lax.dot_general(
                mine, keys, (((1,), (1,)), ((), ())), preferred_element_type=F32
            )
            scores = jnp.where(there, scores, -BIG)
            probs = jnp.exp(scores - jnp.max(scores, axis=1, keepdims=True))
            total = jnp.sum(probs, axis=1, keepdims=True)
            mixed = jnp.dot(probs.astype(BF16), values, preferred_element_type=F32)
            merged = jnp.where(head == h, mixed * (1.0 / total), merged)
        merged = merged.astype(BF16)
        for k in range(members):
            out_refs[-1 - k][:, t * width : (t + 1) * width] = merged[k * own : (k + 1) * own]


def place_kernel(members, keep_ref, *refs):
    out_ref = refs[-1]
    own, cols = refs[0].shape
    me = lax.axis_index("gx")
    row = iota((8, cols), 0)
    keep = jnp.zeros((8, cols), F32)
    for b in range(4):
        keep = jnp.where(row // 2 == b, jnp.broadcast_to(keep_ref[b : b + 1, :cols], (8, cols)), keep)
    for k in range(members):
        value = refs[members - 1 - k][...].astype(F32).reshape(own // 8, 8, cols)
        value = jnp.where((keep > 0)[None], value, 0.0).reshape(own, cols).astype(BF16)
        if cols % 128 == 0:
            out_ref[0, :, pl.ds(pl.multiple_of((me ^ k) * cols, cols), cols)] = value
        else:
            out_ref[k] = value


VM = pl.BlockSpec(memory_space=pltpu.VMEM)


def call(kernel, name, specs, out, args, scratch=(), flops=0, nbytes=0, mib=16):
    return pl.pallas_call(
        kernel,
        out_shape=out,
        in_specs=list(specs),
        out_specs=jax.tree.map(lambda _: VM, out),
        scratch_shapes=list(scratch),
        name=name,
        cost_estimate=pl.CostEstimate(flops=flops, bytes_accessed=nbytes, transcendentals=0),
        compiler_params=pltpu.CompilerParams(vmem_limit_bytes=mib * 2**20),
    )(*args)


def shape(*dims, dtype=BF16):
    return jax.ShapeDtypeStruct(dims, dtype)


def pairing(n, odd, closed):
    partner = {i: (i ^ 1 if not odd else (i + 1 if i % 2 else i - 1)) for i in range(n)}
    if closed:
        partner = {i: j % n for i, j in partner.items()}
    return {i: j for i, j in partner.items() if 0 <= j < n and i != j}


def body(features, occupancy, norm_gain, norm_shift, conv_weight, conv_bias, qkv_weight):
    sx, sy, sb, lanes = features.shape
    nx, ny, nz = (lax.axis_size(a) for a in ALL)
    devices = nx * ny * nz
    narrow = nx == 4 and ny == 2 and nz == 4
    own = sx // 2 * (sy // 4) * sb * 2
    ex = sx + 4
    row_shape = [] if narrow else [shape(devices, 128, dtype=F32)]

    slab = sy * 8 + TAIL
    keep, keys, coded, first, second, tail, *stats = call(
        functools.partial(pre_kernel, nx), "pre", (VM, VM),
        [shape(8, lanes, dtype=F32), shape(8, own * nx, dtype=F32),
         shape(sx * sy * 8, lanes), shape(slab, lanes), shape(slab, lanes), shape(TAIL, lanes)]
        + row_shape,
        (occupancy, features), nbytes=10**6,
    )
    stats = [lax.all_to_all(s, ALL, 0, 0, tiled=True) for s in stats]
    got = [
        lax.ppermute(first, "gx", list(pairing(nx, False, False).items())),
        lax.ppermute(second, "gx", list(pairing(nx, True, narrow).items())),
    ]
    tails = [tail]
    if narrow:
        tails.append(lax.ppermute(tail, "gx", [(i, i ^ 2) for i in range(nx)]))
    band = shape(3, 4 * lanes, lanes)
    pars = jnp.concatenate([norm_gain, norm_shift, conv_bias], axis=0)
    later = shape(1, *conv_weight.shape[1:])
    band0, later = call(
        band_kernel, "band0", (VM,), [band, later], (conv_weight,), nbytes=8 * 10**6,
    )
    band1, rows = call(
        band_kernel, "band1", (VM,) * 2, [band, shape(8, lanes, dtype=F32)], (later, pars),
        nbytes=8 * 10**6,
    )
    count = ex * sy
    ext, mine = call(
        functools.partial(line_kernel, narrow, sy, sb), "line", (VM,) * (4 + len(tails)),
        [shape(count * 8, lanes), shape(count + TAIL, lanes)],
        (later, coded, *got, *tails),
        [pltpu.VMEM((lanes // 128, count * 8, 128), F32)], nbytes=10**6,
    )
    core = lax.ppermute(mine, "gz", list(pairing(nz, False, False).items()))

    faces = 1 if ny == 2 else 2
    gap = corner_rows(ex)
    near, far = ex * 8 + 2 * gap + TAIL, 2 * gap + TAIL
    zface, *yfaces = call(
        functools.partial(chip_kernel, sb, sy), "chip", (VM,) * 3,
        [shape(count + TAIL, lanes)] + [shape(near, lanes), shape(far, lanes)] * faces,
        (ext, mine, core),
        [pltpu.VMEM((lanes // 128, count * 8, 128), F32),
         pltpu.VMEM((lanes // 128, count, 128), F32)], nbytes=10**6,
    )
    odd_z = pairing(nz, True, narrow)
    own_tail = zface
    zgot = lax.ppermute(zface, "gz", list(odd_z.items()))
    ygot = []
    for k in range(faces):
        along = pairing(ny, k == 1, False)
        ygot.append(lax.ppermute(yfaces[2 * k], "gy", list(along.items())))
        both = [
            (y * nz + z, along[y] * nz + odd_z[z]) for y in along for z in odd_z
        ]
        ygot.append(lax.ppermute(yfaces[2 * k + 1], ("gy", "gz"), both))

    cols, feats = qkv_weight.shape[1:]
    turned = call(
        turn_kernel, "turn", (VM,), shape(feats, 3 * cols), (qkv_weight,),
        flops=2 * 3 * cols * feats * feats, nbytes=6 * 10**6,
    )

    ey, oy = sy + 4, sy + 2
    size = (sx + 2) * oy * 8
    mid, mine, there = call(
        functools.partial(first_kernel, narrow, faces, sy, sb), "first",
        (VM,) * (7 + 2 * faces + len(stats)),
        [shape(size, lanes, dtype=F32), shape(devices, 128, dtype=F32),
         shape(ex * ey * 8, 128, dtype=F32)],
        (ext, own_tail, core, zgot, *ygot, *stats, keep, band0, rows),
        [pltpu.VMEM((lanes // 128, ex * ey * 8, 128), F32),
         pltpu.VMEM((ex * oy * 8, 4 * lanes), BF16)],
        flops=2 * 10**9, nbytes=4 * 10**6, mib=20,
    )
    stats = lax.all_to_all(mine, ALL, 0, 0, tiled=True)
    field, tokens, *parts = call(
        functools.partial(second_kernel, sx, sy, sb), "second", (VM,) * 6,
        [shape(sx * sy * 4, lanes), shape(own, feats)] + [shape(own // 2, feats)] * 2,
        (stats, mid, there, band1, rows, coded),
        [pltpu.VMEM(((sx + 2) * sy * 4, 4 * lanes), BF16)],
        flops=10**9, nbytes=4 * 10**6,
    )
    fine_out = call(
        fine_kernel, "fine", (VM,), shape(*features.shape), (field,), nbytes=4 * 10**6, mib=8,
    )
    swaps = [[(i, i ^ k) for i in range(nx)] for k in range(nx)]
    blocks = {0: parts}
    for k in sorted(range(1, nx), key=lambda k: (bin(k).count("1"), -k)):
        low = k & -k
        source = [tokens] if k == 1 else blocks[k ^ low]
        blocks[k] = [lax.ppermute(v, "gx", swaps[low]) for v in source]
    blocks = [tokens] + [v for k in range(1, nx) for v in blocks[k]]
    outs = call(
        functools.partial(attend_kernel, nx), "attend", (VM,) * (2 + len(blocks)),
        [shape(own, cols)] * nx, (keys, turned, *blocks),
        [pltpu.VMEM((own * nx, feats), BF16), pltpu.VMEM((own * nx, 3 * cols), BF16)],
        flops=10**9, nbytes=3 * 10**6, mib=16 if narrow else 40,
    )
    moved = [lax.ppermute(v, "gx", swaps[nx - 1 - i]) for i, v in enumerate(outs[:-1])]
    outs = moved + [outs[-1]]
    lined = cols % 128 == 0
    attention = call(
        functools.partial(place_kernel, nx), "place", (VM,) * (1 + nx),
        shape(1, own, nx * cols) if lined else shape(nx, own, cols), (keep, *outs),
        nbytes=3 * 10**5, mib=8,
    )
    if not lined:
        me = lax.axis_index("gx")
        attention = jnp.concatenate(
            [lax.dynamic_index_in_dim(attention, me ^ j, 0, keepdims=False) for j in range(nx)],
            axis=1,
        )[None]
    return (fine_out, attention)


def solution(mesh):
    placed = (
        P("gx", "gy", "gz", None),
        P(None, "gy", "gz"),
        P(),
        P(),
        P(),
        P(),
        P(None, "gx", None),
    )
    return jax.shard_map(
        body,
        mesh=mesh,
        in_specs=placed,
        out_specs=(P("gx", "gy", "gz", None), P(("gy", "gz"), "gx", None)),
        check_vma=False,
    )
```
